32 devices in a mesh: batch: 8 (over z, x), height: 4 (over y, core).
Axes of the slice: x: 2, y: 2, z: 4, core: 2. Of those that a mesh axis runs over, the one named last changes fastest.
Arguments:
- image_small: bfloat16 [96, 16, 10, 1024], P('batch', 'height'), may hold values from -6 to 6
- image_medium: bfloat16 [96, 24, 14, 1024], P('batch', 'height'), may hold values from -6 to 6
- image_large: bfloat16 [96, 32, 18, 1024], P('batch', 'height'), may hold values from -6 to 6
- row_counts: int32 [3, 4], replicated, may hold values from 1 to 4, as said below
- reduce_a: bfloat16 [1024, 512], replicated, may hold values from -0.1875 to 0.1875
- first_spatial_weight: bfloat16 [3, 3, 512, 512], replicated, may hold values from -0.09375 to 0.09375
- expand_a: bfloat16 [512, 2048], replicated, may hold values from -0.25 to 0.25
- shortcut_a: bfloat16 [1024, 2048], replicated, may hold values from -0.1875 to 0.1875
- reduce_b: bfloat16 [2048, 512], replicated, may hold values from -0.125 to 0.125
- second_spatial_weight: bfloat16 [3, 3, 512, 512], replicated, may hold values from -0.09375 to 0.09375
- expand_b: bfloat16 [512, 2048], replicated, may hold values from -0.25 to 0.25
- gain_mid: float32 [4, 512], replicated, may hold values from 0.25 to 1.75
- shift_mid: float32 [4, 512], replicated, may hold values from -3 to 3
- gain_out: float32 [3, 2048], replicated, may hold values from 0.25 to 1.75
- shift_out: float32 [3, 2048], replicated, may hold values from -3 to 3
- upstream_small: bfloat16 [96, 2048], P('batch'), may hold values from -6 to 6
- upstream_medium: bfloat16 [96, 2048], P('batch'), may hold values from -6 to 6
- upstream_large: bfloat16 [96, 2048], P('batch'), may hold values from -6 to 6
Outputs:
- pooled_small: float32 [96, 2048], P('batch')
- pooled_medium: float32 [96, 2048], P('batch')
- pooled_large: float32 [96, 2048], P('batch')
- back_small: bfloat16 [96, 16, 10, 1024], P('batch', 'height')
- back_medium: bfloat16 [96, 24, 14, 1024], P('batch', 'height')
- back_large: bfloat16 [96, 32, 18, 1024], P('batch', 'height')
- reduce_a_grad: float32 [1024, 512], P('batch')
- spatial_a_grad: float32 [3, 3, 512, 512], P(None, None, 'batch')
- expand_a_grad: float32 [512, 2048], P('batch')
- shortcut_a_grad: float32 [1024, 2048], P('batch')
- reduce_b_grad: float32 [2048, 512], P('batch')
- spatial_b_grad: float32 [3, 3, 512, 512], P(None, None, 'batch')
- expand_b_grad: float32 [512, 2048], P('batch')
- gain_mid_grad: float32 [4, 512], replicated
- shift_mid_grad: float32 [4, 512], replicated
- gain_out_grad: float32 [3, 2048], replicated
- shift_out_grad: float32 [3, 2048], replicated
The draws below stay inside these ranges and needn't reach their ends.
Inputs may be any that keep to these rules, and one draw needn't show every extreme that they name: Row g of row_counts gives the output rows of each band of height for group g (small, medium, large); row sums are 5, 7, 9; the largest entry of row g is exactly 2, 3, 4.
All inputs are finite; a program needn't handle non-finite values.
Results may differ from the reference program's by a relative error of at most 0.019.
Values may be sent and summed in bfloat16 or wider, within the bound.
A program may use at most 320 MiB of HBM per device.

```python
import jax
import jax.numpy as jnp
from jax import lax

C_IN = 1024
C_MID = 512
C_OUT = 2048
OUT_S = 5
OUT_M = 7
OUT_L = 9
CAP_S = 2
CAP_M = 3
CAP_L = 4
IMAGES = 96
N_HEIGHT = 4


def draw_row_counts(key, part):
    key = jax.random.fold_in(key, 1)
    patterns = jnp.array([[2, 1, 1, 1], [3, 2, 1, 1], [4, 3, 1, 1]], jnp.int32)
    rows_list = []
    for picture_batches in range(3):
        order = jax.random.permutation(jax.random.fold_in(key, picture_batches), N_HEIGHT).astype(jnp.int32)
        rows_list.append(jnp.take(patterns[picture_batches], order))
    return jnp.stack(rows_list).astype(jnp.int32)


def block_scale(rng, dims, split, low, high):
    level = 1.0
    for dim, shards_of in split:
        steps = jax.random.uniform(jax.random.fold_in(jax.random.fold_in(rng, 6), dim), (shards_of,), jnp.float32, low / len(split), high / len(split))
        level = level * jnp.repeat(jnp.exp(steps), dims[dim] // shards_of).reshape((-1,) + (1,) * (len(dims) - 1 - dim))
    return level


def scatter_about(rng, shape, scale, reach, pieces=(), kind=jnp.bfloat16):
    values = scale * jax.random.normal(rng, shape, jnp.float32)
    if pieces:
        values = values * block_scale(rng, shape, pieces, -0.22, 0.18)
    return jnp.clip(values, -reach, reach).astype(kind)


def setup_inputs(seed: int = 0) -> dict:
    key_list = jax.random.split(jax.random.key(seed), 19)
    return {
        "image_small": scatter_about(key_list[0], (IMAGES, 2 * CAP_S * N_HEIGHT, 2 * OUT_S, C_IN), 1.0, 6.0, ((0, 8), (1, 4))),
        "image_medium": scatter_about(key_list[1], (IMAGES, 2 * CAP_M * N_HEIGHT, 2 * OUT_M, C_IN), 1.0, 6.0, ((0, 8), (1, 4))),
        "image_large": scatter_about(key_list[2], (IMAGES, 2 * CAP_L * N_HEIGHT, 2 * OUT_L, C_IN), 1.0, 6.0, ((0, 8), (1, 4))),
        "row_counts": draw_row_counts(jax.random.fold_in(key_list[18], 71), 0),
        "reduce_a": scatter_about(key_list[4], (C_IN, C_MID), C_IN ** -0.5, 0.1875),
        "first_spatial_weight": scatter_about(key_list[5], (3, 3, C_MID, C_MID), (9 * C_MID) ** -0.5, 0.09375),
        "expand_a": scatter_about(key_list[6], (C_MID, C_OUT), C_MID ** -0.5, 0.25),
        "shortcut_a": scatter_about(key_list[7], (C_IN, C_OUT), C_IN ** -0.5, 0.1875),
        "reduce_b": scatter_about(key_list[8], (C_OUT, C_MID), C_OUT ** -0.5, 0.125),
        "second_spatial_weight": scatter_about(key_list[9], (3, 3, C_MID, C_MID), (9 * C_MID) ** -0.5, 0.09375),
        "expand_b": scatter_about(key_list[10], (C_MID, C_OUT), C_MID ** -0.5, 0.25),
        "gain_mid": jnp.clip(1.0 + 0.15 * jax.random.normal(key_list[11], (4, C_MID), jnp.float32), 0.25, 1.75),
        "shift_mid": scatter_about(key_list[12], (4, C_MID), 0.5, 3.0, (), jnp.float32),
        "gain_out": jnp.clip(1.0 + 0.15 * jax.random.normal(key_list[13], (3, C_OUT), jnp.float32), 0.25, 1.75),
        "shift_out": scatter_about(key_list[14], (3, C_OUT), 0.5, 3.0, (), jnp.float32),
        "upstream_small": scatter_about(key_list[15], (IMAGES, C_OUT), 1.0, 6.0, ((0, 8),)),
        "upstream_medium": scatter_about(key_list[16], (IMAGES, C_OUT), 1.0, 6.0, ((0, 8),)),
        "upstream_large": scatter_about(key_list[17], (IMAGES, C_OUT), 1.0, 6.0, ((0, 8),)),
    }


epsilon = 1e-05

@jax.custom_vjp
def low(v):
    return lax.optimization_barrier(v.astype(jnp.bfloat16)).astype(jnp.float32)

@jax.custom_vjp
def low_back(v):
    return v

def low_keep(v):
    return (low(v), None)

def low_pass(kept, grad):
    return (grad,)

def back_keep(v):
    return (v, None)

def back_low(kept, grad):
    return (low(grad),)
low.defvjp(low_keep, low_pass)
low_back.defvjp(back_keep, back_low)

def band_starts(counts):
    return (jnp.cumsum(counts) - counts).astype(jnp.int32)

def assemble(slab_data, counts):
    band_count = counts.shape[0]
    slab_rows = slab_data.shape[1] // band_count
    height = slab_data.shape[2]
    starts = (2 * band_starts(counts)).astype(jnp.int32)
    rows_all = jnp.arange(height, dtype=jnp.int32)
    owners = lax.optimization_barrier(jnp.sum((starts[None, 1:] <= rows_all[:, None]).astype(jnp.int32), axis=1)).astype(jnp.int32)
    source = (owners * slab_rows + rows_all - jnp.take(starts, owners)).astype(jnp.int32)
    return jnp.take(slab_data, source, axis=1)

def split_bands(whole, counts, slab_rows):
    band_count = counts.shape[0]
    height = whole.shape[1]
    starts = (2 * band_starts(counts)).astype(jnp.int32)
    slot_ids = jnp.arange(band_count * slab_rows, dtype=jnp.int32)
    owners = (slot_ids // slab_rows).astype(jnp.int32)
    offset = (slot_ids % slab_rows).astype(jnp.int32)
    live_mask = offset < 2 * jnp.take(counts, owners)
    source = jnp.minimum(jnp.take(starts, owners) + offset, height - 1).astype(jnp.int32)
    return jnp.take(whole, source, axis=1) * live_mask.astype(whole.dtype)[None, :, None, None]

def project(values, weight):
    return jnp.einsum('ihwc,cd->ihwd', values, weight, precision=lax.Precision.HIGHEST)

def spatial_kernel(values, weight, stride):
    out_rows = values.shape[1] // stride
    out_cols = values.shape[2] // stride
    if stride == 2:
        padded = jnp.pad(values, ((0, 0), (1, 0), (1, 0), (0, 0)))
    else:
        padded = jnp.pad(values, ((0, 0), (1, 1), (1, 1), (0, 0)))
    summed = None
    for row_tap in range(3):
        for col_tap in range(3):
            window = padded[:, row_tap:row_tap + stride * (out_rows - 1) + 1:stride, col_tap:col_tap + stride * (out_cols - 1) + 1:stride]
            product = project(window, weight[row_tap, col_tap])
            summed = product if summed is None else summed + product
    return summed

def normalize(tensors, gain, shift):
    number = sum((member.shape[0] * member.shape[1] * member.shape[2] for member in tensors))
    centre = sum((lax.optimization_barrier(jnp.sum(member, axis=(0, 1, 2))) for member in tensors)) / number
    square = sum((lax.optimization_barrier(jnp.sum(member * member, axis=(0, 1, 2))) for member in tensors)) / number
    factor = lax.rsqrt(square - centre * centre + epsilon) * gain
    return [(member - centre) * factor + shift for member in tensors]

def forward(pictures, reduce_a, first_spatial_weight, expand_a, shortcut_a, reduce_b, second_spatial_weight, expand_b, gain_mid, shift_mid, gain_out, shift_out):
    first_out = [low_back(project(picture, reduce_a)) for picture in pictures]
    act_one = [low(jax.nn.silu(member)) for member in normalize(first_out, gain_mid[0], shift_mid[0])]
    second_out = [low_back(spatial_kernel(member, first_spatial_weight, 2)) for member in act_one]
    act_two = [low(jax.nn.silu(member)) for member in normalize(second_out, gain_mid[1], shift_mid[1])]
    third_out = [low_back(project(member, expand_a)) for member in act_two]
    side_out = [low_back(project(picture[:, ::2, ::2], shortcut_a)) for picture in pictures]
    main_normed = normalize(third_out, gain_out[0], shift_out[0])
    side_normed = normalize(side_out, gain_out[1], shift_out[1])
    middle = [jax.nn.silu(main_part + side_part) for main_part, side_part in zip(main_normed, side_normed)]
    fourth_out = [low_back(project(low(member), reduce_b)) for member in middle]
    act_four = [low(jax.nn.silu(member)) for member in normalize(fourth_out, gain_mid[2], shift_mid[2])]
    fifth_out = [low_back(spatial_kernel(member, second_spatial_weight, 1)) for member in act_four]
    act_five = [low(jax.nn.silu(member)) for member in normalize(fifth_out, gain_mid[3], shift_mid[3])]
    sixth_out = [low_back(project(member, expand_b)) for member in act_five]
    last_normed = normalize(sixth_out, gain_out[2], shift_out[2])
    final = [jax.nn.silu(main_part + skip_part) for main_part, skip_part in zip(last_normed, middle)]
    return tuple((lax.optimization_barrier(jnp.mean(member, axis=(1, 2))) for member in final))

def reference(image_small, image_medium, image_large, row_counts, reduce_a, first_spatial_weight, expand_a, shortcut_a, reduce_b, second_spatial_weight, expand_b, gain_mid, shift_mid, gain_out, shift_out, upstream_small, upstream_medium, upstream_large):
    slabs = (image_small, image_medium, image_large)
    wholes = [assemble(slabs[picture_batches].astype(jnp.float32), row_counts[picture_batches]) for picture_batches in range(3)]
    weight_list = [member.astype(jnp.float32) for member in (reduce_a, first_spatial_weight, expand_a, shortcut_a, reduce_b, second_spatial_weight, expand_b)]
    pooled, pullback = jax.vjp(forward, wholes, *weight_list, gain_mid, shift_mid, gain_out, shift_out)
    gradients = pullback((upstream_small.astype(jnp.float32), upstream_medium.astype(jnp.float32), upstream_large.astype(jnp.float32)))
    backs = [split_bands(gradients[0][picture_batches], row_counts[picture_batches], slabs[picture_batches].shape[1] // row_counts.shape[1]).astype(jnp.bfloat16) for picture_batches in range(3)]
    return (pooled[0], pooled[1], pooled[2], backs[0], backs[1], backs[2], gradients[1], gradients[2], gradients[3], gradients[4], gradients[5], gradients[6], gradients[7], gradients[8], gradients[9], gradients[10], gradients[11])
```

```python
import functools

import jax
import jax.numpy as jnp
from jax import lax
from jax.experimental import pallas as pl
from jax.experimental.pallas import tpu as pltpu
from jax.sharding import PartitionSpec as P

epsilon = 1e-05

MESH = pl.DeviceIdType.MESH


def sum_kernel(n_batch, n_height, value_ref, out_ref, height_slots, batch_slots, send_sem, recv_sem):
    b, h = lax.axis_index("batch"), lax.axis_index("height")
    barrier = pltpu.get_barrier_semaphore()
    for k in range(1, n_height):
        pl.semaphore_signal(
            barrier, inc=1, device_id=(b, lax.rem(h + k, n_height)), device_id_type=MESH
        )

    @pl.loop(1, n_batch)
    def _(k):
        pl.semaphore_signal(
            barrier, inc=1, device_id=(lax.rem(b + k, n_batch), h), device_id_type=MESH
        )

    pl.semaphore_wait(barrier, n_height + n_batch - 2)
    for slots, me, count, level, peer in (
        (height_slots, h, n_height, 0, lambda p: (b, p)),
        (batch_slots, b, n_batch, 1, lambda p: (p, h)),
    ):
        slots[me] = value_ref[...] if level == 0 else jnp.sum(height_slots[...], axis=0)

        @pl.loop(1, count)
        def _(k):
            pltpu.make_async_remote_copy(
                src_ref=slots.at[me],
                dst_ref=slots.at[me],
                send_sem=send_sem.at[level],
                recv_sem=recv_sem.at[level],
                device_id=peer(lax.rem(me + k, count)),
                device_id_type=MESH,
            ).start()

        others = slots.at[0 : count - 1]
        pltpu.make_async_copy(others, others, send_sem.at[level]).wait()
        pltpu.make_async_copy(others, others, recv_sem.at[level]).wait()
    out_ref[...] = jnp.sum(batch_slots[...], axis=0)


def sum_over_all(stacked):
    flat = (stacked.size // 128, 128)
    n_batch, n_height = lax.axis_size("batch"), lax.axis_size("height")
    summed = pl.pallas_call(
        functools.partial(sum_kernel, n_batch, n_height),
        out_shape=jax.ShapeDtypeStruct(flat, jnp.float32),
        in_specs=[pl.BlockSpec(memory_space=pltpu.VMEM)],
        out_specs=pl.BlockSpec(memory_space=pltpu.VMEM),
        scratch_shapes=[
            pltpu.VMEM((n_height,) + flat, jnp.float32),
            pltpu.VMEM((n_batch,) + flat, jnp.float32),
            pltpu.SemaphoreType.DMA((2,)),
            pltpu.SemaphoreType.DMA((2,)),
        ],
        compiler_params=pltpu.CompilerParams(
            collective_id=stacked.size.bit_length() - 10, has_side_effects=True
        ),
        name="sum_over_all",
    )(stacked.reshape(flat))
    return summed.reshape(stacked.shape)


def passed_along(value, axis, steps):
    count = lax.axis_size(axis)
    first, last = (max(0, -steps), min(count, count - steps))
    return lax.ppermute(value, axis, [(source, source + steps) for source in range(first, last)])


def extended(value, sides, width):
    for axis, dim in sides:
        peers, length = (lax.axis_size(axis), value.shape[dim])
        up = [(i, (i + 1) % peers) for i in range(peers - 1)]
        down = [(j, i) for i, j in up]
        last = lax.slice_in_dim(value, length - width, length, axis=dim)
        first = lax.slice_in_dim(value, 0, width, axis=dim)
        before = lax.ppermute(last, axis, up)
        after = lax.ppermute(first, axis, down)
        value = jnp.concatenate([before, value, after], axis=dim)
    return value


def sigmoid_slope(values):
    logistic = jax.nn.sigmoid(values)
    return logistic * (1.0 + values * (1.0 - logistic))


def project(values, weight):
    return jnp.einsum("hwic,cd->hwid", values, weight, preferred_element_type=jnp.float32)


def project_back(grad_in, weight):
    return jnp.einsum("hwid,cd->hwic", grad_in, weight, preferred_element_type=jnp.float32)


def weight_term(values, grad_in):
    return jnp.einsum("hwic,hwid->cd", values, grad_in, preferred_element_type=jnp.float32)


def tap_window(padded, stride, out_rows, out_cols, row_tap, col_tap):
    return padded[
        row_tap : row_tap + stride * (out_rows - 1) + 1 : stride,
        col_tap : col_tap + stride * (out_cols - 1) + 1 : stride,
    ]


def spatial_kernel(padded, weight, stride, out_rows, out_cols):
    summed = None
    for row_tap in range(3):
        for col_tap in range(3):
            product = project(
                tap_window(padded, stride, out_rows, out_cols, row_tap, col_tap),
                weight[row_tap, col_tap],
            )
            summed = product if summed is None else summed + product
    return summed


def spatial_back(padded, weight, grad_in, stride, out_rows, out_cols):
    padded_grad = jnp.zeros(padded.shape, jnp.float32)
    tap_grads = []
    for row_tap in range(3):
        row_list = []
        for col_tap in range(3):
            window = tap_window(padded, stride, out_rows, out_cols, row_tap, col_tap)
            row_list.append(weight_term(window, grad_in))
            padded_grad = padded_grad.at[
                row_tap : row_tap + stride * (out_rows - 1) + 1 : stride,
                col_tap : col_tap + stride * (out_cols - 1) + 1 : stride,
            ].add(project_back(grad_in, weight[row_tap, col_tap]))
        tap_grads.append(jnp.stack(row_list))
    return (jnp.stack(tap_grads), padded_grad)


def gather_stats(levels, numbers):
    local_sums = []
    for tensors in levels:
        local_sums.append(sum((jnp.sum(member, axis=(0, 1, 2)) for member in tensors)))
        local_sums.append(sum((jnp.sum(member * member, axis=(0, 1, 2)) for member in tensors)))
    summed = sum_over_all(jnp.stack(local_sums))
    result = []
    for position in range(len(levels)):
        centre = summed[2 * position] / numbers[position]
        square = summed[2 * position + 1] / numbers[position]
        result.append((centre, lax.rsqrt(square - centre * centre + epsilon)))
    return result


def grad_stats(triples):
    local_sums = []
    for grad_list, value_list, stat in triples:
        centre, inv_root = stat
        local_sums.append(
            sum(
                (
                    jnp.sum(grad_list[picture_batches], axis=(0, 1, 2))
                    for picture_batches in range(3)
                )
            )
        )
        local_sums.append(
            sum(
                (
                    jnp.sum(
                        grad_list[picture_batches]
                        * (value_list[picture_batches] - centre)
                        * inv_root,
                        axis=(0, 1, 2),
                    )
                    for picture_batches in range(3)
                )
            )
        )
    summed = sum_over_all(jnp.stack(local_sums))
    return [(summed[2 * position], summed[2 * position + 1]) for position in range(len(triples))]


def apply_norm(values, stat, gain, shift):
    centre, inv_root = stat
    return (values - centre) * (inv_root * gain) + shift


def norm_back(grad_in, values, stat, gain, grad_sums, number):
    centre, inv_root = stat
    normed = (values - centre) * inv_root
    return gain * inv_root * (grad_in - grad_sums[0] / number - normed * (grad_sums[1] / number))


def per_device(
    image_small,
    image_medium,
    image_large,
    row_counts,
    reduce_a,
    first_spatial_weight,
    expand_a,
    shortcut_a,
    reduce_b,
    second_spatial_weight,
    expand_b,
    gain_mid,
    shift_mid,
    gain_out,
    shift_out,
    upstream_small,
    upstream_medium,
    upstream_large,
):
    raw_images = tuple(jnp.transpose(v, (1, 2, 0, 3)) for v in (image_small, image_medium, image_large))
    upstreams = (upstream_small, upstream_medium, upstream_large)
    band_index = lax.axis_index("height")
    batch_devices = lax.axis_size("batch")
    entering_photos, entering_filters, line_filters, genuine_lines, edge_extents, bucket_limits = (
        [],
        [],
        [],
        [],
        [],
        [],
    )
    total_in = 0
    total_out = 0
    for picture_batches in range(3):
        slab_rows = raw_images[picture_batches].shape[0]
        bucket_limit = slab_rows // 2
        out_side = raw_images[picture_batches].shape[1] // 2
        live = row_counts[picture_batches, band_index]
        mask_low = (jnp.arange(slab_rows, dtype=jnp.int32) < 2 * live).astype(jnp.bfloat16)[

            :, None, None, None
        ]
        entering_photos.append(raw_images[picture_batches] * mask_low)
        entering_filters.append(mask_low.astype(jnp.float32))
        line_filters.append(
            (jnp.arange(bucket_limit, dtype=jnp.int32) < live).astype(jnp.float32)[
            :, None, None, None
            ]
        )
        genuine_lines.append(live)
        edge_extents.append(out_side)
        bucket_limits.append(bucket_limit)
        total_in += batch_devices * raw_images[picture_batches].shape[2] * 4 * out_side * out_side
        total_out += batch_devices * raw_images[picture_batches].shape[2] * out_side * out_side
    width_cuts = [edge_extents[0], edge_extents[0] + edge_extents[1]]
    input_cuts = [2 * edge_extents[0], 2 * edge_extents[0] + 2 * edge_extents[1]]
    first_out = [
        project(entering_photos[picture_batches], reduce_a) for picture_batches in range(3)
    ]
    (stat_one,) = gather_stats([first_out], [total_in])
    pre_one = [
        apply_norm(first_out[picture_batches], stat_one, gain_mid[0], shift_mid[0])
        for picture_batches in range(3)
    ]
    act_one = [
        (jax.nn.silu(pre_one[picture_batches]) * entering_filters[picture_batches]).astype(
            jnp.bfloat16
        )
        for picture_batches in range(3)
    ]
    tail_rows = [
        lax.dynamic_index_in_dim(
            act_one[picture_batches], 2 * genuine_lines[picture_batches] - 1, 0, keepdims=False
        )
        for picture_batches in range(3)
    ]
    rim_rows = passed_along(jnp.concatenate(tail_rows, axis=0), "height", 1)
    rim_parts = jnp.split(rim_rows, input_cuts, axis=0)
    first_padded = []
    for picture_batches in range(3):
        joined = jnp.concatenate(
            [rim_parts[picture_batches][None], act_one[picture_batches]], axis=0
        )
        first_padded.append(jnp.pad(joined, ((0, 0), (1, 0), (0, 0), (0, 0))))
    second_out = [
        spatial_kernel(
            first_padded[picture_batches],
            first_spatial_weight,
            2,
            bucket_limits[picture_batches],
            edge_extents[picture_batches],
        )
        * line_filters[picture_batches]
        for picture_batches in range(3)
    ]
    (stat_two,) = gather_stats([second_out], [total_out])
    pre_two = [
        apply_norm(second_out[picture_batches], stat_two, gain_mid[1], shift_mid[1])
        for picture_batches in range(3)
    ]
    act_two = [
        (jax.nn.silu(pre_two[picture_batches]) * line_filters[picture_batches]).astype(jnp.bfloat16)
        for picture_batches in range(3)
    ]
    third_out = [project(act_two[picture_batches], expand_a) for picture_batches in range(3)]
    side_inputs = [entering_photos[picture_batches][::2, ::2] for picture_batches in range(3)]
    side_out = [project(side_inputs[picture_batches], shortcut_a) for picture_batches in range(3)]
    stat_three, stat_side = gather_stats([third_out, side_out], [total_out, total_out])
    joint_one = [
        apply_norm(third_out[picture_batches], stat_three, gain_out[0], shift_out[0])
        + apply_norm(side_out[picture_batches], stat_side, gain_out[1], shift_out[1])
        for picture_batches in range(3)
    ]
    middle = [
        jax.nn.silu(joint_one[picture_batches]) * line_filters[picture_batches]
        for picture_batches in range(3)
    ]
    middle_low = [middle[picture_batches].astype(jnp.bfloat16) for picture_batches in range(3)]
    fourth_out = [project(middle_low[picture_batches], reduce_b) for picture_batches in range(3)]
    (stat_four,) = gather_stats([fourth_out], [total_out])
    pre_four = [
        apply_norm(fourth_out[picture_batches], stat_four, gain_mid[2], shift_mid[2])
        for picture_batches in range(3)
    ]
    act_four = [
        (jax.nn.silu(pre_four[picture_batches]) * line_filters[picture_batches]).astype(
            jnp.bfloat16
        )
        for picture_batches in range(3)
    ]
    edge_pairs = [
        jnp.stack(
            [
                act_four[picture_batches][0],
                lax.dynamic_index_in_dim(
                    act_four[picture_batches], genuine_lines[picture_batches] - 1, 0, keepdims=False
                ),
            ],
            axis=0,
        )
        for picture_batches in range(3)
    ]
    rim_pairs = extended(jnp.concatenate(edge_pairs, axis=1), (("height", 0),), 1)
    pair_parts = jnp.split(rim_pairs, width_cuts, axis=1)
    fourth_padded = []
    for picture_batches in range(3):
        rim_pair = pair_parts[picture_batches]
        joined = jnp.concatenate(
            [rim_pair[0:1], act_four[picture_batches], jnp.zeros_like(rim_pair[0:1])], axis=0
        )
        joined = lax.dynamic_update_slice_in_dim(
            joined, rim_pair[3:4], genuine_lines[picture_batches] + 1, 0
        )
        fourth_padded.append(jnp.pad(joined, ((0, 0), (1, 1), (0, 0), (0, 0))))
    fifth_out = [
        spatial_kernel(
            fourth_padded[picture_batches],
            second_spatial_weight,
            1,
            bucket_limits[picture_batches],
            edge_extents[picture_batches],
        )
        * line_filters[picture_batches]
        for picture_batches in range(3)
    ]
    (stat_five,) = gather_stats([fifth_out], [total_out])
    pre_five = [
        apply_norm(fifth_out[picture_batches], stat_five, gain_mid[3], shift_mid[3])
        for picture_batches in range(3)
    ]
    act_five = [
        (jax.nn.silu(pre_five[picture_batches]) * line_filters[picture_batches]).astype(
            jnp.bfloat16
        )
        for picture_batches in range(3)
    ]
    sixth_out = [project(act_five[picture_batches], expand_b) for picture_batches in range(3)]
    (stat_six,) = gather_stats([sixth_out], [total_out])
    joint_two = [
        apply_norm(sixth_out[picture_batches], stat_six, gain_out[2], shift_out[2])
        + middle[picture_batches]
        for picture_batches in range(3)
    ]
    final = [
        jax.nn.silu(joint_two[picture_batches]) * line_filters[picture_batches]
        for picture_batches in range(3)
    ]
    pooled_sums = lax.psum(
        jnp.stack(
            [jnp.sum(final[picture_batches], axis=(0, 1)) for picture_batches in range(3)]
        ).astype(jnp.bfloat16),
        "height",
    ).astype(jnp.float32)
    pooled = [
        pooled_sums[picture_batches]
        / (edge_extents[picture_batches] * edge_extents[picture_batches])
        for picture_batches in range(3)
    ]
    d_joint_two = [
        upstreams[picture_batches].astype(jnp.float32)[None, None]
        / (edge_extents[picture_batches] * edge_extents[picture_batches])
        * line_filters[picture_batches]
        * sigmoid_slope(joint_two[picture_batches])
        for picture_batches in range(3)
    ]
    (sums_six,) = grad_stats([(d_joint_two, sixth_out, stat_six)])
    grad_six = [
        (
            norm_back(
                d_joint_two[picture_batches],
                sixth_out[picture_batches],
                stat_six,
                gain_out[2],
                sums_six,
                total_out,
            )
            * line_filters[picture_batches]
        ).astype(jnp.bfloat16)
        for picture_batches in range(3)
    ]
    expand_b_local = sum(
        (
            weight_term(act_five[picture_batches], grad_six[picture_batches])
            for picture_batches in range(3)
        )
    )
    d_five = [
        project_back(grad_six[picture_batches], expand_b)
        * sigmoid_slope(pre_five[picture_batches])
        * line_filters[picture_batches]
        for picture_batches in range(3)
    ]
    (sums_five,) = grad_stats([(d_five, fifth_out, stat_five)])
    fifth_gradient = [
        (
            norm_back(
                d_five[picture_batches],
                fifth_out[picture_batches],
                stat_five,
                gain_mid[3],
                sums_five,
                total_out,
            )
            * line_filters[picture_batches]
        ).astype(jnp.bfloat16)
        for picture_batches in range(3)
    ]
    spatial_b_local = None
    d_swish_four = []
    edge_grads = []
    for picture_batches in range(3):
        tap_grad, padded_grad = spatial_back(
            fourth_padded[picture_batches],
            second_spatial_weight,
            fifth_gradient[picture_batches],
            1,
            bucket_limits[picture_batches],
            edge_extents[picture_batches],
        )
        spatial_b_local = tap_grad if spatial_b_local is None else spatial_b_local + tap_grad
        central_block = padded_grad[:, 1:-1]
        top_grad = central_block[0]
        below_grad = lax.dynamic_index_in_dim(
            central_block, genuine_lines[picture_batches] + 1, 0, keepdims=False
        )
        d_swish_four.append(central_block[1 : bucket_limits[picture_batches] + 1])
        edge_grads.append(jnp.stack([top_grad, below_grad], axis=0))
    returned = extended(
        jnp.concatenate(edge_grads, axis=1).astype(jnp.bfloat16), (("height", 0),), 1
    ).astype(jnp.float32)
    returned_parts = jnp.split(returned, width_cuts, axis=1)
    d_four = []
    for picture_batches in range(3):
        grad_rows = (
            d_swish_four[picture_batches].at[0].add(returned_parts[picture_batches][0])
        )
        last_row = (
            lax.dynamic_index_in_dim(
                grad_rows, genuine_lines[picture_batches] - 1, 0, keepdims=False
            )
            + returned_parts[picture_batches][3]
        )
        grad_rows = lax.dynamic_update_index_in_dim(
            grad_rows, last_row, genuine_lines[picture_batches] - 1, 0
        )
        d_four.append(
            grad_rows * sigmoid_slope(pre_four[picture_batches]) * line_filters[picture_batches]
        )
    (sums_four,) = grad_stats([(d_four, fourth_out, stat_four)])
    grad_four = [
        (
            norm_back(
                d_four[picture_batches],
                fourth_out[picture_batches],
                stat_four,
                gain_mid[2],
                sums_four,
                total_out,
            )
            * line_filters[picture_batches]
        ).astype(jnp.bfloat16)
        for picture_batches in range(3)
    ]
    reduce_b_local = sum(
        (
            weight_term(middle_low[picture_batches], grad_four[picture_batches])
            for picture_batches in range(3)
        )
    )
    d_joint_one = [
        (project_back(grad_four[picture_batches], reduce_b) + d_joint_two[picture_batches])
        * sigmoid_slope(joint_one[picture_batches])
        * line_filters[picture_batches]
        for picture_batches in range(3)
    ]
    sums_three, sums_side = grad_stats(
        [(d_joint_one, third_out, stat_three), (d_joint_one, side_out, stat_side)]
    )
    grad_three = [
        (
            norm_back(
                d_joint_one[picture_batches],
                third_out[picture_batches],
                stat_three,
                gain_out[0],
                sums_three,
                total_out,
            )
            * line_filters[picture_batches]
        ).astype(jnp.bfloat16)
        for picture_batches in range(3)
    ]
    grad_side = [
        (
            norm_back(
                d_joint_one[picture_batches],
                side_out[picture_batches],
                stat_side,
                gain_out[1],
                sums_side,
                total_out,
            )
            * line_filters[picture_batches]
        ).astype(jnp.bfloat16)
        for picture_batches in range(3)
    ]
    expand_a_local = sum(
        (
            weight_term(act_two[picture_batches], grad_three[picture_batches])
            for picture_batches in range(3)
        )
    )
    shortcut_a_local = sum(
        (
            weight_term(side_inputs[picture_batches], grad_side[picture_batches])
            for picture_batches in range(3)
        )
    )
    d_two = [
        project_back(grad_three[picture_batches], expand_a)
        * sigmoid_slope(pre_two[picture_batches])
        * line_filters[picture_batches]
        for picture_batches in range(3)
    ]
    (sums_two,) = grad_stats([(d_two, second_out, stat_two)])
    second_gradient = [
        (
            norm_back(
                d_two[picture_batches],
                second_out[picture_batches],
                stat_two,
                gain_mid[1],
                sums_two,
                total_out,
            )
            * line_filters[picture_batches]
        ).astype(jnp.bfloat16)
        for picture_batches in range(3)
    ]
    spatial_a_local = None
    d_act_one = []
    rim_grads = []
    for picture_batches in range(3):
        tap_grad, padded_grad = spatial_back(
            first_padded[picture_batches],
            first_spatial_weight,
            second_gradient[picture_batches],
            2,
            bucket_limits[picture_batches],
            edge_extents[picture_batches],
        )
        spatial_a_local = tap_grad if spatial_a_local is None else spatial_a_local + tap_grad
        rim_grads.append(padded_grad[0, 1:])
        d_act_one.append(padded_grad[1:, 1:])
    rim_back = passed_along(
        jnp.concatenate(rim_grads, axis=0).astype(jnp.bfloat16), "height", -1
    ).astype(jnp.float32)
    rim_back_parts = jnp.split(rim_back, input_cuts, axis=0)
    d_one = []
    for picture_batches in range(3):
        row_place = 2 * genuine_lines[picture_batches] - 1
        last_row = (
            lax.dynamic_index_in_dim(d_act_one[picture_batches], row_place, 0, keepdims=False)
            + rim_back_parts[picture_batches]
        )
        grad_rows = lax.dynamic_update_index_in_dim(
            d_act_one[picture_batches], last_row, row_place, 0
        )
        d_one.append(
            grad_rows * sigmoid_slope(pre_one[picture_batches]) * entering_filters[picture_batches]
        )
    (sums_one,) = grad_stats([(d_one, first_out, stat_one)])
    grad_one = [
        (
            norm_back(
                d_one[picture_batches],
                first_out[picture_batches],
                stat_one,
                gain_mid[0],
                sums_one,
                total_in,
            )
            * entering_filters[picture_batches]
        ).astype(jnp.bfloat16)
        for picture_batches in range(3)
    ]
    reduce_a_local = sum(
        (
            weight_term(entering_photos[picture_batches], grad_one[picture_batches])
            for picture_batches in range(3)
        )
    )
    backs = []
    for picture_batches in range(3):
        image_grad = project_back(grad_one[picture_batches], reduce_a)
        image_grad = image_grad.at[::2, ::2].add(
            project_back(grad_side[picture_batches], shortcut_a)
        )
        backs.append(jnp.transpose(image_grad.astype(jnp.bfloat16), (2, 0, 1, 3)))
    shards = (
        lax.psum_scatter(reduce_a_local, "batch", scatter_dimension=0, tiled=True),
        lax.psum_scatter(spatial_a_local, "batch", scatter_dimension=2, tiled=True),
        lax.psum_scatter(expand_a_local, "batch", scatter_dimension=0, tiled=True),
        lax.psum_scatter(shortcut_a_local, "batch", scatter_dimension=0, tiled=True),
        lax.psum_scatter(reduce_b_local, "batch", scatter_dimension=0, tiled=True),
        lax.psum_scatter(spatial_b_local, "batch", scatter_dimension=2, tiled=True),
        lax.psum_scatter(expand_b_local, "batch", scatter_dimension=0, tiled=True),
    )
    shards = (
        lax.psum(shards[0].astype(jnp.bfloat16), "height").astype(jnp.float32),
        lax.psum(shards[1].astype(jnp.bfloat16), "height").astype(jnp.float32),
        lax.psum(shards[2].astype(jnp.bfloat16), "height").astype(jnp.float32),
        lax.psum(shards[3].astype(jnp.bfloat16), "height").astype(jnp.float32),
        lax.psum(shards[4].astype(jnp.bfloat16), "height").astype(jnp.float32),
        lax.psum(shards[5].astype(jnp.bfloat16), "height").astype(jnp.float32),
        lax.psum(shards[6].astype(jnp.bfloat16), "height").astype(jnp.float32),
    )
    gain_mid_grad = jnp.stack([sums_one[1], sums_two[1], sums_four[1], sums_five[1]])
    shift_mid_grad = jnp.stack([sums_one[0], sums_two[0], sums_four[0], sums_five[0]])
    gain_out_grad = jnp.stack([sums_three[1], sums_side[1], sums_six[1]])
    shift_out_grad = jnp.stack([sums_three[0], sums_side[0], sums_six[0]])
    return (
        pooled[0],
        pooled[1],
        pooled[2],
        backs[0],
        backs[1],
        backs[2],
        shards[0],
        shards[1],
        shards[2],
        shards[3],
        shards[4],
        shards[5],
        shards[6],
        gain_mid_grad,
        shift_mid_grad,
        gain_out_grad,
        shift_out_grad,
    )


def solution(mesh):
    placed = (
        P("batch", "height", None, None),
        P("batch", "height", None, None),
        P("batch", "height", None, None),
        P(),
        P(),
        P(),
        P(),
        P(),
        P(),
        P(),
        P(),
        P(),
        P(),
        P(),
        P(),
        P("batch", None),
        P("batch", None),
        P("batch", None),
    )
    return jax.shard_map(
        per_device,
        mesh=mesh,
        in_specs=placed,
        out_specs=(
            P("batch", None),
            P("batch", None),
            P("batch", None),
            P("batch", "height", None, None),
            P("batch", "height", None, None),
            P("batch", "height", None, None),
            P("batch", None),
            P(None, None, "batch", None),
            P("batch", None),
            P("batch", None),
            P("batch", None),
            P(None, None, "batch", None),
            P("batch", None),
            P(),
            P(),
            P(),
            P(),
        ),
        check_vma=False,
    )
```

```python
import functools

import jax
import jax.numpy as jnp
from jax import lax
from jax.experimental import pallas as pl
from jax.experimental.pallas import tpu as pltpu
from jax.sharding import PartitionSpec as P

epsilon = 1e-05

MESH = pl.DeviceIdType.MESH


def sum_kernel(n_batch, n_height, value_ref, out_ref, height_slots, batch_slots, send_sem, recv_sem):
    b, h = lax.axis_index("batch"), lax.axis_index("height")
    barrier = pltpu.get_barrier_semaphore()
    for k in range(1, n_height):
        pl.semaphore_signal(
            barrier, inc=1, device_id=(b, lax.rem(h + k, n_height)), device_id_type=MESH
        )

    @pl.loop(1, n_batch)
    def _(k):
        pl.semaphore_signal(
            barrier, inc=1, device_id=(lax.rem(b + k, n_batch), h), device_id_type=MESH
        )

    pl.semaphore_wait(barrier, n_height + n_batch - 2)
    for slots, me, count, level, peer in (
        (height_slots, h, n_height, 0, lambda p: (b, p)),
        (batch_slots, b, n_batch, 1, lambda p: (p, h)),
    ):
        slots[me] = value_ref[...] if level == 0 else jnp.sum(height_slots[...], axis=0)

        @pl.loop(1, count)
        def _(k):
            pltpu.make_async_remote_copy(
                src_ref=slots.at[me],
                dst_ref=slots.at[me],
                send_sem=send_sem.at[level],
                recv_sem=recv_sem.at[level],
                device_id=peer(lax.rem(me + k, count)),
                device_id_type=MESH,
            ).start()

        others = slots.at[0 : count - 1]
        pltpu.make_async_copy(others, others, send_sem.at[level]).wait()
        pltpu.make_async_copy(others, others, recv_sem.at[level]).wait()
    out_ref[...] = jnp.sum(batch_slots[...], axis=0)


def sum_over_all(stacked):
    flat = (stacked.size // 128, 128)
    n_batch, n_height = lax.axis_size("batch"), lax.axis_size("height")
    summed = pl.pallas_call(
        functools.partial(sum_kernel, n_batch, n_height),
        out_shape=jax.ShapeDtypeStruct(flat, jnp.float32),
        in_specs=[pl.BlockSpec(memory_space=pltpu.VMEM)],
        out_specs=pl.BlockSpec(memory_space=pltpu.VMEM),
        scratch_shapes=[
            pltpu.VMEM((n_height,) + flat, jnp.float32),
            pltpu.VMEM((n_batch,) + flat, jnp.float32),
            pltpu.SemaphoreType.DMA((2,)),
            pltpu.SemaphoreType.DMA((2,)),
        ],
        compiler_params=pltpu.CompilerParams(
            collective_id=stacked.size.bit_length() - 10, has_side_effects=True
        ),
        name="sum_over_all",
    )(stacked.reshape(flat))
    return summed.reshape(stacked.shape)


N_CHUNKS = 10


def grads_kernel(n_batch, local_ref, out_ref, g, r0, r1, r2, r3, load_sem, send_sem, recv_sem):
    b, h = lax.axis_index("batch"), lax.axis_index("height")
    core, high = lax.rem(h, 2), h // 2
    low, rest = lax.rem(b, 2), b // 2
    n_rest = n_batch // 2
    first = core * low + (1 - core) * high
    second = core * high + (1 - core) * low
    core_peer = (b, h + 1 - 2 * core)
    high_peer = (b, h + 2 - 4 * high)
    low_peer = (b + 1 - 2 * low, h)
    first_peer = (
        core * low_peer[0] + (1 - core) * high_peer[0],
        core * low_peer[1] + (1 - core) * high_peer[1],
    )
    second_peer = (
        core * high_peer[0] + (1 - core) * low_peer[0],
        core * high_peer[1] + (1 - core) * low_peer[1],
    )

    def rest_peer(k):
        return (lax.rem(rest + k, n_rest) * 2 + low, h)

    def load(c):
        return pltpu.make_async_copy(local_ref.at[c], g.at[c], load_sem.at[c])

    for c in range(N_CHUNKS):
        load(c).start()
    barrier = pltpu.get_barrier_semaphore()
    for peer in (core_peer, high_peer, low_peer):
        pl.semaphore_signal(barrier, inc=1, device_id=peer, device_id_type=MESH)

    @pl.loop(1, n_rest)
    def _(k):
        pl.semaphore_signal(barrier, inc=1, device_id=rest_peer(k), device_id_type=MESH)

    pl.semaphore_wait(barrier, 3 + n_rest - 1)

    def copy(level, c, source, target, peer):
        return pltpu.make_async_remote_copy(
            src_ref=source,
            dst_ref=target,
            send_sem=send_sem.at[level, c],
            recv_sem=recv_sem.at[level, c],
            device_id=peer,
            device_id_type=MESH,
        )

    def hop(level, c):
        if level == 0:
            return copy(0, c, g.at[c, 1 - core], r0.at[c], core_peer)
        if level == 1:
            return copy(1, c, g.at[c, core, 1 - first], r1.at[c], first_peer)
        if level == 2:
            return copy(2, c, g.at[c, core, first, 1 - second], r2.at[c], second_peer)
        if level == 4:
            mine = out_ref.at[c, core, high]
            return copy(4, c, mine, mine, high_peer)
        both = out_ref.at[c, core]
        return copy(5, c, both, both, core_peer)

    def add(target, source):
        target[...] = (target[...].astype(jnp.float32) + source[...].astype(jnp.float32)).astype(
            jnp.bfloat16
        )

    def others(c):
        return r3.at[c, 0 : n_rest - 1]

    @pl.loop(0, N_CHUNKS + 6)
    def _(step):
        @pl.when(step < N_CHUNKS)
        def _():
            load(step).wait()
            hop(0, step).start()

        c1 = step - 1

        @pl.when(jnp.logical_and(c1 >= 0, c1 < N_CHUNKS))
        def _():
            hop(0, c1).wait_recv()

            @pl.loop(0, 2)
            def _(i):
                @pl.loop(0, 2)
                def _(j):
                    @pl.loop(0, n_rest)
                    def _(k):
                        add(g.at[c1, core, i, j, k], r0.at[c1, i, j, k])

            hop(1, c1).start()

        c2 = step - 2

        @pl.when(jnp.logical_and(c2 >= 0, c2 < N_CHUNKS))
        def _():
            hop(1, c2).wait_recv()

            @pl.loop(0, 2)
            def _(j):
                @pl.loop(0, n_rest)
                def _(k):
                    add(g.at[c2, core, first, j, k], r1.at[c2, j, k])

            hop(2, c2).start()

        c3 = step - 3

        @pl.when(jnp.logical_and(c3 >= 0, c3 < N_CHUNKS))
        def _():
            hop(2, c3).wait_recv()

            @pl.loop(0, n_rest)
            def _(k):
                add(g.at[c3, core, first, second, k], r2.at[c3, k])

            @pl.loop(1, n_rest)
            def _(k):
                copy(
                    3,
                    c3,
                    g.at[c3, core, first, second, lax.rem(rest + k, n_rest)],
                    r3.at[c3, n_rest - 1 - k],
                    rest_peer(k),
                ).start()

        c4 = step - 4

        @pl.when(jnp.logical_and(c4 >= 0, c4 < N_CHUNKS))
        def _():
            pltpu.make_async_copy(others(c4), others(c4), recv_sem.at[3, c4]).wait()
            total = g[c4, core, first, second, rest].astype(jnp.float32)
            for k in range(n_rest - 1):
                total = total + r3[c4, k].astype(jnp.float32)
            out_ref[c4, core, high] = total.astype(jnp.bfloat16)
            hop(4, c4).start()

        c5 = step - 5

        @pl.when(jnp.logical_and(c5 >= 0, c5 < N_CHUNKS))
        def _():
            hop(4, c5).wait_recv()
            hop(5, c5).start()

        c6 = step - 6

        @pl.when(jnp.logical_and(c6 >= 0, c6 < N_CHUNKS))
        def _():
            hop(5, c6).wait_recv()
            for level in (0, 1, 2, 4, 5):
                hop(level, c6).wait_send()
            pltpu.make_async_copy(others(c6), others(c6), send_sem.at[3, c6]).wait()


def by_piece(value, n_batch, n_height):
    lead = value.shape[0] if value.ndim == 3 else 1
    rows, columns = value.shape[-2:]
    pieces = value.astype(jnp.bfloat16).reshape(
        lead, n_batch // 2, 2, rows // n_batch, n_height // 2, 2, columns // (n_height * 128), 128
    )
    return jnp.transpose(pieces, (5, 4, 2, 1, 0, 3, 6, 7)).reshape(2, 2, 2, n_batch // 2, -1, 128)


def from_piece(piece, shape, n_batch, n_height):
    lead = shape[0] if len(shape) == 3 else 1
    rows, columns = shape[-2:]
    value = piece.reshape(2, 2, lead, rows // n_batch, columns // (n_height * 128), 128)
    value = jnp.transpose(value, (2, 3, 1, 0, 4, 5)).astype(jnp.float32)
    return value.reshape(shape[:-2] + (rows // n_batch, columns))


def reduce_grads(grads):
    n_batch, n_height = lax.axis_size("batch"), lax.axis_size("height")
    shapes = [value.shape for value in grads]
    pieces = [by_piece(value, n_batch, n_height) for value in grads]
    counts = [piece.shape[4] for piece in pieces]
    joined = jnp.concatenate(pieces, axis=4)
    rows = joined.shape[4] // N_CHUNKS
    n_rest = n_batch // 2
    joined = jnp.stack([joined[0], jnp.swapaxes(joined[1], 0, 1)])
    joined = joined.reshape(2, 2, 2, n_rest, N_CHUNKS, rows, 128)
    joined = jnp.transpose(joined, (4, 0, 1, 2, 3, 5, 6))
    summed = pl.pallas_call(
        functools.partial(grads_kernel, n_batch),
        out_shape=jax.ShapeDtypeStruct((N_CHUNKS, 2, 2, rows, 128), jnp.bfloat16),
        in_specs=[pl.BlockSpec(memory_space=pl.ANY)],
        out_specs=pl.BlockSpec(memory_space=pltpu.VMEM),
        scratch_shapes=[
            pltpu.VMEM((N_CHUNKS, 2, 2, 2, n_rest, rows, 128), jnp.bfloat16),
            pltpu.VMEM((N_CHUNKS, 2, 2, n_rest, rows, 128), jnp.bfloat16),
            pltpu.VMEM((N_CHUNKS, 2, n_rest, rows, 128), jnp.bfloat16),
            pltpu.VMEM((N_CHUNKS, n_rest, rows, 128), jnp.bfloat16),
            pltpu.VMEM((N_CHUNKS, n_rest - 1, rows, 128), jnp.bfloat16),
            pltpu.SemaphoreType.DMA((N_CHUNKS,)),
            pltpu.SemaphoreType.DMA((6, N_CHUNKS)),
            pltpu.SemaphoreType.DMA((6, N_CHUNKS)),
        ],
        compiler_params=pltpu.CompilerParams(
            collective_id=5, has_side_effects=True, vmem_limit_bytes=56 << 20
        ),
        name="reduce_grads",
    )(joined)
    summed = jnp.transpose(summed, (1, 2, 0, 3, 4)).reshape(2, 2, -1, 128)
    result, start = [], 0
    for shape, count in zip(shapes, counts):
        result.append(from_piece(summed[:, :, start : start + count], shape, n_batch, n_height))
        start += count
    return result


def passed_along(value, axis, steps):
    count = lax.axis_size(axis)
    first, last = (max(0, -steps), min(count, count - steps))
    return lax.ppermute(value, axis, [(source, source + steps) for source in range(first, last)])


def extended(value, sides, width):
    for axis, dim in sides:
        peers, length = (lax.axis_size(axis), value.shape[dim])
        up = [(i, (i + 1) % peers) for i in range(peers - 1)]
        down = [(j, i) for i, j in up]
        last = lax.slice_in_dim(value, length - width, length, axis=dim)
        first = lax.slice_in_dim(value, 0, width, axis=dim)
        before = lax.ppermute(last, axis, up)
        after = lax.ppermute(first, axis, down)
        value = jnp.concatenate([before, value, after], axis=dim)
    return value


def sigmoid_slope(values):
    logistic = jax.nn.sigmoid(values)
    return logistic * (1.0 + values * (1.0 - logistic))


def project(values, weight):
    return jnp.einsum("hwic,cd->hwid", values, weight, preferred_element_type=jnp.float32)


def project_back(grad_in, weight):
    return jnp.einsum("hwid,cd->hwic", grad_in, weight, preferred_element_type=jnp.float32)


def weight_term(values, grad_in):
    return jnp.einsum("hwic,hwid->cd", values, grad_in, preferred_element_type=jnp.float32)


def tap_window(padded, stride, out_rows, out_cols, row_tap, col_tap):
    return padded[
        row_tap : row_tap + stride * (out_rows - 1) + 1 : stride,
        col_tap : col_tap + stride * (out_cols - 1) + 1 : stride,
    ]


def spatial_kernel(padded, weight, stride, out_rows, out_cols):
    summed = None
    for row_tap in range(3):
        for col_tap in range(3):
            product = project(
                tap_window(padded, stride, out_rows, out_cols, row_tap, col_tap),
                weight[row_tap, col_tap],
            )
            summed = product if summed is None else summed + product
    return summed


def spatial_back(padded, weight, grad_in, stride, out_rows, out_cols):
    padded_grad = jnp.zeros(padded.shape, jnp.float32)
    tap_grads = []
    for row_tap in range(3):
        row_list = []
        for col_tap in range(3):
            window = tap_window(padded, stride, out_rows, out_cols, row_tap, col_tap)
            row_list.append(weight_term(window, grad_in))
            padded_grad = padded_grad.at[
                row_tap : row_tap + stride * (out_rows - 1) + 1 : stride,
                col_tap : col_tap + stride * (out_cols - 1) + 1 : stride,
            ].add(project_back(grad_in, weight[row_tap, col_tap]))
        tap_grads.append(jnp.stack(row_list))
    return (jnp.stack(tap_grads), padded_grad)


def gather_stats(levels, numbers):
    local_sums = []
    for tensors in levels:
        local_sums.append(sum((jnp.sum(member, axis=(0, 1, 2)) for member in tensors)))
        local_sums.append(sum((jnp.sum(member * member, axis=(0, 1, 2)) for member in tensors)))
    summed = sum_over_all(jnp.stack(local_sums))
    result = []
    for position in range(len(levels)):
        centre = summed[2 * position] / numbers[position]
        square = summed[2 * position + 1] / numbers[position]
        result.append((centre, lax.rsqrt(square - centre * centre + epsilon)))
    return result


def grad_stats(triples):
    local_sums = []
    for grad_list, value_list, stat in triples:
        centre, inv_root = stat
        local_sums.append(
            sum(
                (
                    jnp.sum(grad_list[picture_batches], axis=(0, 1, 2))
                    for picture_batches in range(3)
                )
            )
        )
        local_sums.append(
            sum(
                (
                    jnp.sum(
                        grad_list[picture_batches]
                        * (value_list[picture_batches] - centre)
                        * inv_root,
                        axis=(0, 1, 2),
                    )
                    for picture_batches in range(3)
                )
            )
        )
    summed = sum_over_all(jnp.stack(local_sums))
    return [(summed[2 * position], summed[2 * position + 1]) for position in range(len(triples))]


def apply_norm(values, stat, gain, shift):
    centre, inv_root = stat
    return (values - centre) * (inv_root * gain) + shift


def norm_back(grad_in, values, stat, gain, grad_sums, number):
    centre, inv_root = stat
    normed = (values - centre) * inv_root
    return gain * inv_root * (grad_in - grad_sums[0] / number - normed * (grad_sums[1] / number))


def per_device(
    image_small,
    image_medium,
    image_large,
    row_counts,
    reduce_a,
    first_spatial_weight,
    expand_a,
    shortcut_a,
    reduce_b,
    second_spatial_weight,
    expand_b,
    gain_mid,
    shift_mid,
    gain_out,
    shift_out,
    upstream_small,
    upstream_medium,
    upstream_large,
):
    raw_images = tuple(jnp.transpose(v, (1, 2, 0, 3)) for v in (image_small, image_medium, image_large))
    upstreams = (upstream_small, upstream_medium, upstream_large)
    band_index = lax.axis_index("height")
    batch_devices = lax.axis_size("batch")
    entering_photos, entering_filters, line_filters, genuine_lines, edge_extents, bucket_limits = (
        [],
        [],
        [],
        [],
        [],
        [],
    )
    total_in = 0
    total_out = 0
    for picture_batches in range(3):
        slab_rows = raw_images[picture_batches].shape[0]
        bucket_limit = slab_rows // 2
        out_side = raw_images[picture_batches].shape[1] // 2
        live = row_counts[picture_batches, band_index]
        mask_low = (jnp.arange(slab_rows, dtype=jnp.int32) < 2 * live).astype(jnp.bfloat16)[

            :, None, None, None
        ]
        entering_photos.append(raw_images[picture_batches] * mask_low)
        entering_filters.append(mask_low.astype(jnp.float32))
        line_filters.append(
            (jnp.arange(bucket_limit, dtype=jnp.int32) < live).astype(jnp.float32)[
            :, None, None, None
            ]
        )
        genuine_lines.append(live)
        edge_extents.append(out_side)
        bucket_limits.append(bucket_limit)
        total_in += batch_devices * raw_images[picture_batches].shape[2] * 4 * out_side * out_side
        total_out += batch_devices * raw_images[picture_batches].shape[2] * out_side * out_side
    width_cuts = [edge_extents[0], edge_extents[0] + edge_extents[1]]
    input_cuts = [2 * edge_extents[0], 2 * edge_extents[0] + 2 * edge_extents[1]]
    first_out = [
        project(entering_photos[picture_batches], reduce_a) for picture_batches in range(3)
    ]
    (stat_one,) = gather_stats([first_out], [total_in])
    pre_one = [
        apply_norm(first_out[picture_batches], stat_one, gain_mid[0], shift_mid[0])
        for picture_batches in range(3)
    ]
    act_one = [
        (jax.nn.silu(pre_one[picture_batches]) * entering_filters[picture_batches]).astype(
            jnp.bfloat16
        )
        for picture_batches in range(3)
    ]
    tail_rows = [
        lax.dynamic_index_in_dim(
            act_one[picture_batches], 2 * genuine_lines[picture_batches] - 1, 0, keepdims=False
        )
        for picture_batches in range(3)
    ]
    rim_rows = passed_along(jnp.concatenate(tail_rows, axis=0), "height", 1)
    rim_parts = jnp.split(rim_rows, input_cuts, axis=0)
    first_padded = []
    for picture_batches in range(3):
        joined = jnp.concatenate(
            [rim_parts[picture_batches][None], act_one[picture_batches]], axis=0
        )
        first_padded.append(jnp.pad(joined, ((0, 0), (1, 0), (0, 0), (0, 0))))
    second_out = [
        spatial_kernel(
            first_padded[picture_batches],
            first_spatial_weight,
            2,
            bucket_limits[picture_batches],
            edge_extents[picture_batches],
        )
        * line_filters[picture_batches]
        for picture_batches in range(3)
    ]
    (stat_two,) = gather_stats([second_out], [total_out])
    pre_two = [
        apply_norm(second_out[picture_batches], stat_two, gain_mid[1], shift_mid[1])
        for picture_batches in range(3)
    ]
    act_two = [
        (jax.nn.silu(pre_two[picture_batches]) * line_filters[picture_batches]).astype(jnp.bfloat16)
        for picture_batches in range(3)
    ]
    third_out = [project(act_two[picture_batches], expand_a) for picture_batches in range(3)]
    side_inputs = [entering_photos[picture_batches][::2, ::2] for picture_batches in range(3)]
    side_out = [project(side_inputs[picture_batches], shortcut_a) for picture_batches in range(3)]
    stat_three, stat_side = gather_stats([third_out, side_out], [total_out, total_out])
    joint_one = [
        apply_norm(third_out[picture_batches], stat_three, gain_out[0], shift_out[0])
        + apply_norm(side_out[picture_batches], stat_side, gain_out[1], shift_out[1])
        for picture_batches in range(3)
    ]
    middle = [
        jax.nn.silu(joint_one[picture_batches]) * line_filters[picture_batches]
        for picture_batches in range(3)
    ]
    middle_low = [middle[picture_batches].astype(jnp.bfloat16) for picture_batches in range(3)]
    fourth_out = [project(middle_low[picture_batches], reduce_b) for picture_batches in range(3)]
    (stat_four,) = gather_stats([fourth_out], [total_out])
    pre_four = [
        apply_norm(fourth_out[picture_batches], stat_four, gain_mid[2], shift_mid[2])
        for picture_batches in range(3)
    ]
    act_four = [
        (jax.nn.silu(pre_four[picture_batches]) * line_filters[picture_batches]).astype(
            jnp.bfloat16
        )
        for picture_batches in range(3)
    ]
    edge_pairs = [
        jnp.stack(
            [
                act_four[picture_batches][0],
                lax.dynamic_index_in_dim(
                    act_four[picture_batches], genuine_lines[picture_batches] - 1, 0, keepdims=False
                ),
            ],
            axis=0,
        )
        for picture_batches in range(3)
    ]
    rim_pairs = extended(jnp.concatenate(edge_pairs, axis=1), (("height", 0),), 1)
    pair_parts = jnp.split(rim_pairs, width_cuts, axis=1)
    fourth_padded = []
    for picture_batches in range(3):
        rim_pair = pair_parts[picture_batches]
        joined = jnp.concatenate(
            [rim_pair[0:1], act_four[picture_batches], jnp.zeros_like(rim_pair[0:1])], axis=0
        )
        joined = lax.dynamic_update_slice_in_dim(
            joined, rim_pair[3:4], genuine_lines[picture_batches] + 1, 0
        )
        fourth_padded.append(jnp.pad(joined, ((0, 0), (1, 1), (0, 0), (0, 0))))
    fifth_out = [
        spatial_kernel(
            fourth_padded[picture_batches],
            second_spatial_weight,
            1,
            bucket_limits[picture_batches],
            edge_extents[picture_batches],
        )
        * line_filters[picture_batches]
        for picture_batches in range(3)
    ]
    (stat_five,) = gather_stats([fifth_out], [total_out])
    pre_five = [
        apply_norm(fifth_out[picture_batches], stat_five, gain_mid[3], shift_mid[3])
        for picture_batches in range(3)
    ]
    act_five = [
        (jax.nn.silu(pre_five[picture_batches]) * line_filters[picture_batches]).astype(
            jnp.bfloat16
        )
        for picture_batches in range(3)
    ]
    sixth_out = [project(act_five[picture_batches], expand_b) for picture_batches in range(3)]
    (stat_six,) = gather_stats([sixth_out], [total_out])
    joint_two = [
        apply_norm(sixth_out[picture_batches], stat_six, gain_out[2], shift_out[2])
        + middle[picture_batches]
        for picture_batches in range(3)
    ]
    final = [
        jax.nn.silu(joint_two[picture_batches]) * line_filters[picture_batches]
        for picture_batches in range(3)
    ]
    pooled_sums = lax.psum(
        jnp.stack(
            [jnp.sum(final[picture_batches], axis=(0, 1)) for picture_batches in range(3)]
        ).astype(jnp.bfloat16),
        "height",
    ).astype(jnp.float32)
    pooled = [
        pooled_sums[picture_batches]
        / (edge_extents[picture_batches] * edge_extents[picture_batches])
        for picture_batches in range(3)
    ]
    d_joint_two = [
        upstreams[picture_batches].astype(jnp.float32)[None, None]
        / (edge_extents[picture_batches] * edge_extents[picture_batches])
        * line_filters[picture_batches]
        * sigmoid_slope(joint_two[picture_batches])
        for picture_batches in range(3)
    ]
    (sums_six,) = grad_stats([(d_joint_two, sixth_out, stat_six)])
    grad_six = [
        (
            norm_back(
                d_joint_two[picture_batches],
                sixth_out[picture_batches],
                stat_six,
                gain_out[2],
                sums_six,
                total_out,
            )
            * line_filters[picture_batches]
        ).astype(jnp.bfloat16)
        for picture_batches in range(3)
    ]
    expand_b_local = sum(
        (
            weight_term(act_five[picture_batches], grad_six[picture_batches])
            for picture_batches in range(3)
        )
    )
    d_five = [
        project_back(grad_six[picture_batches], expand_b)
        * sigmoid_slope(pre_five[picture_batches])
        * line_filters[picture_batches]
        for picture_batches in range(3)
    ]
    (sums_five,) = grad_stats([(d_five, fifth_out, stat_five)])
    fifth_gradient = [
        (
            norm_back(
                d_five[picture_batches],
                fifth_out[picture_batches],
                stat_five,
                gain_mid[3],
                sums_five,
                total_out,
            )
            * line_filters[picture_batches]
        ).astype(jnp.bfloat16)
        for picture_batches in range(3)
    ]
    spatial_b_local = None
    d_swish_four = []
    edge_grads = []
    for picture_batches in range(3):
        tap_grad, padded_grad = spatial_back(
            fourth_padded[picture_batches],
            second_spatial_weight,
            fifth_gradient[picture_batches],
            1,
            bucket_limits[picture_batches],
            edge_extents[picture_batches],
        )
        spatial_b_local = tap_grad if spatial_b_local is None else spatial_b_local + tap_grad
        central_block = padded_grad[:, 1:-1]
        top_grad = central_block[0]
        below_grad = lax.dynamic_index_in_dim(
            central_block, genuine_lines[picture_batches] + 1, 0, keepdims=False
        )
        d_swish_four.append(central_block[1 : bucket_limits[picture_batches] + 1])
        edge_grads.append(jnp.stack([top_grad, below_grad], axis=0))
    returned = extended(
        jnp.concatenate(edge_grads, axis=1).astype(jnp.bfloat16), (("height", 0),), 1
    ).astype(jnp.float32)
    returned_parts = jnp.split(returned, width_cuts, axis=1)
    d_four = []
    for picture_batches in range(3):
        grad_rows = (
            d_swish_four[picture_batches].at[0].add(returned_parts[picture_batches][0])
        )
        last_row = (
            lax.dynamic_index_in_dim(
                grad_rows, genuine_lines[picture_batches] - 1, 0, keepdims=False
            )
            + returned_parts[picture_batches][3]
        )
        grad_rows = lax.dynamic_update_index_in_dim(
            grad_rows, last_row, genuine_lines[picture_batches] - 1, 0
        )
        d_four.append(
            grad_rows * sigmoid_slope(pre_four[picture_batches]) * line_filters[picture_batches]
        )
    (sums_four,) = grad_stats([(d_four, fourth_out, stat_four)])
    grad_four = [
        (
            norm_back(
                d_four[picture_batches],
                fourth_out[picture_batches],
                stat_four,
                gain_mid[2],
                sums_four,
                total_out,
            )
            * line_filters[picture_batches]
        ).astype(jnp.bfloat16)
        for picture_batches in range(3)
    ]
    reduce_b_local = sum(
        (
            weight_term(middle_low[picture_batches], grad_four[picture_batches])
            for picture_batches in range(3)
        )
    )
    d_joint_one = [
        (project_back(grad_four[picture_batches], reduce_b) + d_joint_two[picture_batches])
        * sigmoid_slope(joint_one[picture_batches])
        * line_filters[picture_batches]
        for picture_batches in range(3)
    ]
    sums_three, sums_side = grad_stats(
        [(d_joint_one, third_out, stat_three), (d_joint_one, side_out, stat_side)]
    )
    grad_three = [
        (
            norm_back(
                d_joint_one[picture_batches],
                third_out[picture_batches],
                stat_three,
                gain_out[0],
                sums_three,
                total_out,
            )
            * line_filters[picture_batches]
        ).astype(jnp.bfloat16)
        for picture_batches in range(3)
    ]
    grad_side = [
        (
            norm_back(
                d_joint_one[picture_batches],
                side_out[picture_batches],
                stat_side,
                gain_out[1],
                sums_side,
                total_out,
            )
            * line_filters[picture_batches]
        ).astype(jnp.bfloat16)
        for picture_batches in range(3)
    ]
    expand_a_local = sum(
        (
            weight_term(act_two[picture_batches], grad_three[picture_batches])
            for picture_batches in range(3)
        )
    )
    shortcut_a_local = sum(
        (
            weight_term(side_inputs[picture_batches], grad_side[picture_batches])
            for picture_batches in range(3)
        )
    )
    d_two = [
        project_back(grad_three[picture_batches], expand_a)
        * sigmoid_slope(pre_two[picture_batches])
        * line_filters[picture_batches]
        for picture_batches in range(3)
    ]
    (sums_two,) = grad_stats([(d_two, second_out, stat_two)])
    second_gradient = [
        (
            norm_back(
                d_two[picture_batches],
                second_out[picture_batches],
                stat_two,
                gain_mid[1],
                sums_two,
                total_out,
            )
            * line_filters[picture_batches]
        ).astype(jnp.bfloat16)
        for picture_batches in range(3)
    ]
    spatial_a_local = None
    d_act_one = []
    rim_grads = []
    for picture_batches in range(3):
        tap_grad, padded_grad = spatial_back(
            first_padded[picture_batches],
            first_spatial_weight,
            second_gradient[picture_batches],
            2,
            bucket_limits[picture_batches],
            edge_extents[picture_batches],
        )
        spatial_a_local = tap_grad if spatial_a_local is None else spatial_a_local + tap_grad
        rim_grads.append(padded_grad[0, 1:])
        d_act_one.append(padded_grad[1:, 1:])
    rim_back = passed_along(
        jnp.concatenate(rim_grads, axis=0).astype(jnp.bfloat16), "height", -1
    ).astype(jnp.float32)
    rim_back_parts = jnp.split(rim_back, input_cuts, axis=0)
    d_one = []
    for picture_batches in range(3):
        row_place = 2 * genuine_lines[picture_batches] - 1
        last_row = (
            lax.dynamic_index_in_dim(d_act_one[picture_batches], row_place, 0, keepdims=False)
            + rim_back_parts[picture_batches]
        )
        grad_rows = lax.dynamic_update_index_in_dim(
            d_act_one[picture_batches], last_row, row_place, 0
        )
        d_one.append(
            grad_rows * sigmoid_slope(pre_one[picture_batches]) * entering_filters[picture_batches]
        )
    (sums_one,) = grad_stats([(d_one, first_out, stat_one)])
    grad_one = [
        (
            norm_back(
                d_one[picture_batches],
                first_out[picture_batches],
                stat_one,
                gain_mid[0],
                sums_one,
                total_in,
            )
            * entering_filters[picture_batches]
        ).astype(jnp.bfloat16)
        for picture_batches in range(3)
    ]
    reduce_a_local = sum(
        (
            weight_term(entering_photos[picture_batches], grad_one[picture_batches])
            for picture_batches in range(3)
        )
    )
    backs = []
    for picture_batches in range(3):
        image_grad = project_back(grad_one[picture_batches], reduce_a)
        image_grad = image_grad.at[::2, ::2].add(
            project_back(grad_side[picture_batches], shortcut_a)
        )
        backs.append(jnp.transpose(image_grad.astype(jnp.bfloat16), (2, 0, 1, 3)))
    nine = (9,) + spatial_a_local.shape[2:]
    shards = reduce_grads(
        [
            reduce_a_local,
            spatial_a_local.reshape(nine),
            expand_a_local,
            shortcut_a_local,
            reduce_b_local,
            spatial_b_local.reshape(nine),
            expand_b_local,
        ]
    )
    for place in (1, 5):
        shards[place] = shards[place].reshape((3, 3) + shards[place].shape[1:])
    gain_mid_grad = jnp.stack([sums_one[1], sums_two[1], sums_four[1], sums_five[1]])
    shift_mid_grad = jnp.stack([sums_one[0], sums_two[0], sums_four[0], sums_five[0]])
    gain_out_grad = jnp.stack([sums_three[1], sums_side[1], sums_six[1]])
    shift_out_grad = jnp.stack([sums_three[0], sums_side[0], sums_six[0]])
    return (
        pooled[0],
        pooled[1],
        pooled[2],
        backs[0],
        backs[1],
        backs[2],
        shards[0],
        shards[1],
        shards[2],
        shards[3],
        shards[4],
        shards[5],
        shards[6],
        gain_mid_grad,
        shift_mid_grad,
        gain_out_grad,
        shift_out_grad,
    )


def solution(mesh):
    placed = (
        P("batch", "height", None, None),
        P("batch", "height", None, None),
        P("batch", "height", None, None),
        P(),
        P(),
        P(),
        P(),
        P(),
        P(),
        P(),
        P(),
        P(),
        P(),
        P(),
        P(),
        P("batch", None),
        P("batch", None),
        P("batch", None),
    )
    return jax.shard_map(
        per_device,
        mesh=mesh,
        in_specs=placed,
        out_specs=(
            P("batch", None),
            P("batch", None),
            P("batch", None),
            P("batch", "height", None, None),
            P("batch", "height", None, None),
            P("batch", "height", None, None),
            P("batch", None),
            P(None, None, "batch", None),
            P("batch", None),
            P("batch", None),
            P("batch", None),
            P(None, None, "batch", None),
            P("batch", None),
            P(),
            P(),
            P(),
            P(),
        ),
        check_vma=False,
    )
```

```python
import functools

import jax
import jax.numpy as jnp
from jax import lax
from jax.experimental import pallas as pl
from jax.experimental.pallas import tpu as pltpu
from jax.sharding import PartitionSpec as P

epsilon = 1e-05
MESH = pl.DeviceIdType.MESH
N_CHUNKS = 10


def grads_kernel(n_batch, local_ref, out_ref, g, r0, r1, r2, r3, load_sem, send_sem, recv_sem):
    b, h = lax.axis_index("batch"), lax.axis_index("height")
    core, high = lax.rem(h, 2), h // 2
    low, rest = lax.rem(b, 2), b // 2
    n_rest = n_batch // 2
    first = core * low + (1 - core) * high
    second = core * high + (1 - core) * low
    core_peer = (b, h + 1 - 2 * core)
    high_peer = (b, h + 2 - 4 * high)
    low_peer = (b + 1 - 2 * low, h)
    first_peer = (
        core * low_peer[0] + (1 - core) * high_peer[0],
        core * low_peer[1] + (1 - core) * high_peer[1],
    )
    second_peer = (
        core * high_peer[0] + (1 - core) * low_peer[0],
        core * high_peer[1] + (1 - core) * low_peer[1],
    )

    def rest_peer(k):
        return (lax.rem(rest + k, n_rest) * 2 + low, h)

    def load(c):
        return pltpu.make_async_copy(local_ref.at[c], g.at[c], load_sem.at[c])

    for c in range(N_CHUNKS):
        load(c).start()
    barrier = pltpu.get_barrier_semaphore()
    for peer in (core_peer, high_peer, low_peer):
        pl.semaphore_signal(barrier, inc=1, device_id=peer, device_id_type=MESH)

    @pl.loop(1, n_rest)
    def _(k):
        pl.semaphore_signal(barrier, inc=1, device_id=rest_peer(k), device_id_type=MESH)

    pl.semaphore_wait(barrier, 3 + n_rest - 1)

    def copy(level, c, source, target, peer):
        return pltpu.make_async_remote_copy(
            src_ref=source,
            dst_ref=target,
            send_sem=send_sem.at[level, c],
            recv_sem=recv_sem.at[level, c],
            device_id=peer,
            device_id_type=MESH,
        )

    def hop(level, c):
        if level == 0:
            return copy(0, c, g.at[c, 1 - core], r0.at[c], core_peer)
        if level == 1:
            return copy(1, c, g.at[c, core, 1 - first], r1.at[c], first_peer)
        if level == 2:
            return copy(2, c, g.at[c, core, first, 1 - second], r2.at[c], second_peer)
        if level == 4:
            mine = out_ref.at[c, core, high]
            return copy(4, c, mine, mine, high_peer)
        both = out_ref.at[c, core]
        return copy(5, c, both, both, core_peer)

    def add(target, source):
        target[...] = (target[...].astype(jnp.float32) + source[...].astype(jnp.float32)).astype(
            jnp.bfloat16
        )

    def others(c):
        return r3.at[c, 0 : n_rest - 1]

    @pl.loop(0, N_CHUNKS + 6)
    def _(step):
        @pl.when(step < N_CHUNKS)
        def _():
            load(step).wait()
            hop(0, step).start()

        c1 = step - 1

        @pl.when(jnp.logical_and(c1 >= 0, c1 < N_CHUNKS))
        def _():
            hop(0, c1).wait_recv()

            @pl.loop(0, 2)
            def _(i):
                @pl.loop(0, 2)
                def _(j):
                    @pl.loop(0, n_rest)
                    def _(k):
                        add(g.at[c1, core, i, j, k], r0.at[c1, i, j, k])

            hop(1, c1).start()

        c2 = step - 2

        @pl.when(jnp.logical_and(c2 >= 0, c2 < N_CHUNKS))
        def _():
            hop(1, c2).wait_recv()

            @pl.loop(0, 2)
            def _(j):
                @pl.loop(0, n_rest)
                def _(k):
                    add(g.at[c2, core, first, j, k], r1.at[c2, j, k])

            hop(2, c2).start()

        c3 = step - 3

        @pl.when(jnp.logical_and(c3 >= 0, c3 < N_CHUNKS))
        def _():
            hop(2, c3).wait_recv()

            @pl.loop(0, n_rest)
            def _(k):
                add(g.at[c3, core, first, second, k], r2.at[c3, k])

            @pl.loop(1, n_rest)
            def _(k):
                copy(
                    3,
                    c3,
                    g.at[c3, core, first, second, lax.rem(rest + k, n_rest)],
                    r3.at[c3, n_rest - 1 - k],
                    rest_peer(k),
                ).start()

        c4 = step - 4

        @pl.when(jnp.logical_and(c4 >= 0, c4 < N_CHUNKS))
        def _():
            pltpu.make_async_copy(others(c4), others(c4), recv_sem.at[3, c4]).wait()
            total = g[c4, core, first, second, rest].astype(jnp.float32)
            for k in range(n_rest - 1):
                total = total + r3[c4, k].astype(jnp.float32)
            out_ref[c4, core, high] = total.astype(jnp.bfloat16)
            hop(4, c4).start()

        c5 = step - 5

        @pl.when(jnp.logical_and(c5 >= 0, c5 < N_CHUNKS))
        def _():
            hop(4, c5).wait_recv()
            hop(5, c5).start()

        c6 = step - 6

        @pl.when(jnp.logical_and(c6 >= 0, c6 < N_CHUNKS))
        def _():
            hop(5, c6).wait_recv()
            for level in (0, 1, 2, 4, 5):
                hop(level, c6).wait_send()
            pltpu.make_async_copy(others(c6), others(c6), send_sem.at[3, c6]).wait()


def by_piece(value, n_batch, n_height):
    lead = value.shape[0] if value.ndim == 3 else 1
    rows, columns = value.shape[-2:]
    pieces = value.astype(jnp.bfloat16).reshape(
        lead, n_batch // 2, 2, rows // n_batch, n_height // 2, 2, columns // (n_height * 128), 128
    )
    return jnp.transpose(pieces, (5, 4, 2, 1, 0, 3, 6, 7)).reshape(2, 2, 2, n_batch // 2, -1, 128)


def from_piece(piece, shape, n_batch, n_height):
    lead = shape[0] if len(shape) == 3 else 1
    rows, columns = shape[-2:]
    value = piece.reshape(2, 2, lead, rows // n_batch, columns // (n_height * 128), 128)
    value = jnp.transpose(value, (2, 3, 1, 0, 4, 5)).astype(jnp.float32)
    return value.reshape(shape[:-2] + (rows // n_batch, columns))


def reduce_grads(grads):
    n_batch, n_height = lax.axis_size("batch"), lax.axis_size("height")
    shapes = [value.shape for value in grads]
    pieces = [by_piece(value, n_batch, n_height) for value in grads]
    counts = [piece.shape[4] for piece in pieces]
    joined = jnp.concatenate(pieces, axis=4)
    rows = joined.shape[4] // N_CHUNKS
    n_rest = n_batch // 2
    joined = jnp.stack([joined[0], jnp.swapaxes(joined[1], 0, 1)])
    joined = joined.reshape(2, 2, 2, n_rest, N_CHUNKS, rows, 128)
    joined = jnp.transpose(joined, (4, 0, 1, 2, 3, 5, 6))
    summed = pl.pallas_call(
        functools.partial(grads_kernel, n_batch),
        out_shape=jax.ShapeDtypeStruct((N_CHUNKS, 2, 2, rows, 128), jnp.bfloat16),
        in_specs=[pl.BlockSpec(memory_space=pl.ANY)],
        out_specs=pl.BlockSpec(memory_space=pltpu.VMEM),
        scratch_shapes=[
            pltpu.VMEM((N_CHUNKS, 2, 2, 2, n_rest, rows, 128), jnp.bfloat16),
            pltpu.VMEM((N_CHUNKS, 2, 2, n_rest, rows, 128), jnp.bfloat16),
            pltpu.VMEM((N_CHUNKS, 2, n_rest, rows, 128), jnp.bfloat16),
            pltpu.VMEM((N_CHUNKS, n_rest, rows, 128), jnp.bfloat16),
            pltpu.VMEM((N_CHUNKS, n_rest - 1, rows, 128), jnp.bfloat16),
            pltpu.SemaphoreType.DMA((N_CHUNKS,)),
            pltpu.SemaphoreType.DMA((6, N_CHUNKS)),
            pltpu.SemaphoreType.DMA((6, N_CHUNKS)),
        ],
        compiler_params=pltpu.CompilerParams(
            collective_id=5, has_side_effects=True, vmem_limit_bytes=56 << 20
        ),
        name="reduce_grads",
    )(joined)
    summed = jnp.transpose(summed, (1, 2, 0, 3, 4)).reshape(2, 2, -1, 128)
    result, start = [], 0
    for shape, count in zip(shapes, counts):
        result.append(from_piece(summed[:, :, start : start + count], shape, n_batch, n_height))
        start += count
    return result


WIDE = 512
ROWS = 16
STEP = 64


def sigmoid(values):
    return 0.5 * jnp.tanh(0.5 * values) + 0.5


def up32(values):
    return values.astype(jnp.float32)


def low(values):
    return values.astype(jnp.bfloat16)


def times(left, right):
    return jnp.dot(left, right, preferred_element_type=jnp.float32)


def times_t(left, right):
    return lax.dot_general(
        left, right, (((1,), (1,)), ((), ())), preferred_element_type=jnp.float32
    )


def t_times(left, right):
    return lax.dot_general(
        left, right, (((0,), (0,)), ((), ())), preferred_element_type=jnp.float32
    )


def fold(values):
    return jnp.sum(values.reshape(-1, 8, values.shape[-1]), axis=0)


def one_row(values):
    return jnp.sum(values, axis=0, keepdims=True)


def wide_mask(mask):
    return jnp.concatenate([mask] * (WIDE // 128), axis=1)


def grids(heights, widths):
    counts = [k * (o + 1) for k, o in zip(heights, widths)]
    starts = [sum(counts[:g]) for g in range(3)]
    top_sizes = [(k + 1) * (o + 1) + 1 for k, o in zip(heights, widths)]
    top_starts = [sum(top_sizes[:g]) for g in range(3)]
    both_sizes = [(k + 2) * (o + 1) + 2 for k, o in zip(heights, widths)]
    both_starts = [sum(both_sizes[:g]) for g in range(3)]
    halo_starts = [sum(widths[:g]) for g in range(3)]
    return counts, starts, sum(top_sizes), top_starts, sum(both_sizes), both_starts, halo_starts


def main_kernel(
    n_batch, n_height, heights, widths, total_in, total_out,
    x, reduce_a, spatial_a, expand_a, shortcut_a, reduce_b, spatial_b, expand_b,
    edge_ref, mask_ref, gain_mid, shift_mid, gain_out, shift_out, up_ref,
    pooled, dx, g_reduce_a, g_spatial_a, g_expand_a, g_shortcut_a, g_reduce_b, g_spatial_b,
    g_expand_b, mid_sums, out_sums, h1_kept, a1_kept,
    big_b, big_a, h3, side, mb, h2, a2, h4, h5, a5, a4p, dhp, acc, wp, wq, w2,
    halo_a, halo_up, halo_down, halo_in, staged, pool_slots,
    thin_h, thin_b, wide_h, wide_b, stat_mid, stat_out,
    w_sem, x_sem, g_sem, dx_sem, spill_sem, ar_send, ar_recv, halo_send, halo_recv, pool_sem,
):
    b, h = lax.axis_index("batch"), lax.axis_index("height")
    counts, starts, top_total, top_starts, both_total, both_starts, halo_starts = grids(
        heights, widths
    )
    total = sum(counts) * ROWS
    half = total // 2
    groups = range(3)
    h1, dz, h6 = big_b, big_b, big_a

    def rows_at(start, count):
        return pl.ds(pl.multiple_of(start * ROWS, ROWS), count * ROWS)

    def steps(index):
        return pl.ds(pl.multiple_of(index * STEP, STEP), STEP)

    def fetch(source, target, sem):
        pltpu.make_async_copy(source, target, sem).start()

    def arrived(target, sem):
        pltpu.make_async_copy(target, target, sem).wait()

    def columns(k):
        return pl.ds(k * WIDE, WIDE)

    def fetch_columns(weight, target, first, sem):
        for n in range(4):
            fetch(weight.at[:, columns(n)], target.at[first + n], sem)

    def fetch_shortcut():
        for n in range(4):
            for k in range(2):
                fetch(shortcut_a.at[columns(k), columns(n)], wq.at[2 * n + k], w_sem.at[1])

    for k in range(2):
        fetch(x.at[:, :, columns(k)], (h3, mb)[k], x_sem.at[k])
    for k in range(2):
        fetch(reduce_a.at[columns(k)], w2.at[k], w_sem.at[3])
    fetch_shortcut()
    fetch(spatial_a, wp, w_sem.at[0])

    halo_down[...] = jnp.zeros_like(halo_down)
    halo_up[...] = jnp.zeros_like(halo_up)
    halo_in[...] = jnp.zeros_like(halo_in)

    @pl.loop(0, both_total // 2)
    def _(i):
        rows = rows_at(i * 2, 2)
        a4p[rows] = jnp.zeros((2 * ROWS, WIDE), jnp.bfloat16)
        dhp[rows] = jnp.zeros((2 * ROWS, WIDE), jnp.bfloat16)

    for g in groups:
        count = widths[g] + 2
        for p in range(4):
            big_a[p, top_starts[g] * ROWS : (top_starts[g] + count) * ROWS] = jnp.zeros(
                (count * ROWS, WIDE), jnp.bfloat16
            )

    barrier = pltpu.get_barrier_semaphore()
    for k in range(1, n_height):
        pl.semaphore_signal(
            barrier, inc=1, device_id=(b, lax.rem(h + k, n_height)), device_id_type=MESH
        )

    @pl.loop(1, n_batch)
    def _(k):
        pl.semaphore_signal(
            barrier, inc=1, device_id=(lax.rem(b + k, n_batch), h), device_id_type=MESH
        )

    pl.semaphore_wait(barrier, n_height + n_batch - 2)

    turn = {"thin": 0, "wide": 0}

    def ar_spread(slots, me, count, peer, level, slot, sem):
        @pl.loop(1, count)
        def _(k):
            pltpu.make_async_remote_copy(
                src_ref=slots.at[slot, me],
                dst_ref=slots.at[slot, me],
                send_sem=ar_send.at[sem, level, slot],
                recv_sem=ar_recv.at[sem, level, slot],
                device_id=peer(lax.rem(me + k, count)),
                device_id_type=MESH,
            ).start()

    def ar_wait(slots, count, level, slot, sem, sems):
        others = slots.at[slot, 0 : count - 1]
        pltpu.make_async_copy(others, others, sems.at[sem, level, slot]).wait()

    def sums_start(kind, vectors):
        slot = turn[kind] % 2
        turn[kind] += 1
        if kind == "thin":
            first, second, sem = thin_h, thin_b, 0
            for v, vector in enumerate(vectors):
                for j in range(4):
                    first[slot, h, 4 * v + j : 4 * v + j + 1, :] = vector[
                        :, 128 * j : 128 * (j + 1)
                    ]
        else:
            first, second, sem = wide_h, wide_b, 1
            first[slot, h] = stat_out[...]
        ar_spread(first, h, n_height, lambda p: (b, p), 0, slot, sem)
        return first, second, sem, slot

    def sums_middle(state):
        first, second, sem, slot = state
        ar_wait(first, n_height, 0, slot, sem, ar_recv)
        second[slot, b] = jnp.sum(first[slot], axis=0)
        ar_spread(second, b, n_batch, lambda p: (p, h), 1, slot, sem)

    def sums_end(state):
        first, second, sem, slot = state
        ar_wait(second, n_batch, 1, slot, sem, ar_recv)
        summed = jnp.sum(second[slot], axis=0)
        ar_wait(first, n_height, 0, slot, sem, ar_send)
        ar_wait(second, n_batch, 1, slot, sem, ar_send)
        if sem == 0:
            return [
                jnp.concatenate([summed[4 * v + j : 4 * v + j + 1] for j in range(4)], axis=1)
                for v in range(2)
            ]
        stat_out[...] = summed
        return None

    def keep_stats(kept, index, sums, number, gain, shift):
        centre = sums[0] * (1.0 / number)
        root = lax.rsqrt(sums[1] * (1.0 / number) - centre * centre + epsilon)
        scale = root * gain
        kept[index, 0:1] = centre
        kept[index, 1:2] = root
        kept[index, 2:3] = scale
        kept[index, 3:4] = shift - centre * scale
        kept[index, 4:5] = -centre * root

    def back_factors(kept, index, sums, number, gain):
        centre, root = kept[index, 0:1], kept[index, 1:2]
        main = gain * root
        slope = -main * root * sums[1] * (1.0 / number)
        return main, slope, -main * sums[0] * (1.0 / number) - slope * centre

    def halo_copy(source, target, sem, peer):
        return pltpu.make_async_remote_copy(
            src_ref=source,
            dst_ref=target,
            send_sem=halo_send.at[sem],
            recv_sem=halo_recv.at[sem],
            device_id=(b, peer),
            device_id_type=MESH,
        )

    def halo_rows(g):
        return slice(halo_starts[g] * ROWS, (halo_starts[g] + widths[g]) * ROWS)

    def top_row(padded, start, g):
        return padded.at[pl.ds((start + 1) * ROWS, widths[g] * ROWS)]

    def send_down(buffer, padded, sem):
        @pl.when(h < n_height - 1)
        def _():
            for g in groups:
                halo_copy(
                    buffer.at[halo_rows(g)], top_row(padded, both_starts[g], g), sem, h + 1
                ).start()

    def send_up(buffer, sem):
        @pl.when(h > 0)
        def _():
            halo_copy(buffer, halo_in, sem, h - 1).start()

    def halo_wait(buffer, sems, sem, condition):
        @pl.when(condition)
        def _():
            arrived(buffer, sems.at[sem])

    def place_below(padded):
        for g in groups:
            stride = widths[g] + 1
            for y in range(1, heights[g] + 1):
                is_edge = edge(g, y - 1)

                @pl.loop(0, widths[g])
                def _(col):
                    rows = rows_at(both_starts[g] + 1 + (y + 1) * stride + col, 1)
                    value = up32(halo_in[rows_at(halo_starts[g] + col, 1)]) * is_edge
                    if y < heights[g]:
                        value = value + up32(padded[rows])
                    padded[rows] = low(value)

    def edge(g, y):
        return wide_mask(edge_ref[g, y, 0:1])

    def first_row(source, g, row=0):
        start = (starts[g] + row * (widths[g] + 1)) * ROWS
        return up32(source[start : start + widths[g] * ROWS])

    def last_row(source, g):
        value = first_row(source, g) * edge(g, 0)
        for y in range(1, heights[g]):
            value = value + first_row(source, g, y) * edge(g, y)
        return value

    done = [0]

    def store_tile(index, value, target):
        slot = lax.rem(index, 2)

        @pl.when(index >= 2)
        def _():
            arrived(staged.at[slot], g_sem.at[slot])

        staged[slot] = low(value)
        fetch(staged.at[slot], target, g_sem.at[slot])

    def store_tiles(count, value_of, target_of):
        first = done[0]
        done[0] += count

        @pl.loop(0, count)
        def _(t):
            store_tile(first + t, value_of(t), target_of(t))

    def wide_rows(reference, t):
        return reference.at[pl.ds(pl.multiple_of(t * WIDE, WIDE), WIDE)]

    def wide_columns(reference, t):
        return reference.at[:, pl.ds(pl.multiple_of(t * WIDE, WIDE), WIDE)]

    zero8 = jnp.zeros((8, WIDE), jnp.float32)

    arrived(w2, w_sem.at[3])
    for k in range(2):
        arrived((h3, mb)[k], x_sem.at[k])

    def first_reduction(i, carry):
        p = i // 2
        rows = pl.ds(pl.multiple_of(lax.rem(i, 2) * half, ROWS), half)
        value = times(h3[p, rows], w2[0]) + times(mb[p, rows], w2[1])
        h1[p, rows] = low(value)
        return carry[0] + fold(value), carry[1] + fold(value * value)

    sums = lax.fori_loop(0, 8, first_reduction, (zero8, zero8))
    state = sums_start("thin", [one_row(v) for v in sums])

    arrived(wq, w_sem.at[1])

    def shortcut_product(n, carry):
        value = times(h3[0], wq[2 * n]) + times(mb[0], wq[2 * n + 1])
        side[n] = low(value)
        stat_out[pl.ds(8 + n, 1)] = one_row(fold(value))
        stat_out[pl.ds(12 + n, 1)] = one_row(fold(value * value))
        return carry

    lax.fori_loop(0, 2, shortcut_product, 0)
    sums_middle(state)
    lax.fori_loop(2, 4, shortcut_product, 0)
    fetch_columns(expand_a, wq, 0, w_sem.at[1])
    for k in range(4):
        fetch(reduce_b.at[columns(k)], wq.at[4 + k], w_sem.at[2])
    sums = sums_end(state)
    keep_stats(stat_mid, 0, sums, total_in, gain_mid[0:1], shift_mid[0:1])

    scale, offset = stat_mid[0, 2:3], stat_mid[0, 3:4]
    for column in range(2):
        for g in groups:
            pre = last_row(h1.at[2 + column], g) * scale + offset
            mask = wide_mask(mask_ref[starts[g] * ROWS : (starts[g] + widths[g]) * ROWS])
            halo_a[column, halo_rows(g)] = low(pre * sigmoid(pre) * mask)

    @pl.when(h < n_height - 1)
    def _():
        for column in range(2):
            for g in groups:
                halo_copy(
                    halo_a.at[column, halo_rows(g)],
                    top_row(big_a.at[2 + column], top_starts[g], g),
                    0,
                    h + 1,
                ).start()

    for g in groups:
        per = counts[g] * ROWS // STEP
        base = (top_starts[g] + 1 + widths[g] + 1) * ROWS

        @pl.loop(0, 4)
        def _(p):
            @pl.loop(0, per)
            def _(i):
                rows = pl.ds(pl.multiple_of(starts[g] * ROWS + i * STEP, ROWS), STEP)
                pre = up32(h1[p, rows]) * scale + offset
                value = pre * sigmoid(pre) * wide_mask(mask_ref[rows])
                big_a[p, pl.ds(pl.multiple_of(base + i * STEP, ROWS), STEP)] = low(value)

    fetch(h1, h1_kept, spill_sem.at[0])

    def group_rows(g):
        return slice(starts[g] * ROWS, (starts[g] + counts[g]) * ROWS)

    def window(padded, start, g, dy, dx_):
        first = start + 1 + (1 + dy) * (widths[g] + 1) + dx_
        return padded[rows_at(first, counts[g])]

    def window_a(g, a, c):
        py, dy = lax.rem(a + 1, 2), (a + 1) // 2 - 1
        px, dx_ = lax.rem(c + 1, 2), (c + 1) // 2 - 1
        first = top_starts[g] + 1 + (1 + dy) * (widths[g] + 1) + dx_
        return big_a[2 * py + px, rows_at(first, counts[g])]

    def clear_acc():
        @pl.loop(0, total // STEP)
        def _(i):
            acc[steps(i)] = jnp.zeros((STEP, WIDE), jnp.float32)

    def conv_taps(first, last, window_of, product):
        @pl.loop(first, last)
        def _(t):
            for g in groups:
                acc[group_rows(g)] += product(window_of(g, t // 3, lax.rem(t, 3)), wp[t])

    def masked_sums(target):
        def body(i, carry):
            rows = steps(i)
            value = acc[rows] * wide_mask(mask_ref[rows])
            target[rows] = low(value)
            return carry[0] + fold(value), carry[1] + fold(value * value)

        return lax.fori_loop(0, total // STEP, body, (zero8, zero8))

    clear_acc()
    arrived(wp, w_sem.at[0])
    conv_taps(3, 9, window_a, times)
    halo_wait(halo_a, halo_recv, 0, h > 0)
    conv_taps(0, 3, window_a, times)
    sums = masked_sums(h2)
    state = sums_start("thin", [one_row(v) for v in sums])
    fetch(spatial_b, wp, w_sem.at[0])
    fetch(big_a, a1_kept, spill_sem.at[1])
    halo_wait(halo_a, halo_send, 0, h < n_height - 1)
    sums_middle(state)
    sums = sums_end(state)
    keep_stats(stat_mid, 1, sums, total_out, gain_mid[1:2], shift_mid[1:2])

    def activate(source, target, index):
        scale, offset = stat_mid[index, 2:3], stat_mid[index, 3:4]

        @pl.loop(0, total // STEP)
        def _(i):
            rows = steps(i)
            pre = up32(source[rows]) * scale + offset
            target[rows] = low(pre * sigmoid(pre) * wide_mask(mask_ref[rows]))

    activate(h2, a2, 1)
    arrived(wq.at[0:4], w_sem.at[1])

    def expansion(source, target):
        @pl.loop(0, 4)
        def _(n):
            value = times(source[...], wq[n])
            target[n, 0:total] = low(value)
            stat_out[pl.ds(n, 1)] = one_row(fold(value))
            stat_out[pl.ds(4 + n, 1)] = one_row(fold(value * value))

    expansion(a2, h3)
    state = sums_start("wide", None)
    fetch_columns(expand_b, wq, 0, w_sem.at[1])
    sums_middle(state)
    sums_end(state)

    def out_stats(index, n, row):
        keep_stats(
            mid_or_out,
            4 * index + n,
            [stat_out[row + n : row + n + 1], stat_out[row + 4 + n : row + 5 + n]],
            total_out,
            gain_out[index, n : n + 1],
            shift_out[index, n : n + 1],
        )

    mid_or_out = stat_mid.at[4:16]
    for n in range(4):
        out_stats(0, n, 0)
        out_stats(1, n, 8)

    def out_stat(index, n, row):
        return stat_mid[4 + 4 * index + n, row : row + 1]

    def joint(n, rows):
        return (
            up32(h3[n, rows]) * out_stat(0, n, 2)
            + up32(side[n, rows]) * out_stat(1, n, 2)
            + (out_stat(0, n, 3) + out_stat(1, n, 3))
        )

    arrived(wq.at[4:8], w_sem.at[2])
    clear_acc()

    @pl.loop(0, 4)
    def _(n):
        @pl.loop(0, 2)
        def _(i):
            rows = pl.ds(pl.multiple_of(i * half, ROWS), half)
            value = joint(n, rows)
            value = low(value * sigmoid(value) * wide_mask(mask_ref[rows]))
            mb[n, rows] = value
            acc[rows] += times(value, wq[4 + n])

    def plain_sums(target):
        def body(i, carry):
            rows = steps(i)
            value = acc[rows]
            target[rows] = low(value)
            return carry[0] + fold(value), carry[1] + fold(value * value)

        return lax.fori_loop(0, total // STEP, body, (zero8, zero8))

    sums = plain_sums(h4)
    state = sums_start("thin", [one_row(v) for v in sums])
    sums_middle(state)
    clear_acc()
    sums = sums_end(state)
    keep_stats(stat_mid, 2, sums, total_out, gain_mid[2:3], shift_mid[2:3])

    scale, offset = stat_mid[2, 2:3], stat_mid[2, 3:4]
    for g in groups:
        pre = last_row(h4, g) * scale + offset
        mask = wide_mask(mask_ref[starts[g] * ROWS : (starts[g] + widths[g]) * ROWS])
        halo_down[halo_rows(g)] = low(pre * sigmoid(pre) * mask)
    send_down(halo_down, a4p, 1)
    for g in groups:
        pre = first_row(h4, g) * scale + offset
        mask = wide_mask(mask_ref[starts[g] * ROWS : (starts[g] + widths[g]) * ROWS])
        halo_up[halo_rows(g)] = low(pre * sigmoid(pre) * mask)
    send_up(halo_up, 2)

    def both_base(g):
        return (both_starts[g] + 1 + widths[g] + 1) * ROWS

    for g in groups:

        @pl.loop(0, counts[g] * ROWS // STEP)
        def _(i):
            rows = pl.ds(pl.multiple_of(starts[g] * ROWS + i * STEP, ROWS), STEP)
            pre = up32(h4[rows]) * scale + offset
            value = low(pre * sigmoid(pre) * wide_mask(mask_ref[rows]))
            a4p[pl.ds(pl.multiple_of(both_base(g) + i * STEP, ROWS), STEP)] = value

    def window_b(g, a, c):
        return window(a4p, both_starts[g], g, a - 1, c - 1)

    def window_b_back(g, a, c):
        return window(dhp, both_starts[g], g, 1 - a, 1 - c)

    arrived(wp, w_sem.at[0])
    conv_taps(3, 6, window_b, times)
    halo_wait(halo_down, halo_recv, 1, h > 0)
    halo_wait(halo_in, halo_recv, 2, h < n_height - 1)
    place_below(a4p)
    conv_taps(0, 3, window_b, times)
    conv_taps(6, 9, window_b, times)
    sums = masked_sums(h5)
    state = sums_start("thin", [one_row(v) for v in sums])
    halo_wait(halo_down, halo_send, 1, h < n_height - 1)
    halo_wait(halo_up, halo_send, 2, h > 0)
    sums_middle(state)
    sums = sums_end(state)
    keep_stats(stat_mid, 3, sums, total_out, gain_mid[3:4], shift_mid[3:4])

    activate(h5, a5, 3)
    arrived(wq.at[0:4], w_sem.at[1])
    arrived(big_a, spill_sem.at[1])
    expansion(a5, h6)
    for row in range(8, 16):
        stat_out[row : row + 1] = jnp.zeros((1, WIDE), jnp.float32)
    state = sums_start("wide", None)
    sums_middle(state)
    arrived(h1, spill_sem.at[0])
    sums_end(state)
    for n in range(4):
        out_stats(2, n, 0)

    @pl.loop(0, 4)
    def _(n):
        index = 12 + n
        root, scale = stat_mid[index, 1:2], stat_mid[index, 2:3]
        offset, back = stat_mid[index, 3:4], stat_mid[index, 4:5]
        zero = jnp.zeros((ROWS, WIDE), jnp.float32)
        total_grad, total_dot = zero, zero
        for g in groups:

            def body(i, carry):
                rows = rows_at(starts[g] + i, 1)
                value = up32(h6[n, rows])
                mask = wide_mask(mask_ref[rows])
                z = value * scale + offset + up32(mb[n, rows])
                s = sigmoid(z)
                grad = up_ref[g, n] * (s * (1.0 + z * (1.0 - s))) * mask
                dz[n, rows] = low(grad)
                return (
                    carry[0] + z * s * mask,
                    carry[1] + grad,
                    carry[2] + grad * (value * root + back),
                )

            pool, total_grad, total_dot = lax.fori_loop(
                0, counts[g], body, (zero, total_grad, total_dot)
            )
            pool_slots[h, n, g * ROWS : (g + 1) * ROWS] = low(pool)
        stat_out[pl.ds(n, 1)] = one_row(fold(total_grad))
        stat_out[pl.ds(4 + n, 1)] = one_row(fold(total_dot))

    state = sums_start("wide", None)

    for k in range(1, n_height):
        pltpu.make_async_remote_copy(
            src_ref=pool_slots.at[h],
            dst_ref=pool_slots.at[h],
            send_sem=pool_sem.at[0],
            recv_sem=pool_sem.at[1],
            device_id=(b, lax.rem(h + k, n_height)),
            device_id_type=MESH,
        ).start()
    sums_middle(state)
    clear_acc()
    sums_end(state)

    def out_back(index, sum_row, dot_row, n):
        sums = [stat_out[pl.ds(sum_row + n, 1)], stat_out[pl.ds(dot_row + n, 1)]]
        out_sums[index, 0, pl.ds(n, 1)] = sums[0]
        out_sums[index, 1, pl.ds(n, 1)] = sums[1]
        return back_factors(
            stat_mid, 4 + 4 * index + n, sums, total_out, gain_out[index, pl.ds(n, 1)]
        )

    def mid_back(index, place, sums, number):
        mid_sums[place, 0:1] = sums[0]
        mid_sums[place, 1:2] = sums[1]
        return back_factors(stat_mid, index, sums, number, gain_mid[place : place + 1])

    def mid_gradient(source, index):
        root, scale = stat_mid[index, 1:2], stat_mid[index, 2:3]
        offset, back = stat_mid[index, 3:4], stat_mid[index, 4:5]

        def body(i, carry):
            rows = steps(i)
            value = up32(source[rows])
            pre = value * scale + offset
            s = sigmoid(pre)
            grad = acc[rows] * (s * (1.0 + pre * (1.0 - s))) * wide_mask(mask_ref[rows])
            acc[rows] = grad
            return carry[0] + fold(grad), carry[1] + fold(grad * (value * root + back))

        sums = lax.fori_loop(0, total // STEP, body, (zero8, zero8))
        return [one_row(v) for v in sums]

    @pl.loop(0, 4)
    def _(n):
        main, slope, constant = out_back(2, 0, 4, n)

        @pl.loop(0, 2)
        def _(i):
            rows = pl.ds(pl.multiple_of(i * half, ROWS), half)
            grad = main * up32(dz[n, rows]) + slope * up32(h6[n, rows]) + constant
            grad = low(grad * wide_mask(mask_ref[rows]))
            h6[n, rows] = grad
            acc[rows] += times_t(grad, wq[n])

    sums = mid_gradient(h5, 3)
    state = sums_start("thin", sums)
    fetch_columns(expand_a, wq, 0, w_sem.at[1])
    sums_middle(state)
    store_tiles(
        4, lambda t: t_times(a5[...], h6[t, 0:total]), lambda t: wide_columns(g_expand_b, t)
    )
    fetch(a1_kept, big_a, spill_sem.at[1])
    sums = sums_end(state)

    def mid_step(target, factors, padded):
        main, slope, constant = factors

        def tile(rows):
            grad = main * acc[rows] + slope * up32(target[rows]) + constant
            return low(grad * wide_mask(mask_ref[rows]))

        for g in groups:

            @pl.loop(0, counts[g] * ROWS // STEP)
            def _(i):
                rows = pl.ds(pl.multiple_of(starts[g] * ROWS + i * STEP, ROWS), STEP)
                grad = tile(rows)
                target[rows] = grad
                if padded is not None:
                    padded[pl.ds(pl.multiple_of(both_base(g) + i * STEP, ROWS), STEP)] = grad

    mid_step(h5, mid_back(3, 3, sums, total_out), dhp)
    for g in groups:
        halo_down[halo_rows(g)] = low(last_row(h5, g))
        halo_up[halo_rows(g)] = low(first_row(h5, g))
    send_down(halo_down, dhp, 1)
    send_up(halo_up, 2)
    clear_acc()
    conv_taps(3, 6, window_b_back, times_t)
    halo_wait(halo_down, halo_recv, 1, h > 0)
    halo_wait(halo_in, halo_recv, 2, h < n_height - 1)
    place_below(dhp)
    conv_taps(0, 3, window_b_back, times_t)
    conv_taps(6, 9, window_b_back, times_t)
    fetch(spatial_a, wp, w_sem.at[0])
    sums = mid_gradient(h4, 2)
    state = sums_start("thin", sums)
    halo_wait(halo_down, halo_send, 1, h < n_height - 1)
    halo_wait(halo_up, halo_send, 2, h > 0)
    sums_middle(state)

    def spatial_tile(window_of, grads):
        def value_of(t):
            parts = [
                t_times(window_of(g, t // 3, lax.rem(t, 3)), grads[group_rows(g)]) for g in groups
            ]
            return parts[0] + parts[1] + parts[2]

        return value_of

    store_tiles(9, spatial_tile(window_b, h5), lambda t: g_spatial_b.at[t])
    sums = sums_end(state)

    mid_step(h4, mid_back(2, 2, sums, total_out), None)
    fetch(x.at[0, :, columns(1)], a4p.at[0:total], x_sem.at[1])

    @pl.loop(0, 4)
    def _(n):
        def body(i, carry):
            rows = pl.ds(pl.multiple_of(i * half, ROWS), half)
            grad = times_t(h4[rows], wq[4 + n]) + up32(dz[n, rows])
            z = joint(n, rows)
            s = sigmoid(z)
            grad = grad * (s * (1.0 + z * (1.0 - s))) * wide_mask(mask_ref[rows])
            dz[n, rows] = low(grad)
            main_hat = up32(h3[n, rows]) * out_stat(0, n, 1) + out_stat(0, n, 4)
            side_hat = up32(side[n, rows]) * out_stat(1, n, 1) + out_stat(1, n, 4)
            return (
                carry[0] + fold(grad),
                carry[1] + fold(grad * main_hat),
                carry[2] + fold(grad * side_hat),
            )

        sums = lax.fori_loop(0, 2, body, (zero8, zero8, zero8))
        for v in range(3):
            stat_out[pl.ds(4 * v + n, 1)] = one_row(sums[v])

    state = sums_start("wide", None)
    sums_middle(state)
    store_tiles(
        4, lambda t: t_times(mb[t], h4[...]), lambda t: wide_rows(g_reduce_b, t)
    )
    fetch(x.at[:, :, columns(0)], mb, x_sem.at[0])
    clear_acc()
    sums_end(state)

    arrived(wq.at[0:4], w_sem.at[1])

    @pl.loop(0, 4)
    def _(n):
        main, slope, constant = out_back(0, 0, 4, n)
        main2, slope2, constant2 = out_back(1, 0, 8, n)

        @pl.loop(0, 2)
        def _(i):
            rows = pl.ds(pl.multiple_of(i * half, ROWS), half)
            grad_in = up32(dz[n, rows])
            mask = wide_mask(mask_ref[rows])
            grad = low((main * grad_in + slope * up32(h3[n, rows]) + constant) * mask)
            h3[n, rows] = grad
            acc[rows] += times_t(grad, wq[n])
            other = main2 * grad_in + slope2 * up32(side[n, rows]) + constant2
            side[n, rows] = low(other * mask)

    fetch(h1_kept, h1, spill_sem.at[0])
    fetch_shortcut()
    sums = mid_gradient(h2, 1)
    state = sums_start("thin", sums)
    sums_middle(state)
    store_tiles(4, lambda t: t_times(a2[...], h3[t]), lambda t: wide_columns(g_expand_a, t))
    arrived(mb, x_sem.at[0])
    arrived(a4p.at[0:total], x_sem.at[1])
    store_tiles(
        4,
        lambda t: t_times(mb[0], side[t]),
        lambda t: wide_columns(g_shortcut_a.at[0:WIDE], t),
    )
    store_tiles(
        4,
        lambda t: t_times(a4p[0:total], side[t]),
        lambda t: wide_columns(g_shortcut_a.at[WIDE : 2 * WIDE], t),
    )
    sums = sums_end(state)

    mid_step(h2, mid_back(1, 1, sums, total_out), dhp)
    for g in groups:
        halo_up[halo_rows(g)] = low(first_row(h2, g))
    send_up(halo_up, 2)
    arrived(wp, w_sem.at[0])
    arrived(h1, spill_sem.at[0])
    root, scale = stat_mid[0, 1:2], stat_mid[0, 2:3]
    offset, back = stat_mid[0, 3:4], stat_mid[0, 4:5]
    carry = (zero8, zero8)
    for p in range(4):
        py, px = p // 2, p % 2
        row_taps = ((1, 0),) if py == 0 else ((0, 1), (2, 0))
        column_taps = ((1, 0),) if px == 0 else ((0, 1), (2, 0))
        if p == 2:
            halo_wait(halo_in, halo_recv, 2, h < n_height - 1)
            place_below(dhp)
        for g in groups:
            value = None
            for a, dy in row_taps:
                for c, dx_ in column_taps:
                    product = times_t(window(dhp, both_starts[g], g, dy, dx_), wp[3 * a + c])
                    value = product if value is None else value + product
            acc[group_rows(g)] = value

        def body(i, carry):
            rows = steps(i)
            value = up32(h1[p, rows])
            pre = value * scale + offset
            s = sigmoid(pre)
            grad = acc[rows] * (s * (1.0 + pre * (1.0 - s))) * wide_mask(mask_ref[rows])
            h3[p, rows] = low(grad)
            return carry[0] + fold(grad), carry[1] + fold(grad * (value * root + back))

        carry = lax.fori_loop(0, total // STEP, body, carry)
    state = sums_start("thin", [one_row(v) for v in carry])
    halo_wait(halo_up, halo_send, 2, h > 0)
    sums_middle(state)
    arrived(big_a, spill_sem.at[1])
    store_tiles(9, spatial_tile(window_a, h2), lambda t: g_spatial_a.at[t])
    fetch(x.at[:, :, columns(1)], big_a.at[:, 0:total], x_sem.at[1])
    sums = sums_end(state)

    main, slope, constant = mid_back(0, 0, sums, total_in)

    @pl.loop(0, 4)
    def _(p):
        @pl.loop(0, total // STEP)
        def _(i):
            rows = steps(i)
            grad = main * up32(h3[p, rows]) + slope * up32(h1[p, rows]) + constant
            h1[p, rows] = low(grad * wide_mask(mask_ref[rows]))

    arrived(wq, w_sem.at[1])
    for k in range(2):

        @pl.loop(0, 2)
        def _(i):
            rows = pl.ds(pl.multiple_of(i * half, ROWS), half)
            value = times_t(h1[0, rows], w2[k])
            for n in range(4):
                value = value + times_t(side[n, rows], wq[2 * n + k])
            if k == 0:
                h3[0, rows] = low(value)
            else:
                a4p[rows] = low(value)

    fetch(h3.at[0], dx.at[0, :, columns(0)], dx_sem.at[0])
    fetch(a4p.at[0:total], dx.at[0, :, columns(1)], dx_sem.at[0])

    @pl.loop(1, 4)
    def _(p):
        h3[p] = low(times_t(h1[p], w2[0]))
        side[p] = low(times_t(h1[p], w2[1]))
        fetch(h3.at[p], dx.at[p, :, columns(0)], dx_sem.at[0])
        fetch(side.at[p], dx.at[p, :, columns(1)], dx_sem.at[0])

    arrived(big_a.at[:, 0:total], x_sem.at[1])

    def last_tile(chunk):
        def value_of(t):
            value = t_times(chunk(0), h1[0])
            for p in range(1, 4):
                value = value + t_times(chunk(p), h1[p])
            return value

        return value_of

    store_tiles(1, last_tile(lambda p: mb[p]), lambda t: g_reduce_a.at[0:WIDE])
    store_tiles(
        1, last_tile(lambda p: big_a[p, 0:total]), lambda t: g_reduce_a.at[WIDE : 2 * WIDE]
    )

    others = pool_slots.at[0 : n_height - 1]
    pltpu.make_async_copy(others, others, pool_sem.at[1]).wait()
    pltpu.make_async_copy(others, others, pool_sem.at[0]).wait()
    for g in groups:
        for n in range(4):
            value = None
            for k in range(n_height):
                part = up32(pool_slots[k, n, g * ROWS : (g + 1) * ROWS])
                value = part if value is None else value + part
            pooled[g, n] = value * (1.0 / (widths[g] * widths[g]))

    for slot in range(2):
        arrived(staged.at[slot], g_sem.at[slot])
    arrived(h3, dx_sem.at[0])
    arrived(h3, dx_sem.at[0])


def to_planes(image, live, images):
    count, rows, cols, channels = image.shape
    value = image.reshape(count, rows // 2, 2, cols // 2, 2, channels)
    value = jnp.transpose(value, (2, 4, 1, 3, 0, 5))
    keep = (jnp.arange(rows // 2, dtype=jnp.int32) < live)[None, None, :, None, None, None]
    value = jnp.where(keep, value, jnp.zeros((), value.dtype))
    value = jnp.pad(value, ((0, 0), (0, 0), (0, 0), (0, 1), (0, images - count), (0, 0)))
    return value.reshape(4, -1, channels)


def from_planes(planes, shape):
    count, rows, cols, channels = shape
    value = planes.reshape(2, 2, rows // 2, cols // 2 + 1, -1, channels)
    value = value[:, :, :, : cols // 2, :count]
    return jnp.transpose(value, (4, 2, 0, 3, 1, 5)).reshape(shape)


def per_device(
    image_small, image_medium, image_large, row_counts, reduce_a, first_spatial_weight, expand_a,
    shortcut_a, reduce_b, second_spatial_weight, expand_b, gain_mid, shift_mid, gain_out,
    shift_out, upstream_small, upstream_medium, upstream_large,
):
    images = (image_small, image_medium, image_large)
    upstreams = (upstream_small, upstream_medium, upstream_large)
    n_batch, n_height = lax.axis_size("batch"), lax.axis_size("height")
    heights = [value.shape[1] // 2 for value in images]
    widths = [value.shape[2] // 2 for value in images]
    count = images[0].shape[0]
    live = row_counts[:, lax.axis_index("height")]
    pixels = sum(o * o for o in widths) * count * n_batch
    counts, starts, top_total, _, both_total, _, _ = grids(heights, widths)
    total = sum(counts) * ROWS
    x = jnp.concatenate([to_planes(images[g], live[g], ROWS) for g in range(3)], axis=1)
    masks = []
    for g in range(3):
        row_ok = (jnp.arange(heights[g], dtype=jnp.int32) < live[g])[:, None, None]
        column_ok = (jnp.arange(widths[g] + 1) < widths[g])[None, :, None]
        image_ok = (jnp.arange(ROWS) < count)[None, None, :]
        masks.append(jnp.logical_and(jnp.logical_and(row_ok, column_ok), image_ok).reshape(-1))
    mask = jnp.concatenate(masks).astype(jnp.float32)
    mask = jnp.broadcast_to(mask[:, None], (total, 128))
    edges = (jnp.arange(max(heights))[None, :] == live[:, None] - 1).astype(jnp.float32)
    edges = jnp.broadcast_to(edges[:, :, None, None], edges.shape + (8, 128))
    up = jnp.stack(
        [
            jnp.pad(
                upstreams[g].astype(jnp.float32) / (widths[g] * widths[g]),
                ((0, ROWS - count), (0, 0)),
            )
            for g in range(3)
        ]
    )
    up = jnp.transpose(up.reshape(3, ROWS, 4, WIDE), (0, 2, 1, 3))
    halo = sum(widths) * ROWS
    bf, f32 = jnp.bfloat16, jnp.float32
    dma = pltpu.SemaphoreType.DMA
    vmem = pl.BlockSpec(memory_space=pltpu.VMEM)
    anywhere = pl.BlockSpec(memory_space=pl.ANY)
    flat_a = first_spatial_weight.reshape(9, WIDE, WIDE)
    flat_b = second_spatial_weight.reshape(9, WIDE, WIDE)
    big = pltpu.VMEM((4, total, WIDE), bf)
    thin = pltpu.VMEM((total, WIDE), bf)
    results = pl.pallas_call(
        functools.partial(
            main_kernel, n_batch, n_height, heights, widths, float(4 * pixels), float(pixels)
        ),
        out_shape=[
            jax.ShapeDtypeStruct((3, 4, ROWS, WIDE), f32),
            jax.ShapeDtypeStruct(x.shape, bf),
            jax.ShapeDtypeStruct(reduce_a.shape, bf),
            jax.ShapeDtypeStruct(flat_a.shape, bf),
            jax.ShapeDtypeStruct(expand_a.shape, bf),
            jax.ShapeDtypeStruct(shortcut_a.shape, bf),
            jax.ShapeDtypeStruct(reduce_b.shape, bf),
            jax.ShapeDtypeStruct(flat_b.shape, bf),
            jax.ShapeDtypeStruct(expand_b.shape, bf),
            jax.ShapeDtypeStruct((4, 2, WIDE), f32),
            jax.ShapeDtypeStruct((3, 2, 4, WIDE), f32),
            jax.ShapeDtypeStruct((4, total, WIDE), bf),
            jax.ShapeDtypeStruct((4, top_total * ROWS, WIDE), bf),
        ],
        in_specs=[anywhere] * 8 + [vmem] * 7,
        out_specs=[vmem] + [anywhere] * 8 + [vmem] * 2 + [anywhere] * 2,
        scratch_shapes=[
            big,
            pltpu.VMEM((4, top_total * ROWS, WIDE), bf),
            big, big, big,
            thin, thin, thin, thin, thin,
            pltpu.VMEM((both_total * ROWS, WIDE), bf),
            pltpu.VMEM((both_total * ROWS, WIDE), bf),
            pltpu.VMEM((total, WIDE), f32),
            pltpu.VMEM((9, WIDE, WIDE), bf),
            pltpu.VMEM((8, WIDE, WIDE), bf),
            pltpu.VMEM((2, WIDE, WIDE), bf),
            pltpu.VMEM((2, halo, WIDE), bf),
            pltpu.VMEM((halo, WIDE), bf),
            pltpu.VMEM((halo, WIDE), bf),
            pltpu.VMEM((halo, WIDE), bf),
            pltpu.VMEM((2, WIDE, WIDE), bf),
            pltpu.VMEM((n_height, 4, 3 * ROWS, WIDE), bf),
            pltpu.VMEM((2, n_height, 8, 128), f32),
            pltpu.VMEM((2, n_batch, 8, 128), f32),
            pltpu.VMEM((2, n_height, 16, WIDE), f32),
            pltpu.VMEM((2, n_batch, 16, WIDE), f32),
            pltpu.VMEM((16, 8, WIDE), f32),
            pltpu.VMEM((16, WIDE), f32),
            dma((4,)), dma((2,)), dma((2,)), dma((1,)), dma((2,)),
            dma((2, 2, 2)), dma((2, 2, 2)), dma((3,)), dma((3,)), dma((2,)),
        ],
        compiler_params=pltpu.CompilerParams(
            collective_id=0, has_side_effects=True, vmem_limit_bytes=63 << 20
        ),
        name="both_blocks",
    )(
        x, reduce_a, flat_a, expand_a, shortcut_a, reduce_b, flat_b, expand_b,
        edges, mask, gain_mid, shift_mid,
        gain_out.reshape(3, 4, WIDE), shift_out.reshape(3, 4, WIDE), up,
    )
    pooled = jnp.transpose(results[0], (0, 2, 1, 3)).reshape(3, ROWS, -1)[:, :count]
    backs = [
        from_planes(
            results[1][:, starts[g] * ROWS : (starts[g] + counts[g]) * ROWS], images[g].shape
        )
        for g in range(3)
    ]
    shards = reduce_grads(results[2:9])
    for place in (1, 5):
        shards[place] = shards[place].reshape((3, 3) + shards[place].shape[1:])
    mid, out = results[9], results[10].reshape(3, 2, -1)
    return (
        pooled[0], pooled[1], pooled[2], backs[0], backs[1], backs[2], *shards,
        mid[:, 1], mid[:, 0], out[:, 1], out[:, 0],
    )


def solution(mesh):
    placed = (
        P("batch", "height", None, None),
        P("batch", "height", None, None),
        P("batch", "height", None, None),
        P(),
        P(),
        P(),
        P(),
        P(),
        P(),
        P(),
        P(),
        P(),
        P(),
        P(),
        P(),
        P("batch", None),
        P("batch", None),
        P("batch", None),
    )
    return jax.shard_map(
        per_device,
        mesh=mesh,
        in_specs=placed,
        out_specs=(
            P("batch", None),
            P("batch", None),
            P("batch", None),
            P("batch", "height", None, None),
            P("batch", "height", None, None),
            P("batch", "height", None, None),
            P("batch", None),
            P(None, None, "batch", None),
            P("batch", None),
            P("batch", None),
            P("batch", None),
            P(None, None, "batch", None),
            P("batch", None),
            P(),
            P(),
            P(),
            P(),
        ),
        check_vma=False,
    )
```

```python
import functools

import jax
import jax.numpy as jnp
from jax import lax
from jax.experimental import pallas as pl
from jax.experimental.pallas import tpu as pltpu
from jax.sharding import PartitionSpec as P

epsilon = 1e-05
MESH = pl.DeviceIdType.MESH

WIDE = 512
ROWS = 16
STEP = 64


def sigmoid(values):
    return 0.5 * jnp.tanh(0.5 * values) + 0.5


def up32(values):
    return values.astype(jnp.float32)


def low(values):
    return values.astype(jnp.bfloat16)


def times(left, right):
    return jnp.dot(left, right, preferred_element_type=jnp.float32)


def times_t(left, right):
    return lax.dot_general(
        left, right, (((1,), (1,)), ((), ())), preferred_element_type=jnp.float32
    )


def t_times(left, right):
    return lax.dot_general(
        left, right, (((0,), (0,)), ((), ())), preferred_element_type=jnp.float32
    )


def fold(values):
    return jnp.sum(values.reshape(-1, 8, values.shape[-1]), axis=0)


def one_row(values):
    return jnp.sum(values, axis=0, keepdims=True)


def wide_mask(mask):
    return jnp.concatenate([up32(mask)] * (WIDE // 128), axis=1)


def grids(heights, widths):
    counts = [k * (o + 1) for k, o in zip(heights, widths)]
    starts = [sum(counts[:g]) for g in range(3)]
    top_sizes = [(k + 1) * (o + 1) + 1 for k, o in zip(heights, widths)]
    top_starts = [sum(top_sizes[:g]) for g in range(3)]
    both_sizes = [(k + 2) * (o + 1) + 2 for k, o in zip(heights, widths)]
    both_starts = [sum(both_sizes[:g]) for g in range(3)]
    halo_starts = [sum(widths[:g]) for g in range(3)]
    return counts, starts, sum(top_sizes), top_starts, sum(both_sizes), both_starts, halo_starts


def main_kernel(
    n_batch, n_height, heights, widths, total_in, total_out,
    x_small, x_medium, x_large, reduce_a, spatial_a, expand_a, shortcut_a, reduce_b, spatial_b, expand_b,
    edge_ref, mask_ref, gain_mid, shift_mid, gain_out, shift_out, up_ref,
    pooled, dx_small, dx_medium, dx_large, g_units, mid_sums, out_sums, h1_kept, a1_kept,
    big_b, big_a, h3, side, mb, h2, a2, h4, h5, a5, a4p, dhp, acc, wp, wq, w2,
    halo_up, halo_down, halo_in, keep, away, r0, r1, r2, r3, final, ready, pool_slots,
    thin_h, thin_b, wide_h, wide_b, stat_mid, stat_out,
    w_sem, x_sem, u_send, u_recv, ready_sem, dx_sem, spill_sem, ar_send, ar_recv, halo_send, halo_recv, pool_sem,
):
    b, h = lax.axis_index("batch"), lax.axis_index("height")
    counts, starts, top_total, top_starts, both_total, both_starts, halo_starts = grids(
        heights, widths
    )
    total = sum(counts) * ROWS
    half = total // 2
    groups = range(3)
    h1, dz, h6 = big_b, big_b, big_a
    halo_a = mb.at[0:2, 0 : sum(widths) * ROWS]

    def rows_at(start, count):
        return pl.ds(pl.multiple_of(start * ROWS, ROWS), count * ROWS)

    def steps(index):
        return pl.ds(pl.multiple_of(index * STEP, STEP), STEP)

    def fetch(source, target, sem):
        pltpu.make_async_copy(source, target, sem).start()

    def arrived(target, sem):
        pltpu.make_async_copy(target, target, sem).wait()

    def columns(k):
        return pl.ds(k * WIDE, WIDE)

    def fetch_columns(weight, target, first, sem):
        for n in range(4):
            fetch(weight.at[:, columns(n)], target.at[first + n], sem)

    def fetch_shortcut():
        for n in range(4):
            for k in range(2):
                fetch(shortcut_a.at[columns(k), columns(n)], wq.at[2 * n + k], w_sem.at[1])

    xs, dxs = (x_small, x_medium, x_large), (dx_small, dx_medium, dx_large)

    def band_row(buffer, g, y):
        return buffer.at[pl.ds(starts[g] + y * (widths[g] + 1), widths[g])]

    def by_position(buffer):
        return buffer.reshape(buffer.shape[0] // ROWS, ROWS, WIDE)

    def fetch_plane(p, k, target, sem):
        for g in groups:
            for y in range(heights[g]):
                fetch(
                    xs[g].at[y, p // 2, :, p % 2, :, columns(k)],
                    band_row(by_position(target), g, y),
                    sem,
                )

    def plane_arrived(target, sem):
        pixels = sum(k * o for k, o in zip(heights, widths)) * ROWS
        arrived(target.at[0:pixels], sem)

    def put_plane(p, k, source):
        for g in groups:
            for y in range(heights[g]):
                fetch(
                    band_row(by_position(source), g, y),
                    dxs[g].at[y, p // 2, :, p % 2, :, columns(k)],
                    dx_sem.at[0],
                )

    for k in range(2):
        for p in range(4):
            for g in groups:
                for y in range(heights[g]):
                    edge_place = (starts[g] + y * (widths[g] + 1) + widths[g]) * ROWS
                    (h3, mb)[k][p, edge_place : edge_place + ROWS] = jnp.zeros(
                        (ROWS, WIDE), jnp.bfloat16
                    )
            fetch_plane(p, k, (h3, mb)[k].at[p], x_sem.at[k])
    for k in range(2):
        fetch(reduce_a.at[columns(k)], w2.at[k], w_sem.at[3])
    fetch_shortcut()
    fetch(spatial_a, wp, w_sem.at[0])

    halo_down[...] = jnp.zeros_like(halo_down)
    halo_up[...] = jnp.zeros_like(halo_up)
    halo_in[...] = jnp.zeros_like(halo_in)

    @pl.loop(0, both_total // 2)
    def _(i):
        rows = rows_at(i * 2, 2)
        a4p[rows] = jnp.zeros((2 * ROWS, WIDE), jnp.bfloat16)
        dhp[rows] = jnp.zeros((2 * ROWS, WIDE), jnp.bfloat16)

    for g in groups:
        count = widths[g] + 2
        for p in range(4):
            big_a[p, top_starts[g] * ROWS : (top_starts[g] + count) * ROWS] = jnp.zeros(
                (count * ROWS, WIDE), jnp.bfloat16
            )

    barrier = pltpu.get_barrier_semaphore()
    for k in range(1, n_height):
        pl.semaphore_signal(
            barrier, inc=1, device_id=(b, lax.rem(h + k, n_height)), device_id_type=MESH
        )

    @pl.loop(1, n_batch)
    def _(k):
        pl.semaphore_signal(
            barrier, inc=1, device_id=(lax.rem(b + k, n_batch), h), device_id_type=MESH
        )

    pl.semaphore_wait(barrier, n_height + n_batch - 2)

    turn = [0]

    def ar_spread(slots, me, count, peer, sems):
        @pl.loop(1, count)
        def _(k):
            pltpu.make_async_remote_copy(
                src_ref=slots.at[me],
                dst_ref=slots.at[me],
                send_sem=ar_send.at[sems],
                recv_sem=ar_recv.at[sems],
                device_id=peer(lax.rem(me + k, count)),
                device_id_type=MESH,
            ).start()

    def ar_wait(slots, count, sems, which):
        others = slots.at[0 : count - 1]
        pltpu.make_async_copy(others, others, which.at[sems]).wait()

    def sums_start(vectors):
        slot = turn[0] % 2
        turn[0] += 1
        first, second = thin_h.at[slot], thin_b.at[slot]
        for v, vector in enumerate(vectors):
            for j in range(4):
                first[h, 4 * v + j : 4 * v + j + 1, :] = vector[:, 128 * j : 128 * (j + 1)]
        ar_spread(first, h, n_height, lambda p: (b, p), (0, 0, slot))
        return first, second, 0, slot

    def wide_start(part):
        count = 16 if part is None else 8
        rows = pl.ds(8 * (part or 0), count)
        first, second = wide_h.at[:, rows], wide_b.at[:, rows]
        first[h] = stat_out[0:count]
        ar_spread(first, h, n_height, lambda p: (b, p), (1, 0, part or 0))
        return first, second, 1, part or 0

    def sums_middle(state):
        first, second, kind, slot = state
        ar_wait(first, n_height, (kind, 0, slot), ar_recv)
        second[b] = jnp.sum(first[...], axis=0)
        ar_spread(second, b, n_batch, lambda p: (p, h), (kind, 1, slot))

    def sums_end(state):
        first, second, kind, slot = state
        ar_wait(second, n_batch, (kind, 1, slot), ar_recv)
        summed = jnp.sum(second[...], axis=0)
        ar_wait(first, n_height, (kind, 0, slot), ar_send)
        ar_wait(second, n_batch, (kind, 1, slot), ar_send)
        if kind == 0:
            return [
                jnp.concatenate([summed[4 * v + j : 4 * v + j + 1] for j in range(4)], axis=1)
                for v in range(2)
            ]
        stat_out[0 : summed.shape[0]] = summed
        return None

    def keep_stats(kept, index, sums, number, gain, shift):
        centre = sums[0] * (1.0 / number)
        root = lax.rsqrt(sums[1] * (1.0 / number) - centre * centre + epsilon)
        scale = root * gain
        kept[index, 0:1] = centre
        kept[index, 1:2] = root
        kept[index, 2:3] = scale
        kept[index, 3:4] = shift - centre * scale
        kept[index, 4:5] = -centre * root

    def back_factors(kept, index, sums, number, gain):
        centre, root = kept[index, 0:1], kept[index, 1:2]
        main = gain * root
        slope = -main * root * sums[1] * (1.0 / number)
        return main, slope, -main * sums[0] * (1.0 / number) - slope * centre

    def halo_copy(source, target, sem, peer):
        return pltpu.make_async_remote_copy(
            src_ref=source,
            dst_ref=target,
            send_sem=halo_send.at[sem],
            recv_sem=halo_recv.at[sem],
            device_id=(b, peer),
            device_id_type=MESH,
        )

    def halo_rows(g):
        return slice(halo_starts[g] * ROWS, (halo_starts[g] + widths[g]) * ROWS)

    def top_row(padded, start, g):
        return padded.at[pl.ds((start + 1) * ROWS, widths[g] * ROWS)]

    def send_down(buffer, padded, sem):
        @pl.when(h < n_height - 1)
        def _():
            for g in groups:
                halo_copy(
                    buffer.at[halo_rows(g)], top_row(padded, both_starts[g], g), sem, h + 1
                ).start()

    def send_up(buffer, sem):
        @pl.when(h > 0)
        def _():
            halo_copy(buffer, halo_in, sem, h - 1).start()

    def halo_wait(buffer, sems, sem, condition):
        @pl.when(condition)
        def _():
            arrived(buffer, sems.at[sem])

    def place_below(padded):
        for g in groups:
            stride = widths[g] + 1
            for y in range(1, heights[g] + 1):
                is_edge = edge(g, y - 1)

                @pl.loop(0, widths[g])
                def _(col):
                    rows = rows_at(both_starts[g] + 1 + (y + 1) * stride + col, 1)
                    value = up32(halo_in[rows_at(halo_starts[g] + col, 1)]) * is_edge
                    if y < heights[g]:
                        value = value + up32(padded[rows])
                    padded[rows] = low(value)

    def edge(g, y):
        return wide_mask(edge_ref[g, y, 0:1])

    def first_row(source, g, row=0):
        start = (starts[g] + row * (widths[g] + 1)) * ROWS
        return up32(source[start : start + widths[g] * ROWS])

    def last_row(source, g):
        value = first_row(source, g) * edge(g, 0)
        for y in range(1, heights[g]):
            value = value + first_row(source, g, y) * edge(g, y)
        return value

    core, high = lax.rem(h, 2), h // 2
    low_bit, rest = lax.rem(b, 2), b // 2
    n_rest = n_batch // 2
    unit_rows = WIDE // n_batch

    def either(is_one, one, zero):
        return is_one * one + (1 - is_one) * zero

    first, second = either(core, low_bit, high), either(core, high, low_bit)
    core_peer = (b, h + 1 - 2 * core)
    high_peer = (b, h + 2 - 4 * high)
    low_peer = (b + 1 - 2 * low_bit, h)
    first_peer = [either(core, low_peer[i], high_peer[i]) for i in range(2)]
    second_peer = [either(core, high_peer[i], low_peer[i]) for i in range(2)]

    def ring(buffer, unit):
        return lax.rem(unit, buffer.shape[0])

    def unit_copy(level, unit, source, target, peer):
        return pltpu.make_async_remote_copy(
            src_ref=source,
            dst_ref=target,
            send_sem=u_send.at[level, lax.rem(unit, 16)],
            recv_sem=u_recv.at[level, lax.rem(unit, 16)],
            device_id=tuple(peer),
            device_id_type=MESH,
        )

    def hop(level, unit):
        kept = keep.at[ring(keep, unit)]
        if level == 0:
            return unit_copy(
                0, unit, away.at[ring(away, unit)], r0.at[ring(r0, unit)], core_peer
            )
        if level == 1:
            return unit_copy(1, unit, kept.at[1 - first], r1.at[ring(r1, unit)], first_peer)
        if level == 2:
            return unit_copy(
                2, unit, kept.at[first, 1 - second], r2.at[ring(r2, unit)], second_peer
            )
        if level == 4:
            mine = final.at[ring(final, unit), core, high]
            return unit_copy(4, unit, mine, mine, high_peer)
        both = final.at[ring(final, unit), core]
        return unit_copy(5, unit, both, both, core_peer)

    def add_to(target, source):
        target[...] = low(up32(target[...]) + up32(source[...]))

    def rest_wait(unit, sems):
        others = r3.at[ring(r3, unit)]
        pltpu.make_async_copy(others, others, sems.at[3, lax.rem(unit, 16)]).wait()

    def round_0(unit):
        hop(0, unit).start()

    def round_1(unit):
        hop(0, unit).wait()
        kept, got = keep.at[ring(keep, unit)], r0.at[ring(r0, unit)]

        @pl.loop(0, n_rest)
        def _(k):
            for i in range(2):
                for j in range(2):
                    add_to(kept.at[i, j, k], got.at[i, j, k])

        hop(1, unit).start()

    def round_2(unit):
        hop(1, unit).wait_recv()
        kept, got = keep.at[ring(keep, unit), first], r1.at[ring(r1, unit)]

        @pl.loop(0, n_rest)
        def _(k):
            for j in range(2):
                add_to(kept.at[j, k], got.at[j, k])

        hop(2, unit).start()

    def round_3(unit):
        hop(2, unit).wait_recv()
        kept, got = keep.at[ring(keep, unit), first, second], r2.at[ring(r2, unit)]

        @pl.loop(0, n_rest)
        def _(k):
            add_to(kept.at[k], got.at[k])

        @pl.loop(1, n_rest)
        def _(k):
            unit_copy(
                3,
                unit,
                kept.at[lax.rem(rest + k, n_rest)],
                r3.at[ring(r3, unit), n_rest - 1 - k],
                (lax.rem(rest + k, n_rest) * 2 + low_bit, h),
            ).start()

    def round_4(unit):
        rest_wait(unit, u_recv)
        value = up32(keep[ring(keep, unit), first, second, rest])
        for k in range(n_rest - 1):
            value = value + up32(r3[ring(r3, unit), k])
        final[ring(final, unit), core, high] = low(value)
        hop(4, unit).start()

    def round_5(unit):
        hop(4, unit).wait_recv()
        hop(5, unit).start()

    def round_6(unit):
        hop(5, unit).wait_recv()
        for level in (1, 2, 4, 5):
            hop(level, unit).wait_send()
        rest_wait(unit, u_send)
        slot = ring(ready, unit)

        @pl.when(unit >= ready.shape[0])
        def _():
            arrived(ready.at[slot], ready_sem.at[slot])

        for c in range(2):
            for i in range(2):
                lane = 128 * (2 * c + i)
                ready[slot, :, lane : lane + 128] = up32(final[ring(final, unit), c, i])
        fetch(ready.at[slot], g_units.at[unit], ready_sem.at[slot])

    rounds = (
        (0, round_0), (2, round_1), (4, round_2), (5, round_3), (7, round_4), (8, round_5),
        (10, round_6),
    )
    clock, made, produced = [0], [0], []

    def advance(index, base, count):
        for lag, act in rounds:
            for start, size, unit in produced:
                from_, to = max(base - lag, start), min(base - lag + count, start + size)
                if from_ >= to:
                    continue
                target = base - lag - start + unit + index
                if to - from_ == count:
                    act(target)
                else:
                    shift = base - lag
                    inside = jnp.logical_and(index >= from_ - shift, index < to - shift)
                    pl.when(inside)(functools.partial(act, target))

    def idle(count):
        base = clock[0]
        clock[0] += count

        @pl.loop(0, count)
        def _(i):
            advance(i, base, count)

    def ticks(count):
        base = clock[0]
        clock[0] += count
        return lambda i: advance(i, base, count)

    def put(value, unit, units, first_shard):
        shard_rows = units * unit_rows
        own_side = core == 0
        left, right = low(value[:, : WIDE // 2]), low(value[:, WIDE // 2 :])
        own, other = jnp.where(own_side, left, right), jnp.where(own_side, right, left)
        for s in range(WIDE // shard_rows):
            shard = first_shard + s
            shard_low, shard_rest = s % 2, shard // 2
            for q in range(units):
                rows = slice(s * shard_rows + q * unit_rows, s * shard_rows + (q + 1) * unit_rows)
                for i in range(2):
                    lanes = slice(128 * i, 128 * (i + 1))
                    keep[
                        ring(keep, unit + q),
                        either(core, shard_low, i),
                        either(core, i, shard_low),
                        shard_rest,
                    ] = own[rows, lanes]
                    away[
                        ring(away, unit + q),
                        either(core, i, shard_low),
                        either(core, shard_low, i),
                        shard_rest,
                    ] = other[rows, lanes]

    def produce(count, units, make):
        base, unit = clock[0], made[0]
        produced.append((base, count * units, unit))
        clock[0] += count * units
        made[0] += count * units

        @pl.loop(0, count)
        def _(t):
            make(t, unit + t * units)
            if units == 1:
                advance(t, base, count)
            else:

                @pl.loop(0, units)
                def _(q):
                    advance(t * units + q, base, count * units)

    zero8 = jnp.zeros((8, WIDE), jnp.float32)

    arrived(w2, w_sem.at[3])
    for k in range(2):
        for p in range(4):
            plane_arrived((h3, mb)[k].at[p], x_sem.at[k])

    def first_reduction(i, carry):
        p = i // 2
        rows = pl.ds(pl.multiple_of(lax.rem(i, 2) * half, ROWS), half)
        value = times(h3[p, rows], w2[0]) + times(mb[p, rows], w2[1])
        value = value * wide_mask(mask_ref[rows])
        h1[p, rows] = low(value)
        return carry[0] + fold(value), carry[1] + fold(value * value)

    sums = lax.fori_loop(0, 8, first_reduction, (zero8, zero8))
    state = sums_start([one_row(v) for v in sums])

    arrived(wq, w_sem.at[1])

    def shortcut_product(n, carry):
        value = times(h3[0], wq[2 * n]) + times(mb[0], wq[2 * n + 1])
        value = value * wide_mask(mask_ref[...])
        side[n] = low(value)
        stat_out[pl.ds(8 + n, 1)] = one_row(fold(value))
        stat_out[pl.ds(12 + n, 1)] = one_row(fold(value * value))
        return carry

    lax.fori_loop(0, 2, shortcut_product, 0)
    sums_middle(state)
    lax.fori_loop(2, 4, shortcut_product, 0)
    fetch_columns(expand_a, wq, 0, w_sem.at[1])
    for k in range(4):
        fetch(reduce_b.at[columns(k)], wq.at[4 + k], w_sem.at[2])
    sums = sums_end(state)
    keep_stats(stat_mid, 0, sums, total_in, gain_mid[0:1], shift_mid[0:1])

    scale, offset = stat_mid[0, 2:3], stat_mid[0, 3:4]
    for column in range(2):
        for g in groups:
            pre = last_row(h1.at[2 + column], g) * scale + offset
            mask = wide_mask(mask_ref[starts[g] * ROWS : (starts[g] + widths[g]) * ROWS])
            halo_a[column, halo_rows(g)] = low(pre * sigmoid(pre) * mask)

    @pl.when(h < n_height - 1)
    def _():
        for column in range(2):
            for g in groups:
                halo_copy(
                    halo_a.at[column, halo_rows(g)],
                    top_row(big_a.at[2 + column], top_starts[g], g),
                    0,
                    h + 1,
                ).start()

    for g in groups:
        per = counts[g] * ROWS // STEP
        base = (top_starts[g] + 1 + widths[g] + 1) * ROWS

        @pl.loop(0, 4)
        def _(p):
            @pl.loop(0, per)
            def _(i):
                rows = pl.ds(pl.multiple_of(starts[g] * ROWS + i * STEP, ROWS), STEP)
                pre = up32(h1[p, rows]) * scale + offset
                value = pre * sigmoid(pre) * wide_mask(mask_ref[rows])
                big_a[p, pl.ds(pl.multiple_of(base + i * STEP, ROWS), STEP)] = low(value)

    fetch(h1, h1_kept, spill_sem.at[0])

    def group_rows(g):
        return slice(starts[g] * ROWS, (starts[g] + counts[g]) * ROWS)

    def window(padded, start, g, dy, dx_):
        first = start + 1 + (1 + dy) * (widths[g] + 1) + dx_
        return padded[rows_at(first, counts[g])]

    def window_a(g, a, c):
        py, dy = lax.rem(a + 1, 2), (a + 1) // 2 - 1
        px, dx_ = lax.rem(c + 1, 2), (c + 1) // 2 - 1
        first = top_starts[g] + 1 + (1 + dy) * (widths[g] + 1) + dx_
        return big_a[2 * py + px, rows_at(first, counts[g])]

    def clear_acc():
        @pl.loop(0, total // STEP)
        def _(i):
            acc[steps(i)] = jnp.zeros((STEP, WIDE), jnp.float32)

    def conv_taps(start, last, window_of, product):
        tick = ticks(last - start) if produced else None

        @pl.loop(start, last)
        def _(t):
            for g in groups:
                acc[group_rows(g)] += product(window_of(g, t // 3, lax.rem(t, 3)), wp[t])
            if tick is not None:
                tick(t - start)

    def masked_sums(target):
        def body(i, carry):
            rows = steps(i)
            value = acc[rows] * wide_mask(mask_ref[rows])
            target[rows] = low(value)
            return carry[0] + fold(value), carry[1] + fold(value * value)

        return lax.fori_loop(0, total // STEP, body, (zero8, zero8))

    clear_acc()
    arrived(wp, w_sem.at[0])
    conv_taps(3, 9, window_a, times)
    halo_wait(halo_a, halo_recv, 0, h > 0)
    conv_taps(0, 3, window_a, times)
    sums = masked_sums(h2)
    state = sums_start([one_row(v) for v in sums])
    fetch(spatial_b, wp, w_sem.at[0])
    fetch(big_a, a1_kept, spill_sem.at[1])
    halo_wait(halo_a, halo_send, 0, h < n_height - 1)
    sums_middle(state)
    sums = sums_end(state)
    keep_stats(stat_mid, 1, sums, total_out, gain_mid[1:2], shift_mid[1:2])

    def activate(source, target, index):
        scale, offset = stat_mid[index, 2:3], stat_mid[index, 3:4]

        @pl.loop(0, total // STEP)
        def _(i):
            rows = steps(i)
            pre = up32(source[rows]) * scale + offset
            target[rows] = low(pre * sigmoid(pre) * wide_mask(mask_ref[rows]))

    activate(h2, a2, 1)
    arrived(wq.at[0:4], w_sem.at[1])

    def expansion(source, target):
        @pl.loop(0, 4)
        def _(n):
            value = times(source[...], wq[n])
            target[n, 0:total] = low(value)
            stat_out[pl.ds(n, 1)] = one_row(fold(value))
            stat_out[pl.ds(4 + n, 1)] = one_row(fold(value * value))

    expansion(a2, h3)
    state = wide_start(None)
    fetch_columns(expand_b, wq, 0, w_sem.at[1])
    sums_middle(state)
    sums_end(state)

    def out_stats(index, n, row):
        keep_stats(
            mid_or_out,
            4 * index + n,
            [stat_out[row + n : row + n + 1], stat_out[row + 4 + n : row + 5 + n]],
            total_out,
            gain_out[index, n : n + 1],
            shift_out[index, n : n + 1],
        )

    mid_or_out = stat_mid.at[4:16]
    for n in range(4):
        out_stats(0, n, 0)
        out_stats(1, n, 8)

    def out_stat(index, n, row):
        return stat_mid[4 + 4 * index + n, row : row + 1]

    def joint(n, rows):
        return (
            up32(h3[n, rows]) * out_stat(0, n, 2)
            + up32(side[n, rows]) * out_stat(1, n, 2)
            + (out_stat(0, n, 3) + out_stat(1, n, 3))
        )

    arrived(wq.at[4:8], w_sem.at[2])
    clear_acc()

    @pl.loop(0, 4)
    def _(n):
        @pl.loop(0, 2)
        def _(i):
            rows = pl.ds(pl.multiple_of(i * half, ROWS), half)
            value = joint(n, rows)
            value = low(value * sigmoid(value) * wide_mask(mask_ref[rows]))
            mb[n, rows] = value
            acc[rows] += times(value, wq[4 + n])

    def plain_sums(target):
        def body(i, carry):
            rows = steps(i)
            value = acc[rows]
            target[rows] = low(value)
            return carry[0] + fold(value), carry[1] + fold(value * value)

        return lax.fori_loop(0, total // STEP, body, (zero8, zero8))

    sums = plain_sums(h4)
    state = sums_start([one_row(v) for v in sums])
    sums_middle(state)
    clear_acc()
    sums = sums_end(state)
    keep_stats(stat_mid, 2, sums, total_out, gain_mid[2:3], shift_mid[2:3])

    scale, offset = stat_mid[2, 2:3], stat_mid[2, 3:4]
    for g in groups:
        pre = last_row(h4, g) * scale + offset
        mask = wide_mask(mask_ref[starts[g] * ROWS : (starts[g] + widths[g]) * ROWS])
        halo_down[halo_rows(g)] = low(pre * sigmoid(pre) * mask)
    send_down(halo_down, a4p, 1)
    for g in groups:
        pre = first_row(h4, g) * scale + offset
        mask = wide_mask(mask_ref[starts[g] * ROWS : (starts[g] + widths[g]) * ROWS])
        halo_up[halo_rows(g)] = low(pre * sigmoid(pre) * mask)
    send_up(halo_up, 2)

    def both_base(g):
        return (both_starts[g] + 1 + widths[g] + 1) * ROWS

    for g in groups:

        @pl.loop(0, counts[g] * ROWS // STEP)
        def _(i):
            rows = pl.ds(pl.multiple_of(starts[g] * ROWS + i * STEP, ROWS), STEP)
            pre = up32(h4[rows]) * scale + offset
            value = low(pre * sigmoid(pre) * wide_mask(mask_ref[rows]))
            a4p[pl.ds(pl.multiple_of(both_base(g) + i * STEP, ROWS), STEP)] = value

    def window_b(g, a, c):
        return window(a4p, both_starts[g], g, a - 1, c - 1)

    def window_b_back(g, a, c):
        return window(dhp, both_starts[g], g, 1 - a, 1 - c)

    arrived(wp, w_sem.at[0])
    conv_taps(3, 6, window_b, times)
    halo_wait(halo_down, halo_recv, 1, h > 0)
    halo_wait(halo_in, halo_recv, 2, h < n_height - 1)
    place_below(a4p)
    conv_taps(0, 3, window_b, times)
    conv_taps(6, 9, window_b, times)
    sums = masked_sums(h5)
    state = sums_start([one_row(v) for v in sums])
    halo_wait(halo_down, halo_send, 1, h < n_height - 1)
    halo_wait(halo_up, halo_send, 2, h > 0)
    sums_middle(state)
    sums = sums_end(state)
    keep_stats(stat_mid, 3, sums, total_out, gain_mid[3:4], shift_mid[3:4])

    activate(h5, a5, 3)
    arrived(wq.at[0:4], w_sem.at[1])
    arrived(big_a, spill_sem.at[1])
    expansion(a5, h6)
    state = wide_start(0)
    sums_middle(state)
    arrived(h1, spill_sem.at[0])
    sums_end(state)
    for n in range(4):
        out_stats(2, n, 0)

    @pl.loop(0, 4)
    def _(n):
        index = 12 + n
        root, scale = stat_mid[index, 1:2], stat_mid[index, 2:3]
        offset, back = stat_mid[index, 3:4], stat_mid[index, 4:5]
        zero = jnp.zeros((ROWS, WIDE), jnp.float32)
        total_grad, total_dot = zero, zero
        for g in groups:
            share = 1.0 / (widths[g] * widths[g])

            def body(i, carry):
                rows = rows_at(starts[g] + i, 1)
                value = up32(h6[n, rows])
                mask = wide_mask(mask_ref[rows])
                z = value * scale + offset + up32(mb[n, rows])
                s = sigmoid(z)
                grad = up32(up_ref[g, n]) * (s * (1.0 + z * (1.0 - s))) * (mask * share)
                dz[n, rows] = low(grad)
                return (
                    carry[0] + z * s * mask,
                    carry[1] + grad,
                    carry[2] + grad * (value * root + back),
                )

            pool, total_grad, total_dot = lax.fori_loop(
                0, counts[g], body, (zero, total_grad, total_dot)
            )
            pool_slots[h, n, g * ROWS : (g + 1) * ROWS] = low(pool)
        stat_out[pl.ds(n, 1)] = one_row(fold(total_grad))
        stat_out[pl.ds(4 + n, 1)] = one_row(fold(total_dot))

    state = wide_start(1)

    for k in range(1, n_height):
        pltpu.make_async_remote_copy(
            src_ref=pool_slots.at[h],
            dst_ref=pool_slots.at[h],
            send_sem=pool_sem.at[0],
            recv_sem=pool_sem.at[1],
            device_id=(b, lax.rem(h + k, n_height)),
            device_id_type=MESH,
        ).start()
    sums_middle(state)
    clear_acc()
    sums_end(state)

    def out_back(index, sum_row, dot_row, n):
        sums = [stat_out[pl.ds(sum_row + n, 1)], stat_out[pl.ds(dot_row + n, 1)]]
        out_sums[index, 0, pl.ds(n, 1)] = sums[0]
        out_sums[index, 1, pl.ds(n, 1)] = sums[1]
        return back_factors(
            stat_mid, 4 + 4 * index + n, sums, total_out, gain_out[index, pl.ds(n, 1)]
        )

    def mid_back(index, place, sums, number):
        mid_sums[place, 0:1] = sums[0]
        mid_sums[place, 1:2] = sums[1]
        return back_factors(stat_mid, index, sums, number, gain_mid[place : place + 1])

    def mid_gradient(source, index):
        root, scale = stat_mid[index, 1:2], stat_mid[index, 2:3]
        offset, back = stat_mid[index, 3:4], stat_mid[index, 4:5]

        def body(i, carry):
            rows = steps(i)
            value = up32(source[rows])
            pre = value * scale + offset
            s = sigmoid(pre)
            grad = acc[rows] * (s * (1.0 + pre * (1.0 - s))) * wide_mask(mask_ref[rows])
            acc[rows] = grad
            return carry[0] + fold(grad), carry[1] + fold(grad * (value * root + back))

        sums = lax.fori_loop(0, total // STEP, body, (zero8, zero8))
        return [one_row(v) for v in sums]

    @pl.loop(0, 4)
    def _(n):
        main, slope, constant = out_back(2, 0, 4, n)

        @pl.loop(0, 2)
        def _(i):
            rows = pl.ds(pl.multiple_of(i * half, ROWS), half)
            grad = main * up32(dz[n, rows]) + slope * up32(h6[n, rows]) + constant
            grad = low(grad * wide_mask(mask_ref[rows]))
            h6[n, rows] = grad
            acc[rows] += times_t(grad, wq[n])

    sums = mid_gradient(h5, 3)
    state = sums_start(sums)
    fetch_columns(expand_a, wq, 0, w_sem.at[1])
    sums_middle(state)
    produce(4, 1, lambda t, unit: put(t_times(a5[...], h6[t, 0:total]), unit, 1, 0))
    fetch(a1_kept, big_a, spill_sem.at[1])
    sums = sums_end(state)

    def mid_step(target, factors, padded):
        main, slope, constant = factors

        def tile(rows):
            grad = main * acc[rows] + slope * up32(target[rows]) + constant
            return low(grad * wide_mask(mask_ref[rows]))

        for g in groups:

            @pl.loop(0, counts[g] * ROWS // STEP)
            def _(i):
                rows = pl.ds(pl.multiple_of(starts[g] * ROWS + i * STEP, ROWS), STEP)
                grad = tile(rows)
                target[rows] = grad
                if padded is not None:
                    padded[pl.ds(pl.multiple_of(both_base(g) + i * STEP, ROWS), STEP)] = grad

    mid_step(h5, mid_back(3, 3, sums, total_out), dhp)
    for g in groups:
        halo_down[halo_rows(g)] = low(last_row(h5, g))
        halo_up[halo_rows(g)] = low(first_row(h5, g))
    send_down(halo_down, dhp, 1)
    send_up(halo_up, 2)
    clear_acc()
    conv_taps(3, 6, window_b_back, times_t)
    halo_wait(halo_down, halo_recv, 1, h > 0)
    halo_wait(halo_in, halo_recv, 2, h < n_height - 1)
    place_below(dhp)
    conv_taps(0, 3, window_b_back, times_t)
    conv_taps(6, 9, window_b_back, times_t)
    fetch(spatial_a, wp, w_sem.at[0])
    sums = mid_gradient(h4, 2)
    state = sums_start(sums)
    halo_wait(halo_down, halo_send, 1, h < n_height - 1)
    halo_wait(halo_up, halo_send, 2, h > 0)
    sums_middle(state)

    def spatial_tile(window_of, grads):
        def value_of(t):
            parts = [
                t_times(window_of(g, t // 3, lax.rem(t, 3)), grads[group_rows(g)]) for g in groups
            ]
            return parts[0] + parts[1] + parts[2]

        return value_of

    tile_b = spatial_tile(window_b, h5)
    produce(9, 1, lambda t, unit: put(tile_b(t), unit, 1, 0))
    sums = sums_end(state)

    mid_step(h4, mid_back(2, 2, sums, total_out), None)
    fetch_plane(0, 1, a4p, x_sem.at[1])

    tick = ticks(8)

    @pl.loop(0, 4)
    def _(n):
        def body(i, carry):
            tick(2 * n + i)
            rows = pl.ds(pl.multiple_of(i * half, ROWS), half)
            grad = times_t(h4[rows], wq[4 + n]) + up32(dz[n, rows])
            z = joint(n, rows)
            s = sigmoid(z)
            grad = grad * (s * (1.0 + z * (1.0 - s))) * wide_mask(mask_ref[rows])
            dz[n, rows] = low(grad)
            main_hat = up32(h3[n, rows]) * out_stat(0, n, 1) + out_stat(0, n, 4)
            side_hat = up32(side[n, rows]) * out_stat(1, n, 1) + out_stat(1, n, 4)
            return (
                carry[0] + fold(grad),
                carry[1] + fold(grad * main_hat),
                carry[2] + fold(grad * side_hat),
            )

        sums = lax.fori_loop(0, 2, body, (zero8, zero8, zero8))
        for v in range(3):
            stat_out[pl.ds(4 * v + n, 1)] = one_row(sums[v])

    state = wide_start(None)
    sums_middle(state)

    def tile_reduce_b(step, unit):
        @pl.loop(0, 4)
        def _(t):
            put(t_times(mb[t], h4[...]), unit, 4, t * (n_batch // 4))

    produce(1, 4, tile_reduce_b)
    for p in range(4):
        fetch_plane(p, 0, mb.at[p], x_sem.at[0])
    clear_acc()
    sums_end(state)

    arrived(wq.at[0:4], w_sem.at[1])
    tick_11 = ticks(8)

    @pl.loop(0, 4)
    def _(n):
        main, slope, constant = out_back(0, 0, 4, n)
        main2, slope2, constant2 = out_back(1, 0, 8, n)

        @pl.loop(0, 2)
        def _(i):
            tick_11(2 * n + i)
            rows = pl.ds(pl.multiple_of(i * half, ROWS), half)
            grad_in = up32(dz[n, rows])
            mask = wide_mask(mask_ref[rows])
            grad = low((main * grad_in + slope * up32(h3[n, rows]) + constant) * mask)
            h3[n, rows] = grad
            acc[rows] += times_t(grad, wq[n])
            other = main2 * grad_in + slope2 * up32(side[n, rows]) + constant2
            side[n, rows] = low(other * mask)

    fetch(h1_kept, h1, spill_sem.at[0])
    fetch_shortcut()
    sums = mid_gradient(h2, 1)
    state = sums_start(sums)
    sums_middle(state)
    produce(4, 1, lambda t, unit: put(t_times(a2[...], h3[t]), unit, 1, 0))
    for p in range(4):
        plane_arrived(mb.at[p], x_sem.at[0])
    plane_arrived(a4p, x_sem.at[1])

    def tile_shortcut(t, unit):
        put(t_times(mb[0], side[t]), unit, 2, 0)
        put(t_times(a4p[0:total], side[t]), unit, 2, n_batch // 2)

    produce(4, 2, tile_shortcut)
    sums = sums_end(state)

    mid_step(h2, mid_back(1, 1, sums, total_out), dhp)
    for g in groups:
        halo_up[halo_rows(g)] = low(first_row(h2, g))
    send_up(halo_up, 2)
    arrived(wp, w_sem.at[0])
    arrived(h1, spill_sem.at[0])
    root, scale = stat_mid[0, 1:2], stat_mid[0, 2:3]
    offset, back = stat_mid[0, 3:4], stat_mid[0, 4:5]
    carry = (zero8, zero8)
    for p in range(4):
        py, px = p // 2, p % 2
        row_taps = ((1, 0),) if py == 0 else ((0, 1), (2, 0))
        column_taps = ((1, 0),) if px == 0 else ((0, 1), (2, 0))
        if p == 2:
            halo_wait(halo_in, halo_recv, 2, h < n_height - 1)
            place_below(dhp)
        for g in groups:
            value = None
            for a, dy in row_taps:
                for c, dx_ in column_taps:
                    product = times_t(window(dhp, both_starts[g], g, dy, dx_), wp[3 * a + c])
                    value = product if value is None else value + product
            acc[group_rows(g)] = value

        def body(i, carry):
            rows = steps(i)
            value = up32(h1[p, rows])
            pre = value * scale + offset
            s = sigmoid(pre)
            grad = acc[rows] * (s * (1.0 + pre * (1.0 - s))) * wide_mask(mask_ref[rows])
            h3[p, rows] = low(grad)
            return carry[0] + fold(grad), carry[1] + fold(grad * (value * root + back))

        carry = lax.fori_loop(0, total // STEP, body, carry)
        idle(2)
    state = sums_start([one_row(v) for v in carry])
    halo_wait(halo_up, halo_send, 2, h > 0)
    sums_middle(state)
    arrived(big_a, spill_sem.at[1])
    tile_a = spatial_tile(window_a, h2)
    produce(9, 1, lambda t, unit: put(tile_a(t), unit, 1, 0))
    for p in range(4):
        fetch_plane(p, 1, big_a.at[p], x_sem.at[1])
    sums = sums_end(state)

    main, slope, constant = mid_back(0, 0, sums, total_in)

    @pl.loop(0, 4)
    def _(p):
        @pl.loop(0, total // STEP)
        def _(i):
            rows = steps(i)
            grad = main * up32(h3[p, rows]) + slope * up32(h1[p, rows]) + constant
            h1[p, rows] = low(grad * wide_mask(mask_ref[rows]))

    for p in range(4):
        plane_arrived(big_a.at[p], x_sem.at[1])

    def last_tile(chunk):
        value = t_times(chunk(0), h1[0])
        for p in range(1, 4):
            value = value + t_times(chunk(p), h1[p])
        return value

    def tile_reduce_a(step, unit):
        put(last_tile(lambda p: mb[p]), unit, 2, 0)
        put(last_tile(lambda p: big_a[p, 0:total]), unit, 2, n_batch // 2)

    produce(1, 2, tile_reduce_a)
    arrived(wq, w_sem.at[1])
    for k in range(2):
        tick_13 = ticks(2)

        @pl.loop(0, 2)
        def _(i):
            rows = pl.ds(pl.multiple_of(i * half, ROWS), half)
            value = times_t(h1[0, rows], w2[k])
            for n in range(4):
                value = value + times_t(side[n, rows], wq[2 * n + k])
            if k == 0:
                h3[0, rows] = low(value)
            else:
                a4p[rows] = low(value)
            tick_13(i)

    put_plane(0, 0, h3.at[0])
    put_plane(0, 1, a4p)
    tick_13p = ticks(3)

    @pl.loop(1, 4)
    def _(p):
        h3[p] = low(times_t(h1[p], w2[0]))
        side[p] = low(times_t(h1[p], w2[1]))
        put_plane(p, 0, h3.at[p])
        put_plane(p, 1, side.at[p])
        tick_13p(p - 1)

    idle(rounds[-1][0] - 6)
    others = pool_slots.at[0 : n_height - 1]
    pltpu.make_async_copy(others, others, pool_sem.at[1]).wait()
    pltpu.make_async_copy(others, others, pool_sem.at[0]).wait()
    for g in groups:
        for n in range(4):
            value = None
            for k in range(n_height):
                part = up32(pool_slots[k, n, g * ROWS : (g + 1) * ROWS])
                value = part if value is None else value + part
            pooled[g, n] = value * (1.0 / (widths[g] * widths[g]))

    for slot in range(ready.shape[0]):
        arrived(ready.at[slot], ready_sem.at[slot])
    for p in range(8):
        plane_arrived(a4p, dx_sem.at[0])


def to_planes(image):
    count, rows, cols, channels = image.shape
    value = jnp.pad(image, ((0, ROWS - count), (0, 0), (0, 0), (0, 0)))
    value = jnp.transpose(value, (1, 2, 0, 3))
    return value.reshape(rows // 2, 2, cols // 2, 2, ROWS, channels)


def from_planes(planes, shape):
    count, rows, cols, channels = shape
    value = planes.reshape(rows, cols, ROWS, channels)[:, :, :count]
    return jnp.transpose(value, (2, 0, 1, 3))


def per_device(
    image_small, image_medium, image_large, row_counts, reduce_a, first_spatial_weight, expand_a,
    shortcut_a, reduce_b, second_spatial_weight, expand_b, gain_mid, shift_mid, gain_out,
    shift_out, upstream_small, upstream_medium, upstream_large,
):
    images = (image_small, image_medium, image_large)
    upstreams = (upstream_small, upstream_medium, upstream_large)
    n_batch, n_height = lax.axis_size("batch"), lax.axis_size("height")
    heights = [value.shape[1] // 2 for value in images]
    widths = [value.shape[2] // 2 for value in images]
    count = images[0].shape[0]
    live = row_counts[:, lax.axis_index("height")]
    pixels = sum(o * o for o in widths) * count * n_batch
    counts, starts, top_total, _, both_total, _, _ = grids(heights, widths)
    total = sum(counts) * ROWS
    planes = [to_planes(image) for image in images]
    masks = []
    for g in range(3):
        row_ok = (jnp.arange(heights[g], dtype=jnp.int32) < live[g])[:, None, None]
        column_ok = (jnp.arange(widths[g] + 1) < widths[g])[None, :, None]
        image_ok = (jnp.arange(ROWS) < count)[None, None, :]
        masks.append(jnp.logical_and(jnp.logical_and(row_ok, column_ok), image_ok).reshape(-1))
    mask = jnp.concatenate(masks).astype(jnp.bfloat16)
    mask = jnp.broadcast_to(mask[:, None], (total, 128))
    edges = (jnp.arange(max(heights))[None, :] == live[:, None] - 1).astype(jnp.float32)
    edges = jnp.broadcast_to(edges[:, :, None, None], edges.shape + (8, 128))
    up = jnp.stack([jnp.pad(value, ((0, ROWS - count), (0, 0))) for value in upstreams])
    up = jnp.transpose(up.reshape(3, ROWS, 4, WIDE), (0, 2, 1, 3))
    halo = sum(widths) * ROWS
    bf, f32 = jnp.bfloat16, jnp.float32
    unit_rows, n_rest = WIDE // n_batch, n_batch // 2
    n_units = sum(
        w.size for w in (reduce_a, first_spatial_weight, expand_a, shortcut_a, reduce_b,
                         second_spatial_weight, expand_b)
    ) // (WIDE * WIDE)
    dma = pltpu.SemaphoreType.DMA
    vmem = pl.BlockSpec(memory_space=pltpu.VMEM)
    anywhere = pl.BlockSpec(memory_space=pl.ANY)
    flat_a = first_spatial_weight.reshape(9, WIDE, WIDE)
    flat_b = second_spatial_weight.reshape(9, WIDE, WIDE)
    big = pltpu.VMEM((4, total, WIDE), bf)
    thin = pltpu.VMEM((total, WIDE), bf)
    results = pl.pallas_call(
        functools.partial(
            main_kernel, n_batch, n_height, heights, widths, float(4 * pixels), float(pixels)
        ),
        out_shape=[
            jax.ShapeDtypeStruct((3, 4, ROWS, WIDE), f32),
            *[jax.ShapeDtypeStruct(value.shape, bf) for value in planes],
            jax.ShapeDtypeStruct((n_units, unit_rows, WIDE), f32),
            jax.ShapeDtypeStruct((4, 2, WIDE), f32),
            jax.ShapeDtypeStruct((3, 2, 4, WIDE), f32),
            jax.ShapeDtypeStruct((4, total, WIDE), bf),
            jax.ShapeDtypeStruct((4, top_total * ROWS, WIDE), bf),
        ],
        in_specs=[anywhere] * 10 + [vmem] * 7,
        out_specs=[vmem] + [anywhere] * 4 + [vmem] * 2 + [anywhere] * 2,
        scratch_shapes=[
            big,
            pltpu.VMEM((4, top_total * ROWS, WIDE), bf),
            big, big, big,
            thin, thin, thin, thin, thin,
            pltpu.VMEM((both_total * ROWS, WIDE), bf),
            pltpu.VMEM((both_total * ROWS, WIDE), bf),
            pltpu.VMEM((total, WIDE), f32),
            pltpu.VMEM((9, WIDE, WIDE), bf),
            pltpu.VMEM((8, WIDE, WIDE), bf),
            pltpu.VMEM((2, WIDE, WIDE), bf),
            pltpu.VMEM((halo, WIDE), bf),
            pltpu.VMEM((halo, WIDE), bf),
            pltpu.VMEM((halo, WIDE), bf),
            pltpu.VMEM((12, 2, 2, n_rest, unit_rows, 128), bf),
            pltpu.VMEM((5, 2, 2, n_rest, unit_rows, 128), bf),
            pltpu.VMEM((6, 2, 2, n_rest, unit_rows, 128), bf),
            pltpu.VMEM((6, 2, n_rest, unit_rows, 128), bf),
            pltpu.VMEM((6, n_rest, unit_rows, 128), bf),
            pltpu.VMEM((6, n_rest - 1, unit_rows, 128), bf),
            pltpu.VMEM((8, 2, 2, unit_rows, 128), bf),
            pltpu.VMEM((3, unit_rows, WIDE), f32),
            pltpu.VMEM((n_height, 4, 3 * ROWS, WIDE), bf),
            pltpu.VMEM((2, n_height, 8, 128), f32),
            pltpu.VMEM((2, n_batch, 8, 128), f32),
            pltpu.VMEM((n_height, 16, WIDE), f32),
            pltpu.VMEM((n_batch, 16, WIDE), f32),
            pltpu.VMEM((16, 8, WIDE), f32),
            pltpu.VMEM((16, WIDE), f32),
            dma((4,)), dma((2,)), dma((6, 16)), dma((6, 16)), dma((3,)), dma((1,)), dma((2,)),
            dma((2, 2, 2)), dma((2, 2, 2)), dma((3,)), dma((3,)), dma((2,)),
        ],
        compiler_params=pltpu.CompilerParams(
            collective_id=0, has_side_effects=True, vmem_limit_bytes=63 << 20
        ),
        name="both_blocks",
    )(
        *planes, reduce_a, flat_a, expand_a, shortcut_a, reduce_b, flat_b, expand_b,
        edges, mask, gain_mid, shift_mid,
        gain_out.reshape(3, 4, WIDE), shift_out.reshape(3, 4, WIDE), up,
    )
    pooled = jnp.transpose(results[0], (0, 2, 1, 3)).reshape(3, ROWS, -1)[:, :count]
    backs = [from_planes(results[1 + g], images[g].shape) for g in range(3)]
    units, place, shards = results[4], 0, {}
    for name, shape in (
        ("expand_b", expand_b.shape),
        ("spatial_b", second_spatial_weight.shape),
        ("reduce_b", reduce_b.shape),
        ("expand_a", expand_a.shape),
        ("shortcut_a", shortcut_a.shape),
        ("spatial_a", first_spatial_weight.shape),
        ("reduce_a", reduce_a.shape),
    ):
        lead = shape[:-2]
        count_units = shape[-2] * shape[-1] // (WIDE * WIDE)
        for size in lead:
            count_units *= size
        value = units[place : place + count_units]
        place += count_units
        rows = shape[-2] // n_batch
        if lead:
            shards[name] = value.reshape(lead + (rows, WIDE))
        else:
            value = value.reshape(shape[1] // WIDE, rows, WIDE)
            shards[name] = jnp.transpose(value, (1, 0, 2)).reshape(rows, shape[1])
    order = (
        "reduce_a", "spatial_a", "expand_a", "shortcut_a", "reduce_b", "spatial_b", "expand_b"
    )
    mid, out = results[5], results[6].reshape(3, 2, -1)
    return (
        pooled[0], pooled[1], pooled[2], backs[0], backs[1], backs[2], *[shards[name] for name in order],
        mid[:, 1], mid[:, 0], out[:, 1], out[:, 0],
    )


def solution(mesh):
    placed = (
        P("batch", "height", None, None),
        P("batch", "height", None, None),
        P("batch", "height", None, None),
        P(),
        P(),
        P(),
        P(),
        P(),
        P(),
        P(),
        P(),
        P(),
        P(),
        P(),
        P(),
        P("batch", None),
        P("batch", None),
        P("batch", None),
    )
    return jax.shard_map(
        per_device,
        mesh=mesh,
        in_specs=placed,
        out_specs=(
            P("batch", None),
            P("batch", None),
            P("batch", None),
            P("batch", "height", None, None),
            P("batch", "height", None, None),
            P("batch", "height", None, None),
            P("batch", None),
            P(None, None, "batch", None),
            P("batch", None),
            P("batch", None),
            P("batch", None),
            P(None, None, "batch", None),
            P("batch", None),
            P(),
            P(),
            P(),
            P(),
        ),
        check_vma=False,
    )
```

```python
import functools

import jax
import jax.numpy as jnp
from jax import lax
from jax.experimental import pallas as pl
from jax.experimental.pallas import tpu as pltpu
from jax.sharding import PartitionSpec as P

epsilon = 1e-05
MESH = pl.DeviceIdType.MESH

WIDE = 512
ROWS = 16
STEP = 64


def sigmoid(values):
    return 0.5 * jnp.tanh(0.5 * values) + 0.5


def up32(values):
    return values.astype(jnp.float32)


def low(values):
    return values.astype(jnp.bfloat16)


def times(left, right):
    return jnp.dot(left, right, preferred_element_type=jnp.float32)


def times_t(left, right):
    return lax.dot_general(
        left, right, (((1,), (1,)), ((), ())), preferred_element_type=jnp.float32
    )


def t_times(left, right):
    return lax.dot_general(
        left, right, (((0,), (0,)), ((), ())), preferred_element_type=jnp.float32
    )


def fold(values):
    return jnp.sum(values.reshape(-1, 8, values.shape[-1]), axis=0)


def one_row(values):
    return jnp.sum(values, axis=0, keepdims=True)


def wide_mask(mask):
    return jnp.concatenate([up32(mask)] * (WIDE // 128), axis=1)


def grids(heights, widths):
    counts = [k * (o + 1) for k, o in zip(heights, widths)]
    starts = [sum(counts[:g]) for g in range(3)]
    top_sizes = [(k + 1) * (o + 1) + 1 for k, o in zip(heights, widths)]
    top_starts = [sum(top_sizes[:g]) for g in range(3)]
    both_sizes = [(k + 2) * (o + 1) + 2 for k, o in zip(heights, widths)]
    both_starts = [sum(both_sizes[:g]) for g in range(3)]
    halo_starts = [sum(widths[:g]) for g in range(3)]
    return counts, starts, sum(top_sizes), top_starts, sum(both_sizes), both_starts, halo_starts


def main_kernel(
    n_batch, n_height, heights, widths, total_in, total_out,
    x_small, x_medium, x_large, reduce_a, spatial_a, expand_a, shortcut_a, reduce_b, spatial_b, expand_b,
    edge_ref, mask_ref, gain_mid, shift_mid, gain_out, shift_out, up_ref,
    pooled, dx_small, dx_medium, dx_large, g_units, mid_sums, out_sums, h1_kept, a1_kept,
    big_b, big_a, h3, side, mb, h2, a2, h4, h5, a5, a4p, dhp, acc, wp, wq, w2,
    halo_up, halo_down, halo_in, keep, away, r0, r1, r2, r3, final, ready, pool_slots,
    thin_h, thin_b, wide_h, wide_b, stat_mid, stat_out,
    w_sem, x_sem, u_send, u_recv, ready_sem, dx_sem, spill_sem, ar_send, ar_recv, halo_send, halo_recv, pool_sem,
):
    b, h = lax.axis_index("batch"), lax.axis_index("height")
    counts, starts, top_total, top_starts, both_total, both_starts, halo_starts = grids(
        heights, widths
    )
    total = sum(counts) * ROWS
    half = total // 2
    groups = range(3)
    h1, dz, h6 = big_b, big_b, big_a
    halo_a = mb.at[0:2, 0 : sum(widths) * ROWS]

    def rows_at(start, count):
        return pl.ds(pl.multiple_of(start * ROWS, ROWS), count * ROWS)

    def steps(index):
        return pl.ds(pl.multiple_of(index * STEP, STEP), STEP)

    def fetch(source, target, sem):
        pltpu.make_async_copy(source, target, sem).start()

    def arrived(target, sem):
        pltpu.make_async_copy(target, target, sem).wait()

    def columns(k):
        return pl.ds(k * WIDE, WIDE)

    def fetch_columns(weight, target, first, sem):
        for n in range(4):
            fetch(weight.at[:, columns(n)], target.at[first + n], sem)

    def fetch_shortcut():
        for n in range(4):
            for k in range(2):
                fetch(shortcut_a.at[columns(k), columns(n)], wq.at[2 * n + k], w_sem.at[1])

    xs, dxs = (x_small, x_medium, x_large), (dx_small, dx_medium, dx_large)

    def band_row(buffer, g, y):
        return buffer.at[pl.ds(starts[g] + y * (widths[g] + 1), widths[g])]

    def by_position(buffer):
        return buffer.reshape(buffer.shape[0] // ROWS, ROWS, WIDE)

    def fetch_plane(p, k, target, sem):
        for g in groups:
            for y in range(heights[g]):
                fetch(
                    xs[g].at[y, p // 2, :, p % 2, :, columns(k)],
                    band_row(by_position(target), g, y),
                    sem,
                )

    def plane_arrived(target, sem):
        pixels = sum(k * o for k, o in zip(heights, widths)) * ROWS
        arrived(target.at[0:pixels], sem)

    def put_plane(p, k, source):
        for g in groups:
            for y in range(heights[g]):
                fetch(
                    band_row(by_position(source), g, y),
                    dxs[g].at[y, p // 2, :, p % 2, :, columns(k)],
                    dx_sem.at[0],
                )

    for k in range(2):
        for p in range(4):
            for g in groups:
                for y in range(heights[g]):
                    edge_place = (starts[g] + y * (widths[g] + 1) + widths[g]) * ROWS
                    (h3, mb)[k][p, edge_place : edge_place + ROWS] = jnp.zeros(
                        (ROWS, WIDE), jnp.bfloat16
                    )
            fetch_plane(p, k, (h3, mb)[k].at[p], x_sem.at[k])
    for k in range(2):
        fetch(reduce_a.at[columns(k)], w2.at[k], w_sem.at[3])
    fetch_shortcut()
    fetch(spatial_a, wp, w_sem.at[0])

    halo_down[...] = jnp.zeros_like(halo_down)
    halo_up[...] = jnp.zeros_like(halo_up)
    halo_in[...] = jnp.zeros_like(halo_in)

    @pl.loop(0, both_total // 2)
    def _(i):
        rows = rows_at(i * 2, 2)
        a4p[rows] = jnp.zeros((2 * ROWS, WIDE), jnp.bfloat16)
        dhp[rows] = jnp.zeros((2 * ROWS, WIDE), jnp.bfloat16)

    for g in groups:
        count = widths[g] + 2
        for p in range(4):
            big_a[p, top_starts[g] * ROWS : (top_starts[g] + count) * ROWS] = jnp.zeros(
                (count * ROWS, WIDE), jnp.bfloat16
            )

    barrier = pltpu.get_barrier_semaphore()
    for k in range(1, n_height):
        pl.semaphore_signal(
            barrier, inc=1, device_id=(b, lax.rem(h + k, n_height)), device_id_type=MESH
        )

    @pl.loop(1, n_batch)
    def _(k):
        pl.semaphore_signal(
            barrier, inc=1, device_id=(lax.rem(b + k, n_batch), h), device_id_type=MESH
        )

    pl.semaphore_wait(barrier, n_height + n_batch - 2)

    turn = [0]

    def ar_spread(slots, me, count, peer, sems):
        @pl.loop(1, count)
        def _(k):
            pltpu.make_async_remote_copy(
                src_ref=slots.at[me],
                dst_ref=slots.at[me],
                send_sem=ar_send.at[sems],
                recv_sem=ar_recv.at[sems],
                device_id=peer(lax.rem(me + k, count)),
                device_id_type=MESH,
            ).start()

    def ar_wait(slots, count, sems, which):
        others = slots.at[0 : count - 1]
        pltpu.make_async_copy(others, others, which.at[sems]).wait()

    def sums_start(vectors):
        slot = turn[0] % 2
        turn[0] += 1
        first, second = thin_h.at[slot], thin_b.at[slot]
        for v, vector in enumerate(vectors):
            for j in range(4):
                first[h, 4 * v + j : 4 * v + j + 1, :] = vector[:, 128 * j : 128 * (j + 1)]
        ar_spread(first, h, n_height, lambda p: (b, p), (0, 0, slot))
        return first, second, 0, slot

    def wide_start(part):
        count = 16 if part is None else 8
        rows = pl.ds(8 * (part or 0), count)
        first, second = wide_h.at[:, rows], wide_b.at[:, rows]
        first[h] = stat_out[0:count]
        ar_spread(first, h, n_height, lambda p: (b, p), (1, 0, part or 0))
        return first, second, 1, part or 0

    def sums_middle(state):
        first, second, kind, slot = state
        ar_wait(first, n_height, (kind, 0, slot), ar_recv)
        second[b] = jnp.sum(first[...], axis=0)
        ar_spread(second, b, n_batch, lambda p: (p, h), (kind, 1, slot))

    def sums_end(state):
        first, second, kind, slot = state
        ar_wait(second, n_batch, (kind, 1, slot), ar_recv)
        summed = jnp.sum(second[...], axis=0)
        ar_wait(first, n_height, (kind, 0, slot), ar_send)
        ar_wait(second, n_batch, (kind, 1, slot), ar_send)
        if kind == 0:
            return [
                jnp.concatenate([summed[4 * v + j : 4 * v + j + 1] for j in range(4)], axis=1)
                for v in range(2)
            ]
        stat_out[0 : summed.shape[0]] = summed
        return None

    def keep_stats(kept, index, sums, number, gain, shift):
        centre = sums[0] * (1.0 / number)
        root = lax.rsqrt(sums[1] * (1.0 / number) - centre * centre + epsilon)
        scale = root * gain
        kept[index, 0:1] = centre
        kept[index, 1:2] = root
        kept[index, 2:3] = scale
        kept[index, 3:4] = shift - centre * scale
        kept[index, 4:5] = -centre * root

    def back_factors(kept, index, sums, number, gain):
        centre, root = kept[index, 0:1], kept[index, 1:2]
        main = gain * root
        slope = -main * root * sums[1] * (1.0 / number)
        return main, slope, -main * sums[0] * (1.0 / number) - slope * centre

    def halo_copy(source, target, sem, peer):
        return pltpu.make_async_remote_copy(
            src_ref=source,
            dst_ref=target,
            send_sem=halo_send.at[sem],
            recv_sem=halo_recv.at[sem],
            device_id=(b, peer),
            device_id_type=MESH,
        )

    def halo_rows(g):
        return slice(halo_starts[g] * ROWS, (halo_starts[g] + widths[g]) * ROWS)

    def top_row(padded, start, g):
        return padded.at[pl.ds((start + 1) * ROWS, widths[g] * ROWS)]

    def send_down(buffer, padded, sem):
        @pl.when(h < n_height - 1)
        def _():
            for g in groups:
                halo_copy(
                    buffer.at[halo_rows(g)], top_row(padded, both_starts[g], g), sem, h + 1
                ).start()

    def send_up(buffer, sem):
        @pl.when(h > 0)
        def _():
            halo_copy(buffer, halo_in, sem, h - 1).start()

    def halo_wait(buffer, sems, sem, condition):
        @pl.when(condition)
        def _():
            arrived(buffer, sems.at[sem])

    def place_below(padded):
        for g in groups:
            stride = widths[g] + 1
            for y in range(1, heights[g] + 1):
                is_edge = edge(g, y - 1)

                @pl.loop(0, widths[g])
                def _(col):
                    rows = rows_at(both_starts[g] + 1 + (y + 1) * stride + col, 1)
                    value = up32(halo_in[rows_at(halo_starts[g] + col, 1)]) * is_edge
                    if y < heights[g]:
                        value = value + up32(padded[rows])
                    padded[rows] = low(value)

    def edge(g, y):
        return wide_mask(edge_ref[g, y, 0:1])

    def first_row(source, g, row=0):
        start = (starts[g] + row * (widths[g] + 1)) * ROWS
        return up32(source[start : start + widths[g] * ROWS])

    def last_row(source, g):
        value = first_row(source, g) * edge(g, 0)
        for y in range(1, heights[g]):
            value = value + first_row(source, g, y) * edge(g, y)
        return value

    core, high = lax.rem(h, 2), h // 2
    low_bit, rest = lax.rem(b, 2), b // 2
    n_rest = n_batch // 2
    unit_rows = WIDE // n_batch

    def either(is_one, one, zero):
        return is_one * one + (1 - is_one) * zero

    first, second = either(core, low_bit, high), either(core, high, low_bit)
    core_peer = (b, h + 1 - 2 * core)
    high_peer = (b, h + 2 - 4 * high)
    low_peer = (b + 1 - 2 * low_bit, h)
    first_peer = [either(core, low_peer[i], high_peer[i]) for i in range(2)]
    second_peer = [either(core, high_peer[i], low_peer[i]) for i in range(2)]

    def ring(buffer, unit):
        return lax.rem(unit, buffer.shape[0])

    def unit_copy(level, unit, source, target, peer):
        return pltpu.make_async_remote_copy(
            src_ref=source,
            dst_ref=target,
            send_sem=u_send.at[level, lax.rem(unit, 16)],
            recv_sem=u_recv.at[level, lax.rem(unit, 16)],
            device_id=tuple(peer),
            device_id_type=MESH,
        )

    def hop(level, unit):
        kept = keep.at[ring(keep, unit)]
        if level == 0:
            return unit_copy(
                0, unit, away.at[ring(away, unit)], r0.at[ring(r0, unit)], core_peer
            )
        if level == 1:
            return unit_copy(1, unit, kept.at[1 - first], r1.at[ring(r1, unit)], first_peer)
        if level == 2:
            return unit_copy(
                2, unit, kept.at[first, 1 - second], r2.at[ring(r2, unit)], second_peer
            )
        if level == 4:
            mine = final.at[ring(final, unit), core, high]
            return unit_copy(4, unit, mine, mine, high_peer)
        both = final.at[ring(final, unit), core]
        return unit_copy(5, unit, both, both, core_peer)

    def add_to(target, source):
        target[...] = low(up32(target[...]) + up32(source[...]))

    def rest_wait(unit, sems):
        others = r3.at[ring(r3, unit)]
        pltpu.make_async_copy(others, others, sems.at[3, lax.rem(unit, 16)]).wait()

    def round_0(unit):
        hop(0, unit).start()

    def round_1(unit):
        hop(0, unit).wait()
        kept, got = keep.at[ring(keep, unit)], r0.at[ring(r0, unit)]

        @pl.loop(0, n_rest)
        def _(k):
            for i in range(2):
                for j in range(2):
                    add_to(kept.at[i, j, k], got.at[i, j, k])

        hop(1, unit).start()

    def round_2(unit):
        hop(1, unit).wait_recv()
        kept, got = keep.at[ring(keep, unit), first], r1.at[ring(r1, unit)]

        @pl.loop(0, n_rest)
        def _(k):
            for j in range(2):
                add_to(kept.at[j, k], got.at[j, k])

        hop(2, unit).start()

    def round_3(unit):
        hop(2, unit).wait_recv()
        kept, got = keep.at[ring(keep, unit), first, second], r2.at[ring(r2, unit)]

        @pl.loop(0, n_rest)
        def _(k):
            add_to(kept.at[k], got.at[k])

        @pl.loop(1, n_rest)
        def _(k):
            unit_copy(
                3,
                unit,
                kept.at[lax.rem(rest + k, n_rest)],
                r3.at[ring(r3, unit), n_rest - 1 - k],
                (lax.rem(rest + k, n_rest) * 2 + low_bit, h),
            ).start()

    def round_4(unit):
        rest_wait(unit, u_recv)
        value = up32(keep[ring(keep, unit), first, second, rest])
        for k in range(n_rest - 1):
            value = value + up32(r3[ring(r3, unit), k])
        final[ring(final, unit), core, high] = low(value)
        hop(4, unit).start()

    def round_5(unit):
        hop(4, unit).wait_recv()
        hop(5, unit).start()

    def round_6(unit):
        hop(5, unit).wait_recv()
        for level in (1, 2, 4, 5):
            hop(level, unit).wait_send()
        rest_wait(unit, u_send)
        slot = ring(ready, unit)

        @pl.when(unit >= ready.shape[0])
        def _():
            arrived(ready.at[slot], ready_sem.at[slot])

        for c in range(2):
            for i in range(2):
                lane = 128 * (2 * c + i)
                ready[slot, :, lane : lane + 128] = up32(final[ring(final, unit), c, i])
        fetch(ready.at[slot], g_units.at[unit], ready_sem.at[slot])

    rounds = (
        (0, round_0), (2, round_1), (4, round_2), (5, round_3), (7, round_4), (8, round_5),
        (10, round_6),
    )
    clock, made, produced = [0], [0], []

    def advance(index, base, count):
        for lag, act in rounds:
            for start, size, unit in produced:
                from_, to = max(base - lag, start), min(base - lag + count, start + size)
                if from_ >= to:
                    continue
                target = base - lag - start + unit + index
                if to - from_ == count:
                    act(target)
                else:
                    shift = base - lag
                    inside = jnp.logical_and(index >= from_ - shift, index < to - shift)
                    pl.when(inside)(functools.partial(act, target))

    def idle(count):
        base = clock[0]
        clock[0] += count

        @pl.loop(0, count)
        def _(i):
            advance(i, base, count)

    def ticks(count):
        base = clock[0]
        clock[0] += count
        return lambda i: advance(i, base, count)

    def put(value, unit, units, first_shard):
        shard_rows = units * unit_rows
        own_side = core == 0
        left, right = low(value[:, : WIDE // 2]), low(value[:, WIDE // 2 :])
        own, other = jnp.where(own_side, left, right), jnp.where(own_side, right, left)
        for s in range(WIDE // shard_rows):
            shard = first_shard + s
            shard_low, shard_rest = s % 2, shard // 2
            for q in range(units):
                rows = slice(s * shard_rows + q * unit_rows, s * shard_rows + (q + 1) * unit_rows)
                for i in range(2):
                    lanes = slice(128 * i, 128 * (i + 1))
                    keep[
                        ring(keep, unit + q),
                        either(core, shard_low, i),
                        either(core, i, shard_low),
                        shard_rest,
                    ] = own[rows, lanes]
                    away[
                        ring(away, unit + q),
                        either(core, i, shard_low),
                        either(core, shard_low, i),
                        shard_rest,
                    ] = other[rows, lanes]

    def run(count, body, make):
        base, unit = clock[0], made[0]
        clock[0] += count
        made[0] += count
        produced.append((base, count, unit))

        @pl.loop(0, count)
        def _(i):
            body(i)
            make(i, unit + i)
            advance(i, base, count)

    def produce(count, units, make):
        base, unit = clock[0], made[0]
        produced.append((base, count * units, unit))
        clock[0] += count * units
        made[0] += count * units

        @pl.loop(0, count)
        def _(t):
            make(t, unit + t * units)
            if units == 1:
                advance(t, base, count)
            else:

                @pl.loop(0, units)
                def _(q):
                    advance(t * units + q, base, count * units)

    zero8 = jnp.zeros((8, WIDE), jnp.float32)

    arrived(w2, w_sem.at[3])
    for k in range(2):
        for p in range(4):
            plane_arrived((h3, mb)[k].at[p], x_sem.at[k])

    def first_reduction(i, carry):
        p = i // 2
        rows = pl.ds(pl.multiple_of(lax.rem(i, 2) * half, ROWS), half)
        value = times(h3[p, rows], w2[0]) + times(mb[p, rows], w2[1])
        value = value * wide_mask(mask_ref[rows])
        h1[p, rows] = low(value)
        return carry[0] + fold(value), carry[1] + fold(value * value)

    sums = lax.fori_loop(0, 8, first_reduction, (zero8, zero8))
    state = sums_start([one_row(v) for v in sums])

    arrived(wq, w_sem.at[1])

    def shortcut_product(n, carry):
        value = times(h3[0], wq[2 * n]) + times(mb[0], wq[2 * n + 1])
        value = value * wide_mask(mask_ref[...])
        side[n] = low(value)
        stat_out[pl.ds(8 + n, 1)] = one_row(fold(value))
        stat_out[pl.ds(12 + n, 1)] = one_row(fold(value * value))
        return carry

    lax.fori_loop(0, 2, shortcut_product, 0)
    sums_middle(state)
    lax.fori_loop(2, 4, shortcut_product, 0)
    fetch_columns(expand_a, wq, 0, w_sem.at[1])
    for k in range(4):
        fetch(reduce_b.at[columns(k)], wq.at[4 + k], w_sem.at[2])
    sums = sums_end(state)
    keep_stats(stat_mid, 0, sums, total_in, gain_mid[0:1], shift_mid[0:1])

    scale, offset = stat_mid[0, 2:3], stat_mid[0, 3:4]
    for column in range(2):
        for g in groups:
            pre = last_row(h1.at[2 + column], g) * scale + offset
            mask = wide_mask(mask_ref[starts[g] * ROWS : (starts[g] + widths[g]) * ROWS])
            halo_a[column, halo_rows(g)] = low(pre * sigmoid(pre) * mask)

    @pl.when(h < n_height - 1)
    def _():
        for column in range(2):
            for g in groups:
                halo_copy(
                    halo_a.at[column, halo_rows(g)],
                    top_row(big_a.at[2 + column], top_starts[g], g),
                    0,
                    h + 1,
                ).start()

    for g in groups:
        per = counts[g] * ROWS // STEP
        base = (top_starts[g] + 1 + widths[g] + 1) * ROWS

        @pl.loop(0, 4)
        def _(p):
            @pl.loop(0, per)
            def _(i):
                rows = pl.ds(pl.multiple_of(starts[g] * ROWS + i * STEP, ROWS), STEP)
                pre = up32(h1[p, rows]) * scale + offset
                value = pre * sigmoid(pre) * wide_mask(mask_ref[rows])
                big_a[p, pl.ds(pl.multiple_of(base + i * STEP, ROWS), STEP)] = low(value)

    fetch(h1, h1_kept, spill_sem.at[0])

    def group_rows(g):
        return slice(starts[g] * ROWS, (starts[g] + counts[g]) * ROWS)

    def window(padded, start, g, dy, dx_):
        first = start + 1 + (1 + dy) * (widths[g] + 1) + dx_
        return padded[rows_at(first, counts[g])]

    def window_a(g, a, c):
        py, dy = lax.rem(a + 1, 2), (a + 1) // 2 - 1
        px, dx_ = lax.rem(c + 1, 2), (c + 1) // 2 - 1
        first = top_starts[g] + 1 + (1 + dy) * (widths[g] + 1) + dx_
        return big_a[2 * py + px, rows_at(first, counts[g])]

    def clear_acc():
        @pl.loop(0, total // STEP)
        def _(i):
            acc[steps(i)] = jnp.zeros((STEP, WIDE), jnp.float32)

    def conv_taps(start, last, window_of, product, make=None):
        def tap(t):
            for g in groups:
                acc[group_rows(g)] += product(window_of(g, t // 3, lax.rem(t, 3)), wp[t])

        if make is not None:
            run(last - start, lambda i: tap(start + i), make)
            return
        tick = ticks(last - start) if produced else None

        @pl.loop(start, last)
        def _(t):
            tap(t)
            if tick is not None:
                tick(t - start)

    def masked_sums(target):
        def body(i, carry):
            rows = steps(i)
            value = acc[rows] * wide_mask(mask_ref[rows])
            target[rows] = low(value)
            return carry[0] + fold(value), carry[1] + fold(value * value)

        return lax.fori_loop(0, total // STEP, body, (zero8, zero8))

    clear_acc()
    arrived(wp, w_sem.at[0])
    conv_taps(3, 9, window_a, times)
    halo_wait(halo_a, halo_recv, 0, h > 0)
    conv_taps(0, 3, window_a, times)
    sums = masked_sums(h2)
    state = sums_start([one_row(v) for v in sums])
    fetch(spatial_b, wp, w_sem.at[0])
    fetch(big_a, a1_kept, spill_sem.at[1])
    halo_wait(halo_a, halo_send, 0, h < n_height - 1)
    sums_middle(state)
    sums = sums_end(state)
    keep_stats(stat_mid, 1, sums, total_out, gain_mid[1:2], shift_mid[1:2])

    def activate(source, target, index):
        scale, offset = stat_mid[index, 2:3], stat_mid[index, 3:4]

        @pl.loop(0, total // STEP)
        def _(i):
            rows = steps(i)
            pre = up32(source[rows]) * scale + offset
            target[rows] = low(pre * sigmoid(pre) * wide_mask(mask_ref[rows]))

    activate(h2, a2, 1)
    arrived(wq.at[0:4], w_sem.at[1])

    def expansion(source, target):
        @pl.loop(0, 4)
        def _(n):
            value = times(source[...], wq[n])
            target[n, 0:total] = low(value)
            stat_out[pl.ds(n, 1)] = one_row(fold(value))
            stat_out[pl.ds(4 + n, 1)] = one_row(fold(value * value))

    expansion(a2, h3)
    state = wide_start(None)
    fetch_columns(expand_b, wq, 0, w_sem.at[1])
    sums_middle(state)
    sums_end(state)

    def out_stats(index, n, row):
        keep_stats(
            mid_or_out,
            4 * index + n,
            [stat_out[row + n : row + n + 1], stat_out[row + 4 + n : row + 5 + n]],
            total_out,
            gain_out[index, n : n + 1],
            shift_out[index, n : n + 1],
        )

    mid_or_out = stat_mid.at[4:16]
    for n in range(4):
        out_stats(0, n, 0)
        out_stats(1, n, 8)

    def out_stat(index, n, row):
        return stat_mid[4 + 4 * index + n, row : row + 1]

    def joint(n, rows):
        return (
            up32(h3[n, rows]) * out_stat(0, n, 2)
            + up32(side[n, rows]) * out_stat(1, n, 2)
            + (out_stat(0, n, 3) + out_stat(1, n, 3))
        )

    arrived(wq.at[4:8], w_sem.at[2])
    clear_acc()

    @pl.loop(0, 4)
    def _(n):
        @pl.loop(0, 2)
        def _(i):
            rows = pl.ds(pl.multiple_of(i * half, ROWS), half)
            value = joint(n, rows)
            value = low(value * sigmoid(value) * wide_mask(mask_ref[rows]))
            mb[n, rows] = value
            acc[rows] += times(value, wq[4 + n])

    def plain_sums(target):
        def body(i, carry):
            rows = steps(i)
            value = acc[rows]
            target[rows] = low(value)
            return carry[0] + fold(value), carry[1] + fold(value * value)

        return lax.fori_loop(0, total // STEP, body, (zero8, zero8))

    sums = plain_sums(h4)
    state = sums_start([one_row(v) for v in sums])
    sums_middle(state)
    clear_acc()
    sums = sums_end(state)
    keep_stats(stat_mid, 2, sums, total_out, gain_mid[2:3], shift_mid[2:3])

    scale, offset = stat_mid[2, 2:3], stat_mid[2, 3:4]
    for g in groups:
        pre = last_row(h4, g) * scale + offset
        mask = wide_mask(mask_ref[starts[g] * ROWS : (starts[g] + widths[g]) * ROWS])
        halo_down[halo_rows(g)] = low(pre * sigmoid(pre) * mask)
    send_down(halo_down, a4p, 1)
    for g in groups:
        pre = first_row(h4, g) * scale + offset
        mask = wide_mask(mask_ref[starts[g] * ROWS : (starts[g] + widths[g]) * ROWS])
        halo_up[halo_rows(g)] = low(pre * sigmoid(pre) * mask)
    send_up(halo_up, 2)

    def both_base(g):
        return (both_starts[g] + 1 + widths[g] + 1) * ROWS

    for g in groups:

        @pl.loop(0, counts[g] * ROWS // STEP)
        def _(i):
            rows = pl.ds(pl.multiple_of(starts[g] * ROWS + i * STEP, ROWS), STEP)
            pre = up32(h4[rows]) * scale + offset
            value = low(pre * sigmoid(pre) * wide_mask(mask_ref[rows]))
            a4p[pl.ds(pl.multiple_of(both_base(g) + i * STEP, ROWS), STEP)] = value

    def window_b(g, a, c):
        return window(a4p, both_starts[g], g, a - 1, c - 1)

    def window_b_back(g, a, c):
        return window(dhp, both_starts[g], g, 1 - a, 1 - c)

    arrived(wp, w_sem.at[0])
    conv_taps(3, 6, window_b, times)
    halo_wait(halo_down, halo_recv, 1, h > 0)
    halo_wait(halo_in, halo_recv, 2, h < n_height - 1)
    place_below(a4p)
    conv_taps(0, 3, window_b, times)
    conv_taps(6, 9, window_b, times)
    sums = masked_sums(h5)
    state = sums_start([one_row(v) for v in sums])
    halo_wait(halo_down, halo_send, 1, h < n_height - 1)
    halo_wait(halo_up, halo_send, 2, h > 0)
    sums_middle(state)
    sums = sums_end(state)
    keep_stats(stat_mid, 3, sums, total_out, gain_mid[3:4], shift_mid[3:4])

    activate(h5, a5, 3)
    arrived(wq.at[0:4], w_sem.at[1])
    arrived(big_a, spill_sem.at[1])
    expansion(a5, h6)
    state = wide_start(0)
    sums_middle(state)
    arrived(h1, spill_sem.at[0])
    sums_end(state)
    for n in range(4):
        out_stats(2, n, 0)

    @pl.loop(0, 4)
    def _(n):
        index = 12 + n
        root, scale = stat_mid[index, 1:2], stat_mid[index, 2:3]
        offset, back = stat_mid[index, 3:4], stat_mid[index, 4:5]
        zero = jnp.zeros((ROWS, WIDE), jnp.float32)
        total_grad, total_dot = zero8, zero8
        for g in groups:
            share = 1.0 / (widths[g] * widths[g])

            up = jnp.concatenate([up32(up_ref[g, n]) * share] * (STEP // ROWS), axis=0)

            def body(i, carry):
                rows = pl.ds(pl.multiple_of(starts[g] * ROWS + i * STEP, ROWS), STEP)
                value = up32(h6[n, rows])
                mask = wide_mask(mask_ref[rows])
                z = value * scale + offset + up32(mb[n, rows])
                s = sigmoid(z)
                grad = up * (s * (1.0 + z * (1.0 - s))) * mask
                dz[n, rows] = low(grad)
                last = (z * s * mask).reshape(STEP // ROWS, ROWS, WIDE)
                return (
                    carry[0] + jnp.sum(last, axis=0),
                    carry[1] + fold(grad),
                    carry[2] + fold(grad * (value * root + back)),
                )

            pool, total_grad, total_dot = lax.fori_loop(
                0, counts[g] * ROWS // STEP, body, (zero, total_grad, total_dot)
            )
            pool_slots[h, n, g * ROWS : (g + 1) * ROWS] = low(pool)
        stat_out[pl.ds(n, 1)] = one_row(total_grad)
        stat_out[pl.ds(4 + n, 1)] = one_row(total_dot)

    state = wide_start(1)

    for k in range(1, n_height):
        pltpu.make_async_remote_copy(
            src_ref=pool_slots.at[h],
            dst_ref=pool_slots.at[h],
            send_sem=pool_sem.at[0],
            recv_sem=pool_sem.at[1],
            device_id=(b, lax.rem(h + k, n_height)),
            device_id_type=MESH,
        ).start()
    sums_middle(state)
    clear_acc()
    sums_end(state)

    def out_back(index, sum_row, dot_row, n):
        sums = [stat_out[pl.ds(sum_row + n, 1)], stat_out[pl.ds(dot_row + n, 1)]]
        out_sums[index, 0, pl.ds(n, 1)] = sums[0]
        out_sums[index, 1, pl.ds(n, 1)] = sums[1]
        return back_factors(
            stat_mid, 4 + 4 * index + n, sums, total_out, gain_out[index, pl.ds(n, 1)]
        )

    def mid_back(index, place, sums, number):
        mid_sums[place, 0:1] = sums[0]
        mid_sums[place, 1:2] = sums[1]
        return back_factors(stat_mid, index, sums, number, gain_mid[place : place + 1])

    def mid_gradient(source, index):
        root, scale = stat_mid[index, 1:2], stat_mid[index, 2:3]
        offset, back = stat_mid[index, 3:4], stat_mid[index, 4:5]

        def body(i, carry):
            rows = steps(i)
            value = up32(source[rows])
            pre = value * scale + offset
            s = sigmoid(pre)
            grad = acc[rows] * (s * (1.0 + pre * (1.0 - s))) * wide_mask(mask_ref[rows])
            acc[rows] = grad
            return carry[0] + fold(grad), carry[1] + fold(grad * (value * root + back))

        sums = lax.fori_loop(0, total // STEP, body, (zero8, zero8))
        return [one_row(v) for v in sums]

    @pl.loop(0, 4)
    def _(n):
        main, slope, constant = out_back(2, 0, 4, n)

        @pl.loop(0, 2)
        def _(i):
            rows = pl.ds(pl.multiple_of(i * half, ROWS), half)
            grad = main * up32(dz[n, rows]) + slope * up32(h6[n, rows]) + constant
            grad = low(grad * wide_mask(mask_ref[rows]))
            h6[n, rows] = grad
            acc[rows] += times_t(grad, wq[n])

    sums = mid_gradient(h5, 3)
    state = sums_start(sums)
    fetch_columns(expand_a, wq, 0, w_sem.at[1])
    sums_middle(state)
    produce(4, 1, lambda t, unit: put(t_times(a5[...], h6[t, 0:total]), unit, 1, 0))
    fetch(a1_kept, big_a, spill_sem.at[1])
    sums = sums_end(state)

    def mid_step(target, factors, padded):
        main, slope, constant = factors

        def tile(rows):
            grad = main * acc[rows] + slope * up32(target[rows]) + constant
            return low(grad * wide_mask(mask_ref[rows]))

        for g in groups:

            @pl.loop(0, counts[g] * ROWS // STEP)
            def _(i):
                rows = pl.ds(pl.multiple_of(starts[g] * ROWS + i * STEP, ROWS), STEP)
                grad = tile(rows)
                target[rows] = grad
                if padded is not None:
                    padded[pl.ds(pl.multiple_of(both_base(g) + i * STEP, ROWS), STEP)] = grad

    mid_step(h5, mid_back(3, 3, sums, total_out), dhp)
    for g in groups:
        halo_down[halo_rows(g)] = low(last_row(h5, g))
        halo_up[halo_rows(g)] = low(first_row(h5, g))
    send_down(halo_down, dhp, 1)
    send_up(halo_up, 2)
    def spatial_tile(window_of, grads):
        def value_of(t):
            parts = [
                t_times(window_of(g, t // 3, lax.rem(t, 3)), grads[group_rows(g)]) for g in groups
            ]
            return parts[0] + parts[1] + parts[2]

        return value_of

    def spatial_maker(window_of, grads):
        tile = spatial_tile(window_of, grads)
        return lambda done: lambda i, unit: put(tile(done + i), unit, 1, 0)

    make_b = spatial_maker(window_b, h5)
    clear_acc()
    conv_taps(3, 6, window_b_back, times_t, make_b(0))
    halo_wait(halo_down, halo_recv, 1, h > 0)
    halo_wait(halo_in, halo_recv, 2, h < n_height - 1)
    place_below(dhp)
    conv_taps(0, 3, window_b_back, times_t, make_b(3))
    conv_taps(6, 9, window_b_back, times_t)
    fetch(spatial_a, wp, w_sem.at[0])
    sums = mid_gradient(h4, 2)
    state = sums_start(sums)
    halo_wait(halo_down, halo_send, 1, h < n_height - 1)
    halo_wait(halo_up, halo_send, 2, h > 0)
    sums_middle(state)

    produce(3, 1, make_b(6))
    sums = sums_end(state)

    mid_step(h4, mid_back(2, 2, sums, total_out), None)
    fetch_plane(0, 1, a4p, x_sem.at[1])

    tick = ticks(8)

    @pl.loop(0, 4)
    def _(n):
        def body(i, carry):
            tick(2 * n + i)
            rows = pl.ds(pl.multiple_of(i * half, ROWS), half)
            grad = times_t(h4[rows], wq[4 + n]) + up32(dz[n, rows])
            z = joint(n, rows)
            s = sigmoid(z)
            grad = grad * (s * (1.0 + z * (1.0 - s))) * wide_mask(mask_ref[rows])
            dz[n, rows] = low(grad)
            main_hat = up32(h3[n, rows]) * out_stat(0, n, 1) + out_stat(0, n, 4)
            side_hat = up32(side[n, rows]) * out_stat(1, n, 1) + out_stat(1, n, 4)
            return (
                carry[0] + fold(grad),
                carry[1] + fold(grad * main_hat),
                carry[2] + fold(grad * side_hat),
            )

        sums = lax.fori_loop(0, 2, body, (zero8, zero8, zero8))
        for v in range(3):
            stat_out[pl.ds(4 * v + n, 1)] = one_row(sums[v])

    state = wide_start(None)
    sums_middle(state)

    def tile_reduce_b(step, unit):
        @pl.loop(0, 4)
        def _(t):
            put(t_times(mb[t], h4[...]), unit, 4, t * (n_batch // 4))

    produce(1, 4, tile_reduce_b)
    for p in range(4):
        fetch_plane(p, 0, mb.at[p], x_sem.at[0])
    clear_acc()
    sums_end(state)

    arrived(wq.at[0:4], w_sem.at[1])

    def expansion_back(n):
        main, slope, constant = out_back(0, 0, 4, n)
        main2, slope2, constant2 = out_back(1, 0, 8, n)

        @pl.loop(0, 2)
        def _(i):
            rows = pl.ds(pl.multiple_of(i * half, ROWS), half)
            grad_in = up32(dz[n, rows])
            mask = wide_mask(mask_ref[rows])
            grad = low((main * grad_in + slope * up32(h3[n, rows]) + constant) * mask)
            h3[n, rows] = grad
            acc[rows] += times_t(grad, wq[n])
            other = main2 * grad_in + slope2 * up32(side[n, rows]) + constant2
            side[n, rows] = low(other * mask)

    run(4, expansion_back, lambda n, unit: put(t_times(a2[...], h3[n]), unit, 1, 0))
    fetch(h1_kept, h1, spill_sem.at[0])
    fetch_shortcut()
    sums = mid_gradient(h2, 1)
    state = sums_start(sums)
    sums_middle(state)
    for p in range(4):
        plane_arrived(mb.at[p], x_sem.at[0])
    plane_arrived(a4p, x_sem.at[1])

    def tile_shortcut(t, unit):
        put(t_times(mb[0], side[t]), unit, 2, 0)
        put(t_times(a4p[0:total], side[t]), unit, 2, n_batch // 2)

    produce(1, 2, lambda step, unit: tile_shortcut(0, unit))
    sums = sums_end(state)

    mid_step(h2, mid_back(1, 1, sums, total_out), dhp)
    for g in groups:
        halo_up[halo_rows(g)] = low(first_row(h2, g))
    send_up(halo_up, 2)
    arrived(wp, w_sem.at[0])
    arrived(h1, spill_sem.at[0])
    root, scale = stat_mid[0, 1:2], stat_mid[0, 2:3]
    offset, back = stat_mid[0, 3:4], stat_mid[0, 4:5]
    carry = (zero8, zero8)
    for p in range(4):
        py, px = p // 2, p % 2
        row_taps = ((1, 0),) if py == 0 else ((0, 1), (2, 0))
        column_taps = ((1, 0),) if px == 0 else ((0, 1), (2, 0))
        if p == 2:
            halo_wait(halo_in, halo_recv, 2, h < n_height - 1)
            place_below(dhp)
        for g in groups:
            value = None
            for a, dy in row_taps:
                for c, dx_ in column_taps:
                    product = times_t(window(dhp, both_starts[g], g, dy, dx_), wp[3 * a + c])
                    value = product if value is None else value + product
            acc[group_rows(g)] = value

        def body(i, carry):
            rows = steps(i)
            value = up32(h1[p, rows])
            pre = value * scale + offset
            s = sigmoid(pre)
            grad = acc[rows] * (s * (1.0 + pre * (1.0 - s))) * wide_mask(mask_ref[rows])
            h3[p, rows] = low(grad)
            return carry[0] + fold(grad), carry[1] + fold(grad * (value * root + back))

        carry = lax.fori_loop(0, total // STEP, body, carry)
        if p > 0:
            produce(1, 2, lambda step, unit: tile_shortcut(p, unit))
    state = sums_start([one_row(v) for v in carry])
    halo_wait(halo_up, halo_send, 2, h > 0)
    sums_middle(state)
    arrived(big_a, spill_sem.at[1])
    make_a = spatial_maker(window_a, h2)
    produce(3, 1, make_a(0))
    sums = sums_end(state)

    main, slope, constant = mid_back(0, 0, sums, total_in)

    def first_back(p):
        @pl.loop(0, total // STEP)
        def _(i):
            rows = steps(i)
            grad = main * up32(h3[p, rows]) + slope * up32(h1[p, rows]) + constant
            h1[p, rows] = low(grad * wide_mask(mask_ref[rows]))

        fetch_plane(p, 1, h3.at[p], x_sem.at[1])

    run(4, first_back, make_a(3))
    produce(2, 1, make_a(7))
    for p in range(4):
        plane_arrived(h3.at[p], x_sem.at[1])

    def last_tile(chunk):
        value = t_times(chunk(0), h1[0])
        for p in range(1, 4):
            value = value + t_times(chunk(p), h1[p])
        return value

    def tile_reduce_a(step, unit):
        put(last_tile(lambda p: mb[p]), unit, 2, 0)
        put(last_tile(lambda p: h3[p]), unit, 2, n_batch // 2)

    produce(1, 2, tile_reduce_a)
    arrived(wq, w_sem.at[1])
    for k in range(2):
        tick_13 = ticks(2)

        @pl.loop(0, 2)
        def _(i):
            rows = pl.ds(pl.multiple_of(i * half, ROWS), half)
            value = times_t(h1[0, rows], w2[k])
            for n in range(4):
                value = value + times_t(side[n, rows], wq[2 * n + k])
            if k == 0:
                big_a[0, rows] = low(value)
            else:
                a4p[rows] = low(value)
            tick_13(i)

    put_plane(0, 0, big_a.at[0])
    put_plane(0, 1, a4p)
    tick_13p = ticks(3)

    @pl.loop(1, 4)
    def _(p):
        big_a[p, 0:total] = low(times_t(h1[p], w2[0]))
        side[p] = low(times_t(h1[p], w2[1]))
        put_plane(p, 0, big_a.at[p])
        put_plane(p, 1, side.at[p])
        tick_13p(p - 1)

    idle(rounds[-1][0] - 6)
    others = pool_slots.at[0 : n_height - 1]
    pltpu.make_async_copy(others, others, pool_sem.at[1]).wait()
    pltpu.make_async_copy(others, others, pool_sem.at[0]).wait()
    for g in groups:
        for n in range(4):
            value = None
            for k in range(n_height):
                part = up32(pool_slots[k, n, g * ROWS : (g + 1) * ROWS])
                value = part if value is None else value + part
            pooled[g, n] = value * (1.0 / (widths[g] * widths[g]))

    for slot in range(ready.shape[0]):
        arrived(ready.at[slot], ready_sem.at[slot])
    for p in range(8):
        plane_arrived(a4p, dx_sem.at[0])


def to_planes(image):
    count, rows, cols, channels = image.shape
    value = jnp.pad(image, ((0, ROWS - count), (0, 0), (0, 0), (0, 0)))
    value = jnp.transpose(value, (1, 2, 0, 3))
    return value.reshape(rows // 2, 2, cols // 2, 2, ROWS, channels)


def from_planes(planes, shape):
    count, rows, cols, channels = shape
    value = planes.reshape(rows, cols, ROWS, channels)[:, :, :count]
    return jnp.transpose(value, (2, 0, 1, 3))


def per_device(
    image_small, image_medium, image_large, row_counts, reduce_a, first_spatial_weight, expand_a,
    shortcut_a, reduce_b, second_spatial_weight, expand_b, gain_mid, shift_mid, gain_out,
    shift_out, upstream_small, upstream_medium, upstream_large,
):
    images = (image_small, image_medium, image_large)
    upstreams = (upstream_small, upstream_medium, upstream_large)
    n_batch, n_height = lax.axis_size("batch"), lax.axis_size("height")
    heights = [value.shape[1] // 2 for value in images]
    widths = [value.shape[2] // 2 for value in images]
    count = images[0].shape[0]
    live = row_counts[:, lax.axis_index("height")]
    pixels = sum(o * o for o in widths) * count * n_batch
    counts, starts, top_total, _, both_total, _, _ = grids(heights, widths)
    total = sum(counts) * ROWS
    planes = [to_planes(image) for image in images]
    masks = []
    for g in range(3):
        row_ok = (jnp.arange(heights[g], dtype=jnp.int32) < live[g])[:, None, None]
        column_ok = (jnp.arange(widths[g] + 1) < widths[g])[None, :, None]
        image_ok = (jnp.arange(ROWS) < count)[None, None, :]
        masks.append(jnp.logical_and(jnp.logical_and(row_ok, column_ok), image_ok).reshape(-1))
    mask = jnp.concatenate(masks).astype(jnp.bfloat16)
    mask = jnp.broadcast_to(mask[:, None], (total, 128))
    edges = (jnp.arange(max(heights))[None, :] == live[:, None] - 1).astype(jnp.float32)
    edges = jnp.broadcast_to(edges[:, :, None, None], edges.shape + (8, 128))
    up = jnp.stack([jnp.pad(value, ((0, ROWS - count), (0, 0))) for value in upstreams])
    up = jnp.transpose(up.reshape(3, ROWS, 4, WIDE), (0, 2, 1, 3))
    halo = sum(widths) * ROWS
    bf, f32 = jnp.bfloat16, jnp.float32
    unit_rows, n_rest = WIDE // n_batch, n_batch // 2
    n_units = sum(
        w.size for w in (reduce_a, first_spatial_weight, expand_a, shortcut_a, reduce_b,
                         second_spatial_weight, expand_b)
    ) // (WIDE * WIDE)
    dma = pltpu.SemaphoreType.DMA
    vmem = pl.BlockSpec(memory_space=pltpu.VMEM)
    anywhere = pl.BlockSpec(memory_space=pl.ANY)
    flat_a = first_spatial_weight.reshape(9, WIDE, WIDE)
    flat_b = second_spatial_weight.reshape(9, WIDE, WIDE)
    big = pltpu.VMEM((4, total, WIDE), bf)
    thin = pltpu.VMEM((total, WIDE), bf)
    results = pl.pallas_call(
        functools.partial(
            main_kernel, n_batch, n_height, heights, widths, float(4 * pixels), float(pixels)
        ),
        out_shape=[
            jax.ShapeDtypeStruct((3, 4, ROWS, WIDE), f32),
            *[jax.ShapeDtypeStruct(value.shape, bf) for value in planes],
            jax.ShapeDtypeStruct((n_units, unit_rows, WIDE), f32),
            jax.ShapeDtypeStruct((4, 2, WIDE), f32),
            jax.ShapeDtypeStruct((3, 2, 4, WIDE), f32),
            jax.ShapeDtypeStruct((4, total, WIDE), bf),
            jax.ShapeDtypeStruct((4, top_total * ROWS, WIDE), bf),
        ],
        in_specs=[anywhere] * 10 + [vmem] * 7,
        out_specs=[vmem] + [anywhere] * 4 + [vmem] * 2 + [anywhere] * 2,
        scratch_shapes=[
            big,
            pltpu.VMEM((4, top_total * ROWS, WIDE), bf),
            big, big, big,
            thin, thin, thin, thin, thin,
            pltpu.VMEM((both_total * ROWS, WIDE), bf),
            pltpu.VMEM((both_total * ROWS, WIDE), bf),
            pltpu.VMEM((total, WIDE), f32),
            pltpu.VMEM((9, WIDE, WIDE), bf),
            pltpu.VMEM((8, WIDE, WIDE), bf),
            pltpu.VMEM((2, WIDE, WIDE), bf),
            pltpu.VMEM((halo, WIDE), bf),
            pltpu.VMEM((halo, WIDE), bf),
            pltpu.VMEM((halo, WIDE), bf),
            pltpu.VMEM((12, 2, 2, n_rest, unit_rows, 128), bf),
            pltpu.VMEM((5, 2, 2, n_rest, unit_rows, 128), bf),
            pltpu.VMEM((6, 2, 2, n_rest, unit_rows, 128), bf),
            pltpu.VMEM((6, 2, n_rest, unit_rows, 128), bf),
            pltpu.VMEM((6, n_rest, unit_rows, 128), bf),
            pltpu.VMEM((6, n_rest - 1, unit_rows, 128), bf),
            pltpu.VMEM((8, 2, 2, unit_rows, 128), bf),
            pltpu.VMEM((3, unit_rows, WIDE), f32),
            pltpu.VMEM((n_height, 4, 3 * ROWS, WIDE), bf),
            pltpu.VMEM((2, n_height, 8, 128), f32),
            pltpu.VMEM((2, n_batch, 8, 128), f32),
            pltpu.VMEM((n_height, 16, WIDE), f32),
            pltpu.VMEM((n_batch, 16, WIDE), f32),
            pltpu.VMEM((16, 8, WIDE), f32),
            pltpu.VMEM((16, WIDE), f32),
            dma((4,)), dma((2,)), dma((6, 16)), dma((6, 16)), dma((3,)), dma((1,)), dma((2,)),
            dma((2, 2, 2)), dma((2, 2, 2)), dma((3,)), dma((3,)), dma((2,)),
        ],
        compiler_params=pltpu.CompilerParams(
            collective_id=0, has_side_effects=True, vmem_limit_bytes=63 << 20
        ),
        name="both_blocks",
    )(
        *planes, reduce_a, flat_a, expand_a, shortcut_a, reduce_b, flat_b, expand_b,
        edges, mask, gain_mid, shift_mid,
        gain_out.reshape(3, 4, WIDE), shift_out.reshape(3, 4, WIDE), up,
    )
    pooled = jnp.transpose(results[0], (0, 2, 1, 3)).reshape(3, ROWS, -1)[:, :count]
    backs = [from_planes(results[1 + g], images[g].shape) for g in range(3)]
    units, place, shards = results[4], 0, {}
    for name, shape in (
        ("expand_b", expand_b.shape),
        ("spatial_b", second_spatial_weight.shape),
        ("reduce_b", reduce_b.shape),
        ("expand_a", expand_a.shape),
        ("shortcut_a", shortcut_a.shape),
        ("spatial_a", first_spatial_weight.shape),
        ("reduce_a", reduce_a.shape),
    ):
        lead = shape[:-2]
        count_units = shape[-2] * shape[-1] // (WIDE * WIDE)
        for size in lead:
            count_units *= size
        value = units[place : place + count_units]
        place += count_units
        rows = shape[-2] // n_batch
        if lead:
            shards[name] = value.reshape(lead + (rows, WIDE))
        else:
            value = value.reshape(shape[1] // WIDE, rows, WIDE)
            shards[name] = jnp.transpose(value, (1, 0, 2)).reshape(rows, shape[1])
    order = (
        "reduce_a", "spatial_a", "expand_a", "shortcut_a", "reduce_b", "spatial_b", "expand_b"
    )
    mid, out = results[5], results[6].reshape(3, 2, -1)
    return (
        pooled[0], pooled[1], pooled[2], backs[0], backs[1], backs[2], *[shards[name] for name in order],
        mid[:, 1], mid[:, 0], out[:, 1], out[:, 0],
    )


def solution(mesh):
    placed = (
        P("batch", "height", None, None),
        P("batch", "height", None, None),
        P("batch", "height", None, None),
        P(),
        P(),
        P(),
        P(),
        P(),
        P(),
        P(),
        P(),
        P(),
        P(),
        P(),
        P(),
        P("batch", None),
        P("batch", None),
        P("batch", None),
    )
    return jax.shard_map(
        per_device,
        mesh=mesh,
        in_specs=placed,
        out_specs=(
            P("batch", None),
            P("batch", None),
            P("batch", None),
            P("batch", "height", None, None),
            P("batch", "height", None, None),
            P("batch", "height", None, None),
            P("batch", None),
            P(None, None, "batch", None),
            P("batch", None),
            P("batch", None),
            P("batch", None),
            P(None, None, "batch", None),
            P("batch", None),
            P(),
            P(),
            P(),
            P(),
        ),
        check_vma=False,
    )
```

```python
import functools

import jax
import jax.numpy as jnp
from jax import lax
from jax.experimental import pallas as pl
from jax.experimental.pallas import tpu as pltpu
from jax.sharding import PartitionSpec as P

epsilon = 1e-05
MESH = pl.DeviceIdType.MESH

WIDE = 512
ROWS = 16
STEP = 64


def sigmoid(values):
    return 0.5 * jnp.tanh(0.5 * values) + 0.5


def up32(values):
    return values.astype(jnp.float32)


def low(values):
    return values.astype(jnp.bfloat16)


def times(left, right):
    return jnp.dot(left, right, preferred_element_type=jnp.float32)


def times_t(left, right):
    return lax.dot_general(
        left, right, (((1,), (1,)), ((), ())), preferred_element_type=jnp.float32
    )


def t_times(left, right):
    return lax.dot_general(
        left, right, (((0,), (0,)), ((), ())), preferred_element_type=jnp.float32
    )


def fold(values):
    return jnp.sum(values.reshape(-1, 8, values.shape[-1]), axis=0)


def one_row(values):
    return jnp.sum(values, axis=0, keepdims=True)


def wide_mask(mask):
    return jnp.concatenate([up32(mask)] * (WIDE // 128), axis=1)


def grids(heights, widths):
    counts = [k * (o + 1) for k, o in zip(heights, widths)]
    starts = [sum(counts[:g]) for g in range(3)]
    top_sizes = [(k + 1) * (o + 1) + 1 for k, o in zip(heights, widths)]
    top_starts = [sum(top_sizes[:g]) for g in range(3)]
    both_sizes = [(k + 2) * (o + 1) + 2 for k, o in zip(heights, widths)]
    both_starts = [sum(both_sizes[:g]) for g in range(3)]
    halo_starts = [sum(widths[:g]) for g in range(3)]
    return counts, starts, sum(top_sizes), top_starts, sum(both_sizes), both_starts, halo_starts


def main_kernel(
    n_batch, n_height, heights, widths, total_in, total_out,
    x_small, x_medium, x_large, reduce_a, spatial_a, expand_a, shortcut_a, reduce_b, spatial_b, expand_b,
    edge_ref, mask_ref, gain_mid, shift_mid, gain_out, shift_out, up_ref,
    pooled, dx_small, dx_medium, dx_large, g_units, mid_sums, out_sums, h1_kept, a1_kept,
    big_b, big_a, h3, side, mb, h2, a2, h4, h5, a5, a4p, dhp, acc, wp, wq, w2,
    halo_up, halo_down, halo_in, keep, away, r0, r1, r2, r3, final, ready, pool_slots,
    thin, wide_h, wide_b, stat_mid, stat_out,
    w_sem, x_sem, u_send, u_recv, ready_sem, dx_sem, spill_sem, ar_send, ar_recv, halo_send, halo_recv, pool_sem,
):
    b, h = lax.axis_index("batch"), lax.axis_index("height")
    counts, starts, top_total, top_starts, both_total, both_starts, halo_starts = grids(
        heights, widths
    )
    total = sum(counts) * ROWS
    half = total // 2
    part = total // 4
    groups = range(3)
    h1, dz, h6 = big_b, big_b, big_a
    halo_a = mb.at[0:2, 0 : sum(widths) * ROWS]

    def rows_at(start, count):
        return pl.ds(pl.multiple_of(start * ROWS, ROWS), count * ROWS)

    def steps(index):
        return pl.ds(pl.multiple_of(index * part, ROWS), part)

    def fetch(source, target, sem):
        pltpu.make_async_copy(source, target, sem).start()

    def arrived(target, sem):
        pltpu.make_async_copy(target, target, sem).wait()

    def columns(k):
        return pl.ds(k * WIDE, WIDE)

    def fetch_columns(weight, target, first, sem):
        for n in range(4):
            fetch(weight.at[:, columns(n)], target.at[first + n], sem)

    def fetch_shortcut():
        for n in range(4):
            for k in range(2):
                fetch(shortcut_a.at[columns(k), columns(n)], wq.at[2 * n + k], w_sem.at[1])

    xs, dxs = (x_small, x_medium, x_large), (dx_small, dx_medium, dx_large)

    def band_row(buffer, g, y):
        return buffer.at[pl.ds(starts[g] + y * (widths[g] + 1), widths[g])]

    def by_position(buffer):
        return buffer.reshape(buffer.shape[0] // ROWS, ROWS, WIDE)

    def fetch_plane(p, k, target, sem):
        for g in groups:
            for y in range(heights[g]):
                fetch(
                    xs[g].at[y, p // 2, :, p % 2, :, columns(k)],
                    band_row(by_position(target), g, y),
                    sem,
                )

    def plane_arrived(target, sem):
        pixels = sum(k * o for k, o in zip(heights, widths)) * ROWS
        arrived(target.at[0:pixels], sem)

    def put_plane(p, k, source):
        for g in groups:
            for y in range(heights[g]):
                fetch(
                    band_row(by_position(source), g, y),
                    dxs[g].at[y, p // 2, :, p % 2, :, columns(k)],
                    dx_sem.at[0],
                )

    for k in range(2):
        for p in range(4):
            for g in groups:
                for y in range(heights[g]):
                    edge_place = (starts[g] + y * (widths[g] + 1) + widths[g]) * ROWS
                    (h3, mb)[k][p, edge_place : edge_place + ROWS] = jnp.zeros(
                        (ROWS, WIDE), jnp.bfloat16
                    )
            fetch_plane(p, k, (h3, mb)[k].at[p], x_sem.at[k])
    for k in range(2):
        fetch(reduce_a.at[columns(k)], w2.at[k], w_sem.at[3])
    fetch_shortcut()
    fetch(spatial_a, wp, w_sem.at[0])

    halo_down[...] = jnp.zeros_like(halo_down)
    halo_up[...] = jnp.zeros_like(halo_up)
    halo_in[...] = jnp.zeros_like(halo_in)

    @pl.loop(0, both_total // 2)
    def _(i):
        rows = rows_at(i * 2, 2)
        a4p[rows] = jnp.zeros((2 * ROWS, WIDE), jnp.bfloat16)
        dhp[rows] = jnp.zeros((2 * ROWS, WIDE), jnp.bfloat16)

    for g in groups:
        count = widths[g] + 2
        for p in range(4):
            big_a[p, top_starts[g] * ROWS : (top_starts[g] + count) * ROWS] = jnp.zeros(
                (count * ROWS, WIDE), jnp.bfloat16
            )

    barrier = pltpu.get_barrier_semaphore()

    @pl.loop(1, n_batch * n_height)
    def _(k):
        other = lax.rem(b * n_height + h + k, n_batch * n_height)
        pl.semaphore_signal(
            barrier,
            inc=1,
            device_id=(other // n_height, lax.rem(other, n_height)),
            device_id_type=MESH,
        )

    pl.semaphore_wait(barrier, n_batch * n_height - 1)

    turn = [0]
    direct = thin.shape[1] == n_batch * n_height

    def ar_spread(slots, me, count, peer, sems):
        @pl.loop(1, count)
        def _(k):
            pltpu.make_async_remote_copy(
                src_ref=slots.at[me],
                dst_ref=slots.at[me],
                send_sem=ar_send.at[sems],
                recv_sem=ar_recv.at[sems],
                device_id=peer(lax.rem(me + k, count)),
                device_id_type=MESH,
            ).start()

    def ar_wait(slots, count, sems, which):
        others = slots.at[0 : count - 1]
        pltpu.make_async_copy(others, others, which.at[sems]).wait()

    def sums_start(vectors):
        slot = turn[0] % 2
        turn[0] += 1
        if not direct:
            first, second = thin.at[slot, 0:n_height], thin.at[slot, n_height:]
            put_rows(first, h, vectors)
            ar_spread(first, h, n_height, lambda p: (b, p), (0, 0, slot))
            return first, second, 2, slot
        slots = thin.at[slot]
        me = b * n_height + h
        put_rows(slots, me, vectors)
        ar_spread(
            slots, me, n_batch * n_height, lambda p: (p // n_height, lax.rem(p, n_height)),
            (0, 0, slot),
        )
        return slots, None, 0, slot

    def put_rows(slots, me, vectors):
        for v, vector in enumerate(vectors):
            for j in range(4):
                slots[me, 4 * v + j : 4 * v + j + 1, :] = vector[:, 128 * j : 128 * (j + 1)]

    def wide_start(part):
        count = 16 if part is None else 8
        rows = pl.ds(8 * (part or 0), count)
        first, second = wide_h.at[:, rows], wide_b.at[:, rows]
        first[h] = stat_out[0:count]
        ar_spread(first, h, n_height, lambda p: (b, p), (1, 0, part or 0))
        return first, second, 1, part or 0

    def sums_middle(state):
        first, second, kind, slot = state
        if kind == 0:
            return
        ar_wait(first, n_height, (kind % 2, 0, slot), ar_recv)
        second[b] = jnp.sum(first[...], axis=0)
        ar_spread(second, b, n_batch, lambda p: (p, h), (kind % 2, 1, slot))

    def sums_end(state):
        first, second, kind, slot = state
        if kind == 0:
            ar_wait(first, n_batch * n_height, (0, 0, slot), ar_recv)
            summed = jnp.sum(first[...], axis=0)
            ar_wait(first, n_batch * n_height, (0, 0, slot), ar_send)
        else:
            ar_wait(second, n_batch, (kind % 2, 1, slot), ar_recv)
            summed = jnp.sum(second[...], axis=0)
            ar_wait(first, n_height, (kind % 2, 0, slot), ar_send)
            ar_wait(second, n_batch, (kind % 2, 1, slot), ar_send)
        if kind == 1:
            stat_out[0 : summed.shape[0]] = summed
            return None
        return [
            jnp.concatenate([summed[4 * v + j : 4 * v + j + 1] for j in range(4)], axis=1)
            for v in range(2)
        ]

    def keep_stats(kept, index, sums, number, gain, shift):
        centre = sums[0] * (1.0 / number)
        root = lax.rsqrt(sums[1] * (1.0 / number) - centre * centre + epsilon)
        scale = root * gain
        kept[index, 0:1] = centre
        kept[index, 1:2] = root
        kept[index, 2:3] = scale
        kept[index, 3:4] = shift - centre * scale
        kept[index, 4:5] = -centre * root

    def back_factors(kept, index, sums, number, gain):
        centre, root = kept[index, 0:1], kept[index, 1:2]
        main = gain * root
        slope = -main * root * sums[1] * (1.0 / number)
        return main, slope, -main * sums[0] * (1.0 / number) - slope * centre

    def halo_copy(source, target, sem, peer):
        return pltpu.make_async_remote_copy(
            src_ref=source,
            dst_ref=target,
            send_sem=halo_send.at[sem],
            recv_sem=halo_recv.at[sem],
            device_id=(b, peer),
            device_id_type=MESH,
        )

    def halo_rows(g):
        return slice(halo_starts[g] * ROWS, (halo_starts[g] + widths[g]) * ROWS)

    def top_row(padded, start, g):
        return padded.at[pl.ds((start + 1) * ROWS, widths[g] * ROWS)]

    def send_down(buffer, padded, sem):
        @pl.when(h < n_height - 1)
        def _():
            for g in groups:
                halo_copy(
                    buffer.at[halo_rows(g)], top_row(padded, both_starts[g], g), sem, h + 1
                ).start()

    def send_up(buffer, sem):
        @pl.when(h > 0)
        def _():
            halo_copy(buffer, halo_in, sem, h - 1).start()

    def halo_wait(buffer, sems, sem, condition):
        @pl.when(condition)
        def _():
            arrived(buffer, sems.at[sem])

    def place_below(padded):
        for g in groups:
            stride = widths[g] + 1
            for y in range(1, heights[g] + 1):
                is_edge = edge(g, y - 1)

                @pl.loop(0, widths[g])
                def _(col):
                    rows = rows_at(both_starts[g] + 1 + (y + 1) * stride + col, 1)
                    value = up32(halo_in[rows_at(halo_starts[g] + col, 1)]) * is_edge
                    if y < heights[g]:
                        value = value + up32(padded[rows])
                    padded[rows] = low(value)

    def edge(g, y):
        return wide_mask(edge_ref[g, y, 0:1])

    def first_row(source, g, row=0):
        start = (starts[g] + row * (widths[g] + 1)) * ROWS
        return up32(source[start : start + widths[g] * ROWS])

    def last_row(source, g):
        value = first_row(source, g) * edge(g, 0)
        for y in range(1, heights[g]):
            value = value + first_row(source, g, y) * edge(g, y)
        return value

    core, high = lax.rem(h, 2), h // 2
    low_bit, rest = lax.rem(b, 2), b // 2
    n_rest = n_batch // 2
    unit_rows = WIDE // n_batch

    def either(is_one, one, zero):
        return is_one * one + (1 - is_one) * zero

    first, second = either(core, low_bit, high), either(core, high, low_bit)
    core_peer = (b, h + 1 - 2 * core)
    high_peer = (b, h + 2 - 4 * high)
    low_peer = (b + 1 - 2 * low_bit, h)
    first_peer = [either(core, low_peer[i], high_peer[i]) for i in range(2)]
    second_peer = [either(core, high_peer[i], low_peer[i]) for i in range(2)]

    def ring(buffer, unit):
        return lax.rem(unit, buffer.shape[0])

    def unit_copy(level, unit, source, target, peer):
        return pltpu.make_async_remote_copy(
            src_ref=source,
            dst_ref=target,
            send_sem=u_send.at[level, lax.rem(unit, 16)],
            recv_sem=u_recv.at[level, lax.rem(unit, 16)],
            device_id=tuple(peer),
            device_id_type=MESH,
        )

    def hop(level, unit):
        kept = keep.at[ring(keep, unit)]
        if level == 0:
            return unit_copy(
                0, unit, away.at[ring(away, unit)], r0.at[ring(r0, unit)], core_peer
            )
        if level == 1:
            return unit_copy(1, unit, kept.at[1 - first], r1.at[ring(r1, unit)], first_peer)
        if level == 2:
            return unit_copy(
                2, unit, kept.at[first, 1 - second], r2.at[ring(r2, unit)], second_peer
            )
        if level == 4:
            mine = final.at[ring(final, unit), core, high]
            return unit_copy(4, unit, mine, mine, high_peer)
        both = final.at[ring(final, unit), core]
        return unit_copy(5, unit, both, both, core_peer)

    def add_to(target, source):
        target[...] = low(up32(target[...]) + up32(source[...]))

    def rest_wait(unit, sems):
        others = r3.at[ring(r3, unit)]
        pltpu.make_async_copy(others, others, sems.at[3, lax.rem(unit, 16)]).wait()

    def round_0(unit):
        hop(0, unit).start()

    def round_1(unit):
        hop(0, unit).wait()
        kept, got = keep.at[ring(keep, unit)], r0.at[ring(r0, unit)]

        @pl.loop(0, n_rest)
        def _(k):
            for i in range(2):
                for j in range(2):
                    add_to(kept.at[i, j, k], got.at[i, j, k])

        hop(1, unit).start()

    def round_2(unit):
        hop(1, unit).wait_recv()
        kept, got = keep.at[ring(keep, unit), first], r1.at[ring(r1, unit)]

        @pl.loop(0, n_rest)
        def _(k):
            for j in range(2):
                add_to(kept.at[j, k], got.at[j, k])

        hop(2, unit).start()

    def round_3(unit):
        hop(2, unit).wait_recv()
        kept, got = keep.at[ring(keep, unit), first, second], r2.at[ring(r2, unit)]

        @pl.loop(0, n_rest)
        def _(k):
            add_to(kept.at[k], got.at[k])

        @pl.loop(1, n_rest)
        def _(k):
            unit_copy(
                3,
                unit,
                kept.at[lax.rem(rest + k, n_rest)],
                r3.at[ring(r3, unit), n_rest - 1 - k],
                (lax.rem(rest + k, n_rest) * 2 + low_bit, h),
            ).start()

    def round_4(unit):
        rest_wait(unit, u_recv)
        value = up32(keep[ring(keep, unit), first, second, rest])
        for k in range(n_rest - 1):
            value = value + up32(r3[ring(r3, unit), k])
        final[ring(final, unit), core, high] = low(value)
        hop(4, unit).start()

    def round_5(unit):
        hop(4, unit).wait_recv()
        hop(5, unit).start()
        for level in (1, 2):
            hop(level, unit).wait_send()
        rest_wait(unit, u_send)

    def round_6(unit):
        hop(5, unit).wait_recv()
        for level in (4, 5):
            hop(level, unit).wait_send()
        slot = ring(ready, unit)

        @pl.when(unit >= ready.shape[0])
        def _():
            arrived(ready.at[slot], ready_sem.at[slot])

        for c in range(2):
            for i in range(2):
                lane = 128 * (2 * c + i)
                ready[slot, :, lane : lane + 128] = up32(final[ring(final, unit), c, i])
        fetch(ready.at[slot], g_units.at[unit], ready_sem.at[slot])

    rounds = (
        (0, round_0), (2, round_1), (4, round_2), (6, round_3), (8, round_4), (10, round_5),
        (12, round_6),
    )
    clock, made, produced = [0], [0], []

    def advance(index, base, count):
        for lag, act in rounds:
            for start, size, unit in produced:
                from_, to = max(base - lag, start), min(base - lag + count, start + size)
                if from_ >= to:
                    continue
                target = base - lag - start + unit + index
                if to - from_ == count:
                    act(target)
                else:
                    shift = base - lag
                    inside = jnp.logical_and(index >= from_ - shift, index < to - shift)
                    pl.when(inside)(functools.partial(act, target))

    def idle(count):
        base = clock[0]
        clock[0] += count

        @pl.loop(0, count)
        def _(i):
            advance(i, base, count)

    def ticks(count):
        base = clock[0]
        clock[0] += count
        return lambda i: advance(i, base, count)

    def put(value, unit, units, first_shard):
        shard_rows = units * unit_rows
        own_side = core == 0
        left, right = low(value[:, : WIDE // 2]), low(value[:, WIDE // 2 :])
        own, other = jnp.where(own_side, left, right), jnp.where(own_side, right, left)
        for s in range(WIDE // shard_rows):
            shard = first_shard + s
            shard_low, shard_rest = s % 2, shard // 2
            for q in range(units):
                rows = slice(s * shard_rows + q * unit_rows, s * shard_rows + (q + 1) * unit_rows)
                for i in range(2):
                    lanes = slice(128 * i, 128 * (i + 1))
                    keep[
                        ring(keep, unit + q),
                        either(core, shard_low, i),
                        either(core, i, shard_low),
                        shard_rest,
                    ] = own[rows, lanes]
                    away[
                        ring(away, unit + q),
                        either(core, i, shard_low),
                        either(core, shard_low, i),
                        shard_rest,
                    ] = other[rows, lanes]

    def run(count, body, make):
        base, unit = clock[0], made[0]
        clock[0] += count
        made[0] += count
        produced.append((base, count, unit))

        @pl.loop(0, count)
        def _(i):
            body(i)
            make(i, unit + i)
            advance(i, base, count)

    def produce(count, units, make):
        base, unit = clock[0], made[0]
        produced.append((base, count * units, unit))
        clock[0] += count * units
        made[0] += count * units

        @pl.loop(0, count)
        def _(t):
            make(t, unit + t * units)
            if units == 1:
                advance(t, base, count)
            else:

                @pl.loop(0, units)
                def _(q):
                    advance(t * units + q, base, count * units)

    zero8 = jnp.zeros((8, WIDE), jnp.float32)

    arrived(w2, w_sem.at[3])
    for k in range(2):
        for p in range(4):
            plane_arrived((h3, mb)[k].at[p], x_sem.at[k])

    def first_reduction(i, carry):
        p = i // 2
        rows = pl.ds(pl.multiple_of(lax.rem(i, 2) * half, ROWS), half)
        value = times(h3[p, rows], w2[0]) + times(mb[p, rows], w2[1])
        value = value * wide_mask(mask_ref[rows])
        h1[p, rows] = low(value)
        return carry[0] + fold(value), carry[1] + fold(value * value)

    sums = lax.fori_loop(0, 8, first_reduction, (zero8, zero8))
    state = sums_start([one_row(v) for v in sums])

    arrived(wq, w_sem.at[1])

    def shortcut_product(n, carry):
        value = times(h3[0], wq[2 * n]) + times(mb[0], wq[2 * n + 1])
        value = value * wide_mask(mask_ref[...])
        side[n] = low(value)
        stat_out[pl.ds(8 + n, 1)] = one_row(fold(value))
        stat_out[pl.ds(12 + n, 1)] = one_row(fold(value * value))
        return carry

    lax.fori_loop(0, 2, shortcut_product, 0)
    sums_middle(state)
    lax.fori_loop(2, 4, shortcut_product, 0)
    fetch_columns(expand_a, wq, 0, w_sem.at[1])
    for k in range(4):
        fetch(reduce_b.at[columns(k)], wq.at[4 + k], w_sem.at[2])
    sums = sums_end(state)
    keep_stats(stat_mid, 0, sums, total_in, gain_mid[0:1], shift_mid[0:1])

    scale, offset = stat_mid[0, 2:3], stat_mid[0, 3:4]
    for column in range(2):
        for g in groups:
            pre = last_row(h1.at[2 + column], g) * scale + offset
            mask = wide_mask(mask_ref[starts[g] * ROWS : (starts[g] + widths[g]) * ROWS])
            halo_a[column, halo_rows(g)] = low(pre * sigmoid(pre) * mask)

    @pl.when(h < n_height - 1)
    def _():
        for column in range(2):
            for g in groups:
                halo_copy(
                    halo_a.at[column, halo_rows(g)],
                    top_row(big_a.at[2 + column], top_starts[g], g),
                    0,
                    h + 1,
                ).start()

    for g in groups:
        per = counts[g] * ROWS // STEP
        base = (top_starts[g] + 1 + widths[g] + 1) * ROWS

        @pl.loop(0, 4)
        def _(p):
            @pl.loop(0, per)
            def _(i):
                rows = pl.ds(pl.multiple_of(starts[g] * ROWS + i * STEP, ROWS), STEP)
                pre = up32(h1[p, rows]) * scale + offset
                value = pre * sigmoid(pre) * wide_mask(mask_ref[rows])
                big_a[p, pl.ds(pl.multiple_of(base + i * STEP, ROWS), STEP)] = low(value)

    fetch(h1, h1_kept, spill_sem.at[0])

    def group_rows(g):
        return slice(starts[g] * ROWS, (starts[g] + counts[g]) * ROWS)

    def window(padded, start, g, dy, dx_):
        first = start + 1 + (1 + dy) * (widths[g] + 1) + dx_
        return padded[rows_at(first, counts[g])]

    def window_a(g, a, c):
        py, dy = lax.rem(a + 1, 2), (a + 1) // 2 - 1
        px, dx_ = lax.rem(c + 1, 2), (c + 1) // 2 - 1
        first = top_starts[g] + 1 + (1 + dy) * (widths[g] + 1) + dx_
        return big_a[2 * py + px, rows_at(first, counts[g])]

    def clear_acc():
        @pl.loop(0, total // part)
        def _(i):
            acc[steps(i)] = jnp.zeros((part, WIDE), jnp.float32)

    def conv_taps(start, last, window_of, product, make=None):
        def tap(t):
            for g in groups:
                acc[group_rows(g)] += product(window_of(g, t // 3, lax.rem(t, 3)), wp[t])

        if make is not None:
            run(last - start, lambda i: tap(start + i), make)
            return
        tick = ticks(last - start) if produced else None

        @pl.loop(start, last)
        def _(t):
            tap(t)
            if tick is not None:
                tick(t - start)

    def masked_sums(target):
        def body(i, carry):
            rows = steps(i)
            value = acc[rows] * wide_mask(mask_ref[rows])
            target[rows] = low(value)
            return carry[0] + fold(value), carry[1] + fold(value * value)

        return lax.fori_loop(0, total // part, body, (zero8, zero8))

    clear_acc()
    arrived(wp, w_sem.at[0])
    conv_taps(3, 9, window_a, times)
    halo_wait(halo_a, halo_recv, 0, h > 0)
    conv_taps(0, 3, window_a, times)
    sums = masked_sums(h2)
    state = sums_start([one_row(v) for v in sums])
    fetch(spatial_b, wp, w_sem.at[0])
    fetch(big_a, a1_kept, spill_sem.at[1])
    halo_wait(halo_a, halo_send, 0, h < n_height - 1)
    sums_middle(state)
    sums = sums_end(state)
    keep_stats(stat_mid, 1, sums, total_out, gain_mid[1:2], shift_mid[1:2])

    def activate(source, target, index):
        scale, offset = stat_mid[index, 2:3], stat_mid[index, 3:4]

        @pl.loop(0, total // part)
        def _(i):
            rows = steps(i)
            pre = up32(source[rows]) * scale + offset
            target[rows] = low(pre * sigmoid(pre) * wide_mask(mask_ref[rows]))

    activate(h2, a2, 1)
    arrived(wq.at[0:4], w_sem.at[1])

    def expansion(source, target):
        @pl.loop(0, 4)
        def _(n):
            value = times(source[...], wq[n])
            target[n, 0:total] = low(value)
            stat_out[pl.ds(n, 1)] = one_row(fold(value))
            stat_out[pl.ds(4 + n, 1)] = one_row(fold(value * value))

    expansion(a2, h3)
    state = wide_start(None)
    fetch_columns(expand_b, wq, 0, w_sem.at[1])
    sums_middle(state)
    sums_end(state)

    def out_stats(index, n, row):
        keep_stats(
            mid_or_out,
            4 * index + n,
            [stat_out[row + n : row + n + 1], stat_out[row + 4 + n : row + 5 + n]],
            total_out,
            gain_out[index, n : n + 1],
            shift_out[index, n : n + 1],
        )

    mid_or_out = stat_mid.at[4:16]
    for n in range(4):
        out_stats(0, n, 0)
        out_stats(1, n, 8)

    def out_stat(index, n, row):
        return stat_mid[4 + 4 * index + n, row : row + 1]

    def joint(n, rows):
        return (
            up32(h3[n, rows]) * out_stat(0, n, 2)
            + up32(side[n, rows]) * out_stat(1, n, 2)
            + (out_stat(0, n, 3) + out_stat(1, n, 3))
        )

    arrived(wq.at[4:8], w_sem.at[2])
    clear_acc()

    @pl.loop(0, 4)
    def _(n):
        @pl.loop(0, 2)
        def _(i):
            rows = pl.ds(pl.multiple_of(i * half, ROWS), half)
            value = joint(n, rows)
            value = low(value * sigmoid(value) * wide_mask(mask_ref[rows]))
            mb[n, rows] = value
            acc[rows] += times(value, wq[4 + n])

    def plain_sums(target):
        def body(i, carry):
            rows = steps(i)
            value = acc[rows]
            target[rows] = low(value)
            return carry[0] + fold(value), carry[1] + fold(value * value)

        return lax.fori_loop(0, total // part, body, (zero8, zero8))

    sums = plain_sums(h4)
    state = sums_start([one_row(v) for v in sums])
    sums_middle(state)
    clear_acc()
    sums = sums_end(state)
    keep_stats(stat_mid, 2, sums, total_out, gain_mid[2:3], shift_mid[2:3])

    scale, offset = stat_mid[2, 2:3], stat_mid[2, 3:4]
    for g in groups:
        pre = last_row(h4, g) * scale + offset
        mask = wide_mask(mask_ref[starts[g] * ROWS : (starts[g] + widths[g]) * ROWS])
        halo_down[halo_rows(g)] = low(pre * sigmoid(pre) * mask)
    send_down(halo_down, a4p, 1)
    for g in groups:
        pre = first_row(h4, g) * scale + offset
        mask = wide_mask(mask_ref[starts[g] * ROWS : (starts[g] + widths[g]) * ROWS])
        halo_up[halo_rows(g)] = low(pre * sigmoid(pre) * mask)
    send_up(halo_up, 2)

    def both_base(g):
        return (both_starts[g] + 1 + widths[g] + 1) * ROWS

    for g in groups:

        @pl.loop(0, counts[g] * ROWS // STEP)
        def _(i):
            rows = pl.ds(pl.multiple_of(starts[g] * ROWS + i * STEP, ROWS), STEP)
            pre = up32(h4[rows]) * scale + offset
            value = low(pre * sigmoid(pre) * wide_mask(mask_ref[rows]))
            a4p[pl.ds(pl.multiple_of(both_base(g) + i * STEP, ROWS), STEP)] = value

    def window_b(g, a, c):
        return window(a4p, both_starts[g], g, a - 1, c - 1)

    def window_b_back(g, a, c):
        return window(dhp, both_starts[g], g, 1 - a, 1 - c)

    arrived(wp, w_sem.at[0])
    conv_taps(3, 6, window_b, times)
    halo_wait(halo_down, halo_recv, 1, h > 0)
    halo_wait(halo_in, halo_recv, 2, h < n_height - 1)
    place_below(a4p)
    conv_taps(0, 3, window_b, times)
    conv_taps(6, 9, window_b, times)
    sums = masked_sums(h5)
    state = sums_start([one_row(v) for v in sums])
    halo_wait(halo_down, halo_send, 1, h < n_height - 1)
    halo_wait(halo_up, halo_send, 2, h > 0)
    sums_middle(state)
    sums = sums_end(state)
    keep_stats(stat_mid, 3, sums, total_out, gain_mid[3:4], shift_mid[3:4])

    activate(h5, a5, 3)
    arrived(wq.at[0:4], w_sem.at[1])
    arrived(big_a, spill_sem.at[1])
    expansion(a5, h6)
    state = wide_start(0)
    sums_middle(state)
    arrived(h1, spill_sem.at[0])
    sums_end(state)
    for n in range(4):
        out_stats(2, n, 0)

    @pl.loop(0, 4)
    def _(n):
        index = 12 + n
        root, scale = stat_mid[index, 1:2], stat_mid[index, 2:3]
        offset, back = stat_mid[index, 3:4], stat_mid[index, 4:5]
        zero = jnp.zeros((ROWS, WIDE), jnp.float32)
        total_grad, total_dot = zero8, zero8
        for g in groups:
            share = 1.0 / (widths[g] * widths[g])

            up = jnp.concatenate([up32(up_ref[g, n]) * share] * (STEP // ROWS), axis=0)

            def body(i, carry):
                rows = pl.ds(pl.multiple_of(starts[g] * ROWS + i * STEP, ROWS), STEP)
                value = up32(h6[n, rows])
                mask = wide_mask(mask_ref[rows])
                z = value * scale + offset + up32(mb[n, rows])
                s = sigmoid(z)
                grad = up * (s * (1.0 + z * (1.0 - s))) * mask
                dz[n, rows] = low(grad)
                last = (z * s * mask).reshape(STEP // ROWS, ROWS, WIDE)
                return (
                    carry[0] + jnp.sum(last, axis=0),
                    carry[1] + fold(grad),
                    carry[2] + fold(grad * (value * root + back)),
                )

            pool, total_grad, total_dot = lax.fori_loop(
                0, counts[g] * ROWS // STEP, body, (zero, total_grad, total_dot)
            )
            pool_slots[h, n, g * ROWS : (g + 1) * ROWS] = low(pool)
        stat_out[pl.ds(n, 1)] = one_row(total_grad)
        stat_out[pl.ds(4 + n, 1)] = one_row(total_dot)

    state = wide_start(1)

    for k in range(1, n_height):
        pltpu.make_async_remote_copy(
            src_ref=pool_slots.at[h],
            dst_ref=pool_slots.at[h],
            send_sem=pool_sem.at[0],
            recv_sem=pool_sem.at[1],
            device_id=(b, lax.rem(h + k, n_height)),
            device_id_type=MESH,
        ).start()
    sums_middle(state)
    clear_acc()
    sums_end(state)

    def out_back(index, sum_row, dot_row, n):
        sums = [stat_out[pl.ds(sum_row + n, 1)], stat_out[pl.ds(dot_row + n, 1)]]
        out_sums[index, 0, pl.ds(n, 1)] = sums[0]
        out_sums[index, 1, pl.ds(n, 1)] = sums[1]
        return back_factors(
            stat_mid, 4 + 4 * index + n, sums, total_out, gain_out[index, pl.ds(n, 1)]
        )

    def mid_back(index, place, sums, number):
        mid_sums[place, 0:1] = sums[0]
        mid_sums[place, 1:2] = sums[1]
        return back_factors(stat_mid, index, sums, number, gain_mid[place : place + 1])

    def mid_gradient(source, index):
        root, scale = stat_mid[index, 1:2], stat_mid[index, 2:3]
        offset, back = stat_mid[index, 3:4], stat_mid[index, 4:5]

        def body(i, carry):
            rows = steps(i)
            value = up32(source[rows])
            pre = value * scale + offset
            s = sigmoid(pre)
            grad = acc[rows] * (s * (1.0 + pre * (1.0 - s))) * wide_mask(mask_ref[rows])
            acc[rows] = grad
            return carry[0] + fold(grad), carry[1] + fold(grad * (value * root + back))

        sums = lax.fori_loop(0, total // part, body, (zero8, zero8))
        return [one_row(v) for v in sums]

    @pl.loop(0, 4)
    def _(n):
        main, slope, constant = out_back(2, 0, 4, n)

        @pl.loop(0, 2)
        def _(i):
            rows = pl.ds(pl.multiple_of(i * half, ROWS), half)
            grad = main * up32(dz[n, rows]) + slope * up32(h6[n, rows]) + constant
            grad = low(grad * wide_mask(mask_ref[rows]))
            h6[n, rows] = grad
            acc[rows] += times_t(grad, wq[n])

    sums = mid_gradient(h5, 3)
    state = sums_start(sums)
    fetch_columns(expand_a, wq, 0, w_sem.at[1])
    sums_middle(state)
    produce(4, 1, lambda t, unit: put(t_times(a5[...], h6[t, 0:total]), unit, 1, 0))
    fetch(a1_kept, big_a, spill_sem.at[1])
    sums = sums_end(state)

    def mid_step(target, factors, padded):
        main, slope, constant = factors

        def tile(rows):
            grad = main * acc[rows] + slope * up32(target[rows]) + constant
            return low(grad * wide_mask(mask_ref[rows]))

        for g in groups:

            @pl.loop(0, counts[g] * ROWS // STEP)
            def _(i):
                rows = pl.ds(pl.multiple_of(starts[g] * ROWS + i * STEP, ROWS), STEP)
                grad = tile(rows)
                target[rows] = grad
                if padded is not None:
                    padded[pl.ds(pl.multiple_of(both_base(g) + i * STEP, ROWS), STEP)] = grad

    mid_step(h5, mid_back(3, 3, sums, total_out), dhp)
    for g in groups:
        halo_down[halo_rows(g)] = low(last_row(h5, g))
        halo_up[halo_rows(g)] = low(first_row(h5, g))
    send_down(halo_down, dhp, 1)
    send_up(halo_up, 2)
    def spatial_tile(window_of, grads):
        def value_of(t):
            parts = [
                t_times(window_of(g, t // 3, lax.rem(t, 3)), grads[group_rows(g)]) for g in groups
            ]
            return parts[0] + parts[1] + parts[2]

        return value_of

    def spatial_maker(window_of, grads):
        tile = spatial_tile(window_of, grads)
        return lambda done: lambda i, unit: put(tile(done + i), unit, 1, 0)

    make_b = spatial_maker(window_b, h5)
    clear_acc()
    conv_taps(3, 6, window_b_back, times_t, make_b(0))
    halo_wait(halo_down, halo_recv, 1, h > 0)
    halo_wait(halo_in, halo_recv, 2, h < n_height - 1)
    place_below(dhp)
    conv_taps(0, 3, window_b_back, times_t, make_b(3))
    conv_taps(6, 9, window_b_back, times_t)
    fetch(spatial_a, wp, w_sem.at[0])
    sums = mid_gradient(h4, 2)
    state = sums_start(sums)
    halo_wait(halo_down, halo_send, 1, h < n_height - 1)
    halo_wait(halo_up, halo_send, 2, h > 0)
    sums_middle(state)

    produce(3, 1, make_b(6))
    sums = sums_end(state)

    mid_step(h4, mid_back(2, 2, sums, total_out), None)
    fetch_plane(0, 1, a4p, x_sem.at[1])

    tick = ticks(8)

    @pl.loop(0, 4)
    def _(n):
        def body(i, carry):
            tick(2 * n + i)
            rows = pl.ds(pl.multiple_of(i * half, ROWS), half)
            grad = times_t(h4[rows], wq[4 + n]) + up32(dz[n, rows])
            z = joint(n, rows)
            s = sigmoid(z)
            grad = grad * (s * (1.0 + z * (1.0 - s))) * wide_mask(mask_ref[rows])
            dz[n, rows] = low(grad)
            main_hat = up32(h3[n, rows]) * out_stat(0, n, 1) + out_stat(0, n, 4)
            side_hat = up32(side[n, rows]) * out_stat(1, n, 1) + out_stat(1, n, 4)
            return (
                carry[0] + fold(grad),
                carry[1] + fold(grad * main_hat),
                carry[2] + fold(grad * side_hat),
            )

        sums = lax.fori_loop(0, 2, body, (zero8, zero8, zero8))
        for v in range(3):
            stat_out[pl.ds(4 * v + n, 1)] = one_row(sums[v])

    state = wide_start(None)
    sums_middle(state)

    def tile_reduce_b(step, unit):
        @pl.loop(0, 4)
        def _(t):
            put(t_times(mb[t], h4[...]), unit, 4, t * (n_batch // 4))

    produce(1, 4, tile_reduce_b)
    for p in range(4):
        fetch_plane(p, 0, mb.at[p], x_sem.at[0])
    clear_acc()
    sums_end(state)

    arrived(wq.at[0:4], w_sem.at[1])

    def expansion_back(n):
        main, slope, constant = out_back(0, 0, 4, n)
        main2, slope2, constant2 = out_back(1, 0, 8, n)

        @pl.loop(0, 2)
        def _(i):
            rows = pl.ds(pl.multiple_of(i * half, ROWS), half)
            grad_in = up32(dz[n, rows])
            mask = wide_mask(mask_ref[rows])
            grad = low((main * grad_in + slope * up32(h3[n, rows]) + constant) * mask)
            h3[n, rows] = grad
            acc[rows] += times_t(grad, wq[n])
            other = main2 * grad_in + slope2 * up32(side[n, rows]) + constant2
            side[n, rows] = low(other * mask)

    run(4, expansion_back, lambda n, unit: put(t_times(a2[...], h3[n]), unit, 1, 0))
    fetch(h1_kept, h1, spill_sem.at[0])
    fetch_shortcut()
    sums = mid_gradient(h2, 1)
    state = sums_start(sums)
    sums_middle(state)
    for p in range(4):
        plane_arrived(mb.at[p], x_sem.at[0])
    plane_arrived(a4p, x_sem.at[1])

    def tile_shortcut(t, unit):
        put(t_times(mb[0], side[t]), unit, 2, 0)
        put(t_times(a4p[0:total], side[t]), unit, 2, n_batch // 2)

    produce(1, 2, lambda step, unit: tile_shortcut(0, unit))
    sums = sums_end(state)

    mid_step(h2, mid_back(1, 1, sums, total_out), dhp)
    for g in groups:
        halo_up[halo_rows(g)] = low(first_row(h2, g))
    send_up(halo_up, 2)
    arrived(wp, w_sem.at[0])
    arrived(h1, spill_sem.at[0])
    root, scale = stat_mid[0, 1:2], stat_mid[0, 2:3]
    offset, back = stat_mid[0, 3:4], stat_mid[0, 4:5]
    carry = (zero8, zero8)
    for p in range(4):
        py, px = p // 2, p % 2
        row_taps = ((1, 0),) if py == 0 else ((0, 1), (2, 0))
        column_taps = ((1, 0),) if px == 0 else ((0, 1), (2, 0))
        if p == 2:
            halo_wait(halo_in, halo_recv, 2, h < n_height - 1)
            place_below(dhp)
        for g in groups:
            value = None
            for a, dy in row_taps:
                for c, dx_ in column_taps:
                    product = times_t(window(dhp, both_starts[g], g, dy, dx_), wp[3 * a + c])
                    value = product if value is None else value + product
            acc[group_rows(g)] = value

        def body(i, carry):
            rows = steps(i)
            value = up32(h1[p, rows])
            pre = value * scale + offset
            s = sigmoid(pre)
            grad = acc[rows] * (s * (1.0 + pre * (1.0 - s))) * wide_mask(mask_ref[rows])
            h3[p, rows] = low(grad)
            return carry[0] + fold(grad), carry[1] + fold(grad * (value * root + back))

        carry = lax.fori_loop(0, total // part, body, carry)
        if p > 0:
            produce(1, 2, lambda step, unit: tile_shortcut(p, unit))
    state = sums_start([one_row(v) for v in carry])
    halo_wait(halo_up, halo_send, 2, h > 0)
    sums_middle(state)
    arrived(big_a, spill_sem.at[1])
    make_a = spatial_maker(window_a, h2)
    produce(3, 1, make_a(0))
    sums = sums_end(state)

    main, slope, constant = mid_back(0, 0, sums, total_in)

    def first_back(p):
        @pl.loop(0, total // part)
        def _(i):
            rows = steps(i)
            grad = main * up32(h3[p, rows]) + slope * up32(h1[p, rows]) + constant
            h1[p, rows] = low(grad * wide_mask(mask_ref[rows]))

        fetch_plane(p, 1, h3.at[p], x_sem.at[1])

    run(4, first_back, make_a(3))
    produce(2, 1, make_a(7))
    for p in range(4):
        plane_arrived(h3.at[p], x_sem.at[1])

    def last_tile(chunk):
        value = t_times(chunk(0), h1[0])
        for p in range(1, 4):
            value = value + t_times(chunk(p), h1[p])
        return value

    def tile_reduce_a(step, unit):
        put(last_tile(lambda p: mb[p]), unit, 2, 0)
        put(last_tile(lambda p: h3[p]), unit, 2, n_batch // 2)

    produce(1, 2, tile_reduce_a)
    arrived(wq, w_sem.at[1])
    for k in range(2):
        tick_13 = ticks(2)

        @pl.loop(0, 2)
        def _(i):
            rows = pl.ds(pl.multiple_of(i * half, ROWS), half)
            value = times_t(h1[0, rows], w2[k])
            for n in range(4):
                value = value + times_t(side[n, rows], wq[2 * n + k])
            if k == 0:
                big_a[0, rows] = low(value)
            else:
                a4p[rows] = low(value)
            tick_13(i)

    put_plane(0, 0, big_a.at[0])
    put_plane(0, 1, a4p)
    tick_13p = ticks(3)

    @pl.loop(1, 4)
    def _(p):
        big_a[p, 0:total] = low(times_t(h1[p], w2[0]))
        side[p] = low(times_t(h1[p], w2[1]))
        put_plane(p, 0, big_a.at[p])
        put_plane(p, 1, side.at[p])
        tick_13p(p - 1)

    idle(rounds[-1][0] - 6)
    others = pool_slots.at[0 : n_height - 1]
    pltpu.make_async_copy(others, others, pool_sem.at[1]).wait()
    pltpu.make_async_copy(others, others, pool_sem.at[0]).wait()
    for g in groups:
        for n in range(4):
            value = None
            for k in range(n_height):
                part = up32(pool_slots[k, n, g * ROWS : (g + 1) * ROWS])
                value = part if value is None else value + part
            pooled[g, n] = value * (1.0 / (widths[g] * widths[g]))

    for slot in range(ready.shape[0]):
        arrived(ready.at[slot], ready_sem.at[slot])
    for p in range(8):
        plane_arrived(a4p, dx_sem.at[0])


def to_planes(image):
    count, rows, cols, channels = image.shape
    value = jnp.pad(image, ((0, ROWS - count), (0, 0), (0, 0), (0, 0)))
    value = jnp.transpose(value, (1, 2, 0, 3))
    return value.reshape(rows // 2, 2, cols // 2, 2, ROWS, channels)


def from_planes(planes, shape):
    count, rows, cols, channels = shape
    value = planes.reshape(rows, cols, ROWS, channels)[:, :, :count]
    return jnp.transpose(value, (2, 0, 1, 3))


def per_device(
    image_small, image_medium, image_large, row_counts, reduce_a, first_spatial_weight, expand_a,
    shortcut_a, reduce_b, second_spatial_weight, expand_b, gain_mid, shift_mid, gain_out,
    shift_out, upstream_small, upstream_medium, upstream_large,
):
    images = (image_small, image_medium, image_large)
    upstreams = (upstream_small, upstream_medium, upstream_large)
    n_batch, n_height = lax.axis_size("batch"), lax.axis_size("height")
    heights = [value.shape[1] // 2 for value in images]
    widths = [value.shape[2] // 2 for value in images]
    count = images[0].shape[0]
    live = row_counts[:, lax.axis_index("height")]
    pixels = sum(o * o for o in widths) * count * n_batch
    counts, starts, top_total, _, both_total, _, _ = grids(heights, widths)
    total = sum(counts) * ROWS
    planes = [to_planes(image) for image in images]
    masks = []
    for g in range(3):
        row_ok = (jnp.arange(heights[g], dtype=jnp.int32) < live[g])[:, None, None]
        column_ok = (jnp.arange(widths[g] + 1) < widths[g])[None, :, None]
        image_ok = (jnp.arange(ROWS) < count)[None, None, :]
        masks.append(jnp.logical_and(jnp.logical_and(row_ok, column_ok), image_ok).reshape(-1))
    mask = jnp.concatenate(masks).astype(jnp.bfloat16)
    mask = jnp.broadcast_to(mask[:, None], (total, 128))
    edges = (jnp.arange(max(heights))[None, :] == live[:, None] - 1).astype(jnp.float32)
    edges = jnp.broadcast_to(edges[:, :, None, None], edges.shape + (8, 128))
    up = jnp.stack([jnp.pad(value, ((0, ROWS - count), (0, 0))) for value in upstreams])
    up = jnp.transpose(up.reshape(3, ROWS, 4, WIDE), (0, 2, 1, 3))
    halo = sum(widths) * ROWS
    bf, f32 = jnp.bfloat16, jnp.float32
    unit_rows, n_rest = WIDE // n_batch, n_batch // 2
    n_thin = n_batch * n_height if n_batch * n_height <= 64 else n_batch + n_height
    n_units = sum(
        w.size for w in (reduce_a, first_spatial_weight, expand_a, shortcut_a, reduce_b,
                         second_spatial_weight, expand_b)
    ) // (WIDE * WIDE)
    dma = pltpu.SemaphoreType.DMA
    vmem = pl.BlockSpec(memory_space=pltpu.VMEM)
    anywhere = pl.BlockSpec(memory_space=pl.ANY)
    flat_a = first_spatial_weight.reshape(9, WIDE, WIDE)
    flat_b = second_spatial_weight.reshape(9, WIDE, WIDE)
    big = pltpu.VMEM((4, total, WIDE), bf)
    thin = pltpu.VMEM((total, WIDE), bf)
    results = pl.pallas_call(
        functools.partial(
            main_kernel, n_batch, n_height, heights, widths, float(4 * pixels), float(pixels)
        ),
        out_shape=[
            jax.ShapeDtypeStruct((3, 4, ROWS, WIDE), f32),
            *[jax.ShapeDtypeStruct(value.shape, bf) for value in planes],
            jax.ShapeDtypeStruct((n_units, unit_rows, WIDE), f32),
            jax.ShapeDtypeStruct((4, 2, WIDE), f32),
            jax.ShapeDtypeStruct((3, 2, 4, WIDE), f32),
            jax.ShapeDtypeStruct((4, total, WIDE), bf),
            jax.ShapeDtypeStruct((4, top_total * ROWS, WIDE), bf),
        ],
        in_specs=[anywhere] * 10 + [vmem] * 7,
        out_specs=[vmem] + [anywhere] * 4 + [vmem] * 2 + [anywhere] * 2,
        scratch_shapes=[
            big,
            pltpu.VMEM((4, top_total * ROWS, WIDE), bf),
            big, big, big,
            thin, thin, thin, thin, thin,
            pltpu.VMEM((both_total * ROWS, WIDE), bf),
            pltpu.VMEM((both_total * ROWS, WIDE), bf),
            pltpu.VMEM((total, WIDE), f32),
            pltpu.VMEM((9, WIDE, WIDE), bf),
            pltpu.VMEM((8, WIDE, WIDE), bf),
            pltpu.VMEM((2, WIDE, WIDE), bf),
            pltpu.VMEM((halo, WIDE), bf),
            pltpu.VMEM((halo, WIDE), bf),
            pltpu.VMEM((halo, WIDE), bf),
            pltpu.VMEM((12, 2, 2, n_rest, unit_rows, 128), bf),
            pltpu.VMEM((5, 2, 2, n_rest, unit_rows, 128), bf),
            pltpu.VMEM((6, 2, 2, n_rest, unit_rows, 128), bf),
            pltpu.VMEM((6, 2, n_rest, unit_rows, 128), bf),
            pltpu.VMEM((6, n_rest, unit_rows, 128), bf),
            pltpu.VMEM((6, n_rest - 1, unit_rows, 128), bf),
            pltpu.VMEM((8, 2, 2, unit_rows, 128), bf),
            pltpu.VMEM((3, unit_rows, WIDE), f32),
            pltpu.VMEM((n_height, 4, 3 * ROWS, WIDE), bf),
            pltpu.VMEM((2, n_thin, 8, 128), f32),
            pltpu.VMEM((n_height, 16, WIDE), f32),
            pltpu.VMEM((n_batch, 16, WIDE), f32),
            pltpu.VMEM((16, 8, WIDE), f32),
            pltpu.VMEM((16, WIDE), f32),
            dma((4,)), dma((2,)), dma((6, 16)), dma((6, 16)), dma((3,)), dma((1,)), dma((2,)),
            dma((2, 2, 2)), dma((2, 2, 2)), dma((3,)), dma((3,)), dma((2,)),
        ],
        compiler_params=pltpu.CompilerParams(
            collective_id=0, has_side_effects=True, vmem_limit_bytes=63 << 20
        ),
        name="both_blocks",
    )(
        *planes, reduce_a, flat_a, expand_a, shortcut_a, reduce_b, flat_b, expand_b,
        edges, mask, gain_mid, shift_mid,
        gain_out.reshape(3, 4, WIDE), shift_out.reshape(3, 4, WIDE), up,
    )
    pooled = jnp.transpose(results[0], (0, 2, 1, 3)).reshape(3, ROWS, -1)[:, :count]
    backs = [from_planes(results[1 + g], images[g].shape) for g in range(3)]
    units, place, shards = results[4], 0, {}
    for name, shape in (
        ("expand_b", expand_b.shape),
        ("spatial_b", second_spatial_weight.shape),
        ("reduce_b", reduce_b.shape),
        ("expand_a", expand_a.shape),
        ("shortcut_a", shortcut_a.shape),
        ("spatial_a", first_spatial_weight.shape),
        ("reduce_a", reduce_a.shape),
    ):
        lead = shape[:-2]
        count_units = shape[-2] * shape[-1] // (WIDE * WIDE)
        for size in lead:
            count_units *= size
        value = units[place : place + count_units]
        place += count_units
        rows = shape[-2] // n_batch
        if lead:
            shards[name] = value.reshape(lead + (rows, WIDE))
        else:
            value = value.reshape(shape[1] // WIDE, rows, WIDE)
            shards[name] = jnp.transpose(value, (1, 0, 2)).reshape(rows, shape[1])
    order = (
        "reduce_a", "spatial_a", "expand_a", "shortcut_a", "reduce_b", "spatial_b", "expand_b"
    )
    mid, out = results[5], results[6].reshape(3, 2, -1)
    return (
        pooled[0], pooled[1], pooled[2], backs[0], backs[1], backs[2], *[shards[name] for name in order],
        mid[:, 1], mid[:, 0], out[:, 1], out[:, 0],
    )


def solution(mesh):
    placed = (
        P("batch", "height", None, None),
        P("batch", "height", None, None),
        P("batch", "height", None, None),
        P(),
        P(),
        P(),
        P(),
        P(),
        P(),
        P(),
        P(),
        P(),
        P(),
        P(),
        P(),
        P("batch", None),
        P("batch", None),
        P("batch", None),
    )
    return jax.shard_map(
        per_device,
        mesh=mesh,
        in_specs=placed,
        out_specs=(
            P("batch", None),
            P("batch", None),
            P("batch", None),
            P("batch", "height", None, None),
            P("batch", "height", None, None),
            P("batch", "height", None, None),
            P("batch", None),
            P(None, None, "batch", None),
            P("batch", None),
            P("batch", None),
            P("batch", None),
            P(None, None, "batch", None),
            P("batch", None),
            P(),
            P(),
            P(),
            P(),
        ),
        check_vma=False,
    )
```

```python
import functools

import jax
import jax.numpy as jnp
from jax import lax
from jax.experimental import pallas as pl
from jax.experimental.pallas import tpu as pltpu
from jax.sharding import PartitionSpec as P

epsilon = 1e-05
MESH = pl.DeviceIdType.MESH

WIDE = 512
ROWS = 16
STEP = 64


def silu_of(half):
    return half + half * jnp.tanh(half)


def slope_of(half):
    t = jnp.tanh(half)
    return (1.0 + t) + half * (1.0 - t * t)


def up32(values):
    return values.astype(jnp.float32)


def low(values):
    return values.astype(jnp.bfloat16)


def times(left, right):
    return jnp.dot(left, right, preferred_element_type=jnp.float32)


def times_t(left, right):
    return lax.dot_general(
        left, right, (((1,), (1,)), ((), ())), preferred_element_type=jnp.float32
    )


def t_times(left, right):
    return lax.dot_general(
        left, right, (((0,), (0,)), ((), ())), preferred_element_type=jnp.float32
    )


def fold(values):
    return jnp.sum(values.reshape(-1, 8, values.shape[-1]), axis=0)


def one_row(values):
    return jnp.sum(values, axis=0, keepdims=True)


def wide_mask(mask):
    return jnp.concatenate([up32(mask)] * (WIDE // 128), axis=1)


def grids(heights, widths):
    counts = [k * (o + 1) for k, o in zip(heights, widths)]
    starts = [sum(counts[:g]) for g in range(3)]
    top_sizes = [(k + 1) * (o + 1) + 1 for k, o in zip(heights, widths)]
    top_starts = [sum(top_sizes[:g]) for g in range(3)]
    both_sizes = [(k + 2) * (o + 1) + 2 for k, o in zip(heights, widths)]
    both_starts = [sum(both_sizes[:g]) for g in range(3)]
    halo_starts = [sum(widths[:g]) for g in range(3)]
    return counts, starts, sum(top_sizes), top_starts, sum(both_sizes), both_starts, halo_starts


def main_kernel(
    n_batch, n_height, heights, widths, images, total_in, total_out,
    x_small, x_medium, x_large, reduce_a, spatial_a, expand_a, shortcut_a, reduce_b, spatial_b, expand_b,
    row_counts, gain_mid, shift_mid, gain_out, shift_out, up_ref,
    pooled, dx_small, dx_medium, dx_large, g_reduce_a, g_spatial_a, g_expand_a,
    g_shortcut_a, g_reduce_b, g_spatial_b, g_expand_b, gain_mid_grad, shift_mid_grad,
    gain_out_grad, shift_out_grad, h1_kept, a1_kept,
    edge_ref, mask_ref, big_b, big_a, h3, side, mb, h2, a2, h4, h5, a5, a4p, dhp, acc, wp, wq, w2,
    halo_up, halo_down, halo_in, keep, away, r0, r1, r2, r3, final, ready, pool_slots,
    thin, wide_h, wide_b, stat_mid, stat_out,
    w_sem, x_sem, u_send, u_recv, ready_sem, dx_sem, spill_sem, ar_send, ar_recv, halo_send, halo_recv, pool_sem,
):
    b, h = lax.axis_index("batch"), lax.axis_index("height")
    counts, starts, top_total, top_starts, both_total, both_starts, halo_starts = grids(
        heights, widths
    )
    total = sum(counts) * ROWS
    half = total // 2
    part = total // 4
    groups = range(3)
    h1, dz, h6 = big_b, big_b, big_a
    halo_a = mb.at[0:2, 0 : sum(widths) * ROWS]

    def rows_at(start, count):
        return pl.ds(pl.multiple_of(start * ROWS, ROWS), count * ROWS)

    def steps(index):
        return pl.ds(pl.multiple_of(index * part, ROWS), part)

    def fetch(source, target, sem):
        pltpu.make_async_copy(source, target, sem).start()

    def arrived(target, sem):
        pltpu.make_async_copy(target, target, sem).wait()

    def columns(k):
        return pl.ds(k * WIDE, WIDE)

    def fetch_columns(weight, target, first, sem):
        for n in range(4):
            fetch(weight.at[:, columns(n)], target.at[first + n], sem)

    def fetch_shortcut():
        for n in range(4):
            for k in range(2):
                fetch(shortcut_a.at[columns(k), columns(n)], wq.at[2 * n + k], w_sem.at[1])

    xs, dxs = (x_small, x_medium, x_large), (dx_small, dx_medium, dx_large)

    def band_row(buffer, g, y):
        return buffer.at[pl.ds(starts[g] + y * (widths[g] + 1), widths[g])]

    def by_position(buffer):
        return buffer.reshape(buffer.shape[0] // ROWS, ROWS, WIDE)

    def fetch_plane(p, k, target, sem):
        for g in groups:
            for y in range(heights[g]):
                fetch(
                    xs[g].at[y, p // 2, :, p % 2, :, columns(k)],
                    band_row(by_position(target), g, y),
                    sem,
                )

    def plane_arrived(target, sem):
        pixels = sum(k * o for k, o in zip(heights, widths)) * ROWS
        arrived(target.at[0:pixels], sem)

    def put_plane(p, k, source):
        for g in groups:
            for y in range(heights[g]):
                fetch(
                    band_row(by_position(source), g, y),
                    dxs[g].at[y, p // 2, :, p % 2, :, columns(k)],
                    dx_sem.at[0],
                )

    for k in range(2):
        for p in range(4):
            for g in groups:
                for y in range(heights[g]):
                    edge_place = (starts[g] + y * (widths[g] + 1) + widths[g]) * ROWS
                    (h3, mb)[k][p, edge_place : edge_place + ROWS] = jnp.zeros(
                        (ROWS, WIDE), jnp.bfloat16
                    )
            fetch_plane(p, k, (h3, mb)[k].at[p], x_sem.at[k])
    for k in range(2):
        fetch(reduce_a.at[columns(k)], w2.at[k], w_sem.at[3])
    fetch_shortcut()
    fetch(spatial_a, wp, w_sem.at[0])

    for g in groups:
        live = row_counts[g, h]
        for y in range(heights[g]):
            row = (starts[g] + y * (widths[g] + 1)) * ROWS
            shape = (widths[g] * ROWS, 128)
            image = lax.rem(lax.broadcasted_iota(jnp.int32, shape, 0), ROWS)
            inside = jnp.where(image < images, 1.0, 0.0)
            alive = jnp.clip(live - y, 0, 1).astype(jnp.float32)
            mask_ref[row : row + shape[0]] = low(inside * alive)
            mask_ref[row + shape[0] : row + shape[0] + ROWS] = jnp.zeros((ROWS, 128), jnp.bfloat16)
            is_last = jnp.maximum(1 - jnp.abs(live - 1 - y), 0).astype(jnp.float32)
            edge_ref[g, y] = jnp.ones((8, 128), jnp.float32) * is_last

    halo_down[...] = jnp.zeros_like(halo_down)
    halo_up[...] = jnp.zeros_like(halo_up)
    halo_in[...] = jnp.zeros_like(halo_in)

    @pl.loop(0, both_total // 2)
    def _(i):
        rows = rows_at(i * 2, 2)
        a4p[rows] = jnp.zeros((2 * ROWS, WIDE), jnp.bfloat16)
        dhp[rows] = jnp.zeros((2 * ROWS, WIDE), jnp.bfloat16)

    for g in groups:
        count = widths[g] + 2
        for p in range(4):
            big_a[p, top_starts[g] * ROWS : (top_starts[g] + count) * ROWS] = jnp.zeros(
                (count * ROWS, WIDE), jnp.bfloat16
            )

    barrier = pltpu.get_barrier_semaphore()

    @pl.loop(1, n_batch * n_height)
    def _(k):
        other = lax.rem(b * n_height + h + k, n_batch * n_height)
        pl.semaphore_signal(
            barrier,
            inc=1,
            device_id=(other // n_height, lax.rem(other, n_height)),
            device_id_type=MESH,
        )

    pl.semaphore_wait(barrier, n_batch * n_height - 1)

    turn = [0]
    direct = thin.shape[1] == n_batch * n_height

    def ar_spread(slots, me, count, peer, sems):
        @pl.loop(1, count)
        def _(k):
            pltpu.make_async_remote_copy(
                src_ref=slots.at[me],
                dst_ref=slots.at[me],
                send_sem=ar_send.at[sems],
                recv_sem=ar_recv.at[sems],
                device_id=peer(lax.rem(me + k, count)),
                device_id_type=MESH,
            ).start()

    def ar_wait(slots, count, sems, which):
        others = slots.at[0 : count - 1]
        pltpu.make_async_copy(others, others, which.at[sems]).wait()

    def sums_start(vectors):
        slot = turn[0] % 2
        turn[0] += 1
        if not direct:
            first, second = thin.at[slot, 0:n_height], thin.at[slot, n_height:]
            put_rows(first, h, vectors)
            ar_spread(first, h, n_height, lambda p: (b, p), (0, 0, slot))
            return first, second, 2, slot
        slots = thin.at[slot]
        me = b * n_height + h
        put_rows(slots, me, vectors)
        ar_spread(
            slots, me, n_batch * n_height, lambda p: (p // n_height, lax.rem(p, n_height)),
            (0, 0, slot),
        )
        return slots, None, 0, slot

    def put_rows(slots, me, vectors):
        for v, vector in enumerate(vectors):
            for j in range(4):
                slots[me, 4 * v + j : 4 * v + j + 1, :] = vector[:, 128 * j : 128 * (j + 1)]

    def wide_start(part):
        count = 16 if part is None else 8
        rows = pl.ds(8 * (part or 0), count)
        first, second = wide_h.at[:, rows], wide_b.at[:, rows]
        first[h] = stat_out[0:count]
        ar_spread(first, h, n_height, lambda p: (b, p), (1, 0, part or 0))
        return first, second, 1, part or 0

    def sums_middle(state):
        first, second, kind, slot = state
        if kind == 0:
            return
        ar_wait(first, n_height, (kind % 2, 0, slot), ar_recv)
        second[b] = jnp.sum(first[...], axis=0)
        ar_spread(second, b, n_batch, lambda p: (p, h), (kind % 2, 1, slot))

    def sums_end(state):
        first, second, kind, slot = state
        if kind == 0:
            ar_wait(first, n_batch * n_height, (0, 0, slot), ar_recv)
            summed = jnp.sum(first[...], axis=0)
            ar_wait(first, n_batch * n_height, (0, 0, slot), ar_send)
        else:
            ar_wait(second, n_batch, (kind % 2, 1, slot), ar_recv)
            summed = jnp.sum(second[...], axis=0)
            ar_wait(first, n_height, (kind % 2, 0, slot), ar_send)
            ar_wait(second, n_batch, (kind % 2, 1, slot), ar_send)
        if kind == 1:
            stat_out[0 : summed.shape[0]] = summed
            return None
        return [
            jnp.concatenate([summed[4 * v + j : 4 * v + j + 1] for j in range(4)], axis=1)
            for v in range(2)
        ]

    def keep_stats(kept, index, sums, number, gain, shift):
        centre = sums[0] * (1.0 / number)
        root = lax.rsqrt(sums[1] * (1.0 / number) - centre * centre + epsilon)
        scale = root * gain
        kept[index, 0:1] = centre
        kept[index, 1:2] = root
        kept[index, 2:3] = scale
        kept[index, 3:4] = shift - centre * scale
        kept[index, 4:5] = -centre * root
        kept[index, 5:6] = 0.5 * scale
        kept[index, 6:7] = 0.5 * (shift - centre * scale)

    def back_factors(kept, index, sums, number, gain):
        centre, root = kept[index, 0:1], kept[index, 1:2]
        main = gain * root
        slope = -main * root * sums[1] * (1.0 / number)
        return main, slope, -main * sums[0] * (1.0 / number) - slope * centre

    def halo_copy(source, target, sem, peer):
        return pltpu.make_async_remote_copy(
            src_ref=source,
            dst_ref=target,
            send_sem=halo_send.at[sem],
            recv_sem=halo_recv.at[sem],
            device_id=(b, peer),
            device_id_type=MESH,
        )

    def halo_rows(g):
        return slice(halo_starts[g] * ROWS, (halo_starts[g] + widths[g]) * ROWS)

    def top_row(padded, start, g):
        return padded.at[pl.ds((start + 1) * ROWS, widths[g] * ROWS)]

    def send_down(buffer, padded, sem):
        @pl.when(h < n_height - 1)
        def _():
            for g in groups:
                halo_copy(
                    buffer.at[halo_rows(g)], top_row(padded, both_starts[g], g), sem, h + 1
                ).start()

    def send_up(buffer, sem):
        @pl.when(h > 0)
        def _():
            halo_copy(buffer, halo_in, sem, h - 1).start()

    def halo_wait(buffer, sems, sem, condition):
        @pl.when(condition)
        def _():
            arrived(buffer, sems.at[sem])

    def place_below(padded):
        for g in groups:
            stride = widths[g] + 1
            for y in range(1, heights[g] + 1):
                is_edge = edge(g, y - 1)

                @pl.loop(0, widths[g])
                def _(col):
                    rows = rows_at(both_starts[g] + 1 + (y + 1) * stride + col, 1)
                    value = up32(halo_in[rows_at(halo_starts[g] + col, 1)]) * is_edge
                    if y < heights[g]:
                        value = value + up32(padded[rows])
                    padded[rows] = low(value)

    def edge(g, y):
        return wide_mask(edge_ref[g, y, 0:1])

    def first_row(source, g, row=0):
        start = (starts[g] + row * (widths[g] + 1)) * ROWS
        return up32(source[start : start + widths[g] * ROWS])

    def last_row(source, g):
        value = first_row(source, g) * edge(g, 0)
        for y in range(1, heights[g]):
            value = value + first_row(source, g, y) * edge(g, y)
        return value

    core, high = lax.rem(h, 2), h // 2
    low_bit, rest = lax.rem(b, 2), b // 2
    n_rest = n_batch // 2
    unit_rows = WIDE // n_batch

    def either(is_one, one, zero):
        return is_one * one + (1 - is_one) * zero

    first, second = either(core, low_bit, high), either(core, high, low_bit)
    core_peer = (b, h + 1 - 2 * core)
    high_peer = (b, h + 2 - 4 * high)
    low_peer = (b + 1 - 2 * low_bit, h)
    first_peer = [either(core, low_peer[i], high_peer[i]) for i in range(2)]
    second_peer = [either(core, high_peer[i], low_peer[i]) for i in range(2)]

    def ring(buffer, unit):
        return lax.rem(unit, buffer.shape[0])

    def unit_copy(level, unit, source, target, peer):
        return pltpu.make_async_remote_copy(
            src_ref=source,
            dst_ref=target,
            send_sem=u_send.at[level, lax.rem(unit, 16)],
            recv_sem=u_recv.at[level, lax.rem(unit, 16)],
            device_id=tuple(peer),
            device_id_type=MESH,
        )

    def hop(level, unit):
        kept = keep.at[ring(keep, unit)]
        if level == 0:
            return unit_copy(
                0, unit, away.at[ring(away, unit)], r0.at[ring(r0, unit)], core_peer
            )
        if level == 1:
            return unit_copy(1, unit, kept.at[1 - first], r1.at[ring(r1, unit)], first_peer)
        if level == 2:
            return unit_copy(
                2, unit, kept.at[first, 1 - second], r2.at[ring(r2, unit)], second_peer
            )
        if level == 4:
            mine = final.at[ring(final, unit), core, high]
            return unit_copy(4, unit, mine, mine, high_peer)
        both = final.at[ring(final, unit), core]
        return unit_copy(5, unit, both, both, core_peer)

    def add_to(target, source):
        target[...] = low(up32(target[...]) + up32(source[...]))

    def rest_wait(unit, sems):
        others = r3.at[ring(r3, unit)]
        pltpu.make_async_copy(others, others, sems.at[3, lax.rem(unit, 16)]).wait()

    def round_0(unit, view):
        hop(0, unit).start()

    def round_1(unit, view):
        hop(0, unit).wait()
        kept, got = keep.at[ring(keep, unit)], r0.at[ring(r0, unit)]

        @pl.loop(0, n_rest)
        def _(k):
            for i in range(2):
                for j in range(2):
                    add_to(kept.at[i, j, k], got.at[i, j, k])

        hop(1, unit).start()

    def round_2(unit, view):
        hop(1, unit).wait_recv()
        kept, got = keep.at[ring(keep, unit), first], r1.at[ring(r1, unit)]

        @pl.loop(0, n_rest)
        def _(k):
            for j in range(2):
                add_to(kept.at[j, k], got.at[j, k])

        hop(2, unit).start()

    def round_3(unit, view):
        hop(2, unit).wait_recv()
        kept, got = keep.at[ring(keep, unit), first, second], r2.at[ring(r2, unit)]

        @pl.loop(0, n_rest)
        def _(k):
            add_to(kept.at[k], got.at[k])

        @pl.loop(1, n_rest)
        def _(k):
            unit_copy(
                3,
                unit,
                kept.at[lax.rem(rest + k, n_rest)],
                r3.at[ring(r3, unit), n_rest - 1 - k],
                (lax.rem(rest + k, n_rest) * 2 + low_bit, h),
            ).start()

    def round_4(unit, view):
        rest_wait(unit, u_recv)
        value = up32(keep[ring(keep, unit), first, second, rest])
        for k in range(n_rest - 1):
            value = value + up32(r3[ring(r3, unit), k])
        final[ring(final, unit), core, high] = low(value)
        hop(4, unit).start()

    def round_5(unit, view):
        hop(4, unit).wait_recv()
        hop(5, unit).start()
        for level in (1, 2):
            hop(level, unit).wait_send()
        rest_wait(unit, u_send)

    def round_6(unit, view):
        hop(5, unit).wait_recv()
        for level in (4, 5):
            hop(level, unit).wait_send()
        slot = ring(ready, unit)

        @pl.when(unit >= ready.shape[0])
        def _():
            arrived(ready.at[slot], ready_sem.at[slot])

        for c in range(2):
            for i in range(2):
                lane = 128 * (2 * c + i)
                ready[slot, :, lane : lane + 128] = up32(final[ring(final, unit), c, i])
        fetch(ready.at[slot], view(unit), ready_sem.at[slot])

    rounds = (
        (0, round_0), (2, round_1), (4, round_2), (6, round_3), (8, round_4), (10, round_5),
        (12, round_6),
    )
    clock, made, produced = [0], [0], []

    def advance(index, base, count):
        for lag, act in rounds:
            for start, size, unit, view in produced:
                from_, to = max(base - lag, start), min(base - lag + count, start + size)
                if from_ >= to:
                    continue
                target = base - lag - start + unit + index
                if to - from_ == count:
                    act(target, view)
                else:
                    shift = base - lag
                    inside = jnp.logical_and(index >= from_ - shift, index < to - shift)
                    pl.when(inside)(functools.partial(act, target, view))

    def idle(count):
        base = clock[0]
        clock[0] += count

        @pl.loop(0, count)
        def _(i):
            advance(i, base, count)

    def ticks(count):
        base = clock[0]
        clock[0] += count
        return lambda i: advance(i, base, count)

    def put(value, unit, units, first_shard):
        shard_rows = units * unit_rows
        own_side = core == 0
        left, right = low(value[:, : WIDE // 2]), low(value[:, WIDE // 2 :])
        own, other = jnp.where(own_side, left, right), jnp.where(own_side, right, left)
        for s in range(WIDE // shard_rows):
            shard = first_shard + s
            shard_low, shard_rest = s % 2, shard // 2
            for q in range(units):
                rows = slice(s * shard_rows + q * unit_rows, s * shard_rows + (q + 1) * unit_rows)
                for i in range(2):
                    lanes = slice(128 * i, 128 * (i + 1))
                    keep[
                        ring(keep, unit + q),
                        either(core, shard_low, i),
                        either(core, i, shard_low),
                        shard_rest,
                    ] = own[rows, lanes]
                    away[
                        ring(away, unit + q),
                        either(core, i, shard_low),
                        either(core, shard_low, i),
                        shard_rest,
                    ] = other[rows, lanes]

    views = {
        "expand_b": lambda j: g_expand_b.at[:, lanes_at(j)],
        "spatial_b": lambda j: g_spatial_b.at[j],
        "reduce_b": lambda j: g_reduce_b.at[unit_rows_at(j)],
        "expand_a": lambda j: g_expand_a.at[:, lanes_at(j)],
        "shortcut_a": lambda j: g_shortcut_a.at[unit_rows_at(lax.rem(j, 2)), lanes_at(j // 2)],
        "spatial_a": lambda j: g_spatial_a.at[j],
        "reduce_a": lambda j: g_reduce_a.at[unit_rows_at(j)],
    }
    first_units = {}

    def lanes_at(j):
        return pl.ds(pl.multiple_of(j * WIDE, WIDE), WIDE)

    def unit_rows_at(j):
        return pl.ds(pl.multiple_of(j * unit_rows, unit_rows), unit_rows)

    def view_of(name):
        base = first_units.setdefault(name, made[0])
        return lambda unit: views[name](unit - base)

    def run(name, count, body, make):
        base, unit, view = clock[0], made[0], view_of(name)
        clock[0] += count
        made[0] += count
        produced.append((base, count, unit, view))

        @pl.loop(0, count)
        def _(i):
            body(i)
            make(i, unit + i)
            advance(i, base, count)

    def produce(name, count, units, make):
        base, unit, view = clock[0], made[0], view_of(name)
        produced.append((base, count * units, unit, view))
        clock[0] += count * units
        made[0] += count * units

        @pl.loop(0, count)
        def _(t):
            make(t, unit + t * units)
            if units == 1:
                advance(t, base, count)
            else:

                @pl.loop(0, units)
                def _(q):
                    advance(t * units + q, base, count * units)

    zero8 = jnp.zeros((8, WIDE), jnp.float32)

    def half_mask(rows):
        return wide_mask(0.5 * up32(mask_ref[rows]))


    arrived(w2, w_sem.at[3])
    for k in range(2):
        for p in range(4):
            plane_arrived((h3, mb)[k].at[p], x_sem.at[k])

    def first_reduction(i, carry):
        p = i // 2
        rows = pl.ds(pl.multiple_of(lax.rem(i, 2) * half, ROWS), half)
        value = times(h3[p, rows], w2[0]) + times(mb[p, rows], w2[1])
        value = value * wide_mask(mask_ref[rows])
        h1[p, rows] = low(value)
        return carry[0] + fold(value), carry[1] + fold(value * value)

    sums = lax.fori_loop(0, 8, first_reduction, (zero8, zero8))
    state = sums_start([one_row(v) for v in sums])

    arrived(wq, w_sem.at[1])

    def shortcut_product(n, carry):
        value = times(h3[0], wq[2 * n]) + times(mb[0], wq[2 * n + 1])
        value = value * wide_mask(mask_ref[...])
        side[n] = low(value)
        stat_out[pl.ds(8 + n, 1)] = one_row(fold(value))
        stat_out[pl.ds(12 + n, 1)] = one_row(fold(value * value))
        return carry

    lax.fori_loop(0, 2, shortcut_product, 0)
    sums_middle(state)
    lax.fori_loop(2, 4, shortcut_product, 0)
    fetch_columns(expand_a, wq, 0, w_sem.at[1])
    for k in range(4):
        fetch(reduce_b.at[columns(k)], wq.at[4 + k], w_sem.at[2])
    sums = sums_end(state)
    keep_stats(stat_mid, 0, sums, total_in, gain_mid[0:1], shift_mid[0:1])

    scale, offset = stat_mid[0, 5:6], stat_mid[0, 6:7]
    for column in range(2):
        for g in groups:
            pre = last_row(h1.at[2 + column], g) * scale + offset
            mask = wide_mask(mask_ref[starts[g] * ROWS : (starts[g] + widths[g]) * ROWS])
            halo_a[column, halo_rows(g)] = low(silu_of(pre) * mask)

    @pl.when(h < n_height - 1)
    def _():
        for column in range(2):
            for g in groups:
                halo_copy(
                    halo_a.at[column, halo_rows(g)],
                    top_row(big_a.at[2 + column], top_starts[g], g),
                    0,
                    h + 1,
                ).start()

    for g in groups:
        per = counts[g] * ROWS // STEP
        base = (top_starts[g] + 1 + widths[g] + 1) * ROWS

        @pl.loop(0, 4)
        def _(p):
            @pl.loop(0, per)
            def _(i):
                rows = pl.ds(pl.multiple_of(starts[g] * ROWS + i * STEP, ROWS), STEP)
                pre = up32(h1[p, rows]) * scale + offset
                value = silu_of(pre) * wide_mask(mask_ref[rows])
                big_a[p, pl.ds(pl.multiple_of(base + i * STEP, ROWS), STEP)] = low(value)

    fetch(h1, h1_kept, spill_sem.at[0])

    def group_rows(g):
        return slice(starts[g] * ROWS, (starts[g] + counts[g]) * ROWS)

    def window(padded, start, g, dy, dx_):
        first = start + 1 + (1 + dy) * (widths[g] + 1) + dx_
        return padded[rows_at(first, counts[g])]

    def window_a(g, a, c):
        py, dy = lax.rem(a + 1, 2), (a + 1) // 2 - 1
        px, dx_ = lax.rem(c + 1, 2), (c + 1) // 2 - 1
        first = top_starts[g] + 1 + (1 + dy) * (widths[g] + 1) + dx_
        return big_a[2 * py + px, rows_at(first, counts[g])]

    def clear_acc():
        @pl.loop(0, total // part)
        def _(i):
            acc[steps(i)] = jnp.zeros((part, WIDE), jnp.float32)

    def conv_taps(start, last, window_of, product, make=None):
        def tap(t):
            for g in groups:
                acc[group_rows(g)] += product(window_of(g, t // 3, lax.rem(t, 3)), wp[t])

        if make is not None:
            run("spatial_b", last - start, lambda i: tap(start + i), make)
            return
        tick = ticks(last - start) if produced else None

        @pl.loop(start, last)
        def _(t):
            tap(t)
            if tick is not None:
                tick(t - start)

    def masked_sums(target):
        def body(i, carry):
            rows = steps(i)
            value = acc[rows] * wide_mask(mask_ref[rows])
            target[rows] = low(value)
            return carry[0] + fold(value), carry[1] + fold(value * value)

        return lax.fori_loop(0, total // part, body, (zero8, zero8))

    clear_acc()
    arrived(wp, w_sem.at[0])
    conv_taps(3, 9, window_a, times)
    halo_wait(halo_a, halo_recv, 0, h > 0)
    conv_taps(0, 3, window_a, times)
    sums = masked_sums(h2)
    state = sums_start([one_row(v) for v in sums])
    fetch(spatial_b, wp, w_sem.at[0])
    fetch(big_a, a1_kept, spill_sem.at[1])
    halo_wait(halo_a, halo_send, 0, h < n_height - 1)
    sums_middle(state)
    sums = sums_end(state)
    keep_stats(stat_mid, 1, sums, total_out, gain_mid[1:2], shift_mid[1:2])

    def activate(source, target, index):
        scale, offset = stat_mid[index, 5:6], stat_mid[index, 6:7]

        @pl.loop(0, total // part)
        def _(i):
            rows = steps(i)
            pre = up32(source[rows]) * scale + offset
            target[rows] = low(silu_of(pre) * wide_mask(mask_ref[rows]))

    activate(h2, a2, 1)
    arrived(wq.at[0:4], w_sem.at[1])

    def expansion(source, target):
        @pl.loop(0, 4)
        def _(n):
            value = times(source[...], wq[n])
            target[n, 0:total] = low(value)
            stat_out[pl.ds(n, 1)] = one_row(fold(value))
            stat_out[pl.ds(4 + n, 1)] = one_row(fold(value * value))

    expansion(a2, h3)
    state = wide_start(None)
    fetch_columns(expand_b, wq, 0, w_sem.at[1])
    sums_middle(state)
    sums_end(state)

    def out_stats(index, n, row):
        keep_stats(
            mid_or_out,
            4 * index + n,
            [stat_out[row + n : row + n + 1], stat_out[row + 4 + n : row + 5 + n]],
            total_out,
            gain_out[index : index + 1, n * WIDE : (n + 1) * WIDE],
            shift_out[index : index + 1, n * WIDE : (n + 1) * WIDE],
        )

    mid_or_out = stat_mid.at[4:16]
    for n in range(4):
        out_stats(0, n, 0)
        out_stats(1, n, 8)

    def out_stat(index, n, row):
        return stat_mid[4 + 4 * index + n, row : row + 1]

    def half_joint(n, rows):
        return (
            up32(h3[n, rows]) * out_stat(0, n, 5)
            + up32(side[n, rows]) * out_stat(1, n, 5)
            + (out_stat(0, n, 6) + out_stat(1, n, 6))
        )

    arrived(wq.at[4:8], w_sem.at[2])
    clear_acc()

    @pl.loop(0, 4)
    def _(n):
        @pl.loop(0, 2)
        def _(i):
            rows = pl.ds(pl.multiple_of(i * half, ROWS), half)
            value = low(silu_of(half_joint(n, rows)) * wide_mask(mask_ref[rows]))
            mb[n, rows] = value
            acc[rows] += times(value, wq[4 + n])

    def plain_sums(target):
        def body(i, carry):
            rows = steps(i)
            value = acc[rows]
            target[rows] = low(value)
            return carry[0] + fold(value), carry[1] + fold(value * value)

        return lax.fori_loop(0, total // part, body, (zero8, zero8))

    sums = plain_sums(h4)
    state = sums_start([one_row(v) for v in sums])
    sums_middle(state)
    clear_acc()
    sums = sums_end(state)
    keep_stats(stat_mid, 2, sums, total_out, gain_mid[2:3], shift_mid[2:3])

    scale, offset = stat_mid[2, 5:6], stat_mid[2, 6:7]
    for g in groups:
        pre = last_row(h4, g) * scale + offset
        mask = wide_mask(mask_ref[starts[g] * ROWS : (starts[g] + widths[g]) * ROWS])
        halo_down[halo_rows(g)] = low(silu_of(pre) * mask)
    send_down(halo_down, a4p, 1)
    for g in groups:
        pre = first_row(h4, g) * scale + offset
        mask = wide_mask(mask_ref[starts[g] * ROWS : (starts[g] + widths[g]) * ROWS])
        halo_up[halo_rows(g)] = low(silu_of(pre) * mask)
    send_up(halo_up, 2)

    def both_base(g):
        return (both_starts[g] + 1 + widths[g] + 1) * ROWS

    for g in groups:

        @pl.loop(0, counts[g] * ROWS // STEP)
        def _(i):
            rows = pl.ds(pl.multiple_of(starts[g] * ROWS + i * STEP, ROWS), STEP)
            pre = up32(h4[rows]) * scale + offset
            value = low(silu_of(pre) * wide_mask(mask_ref[rows]))
            a4p[pl.ds(pl.multiple_of(both_base(g) + i * STEP, ROWS), STEP)] = value

    def window_b(g, a, c):
        return window(a4p, both_starts[g], g, a - 1, c - 1)

    def window_b_back(g, a, c):
        return window(dhp, both_starts[g], g, 1 - a, 1 - c)

    arrived(wp, w_sem.at[0])
    conv_taps(3, 6, window_b, times)
    halo_wait(halo_down, halo_recv, 1, h > 0)
    halo_wait(halo_in, halo_recv, 2, h < n_height - 1)
    place_below(a4p)
    conv_taps(0, 3, window_b, times)
    conv_taps(6, 9, window_b, times)
    sums = masked_sums(h5)
    state = sums_start([one_row(v) for v in sums])
    halo_wait(halo_down, halo_send, 1, h < n_height - 1)
    halo_wait(halo_up, halo_send, 2, h > 0)
    sums_middle(state)
    sums = sums_end(state)
    keep_stats(stat_mid, 3, sums, total_out, gain_mid[3:4], shift_mid[3:4])

    activate(h5, a5, 3)
    arrived(wq.at[0:4], w_sem.at[1])
    arrived(big_a, spill_sem.at[1])
    expansion(a5, h6)
    state = wide_start(0)
    sums_middle(state)
    arrived(h1, spill_sem.at[0])
    sums_end(state)
    for n in range(4):
        out_stats(2, n, 0)

    @pl.loop(0, 4)
    def _(n):
        index = 12 + n
        root, scale = stat_mid[index, 1:2], stat_mid[index, 2:3]
        offset, back = stat_mid[index, 3:4], stat_mid[index, 4:5]
        zero = jnp.zeros((ROWS, WIDE), jnp.float32)
        total_grad, total_dot = zero8, zero8
        for g in groups:
            share = 1.0 / (widths[g] * widths[g])

            up = jnp.concatenate([up32(up_ref[g, n]) * (0.5 * share)] * (STEP // ROWS), axis=0)

            def body(i, carry):
                rows = pl.ds(pl.multiple_of(starts[g] * ROWS + i * STEP, ROWS), STEP)
                value = up32(h6[n, rows])
                mask = wide_mask(mask_ref[rows])
                z = value * scale + offset + up32(mb[n, rows])
                z = 0.5 * z
                t = jnp.tanh(z)
                last = z + z * t
                grad = up * ((1.0 + t) + (z - z * t * t)) * mask
                dz[n, rows] = low(grad)
                last = (last * mask).reshape(STEP // ROWS, ROWS, WIDE)
                return (
                    carry[0] + jnp.sum(last, axis=0),
                    carry[1] + fold(grad),
                    carry[2] + fold(grad * (value * root + back)),
                )

            pool, total_grad, total_dot = lax.fori_loop(
                0, counts[g] * ROWS // STEP, body, (zero, total_grad, total_dot)
            )
            pool_slots[h, n, g * ROWS : (g + 1) * ROWS] = low(pool)
        stat_out[pl.ds(n, 1)] = one_row(total_grad)
        stat_out[pl.ds(4 + n, 1)] = one_row(total_dot)

    state = wide_start(1)

    for k in range(1, n_height):
        pltpu.make_async_remote_copy(
            src_ref=pool_slots.at[h],
            dst_ref=pool_slots.at[h],
            send_sem=pool_sem.at[0],
            recv_sem=pool_sem.at[1],
            device_id=(b, lax.rem(h + k, n_height)),
            device_id_type=MESH,
        ).start()
    sums_middle(state)
    clear_acc()
    sums_end(state)

    def out_back(index, sum_row, dot_row, n):
        sums = [stat_out[pl.ds(sum_row + n, 1)], stat_out[pl.ds(dot_row + n, 1)]]
        shift_out_grad[index : index + 1, lanes_at(n)] = sums[0]
        gain_out_grad[index : index + 1, lanes_at(n)] = sums[1]
        return back_factors(
            stat_mid, 4 + 4 * index + n, sums, total_out, gain_out[index : index + 1, lanes_at(n)]
        )

    def mid_back(index, place, sums, number):
        shift_mid_grad[place : place + 1] = sums[0]
        gain_mid_grad[place : place + 1] = sums[1]
        return back_factors(stat_mid, index, sums, number, gain_mid[place : place + 1])

    def mid_gradient(source, index):
        root, scale = stat_mid[index, 1:2], stat_mid[index, 5:6]
        offset, back = stat_mid[index, 6:7], stat_mid[index, 4:5]

        def body(i, carry):
            rows = steps(i)
            value = up32(source[rows])
            slope = slope_of(value * scale + offset)
            grad = acc[rows] * slope * half_mask(rows)
            acc[rows] = grad
            return carry[0] + fold(grad), carry[1] + fold(grad * (value * root + back))

        sums = lax.fori_loop(0, total // part, body, (zero8, zero8))
        return [one_row(v) for v in sums]

    @pl.loop(0, 4)
    def _(n):
        main, slope, constant = out_back(2, 0, 4, n)

        @pl.loop(0, 2)
        def _(i):
            rows = pl.ds(pl.multiple_of(i * half, ROWS), half)
            grad = main * up32(dz[n, rows]) + slope * up32(h6[n, rows]) + constant
            grad = low(grad * wide_mask(mask_ref[rows]))
            h6[n, rows] = grad
            acc[rows] += times_t(grad, wq[n])

    sums = mid_gradient(h5, 3)
    state = sums_start(sums)
    fetch_columns(expand_a, wq, 0, w_sem.at[1])
    sums_middle(state)
    produce("expand_b", 4, 1, lambda t, unit: put(t_times(a5[...], h6[t, 0:total]), unit, 1, 0))
    fetch(a1_kept, big_a, spill_sem.at[1])
    sums = sums_end(state)

    def mid_step(target, factors, padded):
        main, slope, constant = factors

        def tile(rows):
            grad = main * acc[rows] + slope * up32(target[rows]) + constant
            return low(grad * wide_mask(mask_ref[rows]))

        for g in groups:

            @pl.loop(0, counts[g] * ROWS // STEP)
            def _(i):
                rows = pl.ds(pl.multiple_of(starts[g] * ROWS + i * STEP, ROWS), STEP)
                grad = tile(rows)
                target[rows] = grad
                if padded is not None:
                    padded[pl.ds(pl.multiple_of(both_base(g) + i * STEP, ROWS), STEP)] = grad

    mid_step(h5, mid_back(3, 3, sums, total_out), dhp)
    for g in groups:
        halo_down[halo_rows(g)] = low(last_row(h5, g))
        halo_up[halo_rows(g)] = low(first_row(h5, g))
    send_down(halo_down, dhp, 1)
    send_up(halo_up, 2)
    def spatial_tile(window_of, grads):
        def value_of(t):
            parts = [
                t_times(window_of(g, t // 3, lax.rem(t, 3)), grads[group_rows(g)]) for g in groups
            ]
            return parts[0] + parts[1] + parts[2]

        return value_of

    def spatial_maker(window_of, grads):
        tile = spatial_tile(window_of, grads)
        return lambda done: lambda i, unit: put(tile(done + i), unit, 1, 0)

    make_b = spatial_maker(window_b, h5)
    clear_acc()
    conv_taps(3, 6, window_b_back, times_t, make_b(0))
    halo_wait(halo_down, halo_recv, 1, h > 0)
    halo_wait(halo_in, halo_recv, 2, h < n_height - 1)
    place_below(dhp)
    conv_taps(0, 3, window_b_back, times_t, make_b(3))
    conv_taps(6, 9, window_b_back, times_t)
    fetch(spatial_a, wp, w_sem.at[0])
    sums = mid_gradient(h4, 2)
    state = sums_start(sums)
    halo_wait(halo_down, halo_send, 1, h < n_height - 1)
    halo_wait(halo_up, halo_send, 2, h > 0)
    sums_middle(state)

    produce("spatial_b", 3, 1, make_b(6))
    sums = sums_end(state)

    mid_step(h4, mid_back(2, 2, sums, total_out), None)
    fetch_plane(0, 1, a4p, x_sem.at[1])

    tick = ticks(8)

    @pl.loop(0, 4)
    def _(n):
        def body(i, carry):
            tick(2 * n + i)
            rows = pl.ds(pl.multiple_of(i * half, ROWS), half)
            grad = times_t(h4[rows], wq[4 + n]) + up32(dz[n, rows])
            grad = grad * slope_of(half_joint(n, rows)) * half_mask(rows)
            dz[n, rows] = low(grad)
            main_hat = up32(h3[n, rows]) * out_stat(0, n, 1) + out_stat(0, n, 4)
            side_hat = up32(side[n, rows]) * out_stat(1, n, 1) + out_stat(1, n, 4)
            return (
                carry[0] + fold(grad),
                carry[1] + fold(grad * main_hat),
                carry[2] + fold(grad * side_hat),
            )

        sums = lax.fori_loop(0, 2, body, (zero8, zero8, zero8))
        for v in range(3):
            stat_out[pl.ds(4 * v + n, 1)] = one_row(sums[v])

    state = wide_start(None)
    sums_middle(state)

    def tile_reduce_b(step, unit):
        @pl.loop(0, 4)
        def _(t):
            put(t_times(mb[t], h4[...]), unit, 4, t * (n_batch // 4))

    produce("reduce_b", 1, 4, tile_reduce_b)
    for p in range(4):
        fetch_plane(p, 0, mb.at[p], x_sem.at[0])
    clear_acc()
    sums_end(state)

    arrived(wq.at[0:4], w_sem.at[1])

    def expansion_back(n):
        main, slope, constant = out_back(0, 0, 4, n)
        main2, slope2, constant2 = out_back(1, 0, 8, n)

        @pl.loop(0, 2)
        def _(i):
            rows = pl.ds(pl.multiple_of(i * half, ROWS), half)
            grad_in = up32(dz[n, rows])
            mask = wide_mask(mask_ref[rows])
            grad = low((main * grad_in + slope * up32(h3[n, rows]) + constant) * mask)
            h3[n, rows] = grad
            acc[rows] += times_t(grad, wq[n])
            other = main2 * grad_in + slope2 * up32(side[n, rows]) + constant2
            side[n, rows] = low(other * mask)

    run("expand_a", 4, expansion_back, lambda n, unit: put(t_times(a2[...], h3[n]), unit, 1, 0))
    fetch(h1_kept, h1, spill_sem.at[0])
    fetch_shortcut()
    sums = mid_gradient(h2, 1)
    state = sums_start(sums)
    sums_middle(state)
    for p in range(4):
        plane_arrived(mb.at[p], x_sem.at[0])
    plane_arrived(a4p, x_sem.at[1])

    def tile_shortcut(t, unit):
        put(t_times(mb[0], side[t]), unit, 2, 0)
        put(t_times(a4p[0:total], side[t]), unit, 2, n_batch // 2)

    produce("shortcut_a", 1, 2, lambda step, unit: tile_shortcut(0, unit))
    sums = sums_end(state)

    mid_step(h2, mid_back(1, 1, sums, total_out), dhp)
    for g in groups:
        halo_up[halo_rows(g)] = low(first_row(h2, g))
    send_up(halo_up, 2)
    arrived(wp, w_sem.at[0])
    arrived(h1, spill_sem.at[0])
    root, scale = stat_mid[0, 1:2], stat_mid[0, 5:6]
    offset, back = stat_mid[0, 6:7], stat_mid[0, 4:5]
    carry = (zero8, zero8)
    for p in range(4):
        py, px = p // 2, p % 2
        row_taps = ((1, 0),) if py == 0 else ((0, 1), (2, 0))
        column_taps = ((1, 0),) if px == 0 else ((0, 1), (2, 0))
        if p == 2:
            halo_wait(halo_in, halo_recv, 2, h < n_height - 1)
            place_below(dhp)
        for g in groups:
            value = None
            for a, dy in row_taps:
                for c, dx_ in column_taps:
                    product = times_t(window(dhp, both_starts[g], g, dy, dx_), wp[3 * a + c])
                    value = product if value is None else value + product
            acc[group_rows(g)] = value

        def body(i, carry):
            rows = steps(i)
            value = up32(h1[p, rows])
            grad = acc[rows] * slope_of(value * scale + offset) * half_mask(rows)
            h3[p, rows] = low(grad)
            return carry[0] + fold(grad), carry[1] + fold(grad * (value * root + back))

        carry = lax.fori_loop(0, total // part, body, carry)
        if p > 0:
            produce("shortcut_a", 1, 2, lambda step, unit: tile_shortcut(p, unit))
    state = sums_start([one_row(v) for v in carry])
    halo_wait(halo_up, halo_send, 2, h > 0)
    sums_middle(state)
    arrived(big_a, spill_sem.at[1])
    make_a = spatial_maker(window_a, h2)
    produce("spatial_a", 3, 1, make_a(0))
    sums = sums_end(state)

    main, slope, constant = mid_back(0, 0, sums, total_in)

    def first_back(p):
        @pl.loop(0, total // part)
        def _(i):
            rows = steps(i)
            grad = main * up32(h3[p, rows]) + slope * up32(h1[p, rows]) + constant
            h1[p, rows] = low(grad * wide_mask(mask_ref[rows]))

        fetch_plane(p, 1, h3.at[p], x_sem.at[1])

    run("spatial_a", 4, first_back, make_a(3))
    produce("spatial_a", 2, 1, make_a(7))
    for p in range(4):
        plane_arrived(h3.at[p], x_sem.at[1])

    def last_tile(chunk):
        value = t_times(chunk(0), h1[0])
        for p in range(1, 4):
            value = value + t_times(chunk(p), h1[p])
        return value

    def tile_reduce_a(step, unit):
        put(last_tile(lambda p: mb[p]), unit, 2, 0)
        put(last_tile(lambda p: h3[p]), unit, 2, n_batch // 2)

    produce("reduce_a", 1, 2, tile_reduce_a)
    arrived(wq, w_sem.at[1])
    for k in range(2):
        tick_13 = ticks(2)

        @pl.loop(0, 2)
        def _(i):
            rows = pl.ds(pl.multiple_of(i * half, ROWS), half)
            value = times_t(h1[0, rows], w2[k])
            for n in range(4):
                value = value + times_t(side[n, rows], wq[2 * n + k])
            if k == 0:
                big_a[0, rows] = low(value)
            else:
                a4p[rows] = low(value)
            tick_13(i)

    put_plane(0, 0, big_a.at[0])
    put_plane(0, 1, a4p)
    tick_13p = ticks(3)

    @pl.loop(1, 4)
    def _(p):
        big_a[p, 0:total] = low(times_t(h1[p], w2[0]))
        side[p] = low(times_t(h1[p], w2[1]))
        put_plane(p, 0, big_a.at[p])
        put_plane(p, 1, side.at[p])
        tick_13p(p - 1)

    idle(rounds[-1][0] - 6)
    others = pool_slots.at[0 : n_height - 1]
    pltpu.make_async_copy(others, others, pool_sem.at[1]).wait()
    pltpu.make_async_copy(others, others, pool_sem.at[0]).wait()
    for g in groups:
        for n in range(4):
            value = None
            for k in range(n_height):
                part = up32(pool_slots[k, n, g * ROWS : (g + 1) * ROWS])
                value = part if value is None else value + part
            pooled[g, n] = value * (1.0 / (widths[g] * widths[g]))

    for slot in range(ready.shape[0]):
        arrived(ready.at[slot], ready_sem.at[slot])
    for p in range(8):
        plane_arrived(a4p, dx_sem.at[0])


def to_planes(image):
    count, rows, cols, channels = image.shape
    value = jnp.pad(image, ((0, ROWS - count), (0, 0), (0, 0), (0, 0)))
    value = jnp.transpose(value, (1, 2, 0, 3))
    return value.reshape(rows // 2, 2, cols // 2, 2, ROWS, channels)


def from_planes(planes, shape):
    count, rows, cols, channels = shape
    value = planes.reshape(rows, cols, ROWS, channels)[:, :, :count]
    return jnp.transpose(value, (2, 0, 1, 3))


def per_device(
    image_small, image_medium, image_large, row_counts, reduce_a, first_spatial_weight, expand_a,
    shortcut_a, reduce_b, second_spatial_weight, expand_b, gain_mid, shift_mid, gain_out,
    shift_out, upstream_small, upstream_medium, upstream_large,
):
    images = (image_small, image_medium, image_large)
    upstreams = (upstream_small, upstream_medium, upstream_large)
    n_batch, n_height = lax.axis_size("batch"), lax.axis_size("height")
    heights = [value.shape[1] // 2 for value in images]
    widths = [value.shape[2] // 2 for value in images]
    count = images[0].shape[0]
    pixels = sum(o * o for o in widths) * count * n_batch
    counts, starts, top_total, _, both_total, _, _ = grids(heights, widths)
    total = sum(counts) * ROWS
    planes = [to_planes(image) for image in images]
    up = jnp.pad(jnp.stack(upstreams), ((0, 0), (0, ROWS - count), (0, 0)))
    up = jnp.transpose(up.reshape(3, ROWS, 4, WIDE), (0, 2, 1, 3))
    halo = sum(widths) * ROWS
    bf, f32 = jnp.bfloat16, jnp.float32
    unit_rows, n_rest = WIDE // n_batch, n_batch // 2
    n_thin = n_batch * n_height if n_batch * n_height <= 64 else n_batch + n_height
    dma = pltpu.SemaphoreType.DMA
    vmem = pl.BlockSpec(memory_space=pltpu.VMEM)
    anywhere = pl.BlockSpec(memory_space=pl.ANY)
    flat_a = first_spatial_weight.reshape(9, WIDE, WIDE)
    flat_b = second_spatial_weight.reshape(9, WIDE, WIDE)
    big = pltpu.VMEM((4, total, WIDE), bf)
    thin = pltpu.VMEM((total, WIDE), bf)
    results = pl.pallas_call(
        functools.partial(
            main_kernel, n_batch, n_height, heights, widths, count, float(4 * pixels),
            float(pixels)
        ),
        out_shape=[
            jax.ShapeDtypeStruct((3, 4, ROWS, WIDE), f32),
            *[jax.ShapeDtypeStruct(value.shape, bf) for value in planes],
            *[
                jax.ShapeDtypeStruct(w.shape[:-2] + (w.shape[-2] // n_batch, w.shape[-1]), f32)
                for w in (reduce_a, flat_a, expand_a, shortcut_a, reduce_b, flat_b, expand_b)
            ],
            *[jax.ShapeDtypeStruct(w.shape, f32) for w in (gain_mid, shift_mid, gain_out, shift_out)],
            jax.ShapeDtypeStruct((4, total, WIDE), bf),
            jax.ShapeDtypeStruct((4, top_total * ROWS, WIDE), bf),
        ],
        in_specs=[anywhere] * 10 + [pl.BlockSpec(memory_space=pltpu.SMEM)] + [vmem] * 5,
        out_specs=[vmem] + [anywhere] * 10 + [vmem] * 4 + [anywhere] * 2,
        scratch_shapes=[
            pltpu.VMEM((3, max(heights), 8, 128), f32),
            pltpu.VMEM((total, 128), bf),
            big,
            pltpu.VMEM((4, top_total * ROWS, WIDE), bf),
            big, big, big,
            thin, thin, thin, thin, thin,
            pltpu.VMEM((both_total * ROWS, WIDE), bf),
            pltpu.VMEM((both_total * ROWS, WIDE), bf),
            pltpu.VMEM((total, WIDE), f32),
            pltpu.VMEM((9, WIDE, WIDE), bf),
            pltpu.VMEM((8, WIDE, WIDE), bf),
            pltpu.VMEM((2, WIDE, WIDE), bf),
            pltpu.VMEM((halo, WIDE), bf),
            pltpu.VMEM((halo, WIDE), bf),
            pltpu.VMEM((halo, WIDE), bf),
            pltpu.VMEM((12, 2, 2, n_rest, unit_rows, 128), bf),
            pltpu.VMEM((5, 2, 2, n_rest, unit_rows, 128), bf),
            pltpu.VMEM((6, 2, 2, n_rest, unit_rows, 128), bf),
            pltpu.VMEM((6, 2, n_rest, unit_rows, 128), bf),
            pltpu.VMEM((6, n_rest, unit_rows, 128), bf),
            pltpu.VMEM((6, n_rest - 1, unit_rows, 128), bf),
            pltpu.VMEM((8, 2, 2, unit_rows, 128), bf),
            pltpu.VMEM((3, unit_rows, WIDE), f32),
            pltpu.VMEM((n_height, 4, 3 * ROWS, WIDE), bf),
            pltpu.VMEM((2, n_thin, 8, 128), f32),
            pltpu.VMEM((n_height, 16, WIDE), f32),
            pltpu.VMEM((n_batch, 16, WIDE), f32),
            pltpu.VMEM((16, 8, WIDE), f32),
            pltpu.VMEM((16, WIDE), f32),
            dma((4,)), dma((2,)), dma((6, 16)), dma((6, 16)), dma((3,)), dma((1,)), dma((2,)),
            dma((2, 2, 2)), dma((2, 2, 2)), dma((3,)), dma((3,)), dma((2,)),
        ],
        compiler_params=pltpu.CompilerParams(
            collective_id=0, has_side_effects=True, vmem_limit_bytes=63 << 20
        ),
        name="both_blocks",
    )(
        *planes, reduce_a, flat_a, expand_a, shortcut_a, reduce_b, flat_b, expand_b,
        row_counts, gain_mid, shift_mid, gain_out, shift_out, up,
    )
    pooled = jnp.transpose(results[0], (0, 2, 1, 3)).reshape(3, ROWS, -1)[:, :count]
    backs = [from_planes(results[1 + g], images[g].shape) for g in range(3)]
    shards = list(results[4:11])
    for place in (1, 5):
        shards[place] = shards[place].reshape((3, 3) + shards[place].shape[1:])
    return (pooled[0], pooled[1], pooled[2], *backs, *shards, *results[11:15])


def solution(mesh):
    placed = (
        P("batch", "height", None, None),
        P("batch", "height", None, None),
        P("batch", "height", None, None),
        P(),
        P(),
        P(),
        P(),
        P(),
        P(),
        P(),
        P(),
        P(),
        P(),
        P(),
        P(),
        P("batch", None),
        P("batch", None),
        P("batch", None),
    )
    return jax.shard_map(
        per_device,
        mesh=mesh,
        in_specs=placed,
        out_specs=(
            P("batch", None),
            P("batch", None),
            P("batch", None),
            P("batch", "height", None, None),
            P("batch", "height", None, None),
            P("batch", "height", None, None),
            P("batch", None),
            P(None, None, "batch", None),
            P("batch", None),
            P("batch", None),
            P("batch", None),
            P(None, None, "batch", None),
            P("batch", None),
            P(),
            P(),
            P(),
            P(),
        ),
        check_vma=False,
    )
```

```python
import functools

import jax
import jax.numpy as jnp
from jax import lax
from jax.experimental import pallas as pl
from jax.experimental.pallas import tpu as pltpu
from jax.sharding import PartitionSpec as P

epsilon = 1e-05
MESH = pl.DeviceIdType.MESH

WIDE = 512
ROWS = 16
STEP = 64


def silu_of(half):
    return half + half * jnp.tanh(half)


def slope_of(half):
    t = jnp.tanh(half)
    return (1.0 + t) + half * (1.0 - t * t)


def up32(values):
    return values.astype(jnp.float32)


def low(values):
    return values.astype(jnp.bfloat16)


def times(left, right):
    return jnp.dot(left, right, preferred_element_type=jnp.float32)


def times_t(left, right):
    return lax.dot_general(
        left, right, (((1,), (1,)), ((), ())), preferred_element_type=jnp.float32
    )


def t_times(left, right):
    return lax.dot_general(
        left, right, (((0,), (0,)), ((), ())), preferred_element_type=jnp.float32
    )


def fold(values):
    return jnp.sum(values.reshape(-1, 8, values.shape[-1]), axis=0)


def one_row(values):
    return jnp.sum(values, axis=0, keepdims=True)


def wide_mask(mask):
    return jnp.concatenate([up32(mask)] * (WIDE // 128), axis=1)


def grids(heights, widths):
    counts = [k * (o + 1) for k, o in zip(heights, widths)]
    starts = [sum(counts[:g]) for g in range(3)]
    top_sizes = [(k + 1) * (o + 1) + 1 for k, o in zip(heights, widths)]
    top_starts = [sum(top_sizes[:g]) for g in range(3)]
    both_sizes = [(k + 2) * (o + 1) + 2 for k, o in zip(heights, widths)]
    both_starts = [sum(both_sizes[:g]) for g in range(3)]
    halo_starts = [sum(widths[:g]) for g in range(3)]
    return counts, starts, sum(top_sizes), top_starts, sum(both_sizes), both_starts, halo_starts


def main_kernel(
    n_batch, n_height, heights, widths, images, total_in, total_out,
    x_small, x_medium, x_large, reduce_a, spatial_a, expand_a, shortcut_a, reduce_b, spatial_b, expand_b,
    row_counts, gain_mid, shift_mid, gain_out, shift_out, up_ref,
    pooled, dx_small, dx_medium, dx_large, g_reduce_a, g_spatial_a, g_expand_a,
    g_shortcut_a, g_reduce_b, g_spatial_b, g_expand_b, gain_mid_grad, shift_mid_grad,
    gain_out_grad, shift_out_grad, h1_kept, a1_kept,
    edge_ref, mask_ref, big_b, big_a, h3, side, mb, h2, a2, h4, h5, a5, a4p, dhp, acc, wp, wq, w2,
    halo_up, halo_down, halo_in, keep, away, r0, r1, r2, r3, final, ready, pool_slots,
    thin, wide_h, wide_b, stat_mid, stat_out,
    w_sem, x_sem, u_send, u_recv, ready_sem, dx_sem, spill_sem, ar_send, ar_recv, halo_send, halo_recv, pool_sem,
):
    b, h = lax.axis_index("batch"), lax.axis_index("height")
    counts, starts, top_total, top_starts, both_total, both_starts, halo_starts = grids(
        heights, widths
    )
    total = sum(counts) * ROWS
    half = total // 2
    part = total // 4
    groups = range(3)
    h1, dz, h6 = big_b, big_b, big_a
    halo_a = mb.at[0:2, 0 : sum(widths) * ROWS]

    def rows_at(start, count):
        return pl.ds(pl.multiple_of(start * ROWS, ROWS), count * ROWS)

    def steps(index):
        return pl.ds(pl.multiple_of(index * part, ROWS), part)

    def fetch(source, target, sem):
        pltpu.make_async_copy(source, target, sem).start()

    def arrived(target, sem):
        pltpu.make_async_copy(target, target, sem).wait()

    def columns(k):
        return pl.ds(k * WIDE, WIDE)

    def fetch_columns(weight, target, first, sem):
        for n in range(4):
            fetch(weight.at[:, columns(n)], target.at[first + n], sem)

    def fetch_shortcut():
        for n in range(4):
            for k in range(2):
                fetch(shortcut_a.at[columns(k), columns(n)], wq.at[2 * n + k], w_sem.at[1])

    xs, dxs = (x_small, x_medium, x_large), (dx_small, dx_medium, dx_large)

    def band_row(buffer, g, y):
        return buffer.at[pl.ds(starts[g] + y * (widths[g] + 1), widths[g])]

    def by_position(buffer):
        return buffer.reshape(buffer.shape[0] // ROWS, ROWS, WIDE)

    def fetch_plane(p, k, target, sem):
        for g in groups:
            for y in range(heights[g]):
                fetch(
                    xs[g].at[y, p // 2, :, p % 2, :, columns(k)],
                    band_row(by_position(target), g, y),
                    sem,
                )

    def plane_arrived(target, sem):
        pixels = sum(k * o for k, o in zip(heights, widths)) * ROWS
        arrived(target.at[0:pixels], sem)

    def put_plane(p, k, source):
        for g in groups:
            for y in range(heights[g]):
                fetch(
                    band_row(by_position(source), g, y),
                    dxs[g].at[y, p // 2, :, p % 2, :, columns(k)],
                    dx_sem.at[0],
                )

    for k in range(2):
        for p in range(4):
            for g in groups:
                for y in range(heights[g]):
                    edge_place = (starts[g] + y * (widths[g] + 1) + widths[g]) * ROWS
                    (h3, mb)[k][p, edge_place : edge_place + ROWS] = jnp.zeros(
                        (ROWS, WIDE), jnp.bfloat16
                    )
            fetch_plane(p, k, (h3, mb)[k].at[p], x_sem.at[k])
    for k in range(2):
        fetch(reduce_a.at[columns(k)], w2.at[k], w_sem.at[3])
    fetch_shortcut()
    fetch(spatial_a, wp, w_sem.at[0])

    for g in groups:
        live = row_counts[g, h]
        for y in range(heights[g]):
            row = (starts[g] + y * (widths[g] + 1)) * ROWS
            shape = (widths[g] * ROWS, 128)
            image = lax.rem(lax.broadcasted_iota(jnp.int32, shape, 0), ROWS)
            inside = jnp.where(image < images, 1.0, 0.0)
            alive = jnp.clip(live - y, 0, 1).astype(jnp.float32)
            mask_ref[row : row + shape[0]] = low(inside * alive)
            mask_ref[row + shape[0] : row + shape[0] + ROWS] = jnp.zeros((ROWS, 128), jnp.bfloat16)
            is_last = jnp.maximum(1 - jnp.abs(live - 1 - y), 0).astype(jnp.float32)
            edge_ref[g, y] = jnp.ones((8, 128), jnp.float32) * is_last

    halo_down[...] = jnp.zeros_like(halo_down)
    halo_up[...] = jnp.zeros_like(halo_up)
    halo_in[...] = jnp.zeros_like(halo_in)

    @pl.loop(0, both_total // 2)
    def _(i):
        rows = rows_at(i * 2, 2)
        a4p[rows] = jnp.zeros((2 * ROWS, WIDE), jnp.bfloat16)
        dhp[rows] = jnp.zeros((2 * ROWS, WIDE), jnp.bfloat16)

    for g in groups:
        count = widths[g] + 2
        for p in range(4):
            big_a[p, top_starts[g] * ROWS : (top_starts[g] + count) * ROWS] = jnp.zeros(
                (count * ROWS, WIDE), jnp.bfloat16
            )

    barrier = pltpu.get_barrier_semaphore()

    @pl.loop(1, n_batch * n_height)
    def _(k):
        other = lax.rem(b * n_height + h + k, n_batch * n_height)
        pl.semaphore_signal(
            barrier,
            inc=1,
            device_id=(other // n_height, lax.rem(other, n_height)),
            device_id_type=MESH,
        )

    pl.semaphore_wait(barrier, n_batch * n_height - 1)

    turn = [0]
    direct = thin.shape[1] == n_batch * n_height

    def ar_spread(slots, me, count, peer, sems):
        @pl.loop(1, count)
        def _(k):
            pltpu.make_async_remote_copy(
                src_ref=slots.at[me],
                dst_ref=slots.at[me],
                send_sem=ar_send.at[sems],
                recv_sem=ar_recv.at[sems],
                device_id=peer(lax.rem(me + k, count)),
                device_id_type=MESH,
            ).start()

    def ar_wait(slots, count, sems, which):
        others = slots.at[0 : count - 1]
        pltpu.make_async_copy(others, others, which.at[sems]).wait()

    def sums_start(vectors):
        slot = turn[0] % 2
        turn[0] += 1
        if not direct:
            first, second = thin.at[slot, 0:n_height], thin.at[slot, n_height:]
            put_rows(first, h, vectors)
            ar_spread(first, h, n_height, lambda p: (b, p), (0, 0, slot))
            return first, second, 2, slot
        slots = thin.at[slot]
        me = b * n_height + h
        put_rows(slots, me, vectors)
        ar_spread(
            slots, me, n_batch * n_height, lambda p: (p // n_height, lax.rem(p, n_height)),
            (0, 0, slot),
        )
        return slots, None, 0, slot

    def put_rows(slots, me, vectors):
        for v, vector in enumerate(vectors):
            for j in range(4):
                slots[me, 4 * v + j : 4 * v + j + 1, :] = vector[:, 128 * j : 128 * (j + 1)]

    def wide_start(part, at=0):
        count = 16 if part is None else 8
        rows = pl.ds(8 * (part or 0), count)
        first, second = wide_h.at[:, rows], wide_b.at[:, rows]
        first[h] = stat_out[at : at + count]
        ar_spread(first, h, n_height, lambda p: (b, p), (1, 0, part or 0))
        return first, second, 1, part or 0, at

    def sums_middle(state):
        first, second, kind, slot = state[:4]
        if kind == 0:
            return
        ar_wait(first, n_height, (kind % 2, 0, slot), ar_recv)
        second[b] = jnp.sum(first[...], axis=0)
        ar_spread(second, b, n_batch, lambda p: (p, h), (kind % 2, 1, slot))

    def sums_end(state):
        first, second, kind, slot = state[:4]
        if kind == 0:
            ar_wait(first, n_batch * n_height, (0, 0, slot), ar_recv)
            summed = jnp.sum(first[...], axis=0)
            ar_wait(first, n_batch * n_height, (0, 0, slot), ar_send)
        else:
            ar_wait(second, n_batch, (kind % 2, 1, slot), ar_recv)
            summed = jnp.sum(second[...], axis=0)
            ar_wait(first, n_height, (kind % 2, 0, slot), ar_send)
            ar_wait(second, n_batch, (kind % 2, 1, slot), ar_send)
        if kind == 1:
            stat_out[state[4] : state[4] + summed.shape[0]] = summed
            return None
        return [
            jnp.concatenate([summed[4 * v + j : 4 * v + j + 1] for j in range(4)], axis=1)
            for v in range(2)
        ]

    def keep_stats(kept, index, sums, number, gain, shift):
        centre = sums[0] * (1.0 / number)
        root = lax.rsqrt(sums[1] * (1.0 / number) - centre * centre + epsilon)
        scale = root * gain
        kept[index, 0:1] = centre
        kept[index, 1:2] = root
        kept[index, 2:3] = scale
        kept[index, 3:4] = shift - centre * scale
        kept[index, 4:5] = -centre * root
        kept[index, 5:6] = 0.5 * scale
        kept[index, 6:7] = 0.5 * (shift - centre * scale)

    def back_factors(kept, index, sums, number, gain):
        centre, root = kept[index, 0:1], kept[index, 1:2]
        main = gain * root
        slope = -main * root * sums[1] * (1.0 / number)
        return main, slope, -main * sums[0] * (1.0 / number) - slope * centre

    def halo_copy(source, target, sem, peer):
        return pltpu.make_async_remote_copy(
            src_ref=source,
            dst_ref=target,
            send_sem=halo_send.at[sem],
            recv_sem=halo_recv.at[sem],
            device_id=(b, peer),
            device_id_type=MESH,
        )

    def halo_rows(g):
        return slice(halo_starts[g] * ROWS, (halo_starts[g] + widths[g]) * ROWS)

    def top_row(padded, start, g):
        return padded.at[pl.ds((start + 1) * ROWS, widths[g] * ROWS)]

    def send_down(buffer, padded, sem):
        @pl.when(h < n_height - 1)
        def _():
            for g in groups:
                halo_copy(
                    buffer.at[halo_rows(g)], top_row(padded, both_starts[g], g), sem, h + 1
                ).start()

    def send_up(buffer, sem):
        @pl.when(h > 0)
        def _():
            halo_copy(buffer, halo_in, sem, h - 1).start()

    def halo_wait(buffer, sems, sem, condition):
        @pl.when(condition)
        def _():
            arrived(buffer, sems.at[sem])

    def place_below(padded):
        for g in groups:
            stride = widths[g] + 1
            for y in range(1, heights[g] + 1):
                is_edge = edge(g, y - 1)

                @pl.loop(0, widths[g])
                def _(col):
                    rows = rows_at(both_starts[g] + 1 + (y + 1) * stride + col, 1)
                    value = up32(halo_in[rows_at(halo_starts[g] + col, 1)]) * is_edge
                    if y < heights[g]:
                        value = value + up32(padded[rows])
                    padded[rows] = low(value)

    def edge(g, y):
        return wide_mask(edge_ref[g, y, 0:1])

    def first_row(source, g, row=0):
        start = (starts[g] + row * (widths[g] + 1)) * ROWS
        return up32(source[start : start + widths[g] * ROWS])

    def last_row(source, g):
        value = first_row(source, g) * edge(g, 0)
        for y in range(1, heights[g]):
            value = value + first_row(source, g, y) * edge(g, y)
        return value

    core, high = lax.rem(h, 2), h // 2
    low_bit, rest = lax.rem(b, 2), b // 2
    n_rest = n_batch // 2
    unit_rows = WIDE // n_batch

    def either(is_one, one, zero):
        return is_one * one + (1 - is_one) * zero

    first, second = either(core, low_bit, high), either(core, high, low_bit)
    core_peer = (b, h + 1 - 2 * core)
    high_peer = (b, h + 2 - 4 * high)
    low_peer = (b + 1 - 2 * low_bit, h)
    first_peer = [either(core, low_peer[i], high_peer[i]) for i in range(2)]
    second_peer = [either(core, high_peer[i], low_peer[i]) for i in range(2)]

    def ring(buffer, unit):
        return lax.rem(unit, buffer.shape[0])

    def unit_copy(level, unit, source, target, peer):
        return pltpu.make_async_remote_copy(
            src_ref=source,
            dst_ref=target,
            send_sem=u_send.at[level, lax.rem(unit, 16)],
            recv_sem=u_recv.at[level, lax.rem(unit, 16)],
            device_id=tuple(peer),
            device_id_type=MESH,
        )

    def hop(level, unit):
        kept = keep.at[ring(keep, unit)]
        if level == 0:
            return unit_copy(
                0, unit, away.at[ring(away, unit)], r0.at[ring(r0, unit)], core_peer
            )
        if level == 1:
            return unit_copy(1, unit, kept.at[1 - first], r1.at[ring(r1, unit)], first_peer)
        if level == 2:
            return unit_copy(
                2, unit, kept.at[first, 1 - second], r2.at[ring(r2, unit)], second_peer
            )
        if level == 4:
            mine = final.at[ring(final, unit), core, high]
            return unit_copy(4, unit, mine, mine, high_peer)
        both = final.at[ring(final, unit), core]
        return unit_copy(5, unit, both, both, core_peer)

    def add_to(target, source):
        target[...] = low(up32(target[...]) + up32(source[...]))

    def rest_wait(unit, sems):
        others = r3.at[ring(r3, unit)]
        pltpu.make_async_copy(others, others, sems.at[3, lax.rem(unit, 16)]).wait()

    def round_0(unit, view):
        hop(0, unit).start()

    def round_1(unit, view):
        hop(0, unit).wait()
        kept, got = keep.at[ring(keep, unit)], r0.at[ring(r0, unit)]

        @pl.loop(0, n_rest)
        def _(k):
            for i in range(2):
                for j in range(2):
                    add_to(kept.at[i, j, k], got.at[i, j, k])

        hop(1, unit).start()

    def round_2(unit, view):
        hop(1, unit).wait_recv()
        kept, got = keep.at[ring(keep, unit), first], r1.at[ring(r1, unit)]

        @pl.loop(0, n_rest)
        def _(k):
            for j in range(2):
                add_to(kept.at[j, k], got.at[j, k])

        hop(2, unit).start()

    def round_3(unit, view):
        hop(2, unit).wait_recv()
        kept, got = keep.at[ring(keep, unit), first, second], r2.at[ring(r2, unit)]

        @pl.loop(0, n_rest)
        def _(k):
            add_to(kept.at[k], got.at[k])

        @pl.loop(1, n_rest)
        def _(k):
            unit_copy(
                3,
                unit,
                kept.at[lax.rem(rest + k, n_rest)],
                r3.at[ring(r3, unit), n_rest - 1 - k],
                (lax.rem(rest + k, n_rest) * 2 + low_bit, h),
            ).start()

    def round_4(unit, view):
        rest_wait(unit, u_recv)
        value = up32(keep[ring(keep, unit), first, second, rest])
        for k in range(n_rest - 1):
            value = value + up32(r3[ring(r3, unit), k])
        final[ring(final, unit), core, high] = low(value)
        hop(4, unit).start()

    def round_5(unit, view):
        hop(4, unit).wait_recv()
        hop(5, unit).start()
        for level in (1, 2):
            hop(level, unit).wait_send()
        rest_wait(unit, u_send)

    def round_6(unit, view):
        hop(5, unit).wait_recv()
        for level in (4, 5):
            hop(level, unit).wait_send()
        slot = ring(ready, unit)

        @pl.when(unit >= ready.shape[0])
        def _():
            arrived(ready.at[slot], ready_sem.at[slot])

        for c in range(2):
            for i in range(2):
                lane = 128 * (2 * c + i)
                ready[slot, :, lane : lane + 128] = up32(final[ring(final, unit), c, i])
        fetch(ready.at[slot], view(unit), ready_sem.at[slot])

    rounds = (
        (0, round_0), (2, round_1), (4, round_2), (6, round_3), (8, round_4), (10, round_5),
        (12, round_6),
    )
    clock, made, produced = [0], [0], []

    def advance(index, base, count):
        for lag, act in rounds:
            for start, size, unit, view in produced:
                from_, to = max(base - lag, start), min(base - lag + count, start + size)
                if from_ >= to:
                    continue
                target = base - lag - start + unit + index
                if to - from_ == count:
                    act(target, view)
                else:
                    shift = base - lag
                    inside = jnp.logical_and(index >= from_ - shift, index < to - shift)
                    pl.when(inside)(functools.partial(act, target, view))

    def idle(count):
        base = clock[0]
        clock[0] += count

        @pl.loop(0, count)
        def _(i):
            advance(i, base, count)

    def ticks(count):
        base = clock[0]
        clock[0] += count
        return lambda i: advance(i, base, count)

    def put(value, unit, units, first_shard):
        shard_rows = units * unit_rows
        own_side = core == 0
        left, right = low(value[:, : WIDE // 2]), low(value[:, WIDE // 2 :])
        own, other = jnp.where(own_side, left, right), jnp.where(own_side, right, left)
        for s in range(WIDE // shard_rows):
            shard = first_shard + s
            shard_low, shard_rest = s % 2, shard // 2
            for q in range(units):
                rows = slice(s * shard_rows + q * unit_rows, s * shard_rows + (q + 1) * unit_rows)
                for i in range(2):
                    lanes = slice(128 * i, 128 * (i + 1))
                    keep[
                        ring(keep, unit + q),
                        either(core, shard_low, i),
                        either(core, i, shard_low),
                        shard_rest,
                    ] = own[rows, lanes]
                    away[
                        ring(away, unit + q),
                        either(core, i, shard_low),
                        either(core, shard_low, i),
                        shard_rest,
                    ] = other[rows, lanes]

    views = {
        "expand_b": lambda j: g_expand_b.at[:, lanes_at(j)],
        "spatial_b": lambda j: g_spatial_b.at[j],
        "reduce_b": lambda j: g_reduce_b.at[unit_rows_at(j)],
        "expand_a": lambda j: g_expand_a.at[:, lanes_at(j)],
        "shortcut_a": lambda j: g_shortcut_a.at[unit_rows_at(lax.rem(j, 2)), lanes_at(j // 2)],
        "spatial_a": lambda j: g_spatial_a.at[j],
        "reduce_a": lambda j: g_reduce_a.at[unit_rows_at(j)],
    }
    first_units = {}

    def lanes_at(j):
        return pl.ds(pl.multiple_of(j * WIDE, WIDE), WIDE)

    def unit_rows_at(j):
        return pl.ds(pl.multiple_of(j * unit_rows, unit_rows), unit_rows)

    def view_of(name):
        base = first_units.setdefault(name, made[0])
        return lambda unit: views[name](unit - base)

    def run(name, count, body, make):
        base, unit, view = clock[0], made[0], view_of(name)
        clock[0] += count
        made[0] += count
        produced.append((base, count, unit, view))

        @pl.loop(0, count)
        def _(i):
            body(i)
            make(i, unit + i)
            advance(i, base, count)

    def produce(name, count, units, make):
        base, unit, view = clock[0], made[0], view_of(name)
        produced.append((base, count * units, unit, view))
        clock[0] += count * units
        made[0] += count * units

        @pl.loop(0, count)
        def _(t):
            make(t, unit + t * units)
            if units == 1:
                advance(t, base, count)
            else:

                @pl.loop(0, units)
                def _(q):
                    advance(t * units + q, base, count * units)

    zero8 = jnp.zeros((8, WIDE), jnp.float32)

    def half_mask(rows):
        return wide_mask(0.5 * up32(mask_ref[rows]))


    arrived(w2, w_sem.at[3])
    for k in range(2):
        for p in range(4):
            plane_arrived((h3, mb)[k].at[p], x_sem.at[k])

    def first_reduction(i, carry):
        p = i // 2
        rows = pl.ds(pl.multiple_of(lax.rem(i, 2) * half, ROWS), half)
        value = times(h3[p, rows], w2[0]) + times(mb[p, rows], w2[1])
        value = value * wide_mask(mask_ref[rows])
        h1[p, rows] = low(value)
        return carry[0] + fold(value), carry[1] + fold(value * value)

    sums = lax.fori_loop(0, 8, first_reduction, (zero8, zero8))
    state = sums_start([one_row(v) for v in sums])

    arrived(wq, w_sem.at[1])

    def shortcut_product(n, carry):
        value = times(h3[0], wq[2 * n]) + times(mb[0], wq[2 * n + 1])
        value = value * wide_mask(mask_ref[...])
        side[n] = low(value)
        stat_out[pl.ds(8 + n, 1)] = one_row(fold(value))
        stat_out[pl.ds(12 + n, 1)] = one_row(fold(value * value))
        return carry

    lax.fori_loop(0, 2, shortcut_product, 0)
    sums_middle(state)
    lax.fori_loop(2, 4, shortcut_product, 0)
    side_state = wide_start(1, 8)
    fetch_columns(expand_a, wq, 0, w_sem.at[1])
    for k in range(4):
        fetch(reduce_b.at[columns(k)], wq.at[4 + k], w_sem.at[2])
    sums = sums_end(state)
    keep_stats(stat_mid, 0, sums, total_in, gain_mid[0:1], shift_mid[0:1])

    scale, offset = stat_mid[0, 5:6], stat_mid[0, 6:7]
    for column in range(2):
        for g in groups:
            pre = last_row(h1.at[2 + column], g) * scale + offset
            mask = wide_mask(mask_ref[starts[g] * ROWS : (starts[g] + widths[g]) * ROWS])
            halo_a[column, halo_rows(g)] = low(silu_of(pre) * mask)

    @pl.when(h < n_height - 1)
    def _():
        for column in range(2):
            for g in groups:
                halo_copy(
                    halo_a.at[column, halo_rows(g)],
                    top_row(big_a.at[2 + column], top_starts[g], g),
                    0,
                    h + 1,
                ).start()

    for g in groups:
        per = counts[g] * ROWS // STEP
        base = (top_starts[g] + 1 + widths[g] + 1) * ROWS

        @pl.loop(0, 4)
        def _(p):
            @pl.loop(0, per)
            def _(i):
                rows = pl.ds(pl.multiple_of(starts[g] * ROWS + i * STEP, ROWS), STEP)
                pre = up32(h1[p, rows]) * scale + offset
                value = silu_of(pre) * wide_mask(mask_ref[rows])
                big_a[p, pl.ds(pl.multiple_of(base + i * STEP, ROWS), STEP)] = low(value)

    fetch(h1, h1_kept, spill_sem.at[0])

    def group_rows(g):
        return slice(starts[g] * ROWS, (starts[g] + counts[g]) * ROWS)

    def window(padded, start, g, dy, dx_):
        first = start + 1 + (1 + dy) * (widths[g] + 1) + dx_
        return padded[rows_at(first, counts[g])]

    def window_a(g, a, c):
        py, dy = lax.rem(a + 1, 2), (a + 1) // 2 - 1
        px, dx_ = lax.rem(c + 1, 2), (c + 1) // 2 - 1
        first = top_starts[g] + 1 + (1 + dy) * (widths[g] + 1) + dx_
        return big_a[2 * py + px, rows_at(first, counts[g])]

    def clear_acc():
        @pl.loop(0, total // part)
        def _(i):
            acc[steps(i)] = jnp.zeros((part, WIDE), jnp.float32)

    def conv_taps(start, last, window_of, product, make=None):
        def tap(t):
            for g in groups:
                acc[group_rows(g)] += product(window_of(g, t // 3, lax.rem(t, 3)), wp[t])

        if make is not None:
            run("spatial_b", last - start, lambda i: tap(start + i), make)
            return
        tick = ticks(last - start) if produced else None

        @pl.loop(start, last)
        def _(t):
            tap(t)
            if tick is not None:
                tick(t - start)

    def masked_sums(target):
        def body(i, carry):
            rows = steps(i)
            value = acc[rows] * wide_mask(mask_ref[rows])
            target[rows] = low(value)
            return carry[0] + fold(value), carry[1] + fold(value * value)

        return lax.fori_loop(0, total // part, body, (zero8, zero8))

    clear_acc()
    arrived(wp, w_sem.at[0])
    conv_taps(3, 9, window_a, times)
    sums_middle(side_state)
    halo_wait(halo_a, halo_recv, 0, h > 0)
    conv_taps(0, 3, window_a, times)
    sums = masked_sums(h2)
    state = sums_start([one_row(v) for v in sums])
    fetch(spatial_b, wp, w_sem.at[0])
    fetch(big_a, a1_kept, spill_sem.at[1])
    halo_wait(halo_a, halo_send, 0, h < n_height - 1)
    sums_middle(state)
    sums = sums_end(state)
    keep_stats(stat_mid, 1, sums, total_out, gain_mid[1:2], shift_mid[1:2])

    def activate(source, target, index):
        scale, offset = stat_mid[index, 5:6], stat_mid[index, 6:7]

        @pl.loop(0, total // part)
        def _(i):
            rows = steps(i)
            pre = up32(source[rows]) * scale + offset
            target[rows] = low(silu_of(pre) * wide_mask(mask_ref[rows]))

    activate(h2, a2, 1)
    arrived(wq.at[0:4], w_sem.at[1])

    def expansion(source, target):
        @pl.loop(0, 4)
        def _(n):
            value = times(source[...], wq[n])
            target[n, 0:total] = low(value)
            stat_out[pl.ds(n, 1)] = one_row(fold(value))
            stat_out[pl.ds(4 + n, 1)] = one_row(fold(value * value))

    expansion(a2, h3)
    state = wide_start(0)
    fetch_columns(expand_b, wq, 0, w_sem.at[1])
    sums_middle(state)
    sums_end(state)

    def out_stats(index, n, row):
        keep_stats(
            mid_or_out,
            4 * index + n,
            [stat_out[row + n : row + n + 1], stat_out[row + 4 + n : row + 5 + n]],
            total_out,
            gain_out[index : index + 1, n * WIDE : (n + 1) * WIDE],
            shift_out[index : index + 1, n * WIDE : (n + 1) * WIDE],
        )

    sums_end(side_state)
    mid_or_out = stat_mid.at[4:16]
    for n in range(4):
        out_stats(0, n, 0)
        out_stats(1, n, 8)

    def out_stat(index, n, row):
        return stat_mid[4 + 4 * index + n, row : row + 1]

    def half_joint(n, rows):
        return (
            up32(h3[n, rows]) * out_stat(0, n, 5)
            + up32(side[n, rows]) * out_stat(1, n, 5)
            + (out_stat(0, n, 6) + out_stat(1, n, 6))
        )

    arrived(wq.at[4:8], w_sem.at[2])
    clear_acc()

    @pl.loop(0, 4)
    def _(n):
        @pl.loop(0, 2)
        def _(i):
            rows = pl.ds(pl.multiple_of(i * half, ROWS), half)
            value = low(silu_of(half_joint(n, rows)) * wide_mask(mask_ref[rows]))
            mb[n, rows] = value
            acc[rows] += times(value, wq[4 + n])

    def plain_sums(target):
        def body(i, carry):
            rows = steps(i)
            value = acc[rows]
            target[rows] = low(value)
            return carry[0] + fold(value), carry[1] + fold(value * value)

        return lax.fori_loop(0, total // part, body, (zero8, zero8))

    sums = plain_sums(h4)
    state = sums_start([one_row(v) for v in sums])
    sums_middle(state)
    clear_acc()
    sums = sums_end(state)
    keep_stats(stat_mid, 2, sums, total_out, gain_mid[2:3], shift_mid[2:3])

    scale, offset = stat_mid[2, 5:6], stat_mid[2, 6:7]
    for g in groups:
        pre = last_row(h4, g) * scale + offset
        mask = wide_mask(mask_ref[starts[g] * ROWS : (starts[g] + widths[g]) * ROWS])
        halo_down[halo_rows(g)] = low(silu_of(pre) * mask)
    send_down(halo_down, a4p, 1)
    for g in groups:
        pre = first_row(h4, g) * scale + offset
        mask = wide_mask(mask_ref[starts[g] * ROWS : (starts[g] + widths[g]) * ROWS])
        halo_up[halo_rows(g)] = low(silu_of(pre) * mask)
    send_up(halo_up, 2)

    def both_base(g):
        return (both_starts[g] + 1 + widths[g] + 1) * ROWS

    for g in groups:

        @pl.loop(0, counts[g] * ROWS // STEP)
        def _(i):
            rows = pl.ds(pl.multiple_of(starts[g] * ROWS + i * STEP, ROWS), STEP)
            pre = up32(h4[rows]) * scale + offset
            value = low(silu_of(pre) * wide_mask(mask_ref[rows]))
            a4p[pl.ds(pl.multiple_of(both_base(g) + i * STEP, ROWS), STEP)] = value

    def window_b(g, a, c):
        return window(a4p, both_starts[g], g, a - 1, c - 1)

    def window_b_back(g, a, c):
        return window(dhp, both_starts[g], g, 1 - a, 1 - c)

    arrived(wp, w_sem.at[0])
    conv_taps(3, 6, window_b, times)
    halo_wait(halo_down, halo_recv, 1, h > 0)
    halo_wait(halo_in, halo_recv, 2, h < n_height - 1)
    place_below(a4p)
    conv_taps(0, 3, window_b, times)
    conv_taps(6, 9, window_b, times)
    sums = masked_sums(h5)
    state = sums_start([one_row(v) for v in sums])
    halo_wait(halo_down, halo_send, 1, h < n_height - 1)
    halo_wait(halo_up, halo_send, 2, h > 0)
    sums_middle(state)
    sums = sums_end(state)
    keep_stats(stat_mid, 3, sums, total_out, gain_mid[3:4], shift_mid[3:4])

    activate(h5, a5, 3)
    arrived(wq.at[0:4], w_sem.at[1])
    arrived(big_a, spill_sem.at[1])
    expansion(a5, h6)
    state = wide_start(0)
    sums_middle(state)
    arrived(h1, spill_sem.at[0])
    sums_end(state)
    for n in range(4):
        out_stats(2, n, 0)

    @pl.loop(0, 4)
    def _(n):
        index = 12 + n
        root, scale = stat_mid[index, 1:2], stat_mid[index, 2:3]
        offset, back = stat_mid[index, 3:4], stat_mid[index, 4:5]
        zero = jnp.zeros((ROWS, WIDE), jnp.float32)
        total_grad, total_dot = zero8, zero8
        for g in groups:
            share = 1.0 / (widths[g] * widths[g])

            up = jnp.concatenate([up32(up_ref[g, n]) * (0.5 * share)] * (STEP // ROWS), axis=0)

            def body(i, carry):
                rows = pl.ds(pl.multiple_of(starts[g] * ROWS + i * STEP, ROWS), STEP)
                value = up32(h6[n, rows])
                mask = wide_mask(mask_ref[rows])
                z = value * scale + offset + up32(mb[n, rows])
                z = 0.5 * z
                t = jnp.tanh(z)
                last = z + z * t
                grad = up * ((1.0 + t) + (z - z * t * t)) * mask
                dz[n, rows] = low(grad)
                last = (last * mask).reshape(STEP // ROWS, ROWS, WIDE)
                return (
                    carry[0] + jnp.sum(last, axis=0),
                    carry[1] + fold(grad),
                    carry[2] + fold(grad * (value * root + back)),
                )

            pool, total_grad, total_dot = lax.fori_loop(
                0, counts[g] * ROWS // STEP, body, (zero, total_grad, total_dot)
            )
            pool_slots[h, n, g * ROWS : (g + 1) * ROWS] = low(pool)
        stat_out[pl.ds(n, 1)] = one_row(total_grad)
        stat_out[pl.ds(4 + n, 1)] = one_row(total_dot)

    state = wide_start(1)

    for k in range(1, n_height):
        pltpu.make_async_remote_copy(
            src_ref=pool_slots.at[h],
            dst_ref=pool_slots.at[h],
            send_sem=pool_sem.at[0],
            recv_sem=pool_sem.at[1],
            device_id=(b, lax.rem(h + k, n_height)),
            device_id_type=MESH,
        ).start()
    sums_middle(state)
    clear_acc()
    sums_end(state)

    def out_back(index, sum_row, dot_row, n):
        sums = [stat_out[pl.ds(sum_row + n, 1)], stat_out[pl.ds(dot_row + n, 1)]]
        shift_out_grad[index : index + 1, lanes_at(n)] = sums[0]
        gain_out_grad[index : index + 1, lanes_at(n)] = sums[1]
        return back_factors(
            stat_mid, 4 + 4 * index + n, sums, total_out, gain_out[index : index + 1, lanes_at(n)]
        )

    def mid_back(index, place, sums, number):
        shift_mid_grad[place : place + 1] = sums[0]
        gain_mid_grad[place : place + 1] = sums[1]
        return back_factors(stat_mid, index, sums, number, gain_mid[place : place + 1])

    def mid_gradient(source, index):
        root, scale = stat_mid[index, 1:2], stat_mid[index, 5:6]
        offset, back = stat_mid[index, 6:7], stat_mid[index, 4:5]

        def body(i, carry):
            rows = steps(i)
            value = up32(source[rows])
            slope = slope_of(value * scale + offset)
            grad = acc[rows] * slope * half_mask(rows)
            acc[rows] = grad
            return carry[0] + fold(grad), carry[1] + fold(grad * (value * root + back))

        sums = lax.fori_loop(0, total // part, body, (zero8, zero8))
        return [one_row(v) for v in sums]

    @pl.loop(0, 4)
    def _(n):
        main, slope, constant = out_back(2, 0, 4, n)

        @pl.loop(0, 2)
        def _(i):
            rows = pl.ds(pl.multiple_of(i * half, ROWS), half)
            grad = main * up32(dz[n, rows]) + slope * up32(h6[n, rows]) + constant
            grad = low(grad * wide_mask(mask_ref[rows]))
            h6[n, rows] = grad
            acc[rows] += times_t(grad, wq[n])

    sums = mid_gradient(h5, 3)
    state = sums_start(sums)
    fetch_columns(expand_a, wq, 0, w_sem.at[1])
    sums_middle(state)
    produce("expand_b", 4, 1, lambda t, unit: put(t_times(a5[...], h6[t, 0:total]), unit, 1, 0))
    fetch(a1_kept, big_a, spill_sem.at[1])
    sums = sums_end(state)

    def mid_step(target, factors, padded):
        main, slope, constant = factors

        def tile(rows):
            grad = main * acc[rows] + slope * up32(target[rows]) + constant
            return low(grad * wide_mask(mask_ref[rows]))

        for g in groups:

            @pl.loop(0, counts[g] * ROWS // STEP)
            def _(i):
                rows = pl.ds(pl.multiple_of(starts[g] * ROWS + i * STEP, ROWS), STEP)
                grad = tile(rows)
                target[rows] = grad
                if padded is not None:
                    padded[pl.ds(pl.multiple_of(both_base(g) + i * STEP, ROWS), STEP)] = grad

    mid_step(h5, mid_back(3, 3, sums, total_out), dhp)
    for g in groups:
        halo_down[halo_rows(g)] = low(last_row(h5, g))
        halo_up[halo_rows(g)] = low(first_row(h5, g))
    send_down(halo_down, dhp, 1)
    send_up(halo_up, 2)
    def spatial_tile(window_of, grads):
        def value_of(t):
            parts = [
                t_times(window_of(g, t // 3, lax.rem(t, 3)), grads[group_rows(g)]) for g in groups
            ]
            return parts[0] + parts[1] + parts[2]

        return value_of

    def spatial_maker(window_of, grads):
        tile = spatial_tile(window_of, grads)
        return lambda done: lambda i, unit: put(tile(done + i), unit, 1, 0)

    make_b = spatial_maker(window_b, h5)
    clear_acc()
    conv_taps(3, 6, window_b_back, times_t, make_b(0))
    halo_wait(halo_down, halo_recv, 1, h > 0)
    halo_wait(halo_in, halo_recv, 2, h < n_height - 1)
    place_below(dhp)
    conv_taps(0, 3, window_b_back, times_t, make_b(3))
    conv_taps(6, 9, window_b_back, times_t)
    fetch(spatial_a, wp, w_sem.at[0])
    sums = mid_gradient(h4, 2)
    state = sums_start(sums)
    halo_wait(halo_down, halo_send, 1, h < n_height - 1)
    halo_wait(halo_up, halo_send, 2, h > 0)
    sums_middle(state)

    produce("spatial_b", 3, 1, make_b(6))
    sums = sums_end(state)

    mid_step(h4, mid_back(2, 2, sums, total_out), None)
    fetch_plane(0, 1, a4p, x_sem.at[1])

    tick = ticks(8)

    @pl.loop(0, 4)
    def _(n):
        def body(i, carry):
            tick(2 * n + i)
            rows = pl.ds(pl.multiple_of(i * half, ROWS), half)
            grad = times_t(h4[rows], wq[4 + n]) + up32(dz[n, rows])
            grad = grad * slope_of(half_joint(n, rows)) * half_mask(rows)
            dz[n, rows] = low(grad)
            main_hat = up32(h3[n, rows]) * out_stat(0, n, 1) + out_stat(0, n, 4)
            side_hat = up32(side[n, rows]) * out_stat(1, n, 1) + out_stat(1, n, 4)
            return (
                carry[0] + fold(grad),
                carry[1] + fold(grad * main_hat),
                carry[2] + fold(grad * side_hat),
            )

        sums = lax.fori_loop(0, 2, body, (zero8, zero8, zero8))
        for v in range(3):
            stat_out[pl.ds(4 * v + n, 1)] = one_row(sums[v])

    state = wide_start(None)
    sums_middle(state)

    def tile_reduce_b(step, unit):
        @pl.loop(0, 4)
        def _(t):
            put(t_times(mb[t], h4[...]), unit, 4, t * (n_batch // 4))

    produce("reduce_b", 1, 4, tile_reduce_b)
    for p in range(4):
        fetch_plane(p, 0, mb.at[p], x_sem.at[0])
    clear_acc()
    sums_end(state)

    arrived(wq.at[0:4], w_sem.at[1])

    def expansion_back(n):
        main, slope, constant = out_back(0, 0, 4, n)
        main2, slope2, constant2 = out_back(1, 0, 8, n)

        @pl.loop(0, 2)
        def _(i):
            rows = pl.ds(pl.multiple_of(i * half, ROWS), half)
            grad_in = up32(dz[n, rows])
            mask = wide_mask(mask_ref[rows])
            grad = low((main * grad_in + slope * up32(h3[n, rows]) + constant) * mask)
            h3[n, rows] = grad
            acc[rows] += times_t(grad, wq[n])
            other = main2 * grad_in + slope2 * up32(side[n, rows]) + constant2
            side[n, rows] = low(other * mask)

    run("expand_a", 4, expansion_back, lambda n, unit: put(t_times(a2[...], h3[n]), unit, 1, 0))
    fetch(h1_kept, h1, spill_sem.at[0])
    fetch_shortcut()
    sums = mid_gradient(h2, 1)
    state = sums_start(sums)
    sums_middle(state)
    for p in range(4):
        plane_arrived(mb.at[p], x_sem.at[0])
    plane_arrived(a4p, x_sem.at[1])

    def tile_shortcut(t, unit):
        put(t_times(mb[0], side[t]), unit, 2, 0)
        put(t_times(a4p[0:total], side[t]), unit, 2, n_batch // 2)

    produce("shortcut_a", 1, 2, lambda step, unit: tile_shortcut(0, unit))
    sums = sums_end(state)

    mid_step(h2, mid_back(1, 1, sums, total_out), dhp)
    for g in groups:
        halo_up[halo_rows(g)] = low(first_row(h2, g))
    send_up(halo_up, 2)
    arrived(wp, w_sem.at[0])
    arrived(h1, spill_sem.at[0])
    root, scale = stat_mid[0, 1:2], stat_mid[0, 5:6]
    offset, back = stat_mid[0, 6:7], stat_mid[0, 4:5]
    carry = (zero8, zero8)
    for p in range(4):
        py, px = p // 2, p % 2
        row_taps = ((1, 0),) if py == 0 else ((0, 1), (2, 0))
        column_taps = ((1, 0),) if px == 0 else ((0, 1), (2, 0))
        if p == 2:
            halo_wait(halo_in, halo_recv, 2, h < n_height - 1)
            place_below(dhp)
        for g in groups:
            value = None
            for a, dy in row_taps:
                for c, dx_ in column_taps:
                    product = times_t(window(dhp, both_starts[g], g, dy, dx_), wp[3 * a + c])
                    value = product if value is None else value + product
            acc[group_rows(g)] = value

        def body(i, carry):
            rows = steps(i)
            value = up32(h1[p, rows])
            grad = acc[rows] * slope_of(value * scale + offset) * half_mask(rows)
            h3[p, rows] = low(grad)
            return carry[0] + fold(grad), carry[1] + fold(grad * (value * root + back))

        carry = lax.fori_loop(0, total // part, body, carry)
        if p > 0:
            produce("shortcut_a", 1, 2, lambda step, unit: tile_shortcut(p, unit))
    state = sums_start([one_row(v) for v in carry])
    halo_wait(halo_up, halo_send, 2, h > 0)
    sums_middle(state)
    arrived(big_a, spill_sem.at[1])
    make_a = spatial_maker(window_a, h2)
    produce("spatial_a", 3, 1, make_a(0))
    sums = sums_end(state)

    main, slope, constant = mid_back(0, 0, sums, total_in)

    def first_back(p):
        @pl.loop(0, total // part)
        def _(i):
            rows = steps(i)
            grad = main * up32(h3[p, rows]) + slope * up32(h1[p, rows]) + constant
            h1[p, rows] = low(grad * wide_mask(mask_ref[rows]))

        fetch_plane(p, 1, h3.at[p], x_sem.at[1])

    run("spatial_a", 4, first_back, make_a(3))
    produce("spatial_a", 2, 1, make_a(7))
    for p in range(4):
        plane_arrived(h3.at[p], x_sem.at[1])

    def last_tile(chunk):
        value = t_times(chunk(0), h1[0])
        for p in range(1, 4):
            value = value + t_times(chunk(p), h1[p])
        return value

    def tile_reduce_a(step, unit):
        put(last_tile(lambda p: mb[p]), unit, 2, 0)
        put(last_tile(lambda p: h3[p]), unit, 2, n_batch // 2)

    produce("reduce_a", 1, 2, tile_reduce_a)
    arrived(wq, w_sem.at[1])
    for k in range(2):
        tick_13 = ticks(2)

        @pl.loop(0, 2)
        def _(i):
            rows = pl.ds(pl.multiple_of(i * half, ROWS), half)
            value = times_t(h1[0, rows], w2[k])
            for n in range(4):
                value = value + times_t(side[n, rows], wq[2 * n + k])
            if k == 0:
                big_a[0, rows] = low(value)
            else:
                a4p[rows] = low(value)
            tick_13(i)

    put_plane(0, 0, big_a.at[0])
    put_plane(0, 1, a4p)
    tick_13p = ticks(3)

    @pl.loop(1, 4)
    def _(p):
        big_a[p, 0:total] = low(times_t(h1[p], w2[0]))
        side[p] = low(times_t(h1[p], w2[1]))
        put_plane(p, 0, big_a.at[p])
        put_plane(p, 1, side.at[p])
        tick_13p(p - 1)

    idle(rounds[-1][0] - 6)
    others = pool_slots.at[0 : n_height - 1]
    pltpu.make_async_copy(others, others, pool_sem.at[1]).wait()
    pltpu.make_async_copy(others, others, pool_sem.at[0]).wait()
    for g in groups:
        for n in range(4):
            value = None
            for k in range(n_height):
                part = up32(pool_slots[k, n, g * ROWS : (g + 1) * ROWS])
                value = part if value is None else value + part
            pooled[g, n] = value * (1.0 / (widths[g] * widths[g]))

    for slot in range(ready.shape[0]):
        arrived(ready.at[slot], ready_sem.at[slot])
    for p in range(8):
        plane_arrived(a4p, dx_sem.at[0])


def to_planes(image):
    count, rows, cols, channels = image.shape
    value = jnp.pad(image, ((0, ROWS - count), (0, 0), (0, 0), (0, 0)))
    value = jnp.transpose(value, (1, 2, 0, 3))
    return value.reshape(rows // 2, 2, cols // 2, 2, ROWS, channels)


def from_planes(planes, shape):
    count, rows, cols, channels = shape
    value = planes.reshape(rows, cols, ROWS, channels)[:, :, :count]
    return jnp.transpose(value, (2, 0, 1, 3))


def per_device(
    image_small, image_medium, image_large, row_counts, reduce_a, first_spatial_weight, expand_a,
    shortcut_a, reduce_b, second_spatial_weight, expand_b, gain_mid, shift_mid, gain_out,
    shift_out, upstream_small, upstream_medium, upstream_large,
):
    images = (image_small, image_medium, image_large)
    upstreams = (upstream_small, upstream_medium, upstream_large)
    n_batch, n_height = lax.axis_size("batch"), lax.axis_size("height")
    heights = [value.shape[1] // 2 for value in images]
    widths = [value.shape[2] // 2 for value in images]
    count = images[0].shape[0]
    pixels = sum(o * o for o in widths) * count * n_batch
    counts, starts, top_total, _, both_total, _, _ = grids(heights, widths)
    total = sum(counts) * ROWS
    planes = [to_planes(image) for image in images]
    up = jnp.pad(jnp.stack(upstreams), ((0, 0), (0, ROWS - count), (0, 0)))
    up = jnp.transpose(up.reshape(3, ROWS, 4, WIDE), (0, 2, 1, 3))
    halo = sum(widths) * ROWS
    bf, f32 = jnp.bfloat16, jnp.float32
    unit_rows, n_rest = WIDE // n_batch, n_batch // 2
    n_thin = n_batch * n_height if n_batch * n_height <= 64 else n_batch + n_height
    dma = pltpu.SemaphoreType.DMA
    vmem = pl.BlockSpec(memory_space=pltpu.VMEM)
    anywhere = pl.BlockSpec(memory_space=pl.ANY)
    flat_a = first_spatial_weight.reshape(9, WIDE, WIDE)
    flat_b = second_spatial_weight.reshape(9, WIDE, WIDE)
    big = pltpu.VMEM((4, total, WIDE), bf)
    thin = pltpu.VMEM((total, WIDE), bf)
    results = pl.pallas_call(
        functools.partial(
            main_kernel, n_batch, n_height, heights, widths, count, float(4 * pixels),
            float(pixels)
        ),
        out_shape=[
            jax.ShapeDtypeStruct((3, 4, ROWS, WIDE), f32),
            *[jax.ShapeDtypeStruct(value.shape, bf) for value in planes],
            *[
                jax.ShapeDtypeStruct(w.shape[:-2] + (w.shape[-2] // n_batch, w.shape[-1]), f32)
                for w in (reduce_a, flat_a, expand_a, shortcut_a, reduce_b, flat_b, expand_b)
            ],
            *[jax.ShapeDtypeStruct(w.shape, f32) for w in (gain_mid, shift_mid, gain_out, shift_out)],
            jax.ShapeDtypeStruct((4, total, WIDE), bf),
            jax.ShapeDtypeStruct((4, top_total * ROWS, WIDE), bf),
        ],
        in_specs=[anywhere] * 10 + [pl.BlockSpec(memory_space=pltpu.SMEM)] + [vmem] * 5,
        out_specs=[vmem] + [anywhere] * 10 + [vmem] * 4 + [anywhere] * 2,
        scratch_shapes=[
            pltpu.VMEM((3, max(heights), 8, 128), f32),
            pltpu.VMEM((total, 128), bf),
            big,
            pltpu.VMEM((4, top_total * ROWS, WIDE), bf),
            big, big, big,
            thin, thin, thin, thin, thin,
            pltpu.VMEM((both_total * ROWS, WIDE), bf),
            pltpu.VMEM((both_total * ROWS, WIDE), bf),
            pltpu.VMEM((total, WIDE), f32),
            pltpu.VMEM((9, WIDE, WIDE), bf),
            pltpu.VMEM((8, WIDE, WIDE), bf),
            pltpu.VMEM((2, WIDE, WIDE), bf),
            pltpu.VMEM((halo, WIDE), bf),
            pltpu.VMEM((halo, WIDE), bf),
            pltpu.VMEM((halo, WIDE), bf),
            pltpu.VMEM((12, 2, 2, n_rest, unit_rows, 128), bf),
            pltpu.VMEM((5, 2, 2, n_rest, unit_rows, 128), bf),
            pltpu.VMEM((6, 2, 2, n_rest, unit_rows, 128), bf),
            pltpu.VMEM((6, 2, n_rest, unit_rows, 128), bf),
            pltpu.VMEM((6, n_rest, unit_rows, 128), bf),
            pltpu.VMEM((6, n_rest - 1, unit_rows, 128), bf),
            pltpu.VMEM((8, 2, 2, unit_rows, 128), bf),
            pltpu.VMEM((3, unit_rows, WIDE), f32),
            pltpu.VMEM((n_height, 4, 3 * ROWS, WIDE), bf),
            pltpu.VMEM((2, n_thin, 8, 128), f32),
            pltpu.VMEM((n_height, 16, WIDE), f32),
            pltpu.VMEM((n_batch, 16, WIDE), f32),
            pltpu.VMEM((16, 8, WIDE), f32),
            pltpu.VMEM((16, WIDE), f32),
            dma((4,)), dma((2,)), dma((6, 16)), dma((6, 16)), dma((3,)), dma((1,)), dma((2,)),
            dma((2, 2, 2)), dma((2, 2, 2)), dma((3,)), dma((3,)), dma((2,)),
        ],
        compiler_params=pltpu.CompilerParams(
            collective_id=0, has_side_effects=True, vmem_limit_bytes=63 << 20
        ),
        name="both_blocks",
    )(
        *planes, reduce_a, flat_a, expand_a, shortcut_a, reduce_b, flat_b, expand_b,
        row_counts, gain_mid, shift_mid, gain_out, shift_out, up,
    )
    pooled = jnp.transpose(results[0], (0, 2, 1, 3)).reshape(3, ROWS, -1)[:, :count]
    backs = [from_planes(results[1 + g], images[g].shape) for g in range(3)]
    shards = list(results[4:11])
    for place in (1, 5):
        shards[place] = shards[place].reshape((3, 3) + shards[place].shape[1:])
    return (pooled[0], pooled[1], pooled[2], *backs, *shards, *results[11:15])


def solution(mesh):
    placed = (
        P("batch", "height", None, None),
        P("batch", "height", None, None),
        P("batch", "height", None, None),
        P(),
        P(),
        P(),
        P(),
        P(),
        P(),
        P(),
        P(),
        P(),
        P(),
        P(),
        P(),
        P("batch", None),
        P("batch", None),
        P("batch", None),
    )
    return jax.shard_map(
        per_device,
        mesh=mesh,
        in_specs=placed,
        out_specs=(
            P("batch", None),
            P("batch", None),
            P("batch", None),
            P("batch", "height", None, None),
            P("batch", "height", None, None),
            P("batch", "height", None, None),
            P("batch", None),
            P(None, None, "batch", None),
            P("batch", None),
            P("batch", None),
            P("batch", None),
            P(None, None, "batch", None),
            P("batch", None),
            P(),
            P(),
            P(),
            P(),
        ),
        check_vma=False,
    )
```

```python
import functools

import jax
import jax.numpy as jnp
from jax import lax
from jax.experimental import pallas as pl
from jax.experimental.pallas import tpu as pltpu
from jax.sharding import PartitionSpec as P

epsilon = 1e-05
MESH = pl.DeviceIdType.MESH

WIDE = 512
ROWS = 16
STEP = 64


def silu_of(half):
    return half + half * jnp.tanh(half)


def slope_of(half):
    t = jnp.tanh(half)
    return (1.0 + t) + half * (1.0 - t * t)


def up32(values):
    return values.astype(jnp.float32)


def low(values):
    return values.astype(jnp.bfloat16)


def times(left, right):
    return jnp.dot(left, right, preferred_element_type=jnp.float32)


def times_t(left, right):
    return lax.dot_general(
        left, right, (((1,), (1,)), ((), ())), preferred_element_type=jnp.float32
    )


def t_times(left, right):
    return lax.dot_general(
        left, right, (((0,), (0,)), ((), ())), preferred_element_type=jnp.float32
    )


def fold(values):
    return jnp.sum(values.reshape(-1, 8, values.shape[-1]), axis=0)


def one_row(values):
    return jnp.sum(values, axis=0, keepdims=True)


def wide_mask(mask):
    return jnp.concatenate([up32(mask)] * (WIDE // 128), axis=1)


def grids(heights, widths):
    counts = [k * (o + 1) for k, o in zip(heights, widths)]
    starts = [sum(counts[:g]) for g in range(3)]
    top_sizes = [(k + 1) * (o + 1) + 1 for k, o in zip(heights, widths)]
    top_starts = [sum(top_sizes[:g]) for g in range(3)]
    both_sizes = [(k + 2) * (o + 1) + 2 for k, o in zip(heights, widths)]
    both_starts = [sum(both_sizes[:g]) for g in range(3)]
    halo_starts = [sum(widths[:g]) for g in range(3)]
    return counts, starts, sum(top_sizes), top_starts, sum(both_sizes), both_starts, halo_starts


def main_kernel(
    n_batch, n_height, heights, widths, images, total_in, total_out,
    x_small, x_medium, x_large, reduce_a, spatial_a, expand_a, shortcut_a, reduce_b, spatial_b, expand_b,
    row_counts, gain_mid, shift_mid, gain_out, shift_out, up_ref,
    pooled, dx_small, dx_medium, dx_large, g_reduce_a, g_spatial_a, g_expand_a,
    g_shortcut_a, g_reduce_b, g_spatial_b, g_expand_b, gain_mid_grad, shift_mid_grad,
    gain_out_grad, shift_out_grad, h1_kept, a1_kept,
    edge_ref, mask_ref, big_b, big_a, h3, side, mb, h2, a2, h4, h5, a5, a4p, dhp, acc, wp, wq, w2,
    halo_up, halo_down, halo_in, keep, away, r0, r1, r2, r3, final, ready, pool_slots,
    thin, wide_h, wide_b, stat_mid, stat_out,
    w_sem, x_sem, u_send, u_recv, ready_sem, dx_sem, spill_sem, ar_send, ar_recv, halo_send, halo_recv, pool_sem,
):
    b, h = lax.axis_index("batch"), lax.axis_index("height")
    counts, starts, top_total, top_starts, both_total, both_starts, halo_starts = grids(
        heights, widths
    )
    total = sum(counts) * ROWS
    half = total // 2
    part = total // 4
    step_of = [ROWS * max(d for d in range(1, 21) if n % d == 0) for n in counts]
    groups = range(3)
    h1, dz, h6 = big_b, big_b, big_a
    halo_a = mb.at[0:2, 0 : sum(widths) * ROWS]

    def rows_at(start, count):
        return pl.ds(pl.multiple_of(start * ROWS, ROWS), count * ROWS)

    def steps(index):
        return pl.ds(pl.multiple_of(index * part, ROWS), part)

    def fetch(source, target, sem):
        pltpu.make_async_copy(source, target, sem).start()

    def arrived(target, sem):
        pltpu.make_async_copy(target, target, sem).wait()

    def columns(k):
        return pl.ds(k * WIDE, WIDE)

    def fetch_columns(weight, target, first, sem):
        for n in range(4):
            fetch(weight.at[:, columns(n)], target.at[first + n], sem)

    def fetch_shortcut():
        for n in range(4):
            for k in range(2):
                fetch(shortcut_a.at[columns(k), columns(n)], wq.at[2 * n + k], w_sem.at[1])

    xs, dxs = (x_small, x_medium, x_large), (dx_small, dx_medium, dx_large)

    def band_row(buffer, g, y):
        return buffer.at[pl.ds(starts[g] + y * (widths[g] + 1), widths[g])]

    def by_position(buffer):
        return buffer.reshape(buffer.shape[0] // ROWS, ROWS, WIDE)

    def fetch_plane(p, k, target, sem):
        for g in groups:
            for y in range(heights[g]):
                fetch(
                    xs[g].at[y, p // 2, :, p % 2, :, columns(k)],
                    band_row(by_position(target), g, y),
                    sem,
                )

    def plane_arrived(target, sem):
        pixels = sum(k * o for k, o in zip(heights, widths)) * ROWS
        arrived(target.at[0:pixels], sem)

    def put_plane(p, k, source):
        for g in groups:
            for y in range(heights[g]):
                fetch(
                    band_row(by_position(source), g, y),
                    dxs[g].at[y, p // 2, :, p % 2, :, columns(k)],
                    dx_sem.at[0],
                )

    for k in range(2):
        for p in range(4):
            for g in groups:
                for y in range(heights[g]):
                    edge_place = (starts[g] + y * (widths[g] + 1) + widths[g]) * ROWS
                    (h3, mb)[k][p, edge_place : edge_place + ROWS] = jnp.zeros(
                        (ROWS, WIDE), jnp.bfloat16
                    )
            fetch_plane(p, k, (h3, mb)[k].at[p], x_sem.at[k])
    for k in range(2):
        fetch(reduce_a.at[columns(k)], w2.at[k], w_sem.at[3])
    fetch_shortcut()
    fetch(spatial_a, wp, w_sem.at[0])

    for g in groups:
        live = row_counts[g, h]
        for y in range(heights[g]):
            row = (starts[g] + y * (widths[g] + 1)) * ROWS
            shape = (widths[g] * ROWS, 128)
            image = lax.rem(lax.broadcasted_iota(jnp.int32, shape, 0), ROWS)
            inside = jnp.where(image < images, 1.0, 0.0)
            alive = jnp.clip(live - y, 0, 1).astype(jnp.float32)
            mask_ref[row : row + shape[0]] = low(inside * alive)
            mask_ref[row + shape[0] : row + shape[0] + ROWS] = jnp.zeros((ROWS, 128), jnp.bfloat16)
            is_last = jnp.maximum(1 - jnp.abs(live - 1 - y), 0).astype(jnp.float32)
            edge_ref[g, y] = jnp.ones((8, 128), jnp.float32) * is_last

    halo_down[...] = jnp.zeros_like(halo_down)
    halo_up[...] = jnp.zeros_like(halo_up)
    halo_in[...] = jnp.zeros_like(halo_in)

    @pl.loop(0, both_total // 2)
    def _(i):
        rows = rows_at(i * 2, 2)
        a4p[rows] = jnp.zeros((2 * ROWS, WIDE), jnp.bfloat16)
        dhp[rows] = jnp.zeros((2 * ROWS, WIDE), jnp.bfloat16)

    for g in groups:
        count = widths[g] + 2
        for p in range(4):
            big_a[p, top_starts[g] * ROWS : (top_starts[g] + count) * ROWS] = jnp.zeros(
                (count * ROWS, WIDE), jnp.bfloat16
            )

    barrier = pltpu.get_barrier_semaphore()

    @pl.loop(1, n_batch * n_height)
    def _(k):
        other = lax.rem(b * n_height + h + k, n_batch * n_height)
        pl.semaphore_signal(
            barrier,
            inc=1,
            device_id=(other // n_height, lax.rem(other, n_height)),
            device_id_type=MESH,
        )

    pl.semaphore_wait(barrier, n_batch * n_height - 1)

    turn = [0]
    direct = thin.shape[1] == n_batch * n_height

    def ar_spread(slots, me, count, peer, sems):
        @pl.loop(1, count)
        def _(k):
            pltpu.make_async_remote_copy(
                src_ref=slots.at[me],
                dst_ref=slots.at[me],
                send_sem=ar_send.at[sems],
                recv_sem=ar_recv.at[sems],
                device_id=peer(lax.rem(me + k, count)),
                device_id_type=MESH,
            ).start()

    def ar_wait(slots, count, sems, which):
        others = slots.at[0 : count - 1]
        pltpu.make_async_copy(others, others, which.at[sems]).wait()

    def sums_start(vectors):
        slot = turn[0] % 2
        turn[0] += 1
        if not direct:
            first, second = thin.at[slot, 0:n_height], thin.at[slot, n_height:]
            put_rows(first, h, vectors)
            ar_spread(first, h, n_height, lambda p: (b, p), (0, 0, slot))
            return first, second, 2, slot
        slots = thin.at[slot]
        me = b * n_height + h
        put_rows(slots, me, vectors)
        ar_spread(
            slots, me, n_batch * n_height, lambda p: (p // n_height, lax.rem(p, n_height)),
            (0, 0, slot),
        )
        return slots, None, 0, slot

    def put_rows(slots, me, vectors):
        for v, vector in enumerate(vectors):
            for j in range(4):
                slots[me, 4 * v + j : 4 * v + j + 1, :] = vector[:, 128 * j : 128 * (j + 1)]

    def wide_start(part, at=0):
        count = 16 if part is None else 8
        rows = pl.ds(8 * (part or 0), count)
        first, second = wide_h.at[:, rows], wide_b.at[:, rows]
        first[h] = stat_out[at : at + count]
        ar_spread(first, h, n_height, lambda p: (b, p), (1, 0, part or 0))
        return first, second, 1, part or 0, at

    def sums_middle(state):
        first, second, kind, slot = state[:4]
        if kind == 0:
            return
        ar_wait(first, n_height, (kind % 2, 0, slot), ar_recv)
        second[b] = jnp.sum(first[...], axis=0)
        ar_spread(second, b, n_batch, lambda p: (p, h), (kind % 2, 1, slot))

    def sums_end(state):
        first, second, kind, slot = state[:4]
        if kind == 0:
            ar_wait(first, n_batch * n_height, (0, 0, slot), ar_recv)
            summed = jnp.sum(first[...], axis=0)
            ar_wait(first, n_batch * n_height, (0, 0, slot), ar_send)
        else:
            ar_wait(second, n_batch, (kind % 2, 1, slot), ar_recv)
            summed = jnp.sum(second[...], axis=0)
            ar_wait(first, n_height, (kind % 2, 0, slot), ar_send)
            ar_wait(second, n_batch, (kind % 2, 1, slot), ar_send)
        if kind == 1:
            stat_out[state[4] : state[4] + summed.shape[0]] = summed
            return None
        return [
            jnp.concatenate([summed[4 * v + j : 4 * v + j + 1] for j in range(4)], axis=1)
            for v in range(2)
        ]

    def keep_stats(kept, index, sums, number, gain, shift):
        centre = sums[0] * (1.0 / number)
        root = lax.rsqrt(sums[1] * (1.0 / number) - centre * centre + epsilon)
        scale = root * gain
        kept[index, 0:1] = centre
        kept[index, 1:2] = root
        kept[index, 2:3] = scale
        kept[index, 3:4] = shift - centre * scale
        kept[index, 4:5] = -centre * root
        kept[index, 5:6] = 0.5 * scale
        kept[index, 6:7] = 0.5 * (shift - centre * scale)

    def back_factors(kept, index, sums, number, gain):
        centre, root = kept[index, 0:1], kept[index, 1:2]
        main = gain * root
        slope = -main * root * sums[1] * (1.0 / number)
        return main, slope, -main * sums[0] * (1.0 / number) - slope * centre

    def halo_copy(source, target, sem, peer):
        return pltpu.make_async_remote_copy(
            src_ref=source,
            dst_ref=target,
            send_sem=halo_send.at[sem],
            recv_sem=halo_recv.at[sem],
            device_id=(b, peer),
            device_id_type=MESH,
        )

    def halo_rows(g):
        return slice(halo_starts[g] * ROWS, (halo_starts[g] + widths[g]) * ROWS)

    def top_row(padded, start, g):
        return padded.at[pl.ds((start + 1) * ROWS, widths[g] * ROWS)]

    def send_down(buffer, padded, sem):
        @pl.when(h < n_height - 1)
        def _():
            for g in groups:
                halo_copy(
                    buffer.at[halo_rows(g)], top_row(padded, both_starts[g], g), sem, h + 1
                ).start()

    def send_up(buffer, sem):
        @pl.when(h > 0)
        def _():
            halo_copy(buffer, halo_in, sem, h - 1).start()

    def halo_wait(buffer, sems, sem, condition):
        @pl.when(condition)
        def _():
            arrived(buffer, sems.at[sem])

    def place_below(padded):
        for g in groups:
            stride = widths[g] + 1
            for y in range(1, heights[g] + 1):
                is_edge = edge(g, y - 1)

                @pl.loop(0, widths[g])
                def _(col):
                    rows = rows_at(both_starts[g] + 1 + (y + 1) * stride + col, 1)
                    value = up32(halo_in[rows_at(halo_starts[g] + col, 1)]) * is_edge
                    if y < heights[g]:
                        value = value + up32(padded[rows])
                    padded[rows] = low(value)

    def edge(g, y):
        return wide_mask(edge_ref[g, y, 0:1])

    def first_row(source, g, row=0):
        start = (starts[g] + row * (widths[g] + 1)) * ROWS
        return up32(source[start : start + widths[g] * ROWS])

    def last_row(source, g):
        value = first_row(source, g) * edge(g, 0)
        for y in range(1, heights[g]):
            value = value + first_row(source, g, y) * edge(g, y)
        return value

    core, high = lax.rem(h, 2), h // 2
    low_bit, rest = lax.rem(b, 2), b // 2
    n_rest = n_batch // 2
    unit_rows = WIDE // n_batch

    def either(is_one, one, zero):
        return is_one * one + (1 - is_one) * zero

    first, second = either(core, low_bit, high), either(core, high, low_bit)
    core_peer = (b, h + 1 - 2 * core)
    high_peer = (b, h + 2 - 4 * high)
    low_peer = (b + 1 - 2 * low_bit, h)
    first_peer = [either(core, low_peer[i], high_peer[i]) for i in range(2)]
    second_peer = [either(core, high_peer[i], low_peer[i]) for i in range(2)]

    def ring(buffer, unit):
        return lax.rem(unit, buffer.shape[0])

    def unit_copy(level, unit, source, target, peer):
        return pltpu.make_async_remote_copy(
            src_ref=source,
            dst_ref=target,
            send_sem=u_send.at[level, lax.rem(unit, 16)],
            recv_sem=u_recv.at[level, lax.rem(unit, 16)],
            device_id=tuple(peer),
            device_id_type=MESH,
        )

    def hop(level, unit):
        kept = keep.at[ring(keep, unit)]
        if level == 0:
            return unit_copy(
                0, unit, away.at[ring(away, unit)], r0.at[ring(r0, unit)], core_peer
            )
        if level == 1:
            return unit_copy(1, unit, kept.at[1 - first], r1.at[ring(r1, unit)], first_peer)
        if level == 2:
            return unit_copy(
                2, unit, kept.at[first, 1 - second], r2.at[ring(r2, unit)], second_peer
            )
        if level == 4:
            mine = final.at[ring(final, unit), core, high]
            return unit_copy(4, unit, mine, mine, high_peer)
        both = final.at[ring(final, unit), core]
        return unit_copy(5, unit, both, both, core_peer)

    def add_to(target, source):
        target[...] = low(up32(target[...]) + up32(source[...]))

    def rest_wait(unit, sems):
        others = r3.at[ring(r3, unit)]
        pltpu.make_async_copy(others, others, sems.at[3, lax.rem(unit, 16)]).wait()

    def round_0(unit, view):
        hop(0, unit).start()

    def round_1(unit, view):
        hop(0, unit).wait()
        kept, got = keep.at[ring(keep, unit)], r0.at[ring(r0, unit)]

        @pl.loop(0, n_rest)
        def _(k):
            for i in range(2):
                for j in range(2):
                    add_to(kept.at[i, j, k], got.at[i, j, k])

        hop(1, unit).start()

    def round_2(unit, view):
        hop(1, unit).wait_recv()
        kept, got = keep.at[ring(keep, unit), first], r1.at[ring(r1, unit)]

        @pl.loop(0, n_rest)
        def _(k):
            for j in range(2):
                add_to(kept.at[j, k], got.at[j, k])

        hop(2, unit).start()

    def round_3(unit, view):
        hop(2, unit).wait_recv()
        kept, got = keep.at[ring(keep, unit), first, second], r2.at[ring(r2, unit)]

        @pl.loop(0, n_rest)
        def _(k):
            add_to(kept.at[k], got.at[k])

        @pl.loop(1, n_rest)
        def _(k):
            unit_copy(
                3,
                unit,
                kept.at[lax.rem(rest + k, n_rest)],
                r3.at[ring(r3, unit), n_rest - 1 - k],
                (lax.rem(rest + k, n_rest) * 2 + low_bit, h),
            ).start()

    def round_4(unit, view):
        rest_wait(unit, u_recv)
        value = up32(keep[ring(keep, unit), first, second, rest])
        for k in range(n_rest - 1):
            value = value + up32(r3[ring(r3, unit), k])
        final[ring(final, unit), core, high] = low(value)
        hop(4, unit).start()

    def round_5(unit, view):
        hop(4, unit).wait_recv()
        hop(5, unit).start()
        for level in (1, 2):
            hop(level, unit).wait_send()
        rest_wait(unit, u_send)

    def round_6(unit, view):
        hop(5, unit).wait_recv()
        for level in (4, 5):
            hop(level, unit).wait_send()
        slot = ring(ready, unit)

        @pl.when(unit >= ready.shape[0])
        def _():
            arrived(ready.at[slot], ready_sem.at[slot])

        for c in range(2):
            for i in range(2):
                lane = 128 * (2 * c + i)
                ready[slot, :, lane : lane + 128] = up32(final[ring(final, unit), c, i])
        fetch(ready.at[slot], view(unit), ready_sem.at[slot])

    rounds = (
        (0, round_0), (2, round_1), (4, round_2), (6, round_3), (8, round_4), (10, round_5),
        (12, round_6),
    )
    clock, made, produced = [0], [0], []

    def advance(index, base, count):
        for lag, act in rounds:
            for start, size, unit, view in produced:
                from_, to = max(base - lag, start), min(base - lag + count, start + size)
                if from_ >= to:
                    continue
                target = base - lag - start + unit + index
                if to - from_ == count:
                    act(target, view)
                else:
                    shift = base - lag
                    inside = jnp.logical_and(index >= from_ - shift, index < to - shift)
                    pl.when(inside)(functools.partial(act, target, view))

    def idle(count):
        base = clock[0]
        clock[0] += count

        @pl.loop(0, count)
        def _(i):
            advance(i, base, count)

    def ticks(count):
        base = clock[0]
        clock[0] += count
        return lambda i: advance(i, base, count)

    def put(value, unit, units, first_shard):
        shard_rows = units * unit_rows
        own_side = core == 0
        left, right = low(value[:, : WIDE // 2]), low(value[:, WIDE // 2 :])
        own, other = jnp.where(own_side, left, right), jnp.where(own_side, right, left)
        for s in range(WIDE // shard_rows):
            shard = first_shard + s
            shard_low, shard_rest = s % 2, shard // 2
            for q in range(units):
                rows = slice(s * shard_rows + q * unit_rows, s * shard_rows + (q + 1) * unit_rows)
                for i in range(2):
                    lanes = slice(128 * i, 128 * (i + 1))
                    keep[
                        ring(keep, unit + q),
                        either(core, shard_low, i),
                        either(core, i, shard_low),
                        shard_rest,
                    ] = own[rows, lanes]
                    away[
                        ring(away, unit + q),
                        either(core, i, shard_low),
                        either(core, shard_low, i),
                        shard_rest,
                    ] = other[rows, lanes]

    views = {
        "expand_b": lambda j: g_expand_b.at[:, lanes_at(j)],
        "spatial_b": lambda j: g_spatial_b.at[j],
        "reduce_b": lambda j: g_reduce_b.at[unit_rows_at(j)],
        "expand_a": lambda j: g_expand_a.at[:, lanes_at(j)],
        "shortcut_a": lambda j: g_shortcut_a.at[unit_rows_at(lax.rem(j, 2)), lanes_at(j // 2)],
        "spatial_a": lambda j: g_spatial_a.at[j],
        "reduce_a": lambda j: g_reduce_a.at[unit_rows_at(j)],
    }
    first_units = {}

    def lanes_at(j):
        return pl.ds(pl.multiple_of(j * WIDE, WIDE), WIDE)

    def unit_rows_at(j):
        return pl.ds(pl.multiple_of(j * unit_rows, unit_rows), unit_rows)

    def view_of(name):
        base = first_units.setdefault(name, made[0])
        return lambda unit: views[name](unit - base)

    def run(name, count, body, make):
        base, unit, view = clock[0], made[0], view_of(name)
        clock[0] += count
        made[0] += count
        produced.append((base, count, unit, view))

        @pl.loop(0, count)
        def _(i):
            body(i)
            make(i, unit + i)
            advance(i, base, count)

    def produce(name, count, units, make):
        base, unit, view = clock[0], made[0], view_of(name)
        produced.append((base, count * units, unit, view))
        clock[0] += count * units
        made[0] += count * units

        @pl.loop(0, count)
        def _(t):
            make(t, unit + t * units)
            if units == 1:
                advance(t, base, count)
            else:

                @pl.loop(0, units)
                def _(q):
                    advance(t * units + q, base, count * units)

    zero8 = jnp.zeros((8, WIDE), jnp.float32)

    def half_mask(rows):
        return wide_mask(0.5 * up32(mask_ref[rows]))


    arrived(w2, w_sem.at[3])
    for k in range(2):
        for p in range(4):
            plane_arrived((h3, mb)[k].at[p], x_sem.at[k])

    def first_reduction(i, carry):
        p = i // 2
        rows = pl.ds(pl.multiple_of(lax.rem(i, 2) * half, ROWS), half)
        value = times(h3[p, rows], w2[0]) + times(mb[p, rows], w2[1])
        value = value * wide_mask(mask_ref[rows])
        h1[p, rows] = low(value)
        return carry[0] + fold(value), carry[1] + fold(value * value)

    sums = lax.fori_loop(0, 8, first_reduction, (zero8, zero8))
    state = sums_start([one_row(v) for v in sums])

    arrived(wq, w_sem.at[1])

    def shortcut_product(n, carry):
        value = times(h3[0], wq[2 * n]) + times(mb[0], wq[2 * n + 1])
        value = value * wide_mask(mask_ref[...])
        side[n] = low(value)
        stat_out[pl.ds(8 + n, 1)] = one_row(fold(value))
        stat_out[pl.ds(12 + n, 1)] = one_row(fold(value * value))
        return carry

    lax.fori_loop(0, 2, shortcut_product, 0)
    sums_middle(state)
    lax.fori_loop(2, 4, shortcut_product, 0)
    side_state = wide_start(1, 8)
    fetch_columns(expand_a, wq, 0, w_sem.at[1])
    for k in range(4):
        fetch(reduce_b.at[columns(k)], wq.at[4 + k], w_sem.at[2])
    sums = sums_end(state)
    keep_stats(stat_mid, 0, sums, total_in, gain_mid[0:1], shift_mid[0:1])

    scale, offset = stat_mid[0, 5:6], stat_mid[0, 6:7]
    for column in range(2):
        for g in groups:
            pre = last_row(h1.at[2 + column], g) * scale + offset
            mask = wide_mask(mask_ref[starts[g] * ROWS : (starts[g] + widths[g]) * ROWS])
            halo_a[column, halo_rows(g)] = low(silu_of(pre) * mask)

    @pl.when(h < n_height - 1)
    def _():
        for column in range(2):
            for g in groups:
                halo_copy(
                    halo_a.at[column, halo_rows(g)],
                    top_row(big_a.at[2 + column], top_starts[g], g),
                    0,
                    h + 1,
                ).start()

    for g in groups:
        step = step_of[g]
        per = counts[g] * ROWS // step
        base = (top_starts[g] + 1 + widths[g] + 1) * ROWS

        @pl.loop(0, 4)
        def _(p):
            @pl.loop(0, per)
            def _(i):
                rows = pl.ds(pl.multiple_of(starts[g] * ROWS + i * step, ROWS), step)
                pre = up32(h1[p, rows]) * scale + offset
                value = silu_of(pre) * wide_mask(mask_ref[rows])
                big_a[p, pl.ds(pl.multiple_of(base + i * step, ROWS), step)] = low(value)

    fetch(h1, h1_kept, spill_sem.at[0])

    def group_rows(g):
        return slice(starts[g] * ROWS, (starts[g] + counts[g]) * ROWS)

    def window(padded, start, g, dy, dx_):
        first = start + 1 + (1 + dy) * (widths[g] + 1) + dx_
        return padded[rows_at(first, counts[g])]

    def window_a(g, a, c):
        py, dy = lax.rem(a + 1, 2), (a + 1) // 2 - 1
        px, dx_ = (c + 1) % 2, (c + 1) // 2 - 1
        first = top_starts[g] + 1 + (1 + dy) * (widths[g] + 1) + dx_
        return big_a[2 * py + px, rows_at(first, counts[g])]

    def clear_acc():
        @pl.loop(0, total // part)
        def _(i):
            acc[steps(i)] = jnp.zeros((part, WIDE), jnp.float32)

    def conv_taps(start, last, window_of, product, make=None):
        def tap(t):
            for g in groups:
                acc[group_rows(g)] += product(window_of(g, t // 3, lax.rem(t, 3)), wp[t])

        if make is not None:
            run("spatial_b", last - start, lambda i: tap(start + i), make)
            return
        if not produced:

            @pl.loop(start // 3, last // 3)
            def _(a):
                for g in groups:
                    parts = [product(window_of(g, a, c), wp[3 * a + c]) for c in range(3)]
                    acc[group_rows(g)] += parts[0] + parts[1] + parts[2]

            return
        tick = ticks(last - start)

        @pl.loop(start, last)
        def _(t):
            tap(t)
            tick(t - start)

    def masked_sums(target):
        def body(i, carry):
            rows = steps(i)
            value = acc[rows] * wide_mask(mask_ref[rows])
            target[rows] = low(value)
            return carry[0] + fold(value), carry[1] + fold(value * value)

        return lax.fori_loop(0, total // part, body, (zero8, zero8))

    clear_acc()
    arrived(wp, w_sem.at[0])
    conv_taps(3, 9, window_a, times)
    sums_middle(side_state)
    halo_wait(halo_a, halo_recv, 0, h > 0)
    conv_taps(0, 3, window_a, times)
    sums = masked_sums(h2)
    state = sums_start([one_row(v) for v in sums])
    fetch(spatial_b, wp, w_sem.at[0])
    fetch(big_a, a1_kept, spill_sem.at[1])
    halo_wait(halo_a, halo_send, 0, h < n_height - 1)
    sums_middle(state)
    sums = sums_end(state)
    keep_stats(stat_mid, 1, sums, total_out, gain_mid[1:2], shift_mid[1:2])

    def activate(source, target, index):
        scale, offset = stat_mid[index, 5:6], stat_mid[index, 6:7]

        @pl.loop(0, total // part)
        def _(i):
            rows = steps(i)
            pre = up32(source[rows]) * scale + offset
            target[rows] = low(silu_of(pre) * wide_mask(mask_ref[rows]))

    activate(h2, a2, 1)
    arrived(wq.at[0:4], w_sem.at[1])

    def expansion(source, target):
        @pl.loop(0, 4)
        def _(n):
            value = times(source[...], wq[n])
            target[n, 0:total] = low(value)
            stat_out[pl.ds(n, 1)] = one_row(fold(value))
            stat_out[pl.ds(4 + n, 1)] = one_row(fold(value * value))

    expansion(a2, h3)
    state = wide_start(0)
    fetch_columns(expand_b, wq, 0, w_sem.at[1])
    sums_middle(state)
    sums_end(state)

    def out_stats(index, n, row):
        keep_stats(
            mid_or_out,
            4 * index + n,
            [stat_out[row + n : row + n + 1], stat_out[row + 4 + n : row + 5 + n]],
            total_out,
            gain_out[index : index + 1, n * WIDE : (n + 1) * WIDE],
            shift_out[index : index + 1, n * WIDE : (n + 1) * WIDE],
        )

    sums_end(side_state)
    mid_or_out = stat_mid.at[4:16]
    for n in range(4):
        out_stats(0, n, 0)
        out_stats(1, n, 8)

    def out_stat(index, n, row):
        return stat_mid[4 + 4 * index + n, row : row + 1]

    def half_joint(n, rows):
        return (
            up32(h3[n, rows]) * out_stat(0, n, 5)
            + up32(side[n, rows]) * out_stat(1, n, 5)
            + (out_stat(0, n, 6) + out_stat(1, n, 6))
        )

    arrived(wq.at[4:8], w_sem.at[2])
    clear_acc()

    @pl.loop(0, 4)
    def _(n):
        @pl.loop(0, 2)
        def _(i):
            rows = pl.ds(pl.multiple_of(i * half, ROWS), half)
            value = low(silu_of(half_joint(n, rows)) * wide_mask(mask_ref[rows]))
            mb[n, rows] = value
            acc[rows] += times(value, wq[4 + n])

    def plain_sums(target):
        def body(i, carry):
            rows = steps(i)
            value = acc[rows]
            target[rows] = low(value)
            return carry[0] + fold(value), carry[1] + fold(value * value)

        return lax.fori_loop(0, total // part, body, (zero8, zero8))

    sums = plain_sums(h4)
    state = sums_start([one_row(v) for v in sums])
    sums_middle(state)
    clear_acc()
    sums = sums_end(state)
    keep_stats(stat_mid, 2, sums, total_out, gain_mid[2:3], shift_mid[2:3])

    scale, offset = stat_mid[2, 5:6], stat_mid[2, 6:7]
    for g in groups:
        pre = last_row(h4, g) * scale + offset
        mask = wide_mask(mask_ref[starts[g] * ROWS : (starts[g] + widths[g]) * ROWS])
        halo_down[halo_rows(g)] = low(silu_of(pre) * mask)
    send_down(halo_down, a4p, 1)
    for g in groups:
        pre = first_row(h4, g) * scale + offset
        mask = wide_mask(mask_ref[starts[g] * ROWS : (starts[g] + widths[g]) * ROWS])
        halo_up[halo_rows(g)] = low(silu_of(pre) * mask)
    send_up(halo_up, 2)

    def both_base(g):
        return (both_starts[g] + 1 + widths[g] + 1) * ROWS

    for g in groups:

        step = step_of[g]

        @pl.loop(0, counts[g] * ROWS // step)
        def _(i):
            rows = pl.ds(pl.multiple_of(starts[g] * ROWS + i * step, ROWS), step)
            pre = up32(h4[rows]) * scale + offset
            value = low(silu_of(pre) * wide_mask(mask_ref[rows]))
            a4p[pl.ds(pl.multiple_of(both_base(g) + i * step, ROWS), step)] = value

    def window_b(g, a, c):
        return window(a4p, both_starts[g], g, a - 1, c - 1)

    def window_b_back(g, a, c):
        return window(dhp, both_starts[g], g, 1 - a, 1 - c)

    arrived(wp, w_sem.at[0])
    conv_taps(3, 6, window_b, times)
    halo_wait(halo_down, halo_recv, 1, h > 0)
    halo_wait(halo_in, halo_recv, 2, h < n_height - 1)
    place_below(a4p)
    conv_taps(0, 3, window_b, times)
    conv_taps(6, 9, window_b, times)
    sums = masked_sums(h5)
    state = sums_start([one_row(v) for v in sums])
    halo_wait(halo_down, halo_send, 1, h < n_height - 1)
    halo_wait(halo_up, halo_send, 2, h > 0)
    sums_middle(state)
    sums = sums_end(state)
    keep_stats(stat_mid, 3, sums, total_out, gain_mid[3:4], shift_mid[3:4])

    activate(h5, a5, 3)
    arrived(wq.at[0:4], w_sem.at[1])
    arrived(big_a, spill_sem.at[1])
    expansion(a5, h6)
    state = wide_start(0)
    sums_middle(state)
    arrived(h1, spill_sem.at[0])
    sums_end(state)
    for n in range(4):
        out_stats(2, n, 0)

    @pl.loop(0, 4)
    def _(n):
        index = 12 + n
        root, scale = stat_mid[index, 1:2], stat_mid[index, 2:3]
        offset, back = stat_mid[index, 3:4], stat_mid[index, 4:5]
        zero = jnp.zeros((ROWS, WIDE), jnp.float32)
        total_grad, total_dot = zero8, zero8
        for g in groups:
            share = 1.0 / (widths[g] * widths[g])

            up = jnp.concatenate([up32(up_ref[g, n]) * (0.5 * share)] * (STEP // ROWS), axis=0)

            def body(i, carry):
                rows = pl.ds(pl.multiple_of(starts[g] * ROWS + i * STEP, ROWS), STEP)
                value = up32(h6[n, rows])
                mask = wide_mask(mask_ref[rows])
                z = value * scale + offset + up32(mb[n, rows])
                z = 0.5 * z
                t = jnp.tanh(z)
                last = z + z * t
                grad = up * ((1.0 + t) + (z - z * t * t)) * mask
                dz[n, rows] = low(grad)
                last = (last * mask).reshape(STEP // ROWS, ROWS, WIDE)
                return (
                    carry[0] + jnp.sum(last, axis=0),
                    carry[1] + fold(grad),
                    carry[2] + fold(grad * (value * root + back)),
                )

            pool, total_grad, total_dot = lax.fori_loop(
                0, counts[g] * ROWS // STEP, body, (zero, total_grad, total_dot)
            )
            pool_slots[h, n, g * ROWS : (g + 1) * ROWS] = low(pool)
        stat_out[pl.ds(n, 1)] = one_row(total_grad)
        stat_out[pl.ds(4 + n, 1)] = one_row(total_dot)

    state = wide_start(1)

    for k in range(1, n_height):
        pltpu.make_async_remote_copy(
            src_ref=pool_slots.at[h],
            dst_ref=pool_slots.at[h],
            send_sem=pool_sem.at[0],
            recv_sem=pool_sem.at[1],
            device_id=(b, lax.rem(h + k, n_height)),
            device_id_type=MESH,
        ).start()
    sums_middle(state)
    clear_acc()
    sums_end(state)

    def out_back(index, sum_row, dot_row, n):
        sums = [stat_out[pl.ds(sum_row + n, 1)], stat_out[pl.ds(dot_row + n, 1)]]
        shift_out_grad[index : index + 1, lanes_at(n)] = sums[0]
        gain_out_grad[index : index + 1, lanes_at(n)] = sums[1]
        return back_factors(
            stat_mid, 4 + 4 * index + n, sums, total_out, gain_out[index : index + 1, lanes_at(n)]
        )

    def mid_back(index, place, sums, number):
        shift_mid_grad[place : place + 1] = sums[0]
        gain_mid_grad[place : place + 1] = sums[1]
        return back_factors(stat_mid, index, sums, number, gain_mid[place : place + 1])

    def mid_gradient(source, index):
        root, scale = stat_mid[index, 1:2], stat_mid[index, 5:6]
        offset, back = stat_mid[index, 6:7], stat_mid[index, 4:5]

        def body(i, carry):
            rows = steps(i)
            value = up32(source[rows])
            slope = slope_of(value * scale + offset)
            grad = acc[rows] * slope * half_mask(rows)
            acc[rows] = grad
            return carry[0] + fold(grad), carry[1] + fold(grad * (value * root + back))

        sums = lax.fori_loop(0, total // part, body, (zero8, zero8))
        return [one_row(v) for v in sums]

    @pl.loop(0, 4)
    def _(n):
        main, slope, constant = out_back(2, 0, 4, n)

        @pl.loop(0, 2)
        def _(i):
            rows = pl.ds(pl.multiple_of(i * half, ROWS), half)
            grad = main * up32(dz[n, rows]) + slope * up32(h6[n, rows]) + constant
            grad = low(grad * wide_mask(mask_ref[rows]))
            h6[n, rows] = grad
            acc[rows] += times_t(grad, wq[n])

    sums = mid_gradient(h5, 3)
    state = sums_start(sums)
    fetch_columns(expand_a, wq, 0, w_sem.at[1])
    sums_middle(state)
    produce("expand_b", 4, 1, lambda t, unit: put(t_times(a5[...], h6[t, 0:total]), unit, 1, 0))
    fetch(a1_kept, big_a, spill_sem.at[1])
    sums = sums_end(state)

    def mid_step(target, factors, padded):
        main, slope, constant = factors

        def tile(rows):
            grad = main * acc[rows] + slope * up32(target[rows]) + constant
            return low(grad * wide_mask(mask_ref[rows]))

        for g in groups:

            step = step_of[g]

            @pl.loop(0, counts[g] * ROWS // step)
            def _(i):
                rows = pl.ds(pl.multiple_of(starts[g] * ROWS + i * step, ROWS), step)
                grad = tile(rows)
                target[rows] = grad
                if padded is not None:
                    padded[pl.ds(pl.multiple_of(both_base(g) + i * step, ROWS), step)] = grad

    mid_step(h5, mid_back(3, 3, sums, total_out), dhp)
    for g in groups:
        halo_down[halo_rows(g)] = low(last_row(h5, g))
        halo_up[halo_rows(g)] = low(first_row(h5, g))
    send_down(halo_down, dhp, 1)
    send_up(halo_up, 2)
    def spatial_tile(window_of, grads):
        def value_of(t):
            parts = [
                t_times(window_of(g, t // 3, lax.rem(t, 3)), grads[group_rows(g)]) for g in groups
            ]
            return parts[0] + parts[1] + parts[2]

        return value_of

    def spatial_maker(window_of, grads):
        tile = spatial_tile(window_of, grads)
        return lambda done: lambda i, unit: put(tile(done + i), unit, 1, 0)

    make_b = spatial_maker(window_b, h5)
    clear_acc()
    conv_taps(3, 6, window_b_back, times_t, make_b(0))
    halo_wait(halo_down, halo_recv, 1, h > 0)
    halo_wait(halo_in, halo_recv, 2, h < n_height - 1)
    place_below(dhp)
    conv_taps(0, 3, window_b_back, times_t, make_b(3))
    conv_taps(6, 9, window_b_back, times_t)
    fetch(spatial_a, wp, w_sem.at[0])
    sums = mid_gradient(h4, 2)
    state = sums_start(sums)
    halo_wait(halo_down, halo_send, 1, h < n_height - 1)
    halo_wait(halo_up, halo_send, 2, h > 0)
    sums_middle(state)

    produce("spatial_b", 3, 1, make_b(6))
    sums = sums_end(state)

    mid_step(h4, mid_back(2, 2, sums, total_out), None)
    fetch_plane(0, 1, a4p, x_sem.at[1])

    tick = ticks(8)

    @pl.loop(0, 4)
    def _(n):
        def body(i, carry):
            tick(2 * n + i)
            rows = pl.ds(pl.multiple_of(i * half, ROWS), half)
            grad = times_t(h4[rows], wq[4 + n]) + up32(dz[n, rows])
            grad = grad * slope_of(half_joint(n, rows)) * half_mask(rows)
            dz[n, rows] = low(grad)
            main_hat = up32(h3[n, rows]) * out_stat(0, n, 1) + out_stat(0, n, 4)
            side_hat = up32(side[n, rows]) * out_stat(1, n, 1) + out_stat(1, n, 4)
            return (
                carry[0] + fold(grad),
                carry[1] + fold(grad * main_hat),
                carry[2] + fold(grad * side_hat),
            )

        sums = lax.fori_loop(0, 2, body, (zero8, zero8, zero8))
        for v in range(3):
            stat_out[pl.ds(4 * v + n, 1)] = one_row(sums[v])

    state = wide_start(None)
    sums_middle(state)

    def tile_reduce_b(step, unit):
        @pl.loop(0, 4)
        def _(t):
            put(t_times(mb[t], h4[...]), unit, 4, t * (n_batch // 4))

    produce("reduce_b", 1, 4, tile_reduce_b)
    for p in range(4):
        fetch_plane(p, 0, mb.at[p], x_sem.at[0])
    clear_acc()
    sums_end(state)

    arrived(wq.at[0:4], w_sem.at[1])

    def expansion_back(n):
        main, slope, constant = out_back(0, 0, 4, n)
        main2, slope2, constant2 = out_back(1, 0, 8, n)

        @pl.loop(0, 2)
        def _(i):
            rows = pl.ds(pl.multiple_of(i * half, ROWS), half)
            grad_in = up32(dz[n, rows])
            mask = wide_mask(mask_ref[rows])
            grad = low((main * grad_in + slope * up32(h3[n, rows]) + constant) * mask)
            h3[n, rows] = grad
            acc[rows] += times_t(grad, wq[n])
            other = main2 * grad_in + slope2 * up32(side[n, rows]) + constant2
            side[n, rows] = low(other * mask)

    run("expand_a", 4, expansion_back, lambda n, unit: put(t_times(a2[...], h3[n]), unit, 1, 0))
    fetch(h1_kept, h1, spill_sem.at[0])
    fetch_shortcut()
    sums = mid_gradient(h2, 1)
    state = sums_start(sums)
    sums_middle(state)
    for p in range(4):
        plane_arrived(mb.at[p], x_sem.at[0])
    plane_arrived(a4p, x_sem.at[1])

    def tile_shortcut(t, unit):
        put(t_times(mb[0], side[t]), unit, 2, 0)
        put(t_times(a4p[0:total], side[t]), unit, 2, n_batch // 2)

    produce("shortcut_a", 1, 2, lambda step, unit: tile_shortcut(0, unit))
    sums = sums_end(state)

    mid_step(h2, mid_back(1, 1, sums, total_out), dhp)
    for g in groups:
        halo_up[halo_rows(g)] = low(first_row(h2, g))
    send_up(halo_up, 2)
    arrived(wp, w_sem.at[0])
    arrived(h1, spill_sem.at[0])
    root, scale = stat_mid[0, 1:2], stat_mid[0, 5:6]
    offset, back = stat_mid[0, 6:7], stat_mid[0, 4:5]
    carry = (zero8, zero8)
    for p in range(4):
        py, px = p // 2, p % 2
        row_taps = ((1, 0),) if py == 0 else ((0, 1), (2, 0))
        column_taps = ((1, 0),) if px == 0 else ((0, 1), (2, 0))
        if p == 2:
            halo_wait(halo_in, halo_recv, 2, h < n_height - 1)
            place_below(dhp)
        for g in groups:
            value = None
            for a, dy in row_taps:
                for c, dx_ in column_taps:
                    product = times_t(window(dhp, both_starts[g], g, dy, dx_), wp[3 * a + c])
                    value = product if value is None else value + product
            acc[group_rows(g)] = value

        def body(i, carry):
            rows = steps(i)
            value = up32(h1[p, rows])
            grad = acc[rows] * slope_of(value * scale + offset) * half_mask(rows)
            h3[p, rows] = low(grad)
            return carry[0] + fold(grad), carry[1] + fold(grad * (value * root + back))

        carry = lax.fori_loop(0, total // part, body, carry)
        if p > 0:
            produce("shortcut_a", 1, 2, lambda step, unit: tile_shortcut(p, unit))
    state = sums_start([one_row(v) for v in carry])
    halo_wait(halo_up, halo_send, 2, h > 0)
    sums_middle(state)
    arrived(big_a, spill_sem.at[1])
    make_a = spatial_maker(window_a, h2)
    produce("spatial_a", 3, 1, make_a(0))
    sums = sums_end(state)

    main, slope, constant = mid_back(0, 0, sums, total_in)

    def first_back(p):
        @pl.loop(0, total // part)
        def _(i):
            rows = steps(i)
            grad = main * up32(h3[p, rows]) + slope * up32(h1[p, rows]) + constant
            h1[p, rows] = low(grad * wide_mask(mask_ref[rows]))

        fetch_plane(p, 1, h3.at[p], x_sem.at[1])

    run("spatial_a", 4, first_back, make_a(3))
    produce("spatial_a", 2, 1, make_a(7))
    for p in range(4):
        plane_arrived(h3.at[p], x_sem.at[1])

    def last_tile(chunk):
        value = t_times(chunk(0), h1[0])
        for p in range(1, 4):
            value = value + t_times(chunk(p), h1[p])
        return value

    def tile_reduce_a(step, unit):
        put(last_tile(lambda p: mb[p]), unit, 2, 0)
        put(last_tile(lambda p: h3[p]), unit, 2, n_batch // 2)

    produce("reduce_a", 1, 2, tile_reduce_a)
    arrived(wq, w_sem.at[1])
    for k in range(2):
        tick_13 = ticks(2)

        @pl.loop(0, 2)
        def _(i):
            rows = pl.ds(pl.multiple_of(i * half, ROWS), half)
            value = times_t(h1[0, rows], w2[k])
            for n in range(4):
                value = value + times_t(side[n, rows], wq[2 * n + k])
            if k == 0:
                big_a[0, rows] = low(value)
            else:
                a4p[rows] = low(value)
            tick_13(i)

    put_plane(0, 0, big_a.at[0])
    put_plane(0, 1, a4p)
    tick_13p = ticks(3)

    @pl.loop(1, 4)
    def _(p):
        big_a[p, 0:total] = low(times_t(h1[p], w2[0]))
        side[p] = low(times_t(h1[p], w2[1]))
        put_plane(p, 0, big_a.at[p])
        put_plane(p, 1, side.at[p])
        tick_13p(p - 1)

    idle(rounds[-1][0] - 6)
    others = pool_slots.at[0 : n_height - 1]
    pltpu.make_async_copy(others, others, pool_sem.at[1]).wait()
    pltpu.make_async_copy(others, others, pool_sem.at[0]).wait()
    for g in groups:
        for n in range(4):
            value = None
            for k in range(n_height):
                part = up32(pool_slots[k, n, g * ROWS : (g + 1) * ROWS])
                value = part if value is None else value + part
            pooled[g, n] = value * (1.0 / (widths[g] * widths[g]))

    for slot in range(ready.shape[0]):
        arrived(ready.at[slot], ready_sem.at[slot])
    for p in range(8):
        plane_arrived(a4p, dx_sem.at[0])


def to_planes(image):
    count, rows, cols, channels = image.shape
    value = jnp.pad(image, ((0, ROWS - count), (0, 0), (0, 0), (0, 0)))
    value = jnp.transpose(value, (1, 2, 0, 3))
    return value.reshape(rows // 2, 2, cols // 2, 2, ROWS, channels)


def from_planes(planes, shape):
    count, rows, cols, channels = shape
    value = planes.reshape(rows, cols, ROWS, channels)[:, :, :count]
    return jnp.transpose(value, (2, 0, 1, 3))


def per_device(
    image_small, image_medium, image_large, row_counts, reduce_a, first_spatial_weight, expand_a,
    shortcut_a, reduce_b, second_spatial_weight, expand_b, gain_mid, shift_mid, gain_out,
    shift_out, upstream_small, upstream_medium, upstream_large,
):
    images = (image_small, image_medium, image_large)
    upstreams = (upstream_small, upstream_medium, upstream_large)
    n_batch, n_height = lax.axis_size("batch"), lax.axis_size("height")
    heights = [value.shape[1] // 2 for value in images]
    widths = [value.shape[2] // 2 for value in images]
    count = images[0].shape[0]
    pixels = sum(o * o for o in widths) * count * n_batch
    counts, starts, top_total, _, both_total, _, _ = grids(heights, widths)
    total = sum(counts) * ROWS
    planes = [to_planes(image) for image in images]
    up = jnp.pad(jnp.stack(upstreams), ((0, 0), (0, ROWS - count), (0, 0)))
    up = jnp.transpose(up.reshape(3, ROWS, 4, WIDE), (0, 2, 1, 3))
    halo = sum(widths) * ROWS
    bf, f32 = jnp.bfloat16, jnp.float32
    unit_rows, n_rest = WIDE // n_batch, n_batch // 2
    n_thin = n_batch * n_height if n_batch * n_height <= 64 else n_batch + n_height
    dma = pltpu.SemaphoreType.DMA
    vmem = pl.BlockSpec(memory_space=pltpu.VMEM)
    anywhere = pl.BlockSpec(memory_space=pl.ANY)
    flat_a = first_spatial_weight.reshape(9, WIDE, WIDE)
    flat_b = second_spatial_weight.reshape(9, WIDE, WIDE)
    big = pltpu.VMEM((4, total, WIDE), bf)
    thin = pltpu.VMEM((total, WIDE), bf)
    results = pl.pallas_call(
        functools.partial(
            main_kernel, n_batch, n_height, heights, widths, count, float(4 * pixels),
            float(pixels)
        ),
        out_shape=[
            jax.ShapeDtypeStruct((3, 4, ROWS, WIDE), f32),
            *[jax.ShapeDtypeStruct(value.shape, bf) for value in planes],
            *[
                jax.ShapeDtypeStruct(w.shape[:-2] + (w.shape[-2] // n_batch, w.shape[-1]), f32)
                for w in (reduce_a, flat_a, expand_a, shortcut_a, reduce_b, flat_b, expand_b)
            ],
            *[jax.ShapeDtypeStruct(w.shape, f32) for w in (gain_mid, shift_mid, gain_out, shift_out)],
            jax.ShapeDtypeStruct((4, total, WIDE), bf),
            jax.ShapeDtypeStruct((4, top_total * ROWS, WIDE), bf),
        ],
        in_specs=[anywhere] * 10 + [pl.BlockSpec(memory_space=pltpu.SMEM)] + [vmem] * 5,
        out_specs=[vmem] + [anywhere] * 10 + [vmem] * 4 + [anywhere] * 2,
        scratch_shapes=[
            pltpu.VMEM((3, max(heights), 8, 128), f32),
            pltpu.VMEM((total, 128), bf),
            big,
            pltpu.VMEM((4, top_total * ROWS, WIDE), bf),
            big, big, big,
            thin, thin, thin, thin, thin,
            pltpu.VMEM((both_total * ROWS, WIDE), bf),
            pltpu.VMEM((both_total * ROWS, WIDE), bf),
            pltpu.VMEM((total, WIDE), f32),
            pltpu.VMEM((9, WIDE, WIDE), bf),
            pltpu.VMEM((8, WIDE, WIDE), bf),
            pltpu.VMEM((2, WIDE, WIDE), bf),
            pltpu.VMEM((halo, WIDE), bf),
            pltpu.VMEM((halo, WIDE), bf),
            pltpu.VMEM((halo, WIDE), bf),
            pltpu.VMEM((12, 2, 2, n_rest, unit_rows, 128), bf),
            pltpu.VMEM((5, 2, 2, n_rest, unit_rows, 128), bf),
            pltpu.VMEM((6, 2, 2, n_rest, unit_rows, 128), bf),
            pltpu.VMEM((6, 2, n_rest, unit_rows, 128), bf),
            pltpu.VMEM((6, n_rest, unit_rows, 128), bf),
            pltpu.VMEM((6, n_rest - 1, unit_rows, 128), bf),
            pltpu.VMEM((8, 2, 2, unit_rows, 128), bf),
            pltpu.VMEM((3, unit_rows, WIDE), f32),
            pltpu.VMEM((n_height, 4, 3 * ROWS, WIDE), bf),
            pltpu.VMEM((2, n_thin, 8, 128), f32),
            pltpu.VMEM((n_height, 16, WIDE), f32),
            pltpu.VMEM((n_batch, 16, WIDE), f32),
            pltpu.VMEM((16, 8, WIDE), f32),
            pltpu.VMEM((16, WIDE), f32),
            dma((4,)), dma((2,)), dma((6, 16)), dma((6, 16)), dma((3,)), dma((1,)), dma((2,)),
            dma((2, 2, 2)), dma((2, 2, 2)), dma((3,)), dma((3,)), dma((2,)),
        ],
        compiler_params=pltpu.CompilerParams(
            collective_id=0, has_side_effects=True, vmem_limit_bytes=63 << 20
        ),
        name="both_blocks",
    )(
        *planes, reduce_a, flat_a, expand_a, shortcut_a, reduce_b, flat_b, expand_b,
        row_counts, gain_mid, shift_mid, gain_out, shift_out, up,
    )
    pooled = jnp.transpose(results[0], (0, 2, 1, 3)).reshape(3, ROWS, -1)[:, :count]
    backs = [from_planes(results[1 + g], images[g].shape) for g in range(3)]
    shards = list(results[4:11])
    for place in (1, 5):
        shards[place] = shards[place].reshape((3, 3) + shards[place].shape[1:])
    return (pooled[0], pooled[1], pooled[2], *backs, *shards, *results[11:15])


def solution(mesh):
    placed = (
        P("batch", "height", None, None),
        P("batch", "height", None, None),
        P("batch", "height", None, None),
        P(),
        P(),
        P(),
        P(),
        P(),
        P(),
        P(),
        P(),
        P(),
        P(),
        P(),
        P(),
        P("batch", None),
        P("batch", None),
        P("batch", None),
    )
    return jax.shard_map(
        per_device,
        mesh=mesh,
        in_specs=placed,
        out_specs=(
            P("batch", None),
            P("batch", None),
            P("batch", None),
            P("batch", "height", None, None),
            P("batch", "height", None, None),
            P("batch", "height", None, None),
            P("batch", None),
            P(None, None, "batch", None),
            P("batch", None),
            P("batch", None),
            P("batch", None),
            P(None, None, "batch", None),
            P("batch", None),
            P(),
            P(),
            P(),
            P(),
        ),
        check_vma=False,
    )
```
